32 devices in a mesh: members: 2 (over y), loop: 8 (over z, x), lat: 2 (over core).
Axes of the slice: x: 2, y: 2, z: 4, core: 2. Of those that a mesh axis runs over, the one named last changes fastest.
Arguments:
- state: float32 [4, 50, 64, 256], P('members', None, 'loop', 'lat'), parts along dimension 0, may hold values from -6 to 6
- observed: float32 [4, 50, 64, 256], P('members', None, 'loop', 'lat'), parts along dimension 0, may hold values from -4.5 to 6
- weight: float32 [50, 64, 256], P(None, 'loop', 'lat'), may hold values from 0.2 to 2
- control: float32 [4, 64, 256], P('members', 'loop', 'lat'), parts along dimension 0, may hold values from -6 to 6
- depth_index: int32 [64, 256], P('loop', 'lat'), may hold values from 0 to 50
- diffusivity: float32 [64, 256], P('loop', 'lat'), may hold values from 0.02 to 0.22
- damping: float32 [64, 256], P('loop', 'lat'), may hold values from 0.25 to 2
- history_step: float32 [16, 2, 64, 256], P('members', None, 'loop', 'lat'), parts along dimension 0, may hold values from -0.5 to 0.5
- history_change: float32 [16, 2, 64, 256], P('members', None, 'loop', 'lat'), parts along dimension 0, may hold values from -2.5 to 2.5, as said below
Outputs:
- state_next: float32 [4, 50, 64, 256], P('members', None, 'loop', 'lat'), parts along dimension 0
- gradient: float32 [4, 64, 256], P('members', 'loop', 'lat'), parts along dimension 0
- direction: float32 [4, 64, 256], P('members', 'loop', 'lat'), parts along dimension 0
The draws below stay inside these ranges and needn't reach their ends.
There are 2 independent parts, one for each index of `members`. The reference program is written for one: setup_inputs(seed, part) draws one part's arguments, and reference() takes and returns one part's arrays. A program takes and returns all parts, laid end to end along the dimension named above; an argument that names none is the same for every part. Nothing has to cross between parts.
Inputs may be any that keep to these rules, and one draw needn't show every extreme that they name: `history_change`: each entry of a stored change has the sign of the matching entry of its step, so that every pair's inner product is positive.
All inputs are finite; a program needn't handle non-finite values.
Results may differ from the reference program's by a relative error of at most 0.0003.
Values sent between devices are 32-bit elements; how exact they have to be, the bound alone decides.
No kernel may reach another device: no remote copies, remote signals or barrier semaphores. Data moves between devices by JAX's collectives and lax.ppermute only.
A program may use at most 64 MiB of HBM per device.

```python
import math
import jax
import jax.numpy as jnp

LEV = 50
ITERS = 3
SUB = 3
HIST = 8
NX = 64
NY = 256


def bump_fields(key, count):
    subkeys = jax.random.split(key, 4)
    wave_x = jax.random.randint(subkeys[0], (count, 2, 1, 1), 1, 4).astype(jnp.float32)
    wave_y = jax.random.randint(subkeys[1], (count, 2, 1, 1), 1, 3).astype(jnp.float32)
    phase_x = jax.random.uniform(subkeys[2], (count, 2, 1, 1), jnp.float32, -math.pi, math.pi)
    phase_y = jax.random.uniform(subkeys[3], (count, 2, 1, 1), jnp.float32, -math.pi, math.pi)
    x_angle = jnp.arange(NX, dtype=jnp.float32)[:, None] * (2.0 * math.pi / NX)
    y_angle = jnp.arange(NY, dtype=jnp.float32)[None, :] * (math.pi / NY)
    return 1.0 + 0.5 * jnp.sin(wave_x * x_angle + phase_x) * jnp.cos(wave_y * y_angle + phase_y)


def stored_steps(key):
    noise_key = jax.random.fold_in(key, 11)
    normal_part = jnp.clip(jax.random.normal(noise_key, (HIST, 2, NX, NY), jnp.float32), -4.0, 4.0)
    noise = normal_part
    bumps = bump_fields(jax.random.fold_in(key, 13), HIST)
    return 0.08 * (noise + bumps)


def draw_observed(key, part):
    key = jax.random.fold_in(key, 5)
    noise_key = jax.random.fold_in(key, 1)
    bump_key = jax.random.fold_in(key, 2)
    noise = jnp.clip(jax.random.normal(noise_key, (2, LEV, NX, NY), jnp.float32), -4.0, 4.0)
    offset = bump_fields(bump_key, 1)[0]
    return noise + offset[:, None]


def draw_history_step(key, part):
    steps = stored_steps(key)
    return steps


def draw_history_change(key, part):
    lowest = math.log(0.5)
    highest = math.log(2.0)
    steps = stored_steps(key)
    key = jax.random.fold_in(key, 7)
    shared = jnp.exp(jax.random.uniform(jax.random.fold_in(key, 1), (1, 2, NX, NY), jnp.float32, lowest, highest))
    per_pair = jnp.exp(jax.random.uniform(jax.random.fold_in(key, 2), (HIST, 2, NX, NY), jnp.float32, math.log(0.8), math.log(1.25)))
    return steps * shared * per_pair


def with_ends(drawn, rng, smallest, high):
    extent = drawn.shape
    index_at = [jax.random.randint(jax.random.fold_in(rng, axis), (), 0, extent[axis]) for axis in range(len(extent))]
    drawn = drawn.at[tuple(index_at)].set(smallest)
    longest = extent.index(max(extent))
    index_at[longest] = (index_at[longest] + 1) % extent[longest]
    return drawn.at[tuple(index_at)].set(high)


def shard_levels(rng, dims, cuts, low, largest):
    def one(axis_at, shards_of):
        draws = jax.random.uniform(jax.random.fold_in(jax.random.fold_in(rng, 6), axis_at), (shards_of,), jnp.float32, low / len(cuts), largest / len(cuts))
        return jnp.repeat(jnp.exp(draws), dims[axis_at] // shards_of).reshape((-1,) + (1,) * (len(dims) - axis_at - 1))

    factor_of = one(*cuts[0])
    for cut in cuts[1:]:
        factor_of = factor_of * one(*cut)
    return factor_of


def gaussian(rng, shape, width, reach, shards=(), kind=jnp.bfloat16):
    values = jax.random.normal(rng, shape, jnp.float32) * width
    if len(shards) > 0:
        values = shard_levels(rng, shape, shards, -0.22, 0.18) * values
    return jnp.clip(values, min=-reach, max=reach).astype(kind)


def setup_inputs(seed: int = 0, part: int = 0) -> dict:
    key_list = jax.random.split(jax.random.key(seed), 10)
    own_keys = jax.random.split(jax.random.fold_in(key_list[9], part), 10)
    state = gaussian(own_keys[0], (2, LEV, NX, NY), 1.0, 6.0, ((2, 8), (3, 2)), jnp.float32)
    observed = draw_observed(jax.random.fold_in(jax.random.fold_in(key_list[9], part), 71), part)
    weight = jnp.clip(jnp.exp(math.log(2.0) - 2.3025851 * jax.random.uniform(key_list[2], (LEV, NX, NY), jnp.float32) ** shard_levels(key_list[2], (LEV, NX, NY), ((1, 8), (2, 2)), -0.2, 0.2)), 0.2, 2.0)
    control = gaussian(own_keys[3], (2, NX, NY), 1.0, 6.0, ((1, 8), (2, 2)), jnp.float32)
    depth_index = with_ends(jax.random.randint(key_list[4], (NX, NY), 0, LEV + 1), jax.random.fold_in(key_list[4], 1), 0, LEV).astype(jnp.int32)
    diffusivity = jnp.clip(jnp.exp(math.log(0.22) - 2.3978953 * jax.random.uniform(key_list[5], (NX, NY), jnp.float32) ** shard_levels(key_list[5], (NX, NY), ((0, 8), (1, 2)), -0.2, 0.2)), 0.02, 0.22)
    damping = jnp.clip(jnp.exp(math.log(2.0) - 2.0794415 * jax.random.uniform(key_list[6], (NX, NY), jnp.float32) ** shard_levels(key_list[6], (NX, NY), ((0, 8), (1, 2)), -0.2, 0.2)), 0.25, 2.0)
    history_step = draw_history_step(jax.random.fold_in(jax.random.fold_in(key_list[9], part), 71), part)
    history_change = draw_history_change(jax.random.fold_in(jax.random.fold_in(key_list[9], part), 71), part)
    return dict(state=state, observed=observed, weight=weight, control=control, depth_index=depth_index, diffusivity=diffusivity, damping=damping, history_step=history_step, history_change=history_change)


SURFACE_GAIN = 5.0
NEIGHBOURS = ((0, 1), (2, 1), (1, 0), (1, 2))


def pad_wrap(array):
    rows = array.shape[-2]
    array = jnp.concatenate([array[..., rows - 1:, :], array, array[..., :1, :]], axis=-2)
    widths = [(0, 0)] * (array.ndim - 1) + [(1, 1)]
    return jnp.pad(array, widths)


def smooth(field, depths, spread, levels):
    rows = field.shape[-2] - 2
    cols = field.shape[-1] - 2
    centre = field[..., 1:rows + 1, 1:cols + 1]
    depth_here = depths[1:rows + 1, 1:cols + 1]
    spread_here = spread[1:rows + 1, 1:cols + 1]
    total = centre
    for row_at, col_at in NEIGHBOURS:
        beside = field[..., row_at:row_at + rows, col_at:col_at + cols]
        depth_there = depths[row_at:row_at + rows, col_at:col_at + cols]
        spread_there = spread[row_at:row_at + rows, col_at:col_at + cols]
        open_face = (levels < jnp.minimum(depth_here, depth_there)).astype(jnp.float32)
        total = total + 0.5 * (spread_here + spread_there) * open_face * (beside - centre)
    return total


def couplings_of(depths, spread):
    rows = depths.shape[0] - 2
    cols = depths.shape[1] - 2
    wet_here = (depths[1:rows + 1, 1:cols + 1] > 0.5).astype(jnp.float32)
    spread_here = spread[1:rows + 1, 1:cols + 1]
    result = []
    for row_at, col_at in NEIGHBOURS:
        wet_there = (depths[row_at:row_at + rows, col_at:col_at + cols] > 0.5).astype(jnp.float32)
        spread_there = spread[row_at:row_at + rows, col_at:col_at + cols]
        result.append(SURFACE_GAIN * 0.5 * (spread_here + spread_there) * wet_here * wet_there)
    return result


def surface_apply(padded, couplings, damping):
    rows = padded.shape[0] - 2
    cols = padded.shape[1] - 2
    centre = padded[1:rows + 1, 1:cols + 1]
    total = damping * centre
    for (row_at, col_at), coupling in zip(NEIGHBOURS, couplings):
        total = total + coupling * (centre - padded[row_at:row_at + rows, col_at:col_at + cols])
    return total


def conjugate(rhs, couplings, damping):
    solution = jnp.zeros_like(rhs)
    residual = rhs
    search = rhs
    norm_now = jnp.sum(residual * residual)
    for sweep in range(ITERS):
        image = surface_apply(pad_wrap(search), couplings, damping)
        alpha = norm_now / jnp.sum(search * image)
        solution = solution + alpha * search
        residual = residual - alpha * image
        norm_next = jnp.sum(residual * residual)
        search = residual + (norm_next / norm_now) * search
        norm_now = norm_next
    return solution


def reference(state, observed, weight, control, depth_index, diffusivity, damping, history_step, history_change):
    levels = jnp.arange(LEV, dtype=jnp.float32)[:, None, None]
    depth = depth_index.astype(jnp.float32)
    depth_pad = pad_wrap(depth)
    spread_pad = pad_wrap(diffusivity)
    column_mask = (levels < depth).astype(jnp.float32)
    sea_top = (depth > 0.5).astype(jnp.float32)
    couplings = couplings_of(depth_pad, spread_pad)
    scale = LEV ** -0.5

    def mixing(field):
        for sweep in range(SUB):
            field = smooth(pad_wrap(field), depth_pad, spread_pad, levels)
        return field

    lifted = state.at[:, 0].add(sea_top * control)
    mixed = mixing(lifted)
    buoyancy = scale * jnp.sum(column_mask * (mixed[0] - mixed[1]), axis=0)
    elevation = conjugate(buoyancy, couplings, damping)
    lowered = column_mask * elevation
    state_next = jnp.stack([mixed[0] - lowered, mixed[1] + lowered])

    misfit = weight * (state_next - observed)
    pressure = jnp.sum(column_mask * (misfit[1] - misfit[0]), axis=0)
    response = conjugate(pressure, couplings, damping)
    raised = scale * column_mask * response
    carried = jnp.stack([misfit[0] + raised, misfit[1] - raised])
    returned = mixing(carried)
    gradient = sea_top * returned[:, 0]

    rho = [1.0 / jnp.sum(history_step[index] * history_change[index]) for index in range(HIST)]
    last = history_change[HIST - 1]
    gamma = jnp.sum(history_step[HIST - 1] * last) / jnp.sum(last * last)
    factors = [None] * HIST
    carry = gradient
    for index in range(HIST - 1, -1, -1):
        factors[index] = rho[index] * jnp.sum(history_step[index] * carry)
        carry = carry - factors[index] * history_change[index]
    result = gamma * carry
    for index in range(HIST):
        beta = rho[index] * jnp.sum(history_change[index] * result)
        result = result + (factors[index] - beta) * history_step[index]
    return state_next, gradient, -result
```

```python
import functools

import jax
import jax.numpy as jnp
from jax import lax
from jax.experimental import pallas as pl
from jax.experimental.pallas import tpu as pltpu
from jax.sharding import PartitionSpec as P

ITERS = 3
SUB = 3
SURFACE_GAIN = 5.0
SLOT = 8
GRID = ("loop", "lat")
VMEM = pl.BlockSpec(memory_space=pltpu.VMEM)
F32 = jnp.float32


def round_up(value, to):
    return (value + to - 1) // to * to


def call(kernel, out_shapes, scratch=(), vmem=32 * 1024 * 1024, name=None):
    return pl.pallas_call(
        kernel,
        out_shape=[jax.ShapeDtypeStruct(shape, F32) for shape in out_shapes],
        out_specs=[VMEM] * len(out_shapes),
        scratch_shapes=list(scratch),
        compiler_params=pltpu.CompilerParams(vmem_limit_bytes=vmem),
        name=name,
    )


def iota(shape, dim):
    return lax.broadcasted_iota(jnp.int32, shape, dim)


def pack_kernel(
    levels, padded, state_ref, control_ref, depth_ref, spread_ref, damping_ref, weight_ref,
    rows_ref, up_ref, down_ref, still_ref,
):
    rows, cols = depth_ref.shape
    depth = depth_ref[...].astype(F32)
    spread = spread_ref[...]
    first = iota((levels, cols), 0) == 0
    rest = jnp.zeros((padded - levels, cols), F32)
    for row in range(rows):
        for tracer in range(2):
            lift = jnp.where(depth[row : row + 1] > 0.5, control_ref[tracer, row : row + 1, :], 0.0)
            value = state_ref[tracer, pl.ds(row, levels, stride=rows), :]
            rows_ref[row, pl.ds(tracer * padded, levels), :] = value + jnp.where(first, lift, 0.0)
            rows_ref[row, pl.ds(tracer * padded + levels, padded - levels), :] = rest
        rows_ref[row, pl.ds(levels, 1), :] = spread[row : row + 1]
        rows_ref[row, pl.ds(levels + 1, 1), :] = depth[row : row + 1]
        if row < SUB:
            down_ref[row] = rows_ref[row]
        if row >= rows - SUB:
            up_ref[row - rows + SUB] = rows_ref[row]
    total = jnp.zeros((rows, cols), F32)
    for level in range(levels):
        total = total + jnp.where(level < depth, weight_ref[pl.ds(level * rows, rows), :], 0.0)
    still_ref[0] = 2.0 * total
    still_ref[1] = weight_ref[pl.ds(0, rows), :]
    still_ref[2] = spread
    still_ref[3] = depth
    still_ref[4] = damping_ref[...]


def edge_of(rows_of, indices, cols, lat):
    lane = iota((1, cols), 1)
    slot = lane // SLOT
    place = lane % SLOT - SUB * lat
    mine = (place >= 0) & (place < SUB)
    total = None
    for index in indices:
        moved = pltpu.roll(rows_of(index), SLOT * index + SUB, 1)
        piece = jnp.where(mine & (slot == index), moved, 0.0)
        total = piece if total is None else total + piece
    return total


def pairs_kernel(rows_ref, step_ref, change_ref, edge_ref, gram_ref):
    rows, _, cols = rows_ref.shape
    lat = lax.axis_index("lat")
    edge_ref[...] = edge_of(lambda i: rows_ref[i - SUB], range(SUB, rows + SUB), cols, lat)
    count = step_ref.shape[0]
    lane = iota((1, cols), 1)
    total = jnp.zeros((1, cols), F32)
    at = 2 * count
    for left_ref in (step_ref, change_ref):
        for i in range(count):
            for j in range(i, count):
                value = jnp.sum(left_ref[i] * change_ref[j], axis=(0, 1), keepdims=True)
                total = total + jnp.where(lane == at, value, 0.0)
                at += 1
    gram_ref[...] = total


def border_kernel(edge_ref, low_ref, high_ref, rows_ref, out_ref):
    cols = edge_ref.shape[-1]
    rows = rows_ref.shape[0]
    lat = lax.axis_index("lat")
    total = edge_ref[...] + edge_of(lambda i: low_ref[i], range(SUB), cols, lat)
    out_ref[...] = total + edge_of(
        lambda i: high_ref[i - rows - SUB], range(rows + SUB, rows + 2 * SUB), cols, lat
    )


def mix_kernel(
    levels, padded, scale, copies,
    rows_ref, low_ref, high_ref, edge_ref, other_ref, weight_ref, observed_ref,
    mixed_ref, fields_ref, work_ref, row_face_ref, col_face_ref, part_ref,
):
    rows, planes, cols = rows_ref.shape
    lat = lax.axis_index("lat")
    lane = iota((1, cols), 1)
    level = iota((padded, cols), 0).astype(F32)
    count = rows + 2 * SUB
    work_ref[pl.ds(0, SUB)] = low_ref[...]
    work_ref[pl.ds(SUB, rows)] = rows_ref[...]
    work_ref[pl.ds(SUB + rows, SUB)] = high_ref[...]

    def left(value, by=1):
        return pltpu.roll(value, cols - by, 1)

    def right(value, by=1):
        return pltpu.roll(value, by, 1)

    def face(depth_here, depth_there, spread_here, spread_there):
        opened = level < jnp.minimum(depth_here, depth_there)
        return jnp.where(opened, 0.5 * (spread_here + spread_there), 0.0)

    spreads = [work_ref[i, pl.ds(levels, 1), :] for i in range(count)]
    depths = [work_ref[i, pl.ds(levels + 1, 1), :] for i in range(count)]
    for i in range(count - 1):
        row_face_ref[i] = face(depths[i], depths[i + 1], spreads[i], spreads[i + 1])
    for i in range(1, count - 1):
        there = jnp.where(lane < cols - 1, left(depths[i]), 0.0)
        col_face_ref[i] = face(depths[i], there, spreads[i], left(spreads[i]))

    strip = edge_ref[...] + other_ref[...]
    spread = strip[levels : levels + 1]
    depth = strip[levels + 1 : levels + 2]
    within = lane % SLOT < 2 * SUB - 1
    strip_col = face(depth, jnp.where(within, left(depth), 0.0), spread, left(spread))
    strip_row = face(depth, left(depth, SLOT), spread, left(spread, SLOT))

    first = lat == 0
    target = jnp.where(first, cols - 1, 0)
    at_border = lane == target
    for tracer in range(2):
        part = strip[tracer * padded : (tracer + 1) * padded]
        here = pl.ds(tracer * padded, padded)
        for sweep in range(1, SUB + 1):
            over_col = strip_col * (left(part) - part)
            inward = jnp.where(first, over_col, -right(over_col))
            last = None
            for i in range(sweep, count - sweep):
                centre = work_ref[i, here, :]
                if last is None:
                    last = row_face_ref[i - 1] * (centre - work_ref[i - 1, here, :])
                over_row = row_face_ref[i] * (work_ref[i + 1, here, :] - centre)
                across = col_face_ref[i] * (left(centre) - centre)
                border = right(inward, (cols - 1 - (SUB - 1) - SLOT * i) % cols)
                value = centre + (over_row - last) + (across - right(across))
                value = value + jnp.where(at_border, border, 0.0)
                last = over_row
                if sweep < SUB:
                    work_ref[i, here, :] = value
                else:
                    work_ref[i, here, :] = value
            if sweep < SUB:
                over_row = strip_row * (left(part, SLOT) - part)
                part = part + (over_col - right(over_col)) + (over_row - right(over_row, SLOT))

    for row in range(rows):
        i = row + SUB
        at = pl.ds(row, levels, stride=rows)
        mixed = [work_ref[i, pl.ds(tracer * padded, levels), :] for tracer in range(2)]
        wet = level[:levels] < depths[i]
        weight = weight_ref[at, :]
        misfit = []
        for tracer in range(2):
            mixed_ref[tracer, at, :] = mixed[tracer]
            misfit.append(weight * (mixed[tracer] - observed_ref[tracer, at, :]))
        here = pl.ds(row, 1)
        part_ref[0, here, :] = scale * jnp.sum(
            jnp.where(wet, mixed[0] - mixed[1], 0.0), axis=0, keepdims=True
        )
        part_ref[1, here, :] = jnp.sum(
            jnp.where(wet, misfit[1] - misfit[0], 0.0), axis=0, keepdims=True
        )
        part_ref[2, here, :] = misfit[0][0:1]
        part_ref[3, here, :] = misfit[1][0:1]
    for copy in range(copies):
        fields_ref[copy] = part_ref[...]


def solve_kernel(
    levels, scale,
    fields_ref, still_ref, mixed_ref, step_ref, change_ref, gram_ref,
    state_ref, gradient_ref, inner_ref, own_ref,
):
    blocks, _, rows, cols = fields_ref.shape
    lats = 2
    loops = blocks // lats
    height = loops * rows
    width = lats * cols
    mine_loop = lax.axis_index("loop")
    mine_lat = lax.axis_index("lat")

    def whole(ref, field):
        return jnp.concatenate(
            [
                jnp.concatenate([ref[lats * i + j, field] for j in range(lats)], axis=1)
                for i in range(loops)
            ],
            axis=0,
        )

    def below(value):
        return pltpu.roll(value, height - 1, 0)

    def above(value):
        return pltpu.roll(value, 1, 0)

    def left(value):
        return pltpu.roll(value, width - 1, 1)

    def right(value):
        return pltpu.roll(value, 1, 1)

    def total(value):
        return jnp.sum(value, axis=(0, 1), keepdims=True)

    buoyancy, pressure_base, base_0, base_1 = (whole(fields_ref, f) for f in range(4))
    response_weight, weight, spread, depth, damping = (whole(still_ref, f) for f in range(5))
    wet = jnp.where(depth > 0.5, 1.0, 0.0)
    inside = iota((height, width), 1) < width - 1
    row_face = 0.5 * (spread + below(spread)) * wet * below(wet)
    col_face = jnp.where(inside, 0.5 * (spread + left(spread)) * wet * left(wet), 0.0)

    def outflow(value):
        over_row = row_face * (value - below(value))
        over_col = col_face * (value - left(value))
        return (over_row - above(over_row)) + (over_col - right(over_col))

    def conjugate(rhs):
        residual = rhs
        search = rhs
        solution = None
        norm_now = total(rhs * rhs)
        for sweep in range(ITERS):
            image = damping * search + SURFACE_GAIN * outflow(search)
            alpha = norm_now / total(search * image)
            solution = alpha * search if solution is None else solution + alpha * search
            if sweep < ITERS - 1:
                residual = residual - alpha * image
                norm_next = total(residual * residual)
                search = residual + (norm_next / norm_now) * search
                norm_now = norm_next
        return solution

    elevation = conjugate(buoyancy)
    response = conjugate(pressure_base + response_weight * elevation)
    lowered = weight * wet * elevation
    raised = scale * wet * response

    def own(value, slot):
        for i in range(loops):
            for j in range(lats):
                own_ref[slot, lats * i + j] = value[
                    i * rows : (i + 1) * rows, j * cols : (j + 1) * cols
                ]
        return own_ref[slot, lats * mine_loop + mine_lat]

    depth_here = still_ref[lats * mine_loop + mine_lat, 3]
    elevation_here = own(elevation, 0)
    for level in range(levels):
        at = pl.ds(level * rows, rows)
        change = jnp.where(level < depth_here, elevation_here, 0.0)
        state_ref[0, at, :] = mixed_ref[0, at, :] - change
        state_ref[1, at, :] = mixed_ref[1, at, :] + change

    for tracer, carried in enumerate((base_0 - lowered + raised, base_1 + lowered - raised)):
        for sweep in range(SUB):
            carried = carried - outflow(carried)
        gradient_ref[tracer] = own(wet * carried, 1 + tracer)

    gradient = [gradient_ref[tracer] for tracer in range(2)]
    lane = iota((1, cols), 1)
    inner = gram_ref[...]
    count = step_ref.shape[0]
    for index, ref in enumerate((step_ref, change_ref)):
        for i in range(count):
            value = ref[i, pl.ds(0, rows), :] * gradient[0] + ref[i, pl.ds(rows, rows), :] * gradient[1]
            inner = inner + jnp.where(lane == index * count + i, total(value), 0.0)
    inner_ref[...] = jnp.broadcast_to(inner[None], inner_ref.shape)


def direction_kernel(inner_ref, gradient_ref, step_ref, change_ref, out_ref):
    count = step_ref.shape[0]
    rows = gradient_ref.shape[1]
    inner = jnp.sum(inner_ref[...], axis=0)

    def scalar(at):
        return inner[:, at : at + 1]

    step_grad = [scalar(i) for i in range(count)]
    change_grad = [scalar(count + i) for i in range(count)]
    at = 2 * count
    step_change = {}
    change_change = {}
    for table in (step_change, change_change):
        for i in range(count):
            for j in range(i, count):
                table[i, j] = table[j, i] = scalar(at)
                at += 1
    gamma = step_change[count - 1, count - 1] / change_change[count - 1, count - 1]
    factors = [None] * count
    for i in range(count - 1, -1, -1):
        factors[i] = step_grad[i] / step_change[i, i]
        for j in range(count):
            if j < i:
                step_grad[j] = step_grad[j] - factors[i] * step_change[j, i]
            change_grad[j] = change_grad[j] - factors[i] * change_change[j, i]
    change_grad = [gamma * value for value in change_grad]
    weights = []
    for i in range(count):
        weights.append(factors[i] - change_grad[i] / step_change[i, i])
        for j in range(i + 1, count):
            change_grad[j] = change_grad[j] + weights[i] * step_change[i, j]
    for tracer in range(2):
        at = pl.ds(tracer * rows, rows)
        value = gradient_ref[tracer]
        for i in range(count - 1, -1, -1):
            value = value - factors[i] * change_ref[i, at, :]
        value = gamma * value
        for i in range(count):
            value = value + weights[i] * step_ref[i, at, :]
        out_ref[tracer] = -value


def on_device(
    state, observed, weight, control, depth_index, diffusivity, damping, history_step, history_change
):
    _, levels, rows, cols = state.shape
    count = history_step.shape[0]
    padded = round_up(levels + 2, 8)
    planes = 2 * padded
    loops = lax.axis_size("loop")
    lats = lax.axis_size("lat")
    blocks = loops * lats
    scale = levels ** (-0.5)
    flat = (2, levels * rows, cols)
    state = state.reshape(flat)
    observed = observed.reshape(flat)
    weight = weight.reshape(flat[1:])
    step = history_step.reshape(count, 2 * rows, cols)
    change = history_change.reshape(count, 2 * rows, cols)

    packed, up, down, still = call(
        functools.partial(pack_kernel, levels, padded),
        [(rows, planes, cols), (SUB, planes, cols), (SUB, planes, cols), (5, rows, cols)],
        name="pack",
    )(state, control, depth_index, diffusivity, damping, weight)
    forward = [(i, (i + 1) % loops) for i in range(loops)]
    backward = [(target, source) for source, target in forward]
    low = lax.ppermute(up, "loop", forward)
    high = lax.ppermute(down, "loop", backward)
    still_all = lax.all_gather(still, GRID)
    edge, gram = call(pairs_kernel, [(planes, cols), (1, cols)], name="pairs")(packed, step, change)
    (edge,) = call(border_kernel, [(planes, cols)], name="border")(edge, low, high, packed)
    other = lax.ppermute(edge, "lat", [(0, 1), (1, 0)])
    mixed, fields = call(
        functools.partial(mix_kernel, levels, padded, scale, blocks),
        [flat, (blocks, 4, rows, cols)],
        scratch=[
            pltpu.VMEM((rows + 2 * SUB, planes, cols), F32),
            pltpu.VMEM((rows + 2 * SUB, padded, cols), F32),
            pltpu.VMEM((rows + 2 * SUB, padded, cols), F32),
            pltpu.VMEM((4, rows, cols), F32),
        ],
        name="mix",
    )(packed, low, high, edge, other, weight, observed)
    fields_all = lax.all_to_all(fields, GRID, 0, 0)
    state_next, gradient, inner = call(
        functools.partial(solve_kernel, levels, scale),
        [flat, (2, rows, cols), (blocks, 1, cols)],
        scratch=[pltpu.VMEM((3, blocks, rows, cols), F32)],
        vmem=56 * 1024 * 1024,
        name="solve",
    )(fields_all, still_all, mixed, step, change, gram)
    inner_all = lax.all_to_all(inner, GRID, 0, 0)
    (direction,) = call(direction_kernel, [(2, rows, cols)], name="direction")(
        inner_all, gradient, step, change
    )
    return (state_next.reshape(2, levels, rows, cols), gradient, direction)


def solution(mesh):
    return jax.shard_map(
        on_device,
        mesh=mesh,
        in_specs=(
            P("members", None, "loop", "lat"),
            P("members", None, "loop", "lat"),
            P(None, "loop", "lat"),
            P("members", "loop", "lat"),
            P("loop", "lat"),
            P("loop", "lat"),
            P("loop", "lat"),
            P("members", None, "loop", "lat"),
            P("members", None, "loop", "lat"),
        ),
        out_specs=(
            P("members", None, "loop", "lat"),
            P("members", "loop", "lat"),
            P("members", "loop", "lat"),
        ),
        check_vma=False,
    )
```

```python
import functools

import jax
import jax.numpy as jnp
from jax import lax
from jax.experimental import pallas as pl
from jax.experimental.pallas import tpu as pltpu
from jax.sharding import PartitionSpec as P

ITERS = 3
SUB = 3
SURFACE_GAIN = 5.0
SLOT = 8
GRID = ("loop", "lat")
VMEM = pl.BlockSpec(memory_space=pltpu.VMEM)
F32 = jnp.float32
VMEM_BYTES = 16 * 1024 * 1024


def round_up(value, to):
    return (value + to - 1) // to * to


def call(kernel, out_shapes, scratch=(), vmem=VMEM_BYTES, name=None):
    return pl.pallas_call(
        kernel,
        out_shape=[jax.ShapeDtypeStruct(shape, F32) for shape in out_shapes],
        out_specs=[VMEM] * len(out_shapes),
        scratch_shapes=list(scratch),
        compiler_params=pltpu.CompilerParams(vmem_limit_bytes=vmem),
        name=name,
    )


def iota(shape, dim):
    return lax.broadcasted_iota(jnp.int32, shape, dim)


def pack_kernel(
    levels, padded, state_hbm, control_hbm, depth_hbm, spread_hbm,
    rows_ref, up_ref, down_ref, state_ref, control_ref, depth_ref, spread_ref, sems,
):
    copies = [
        pltpu.make_async_copy(source, target, sems.at[at])
        for at, (source, target) in enumerate(
            (
                (state_hbm, state_ref),
                (control_hbm, control_ref),
                (depth_hbm, depth_ref),
                (spread_hbm, spread_ref),
            )
        )
    ]
    for copy in copies:
        copy.start()
    for copy in copies:
        copy.wait()
    rows, cols = depth_ref.shape
    depth = depth_ref[...].astype(F32)
    spread = spread_ref[...]
    first = iota((levels, cols), 0) == 0
    rest = jnp.zeros((padded - levels, cols), F32)
    for row in range(rows):
        targets = [rows_ref.at[row]]
        if row < SUB:
            targets.append(down_ref.at[row])
        if row >= rows - SUB:
            targets.append(up_ref.at[row - rows + SUB])
        for tracer in range(2):
            lift = jnp.where(depth[row : row + 1] > 0.5, control_ref[tracer, row : row + 1, :], 0.0)
            value = state_ref[tracer, pl.ds(row, levels, stride=rows), :]
            value = value + jnp.where(first, lift, 0.0)
            for target in targets:
                target[pl.ds(tracer * padded, levels), :] = value
                target[pl.ds(tracer * padded + levels, padded - levels), :] = rest
        for target in targets:
            target[pl.ds(levels, 1), :] = spread[row : row + 1]
            target[pl.ds(levels + 1, 1), :] = depth[row : row + 1]


def edge_of(rows_of, indices, cols, lat):
    lane = iota((1, cols), 1)
    slot = lane // SLOT
    place = lane % SLOT - SUB * lat
    mine = (place >= 0) & (place < SUB)
    total = None
    for index in indices:
        moved = pltpu.roll(rows_of(index), SLOT * index + SUB, 1)
        piece = jnp.where(mine & (slot == index), moved, 0.0)
        total = piece if total is None else total + piece
    return total


def pairs_kernel(
    rows_ref, step_ref, change_ref, depth_ref, spread_ref, damping_ref, weight_ref,
    edge_ref, gram_ref, still_ref,
):
    rows, _, cols = rows_ref.shape
    lat = lax.axis_index("lat")
    edge_ref[...] = edge_of(lambda i: rows_ref[i - SUB], range(SUB, rows + SUB), cols, lat)
    count = step_ref.shape[0]
    lane = iota((1, cols), 1)
    total = jnp.zeros((1, cols), F32)
    at = 2 * count
    for left_ref in (step_ref, change_ref):
        for i in range(count):
            for j in range(i, count):
                value = jnp.sum(left_ref[i] * change_ref[j], axis=(0, 1), keepdims=True)
                total = total + jnp.where(lane == at, value, 0.0)
                at += 1
    gram_ref[...] = total
    depth = depth_ref[...]
    total = jnp.zeros((rows, cols), F32)
    for level in range(weight_ref.shape[0] // rows):
        total = total + jnp.where(level < depth, weight_ref[pl.ds(level * rows, rows), :], 0.0)
    still_ref[0] = 2.0 * total
    still_ref[1] = weight_ref[pl.ds(0, rows), :]
    still_ref[2] = jnp.where(depth > 0, spread_ref[...], 0.0)
    still_ref[3] = damping_ref[...]


def border_kernel(edge_ref, low_ref, high_ref, rows_ref, out_ref):
    cols = edge_ref.shape[-1]
    rows = rows_ref.shape[0]
    lat = lax.axis_index("lat")
    total = edge_ref[...] + edge_of(lambda i: low_ref[i], range(SUB), cols, lat)
    out_ref[...] = total + edge_of(
        lambda i: high_ref[i - rows - SUB], range(rows + SUB, rows + 2 * SUB), cols, lat
    )


def mix_kernel(
    levels, padded, scale, copies,
    rows_ref, low_ref, high_ref, edge_ref, other_ref, weight_ref, observed_ref, still_ref,
    mixed_ref, fields_ref, face_ref, part_ref,
):
    rows, _, cols = rows_ref.shape
    lat = lax.axis_index("lat")
    lane = iota((1, cols), 1)
    place = lane % SLOT
    tall = 8
    count = rows + 2 * SUB

    def left(value, by=1):
        return pltpu.roll(value, cols - by, 1)

    def right(value, by=1):
        return pltpu.roll(value, by, 1)

    def source(i):
        if i < SUB:
            return low_ref, i
        if i < SUB + rows:
            return rows_ref, i - SUB
        return high_ref, i - SUB - rows

    def load(i, start, size):
        ref, at = source(i)
        return ref[at, pl.ds(start, size), :]

    spreads = [load(i, levels, 1) for i in range(count)]
    depths = [load(i, levels + 1, 1) for i in range(count)]
    wide = (tall, cols)
    row_at = lambda i: i
    col_at = lambda i: count + i
    for i in range(count - 1):
        face_ref[0, row_at(i)] = jnp.broadcast_to(jnp.minimum(depths[i], depths[i + 1]), wide)
        face_ref[1, row_at(i)] = jnp.broadcast_to(0.5 * (spreads[i] + spreads[i + 1]), wide)
    for i in range(1, count - 1):
        there = jnp.where(lane < cols - 1, left(depths[i]), 0.0)
        face_ref[0, col_at(i)] = jnp.broadcast_to(jnp.minimum(depths[i], there), wide)
        face_ref[1, col_at(i)] = jnp.broadcast_to(0.5 * (spreads[i] + left(spreads[i])), wide)

    spread = edge_ref[pl.ds(levels, 1), :] + other_ref[pl.ds(levels, 1), :]
    depth = edge_ref[pl.ds(levels + 1, 1), :] + other_ref[pl.ds(levels + 1, 1), :]
    within = place < 2 * SUB - 1
    strip_col_depth = jnp.minimum(depth, jnp.where(within, left(depth), 0.0))
    strip_col_spread = 0.5 * (spread + left(spread))
    strip_row_depth = jnp.minimum(depth, left(depth, SLOT))
    strip_row_spread = 0.5 * (spread + left(spread, SLOT))
    out_of_low = place == jnp.where(lat == 0, SUB - 1, SLOT)
    out_of_high = place == jnp.where(lat == 0, SLOT, SUB)
    start = jnp.where(lat == 0, cols - SUB, 0)
    at_border = (lane >= start) & (lane < start + SUB)

    buoyancy = [None] * rows
    pressure = [None] * rows
    for start in range(0, levels, tall):
        size = min(tall, levels - start)
        level = iota(wide, 0).astype(F32) + float(start)

        def face(at):
            return jnp.where(level < face_ref[0, at], face_ref[1, at], 0.0)

        row_face = [face(row_at(i)) for i in range(count - 1)]
        col_face = [None] + [face(col_at(i)) for i in range(1, count - 1)]
        strip_col = jnp.where(level < strip_col_depth, strip_col_spread, 0.0)
        strip_row = jnp.where(level < strip_row_depth, strip_row_spread, 0.0)
        strip_own = jnp.where(place == SUB - 1, 0.0, strip_col)

        def stripped(value, over_col):
            over_row = strip_row * (left(value, SLOT) - value)
            return value + (over_col - right(over_col)) + (over_row - right(over_row, SLOT))

        mixed = []
        for tracer in range(2):
            here = tracer * padded + start
            value = [load(i, here, tall) for i in range(count)]
            part = edge_ref[pl.ds(here, tall), :] + other_ref[pl.ds(here, tall), :]
            extra = None
            for sweep in range(1, SUB + 1):
                over_col = strip_col * (left(part) - part)
                across = jnp.where(out_of_low, over_col, 0.0) - jnp.where(
                    out_of_high, right(over_col), 0.0
                )
                if extra is None:
                    extra = across
                else:
                    extra = stripped(extra, strip_own * (left(extra) - extra)) + across
                if sweep < SUB:
                    part = stripped(part, over_col)
                after = list(value)
                over_row = [None] * count
                for i in range(sweep - 1, count - sweep):
                    over_row[i] = row_face[i] * (value[i + 1] - value[i])
                for i in range(sweep, count - sweep):
                    flux = col_face[i] * (left(value[i]) - value[i])
                    after[i] = value[i] + (over_row[i] - over_row[i - 1]) + (flux - right(flux))
                value = after
            mixed.append(
                [
                    value[i] + jnp.where(at_border, left(extra, SLOT * i + SUB), 0.0)
                    for i in range(SUB, SUB + rows)
                ]
            )
        for row in range(rows):
            at = pl.ds(start * rows + row, size, stride=rows)
            wet = level[:size] < depths[row + SUB]
            weight = weight_ref[at, :]
            misfit = []
            ends = []
            for tracer in range(2):
                end = mixed[tracer][row][:size]
                ends.append(end)
                mixed_ref[tracer, at, :] = end
                misfit.append(weight * (end - observed_ref[tracer, at, :]))
            up = jnp.where(wet, ends[0] - ends[1], 0.0)
            down = jnp.where(wet, misfit[1] - misfit[0], 0.0)
            if size < tall:
                up = jnp.sum(up, axis=0, keepdims=True)
                down = jnp.sum(down, axis=0, keepdims=True)
                up = jnp.sum(buoyancy[row], axis=0, keepdims=True) + up
                down = jnp.sum(pressure[row], axis=0, keepdims=True) + down
                buoyancy[row], pressure[row] = up, down
            else:
                buoyancy[row] = up if start == 0 else buoyancy[row] + up
                pressure[row] = down if start == 0 else pressure[row] + down
            if start == 0:
                part_ref[2, pl.ds(row, 1), :] = misfit[0][0:1]
                part_ref[3, pl.ds(row, 1), :] = misfit[1][0:1]
    for row in range(rows):
        part_ref[0, pl.ds(row, 1), :] = scale * jnp.sum(buoyancy[row], axis=0, keepdims=True)
        part_ref[1, pl.ds(row, 1), :] = jnp.sum(pressure[row], axis=0, keepdims=True)
    for copy in range(copies):
        for field in range(4):
            fields_ref[copy, field] = part_ref[field]
            fields_ref[copy, 4 + field] = still_ref[field]


def solve_kernel(
    levels, scale, copies,
    mine_ref, other_ref, mixed_ref, depth_ref, step_ref, change_ref, gram_ref,
    state_ref, gradient_ref, inner_ref, kept_ref,
):
    loops, _, rows, cols = mine_ref.shape
    height = loops * rows
    width = 2 * cols
    loop = lax.axis_index("loop")
    closed = jnp.where(lax.axis_index("lat") == 0, width - 1, cols - 1)

    def whole(field):
        return jnp.concatenate(
            [
                jnp.concatenate([mine_ref[i, field], other_ref[i, field]], axis=1)
                for i in range(loops)
            ],
            axis=0,
        )

    def around(field):
        parts = []
        for shift in (loops - 1, 0, 1):
            at = lax.rem(loop + shift, loops)
            parts.append(jnp.concatenate([mine_ref[at, field], other_ref[at, field]], axis=1))
        return jnp.concatenate(parts, axis=0)

    def below(value):
        return pltpu.roll(value, value.shape[0] - 1, 0)

    def above(value):
        return pltpu.roll(value, 1, 0)

    def left(value):
        return pltpu.roll(value, width - 1, 1)

    def right(value):
        return pltpu.roll(value, 1, 1)

    def total(value):
        return jnp.sum(value, axis=(0, 1), keepdims=True)

    def faces(spread):
        wet = spread > 0.0
        inside = iota(spread.shape, 1) != closed
        row_face = jnp.where(wet & (below(spread) > 0.0), 0.5 * (spread + below(spread)), 0.0)
        col_face = jnp.where(
            inside & wet & (left(spread) > 0.0), 0.5 * (spread + left(spread)), 0.0
        )
        return row_face, col_face

    def outflow(value, row_face, col_face):
        over_row = row_face * (value - below(value))
        over_col = col_face * (value - left(value))
        return (over_row - above(over_row)) + (over_col - right(over_col))

    row_face, col_face = (SURFACE_GAIN * face for face in faces(whole(6)))
    damping = whole(7)

    def conjugate(rhs):
        residual = rhs
        search = rhs
        solution = None
        norm_now = total(rhs * rhs)
        for sweep in range(ITERS):
            image = damping * search + outflow(search, row_face, col_face)
            alpha = norm_now / total(search * image)
            solution = alpha * search if solution is None else solution + alpha * search
            if sweep < ITERS - 1:
                residual = residual - alpha * image
                norm_next = total(residual * residual)
                search = residual + (norm_next / norm_now) * search
                norm_now = norm_next
        return solution

    def keep(slot, value):
        for i in range(loops):
            kept_ref[slot, i] = value[i * rows : (i + 1) * rows]

    def kept_around(slot):
        return jnp.concatenate(
            [kept_ref[slot, lax.rem(loop + shift, loops)] for shift in (loops - 1, 0, 1)], axis=0
        )

    elevation = conjugate(whole(0))
    keep(0, elevation)
    response = conjugate(whole(1) + whole(4) * elevation)
    keep(1, response)

    elevation = kept_around(0)
    spread = around(6)
    sea = spread > 0.0
    lowered = jnp.where(sea, around(5) * elevation, 0.0)
    raised = jnp.where(sea, scale * kept_around(1), 0.0)
    near_row, near_col = faces(spread)
    gradient = []
    for tracer in range(2):
        carried = around(2 + tracer)
        carried = carried - lowered + raised if tracer == 0 else carried + lowered - raised
        for sweep in range(SUB):
            carried = carried - outflow(carried, near_row, near_col)
        value = jnp.where(sea, carried, 0.0)[rows : 2 * rows, :cols]
        gradient_ref[tracer] = value
        gradient.append(value)

    lane = iota((1, cols), 1)
    inner = gram_ref[...]
    count = step_ref.shape[0]
    for index, ref in enumerate((step_ref, change_ref)):
        for i in range(count):
            value = ref[i, pl.ds(0, rows), :] * gradient[0] + ref[i, pl.ds(rows, rows), :] * gradient[1]
            inner = inner + jnp.where(lane == index * count + i, total(value), 0.0)
    inner_ref[...] = jnp.broadcast_to(inner[None], inner_ref.shape)

    depth = depth_ref[...]
    here = elevation[rows : 2 * rows, :cols]
    for level in range(levels):
        at = pl.ds(level * rows, rows)
        change = jnp.where(level < depth, here, 0.0)
        state_ref[0, at, :] = mixed_ref[0, at, :] - change
        state_ref[1, at, :] = mixed_ref[1, at, :] + change


def direction_kernel(inner_ref, gradient_ref, step_ref, change_ref, out_ref):
    count = step_ref.shape[0]
    rows = gradient_ref.shape[1]
    inner = jnp.sum(inner_ref[...], axis=0)

    def scalar(at):
        return inner[:, at : at + 1]

    step_grad = [scalar(i) for i in range(count)]
    change_grad = [scalar(count + i) for i in range(count)]
    at = 2 * count
    step_change = {}
    change_change = {}
    for table in (step_change, change_change):
        for i in range(count):
            for j in range(i, count):
                table[i, j] = table[j, i] = scalar(at)
                at += 1
    gamma = step_change[count - 1, count - 1] / change_change[count - 1, count - 1]
    factors = [None] * count
    for i in range(count - 1, -1, -1):
        factors[i] = step_grad[i] / step_change[i, i]
        for j in range(count):
            if j < i:
                step_grad[j] = step_grad[j] - factors[i] * step_change[j, i]
            change_grad[j] = change_grad[j] - factors[i] * change_change[j, i]
    change_grad = [gamma * value for value in change_grad]
    weights = []
    for i in range(count):
        weights.append(factors[i] - change_grad[i] / step_change[i, i])
        for j in range(i + 1, count):
            change_grad[j] = change_grad[j] + weights[i] * step_change[i, j]
    for tracer in range(2):
        at = pl.ds(tracer * rows, rows)
        value = gradient_ref[tracer]
        for i in range(count - 1, -1, -1):
            value = value - factors[i] * change_ref[i, at, :]
        value = gamma * value
        for i in range(count):
            value = value + weights[i] * step_ref[i, at, :]
        out_ref[tracer] = -value


def on_device(
    state, observed, weight, control, depth_index, diffusivity, damping, history_step, history_change
):
    _, levels, rows, cols = state.shape
    count = history_step.shape[0]
    padded = round_up(levels + 2, 8)
    planes = 2 * padded
    loops = lax.axis_size("loop")
    lats = lax.axis_size("lat")
    blocks = loops * lats
    scale = levels ** (-0.5)
    flat = (2, levels * rows, cols)
    state = state.reshape(flat)
    observed = observed.reshape(flat)
    weight = weight.reshape(flat[1:])
    step = history_step.reshape(count, 2 * rows, cols)
    change = history_change.reshape(count, 2 * rows, cols)

    packed, up, down = pl.pallas_call(
        functools.partial(pack_kernel, levels, padded),
        out_shape=[
            jax.ShapeDtypeStruct(shape, F32)
            for shape in ((rows, planes, cols), (SUB, planes, cols), (SUB, planes, cols))
        ],
        in_specs=[pl.BlockSpec(memory_space=pltpu.HBM)] * 4,
        out_specs=[VMEM] * 3,
        scratch_shapes=[
            pltpu.VMEM(flat, F32),
            pltpu.VMEM((2, rows, cols), F32),
            pltpu.VMEM((rows, cols), jnp.int32),
            pltpu.VMEM((rows, cols), F32),
            pltpu.SemaphoreType.DMA((4,)),
        ],
        compiler_params=pltpu.CompilerParams(vmem_limit_bytes=VMEM_BYTES),
        name="pack",
    )(state, control, depth_index, diffusivity)
    forward = [(i, (i + 1) % loops) for i in range(loops)]
    backward = [(target, source) for source, target in forward]
    swap = [(0, 1), (1, 0)]
    low = lax.ppermute(up, "loop", forward)
    high = lax.ppermute(down, "loop", backward)
    edge, gram, still = call(
        pairs_kernel, [(planes, cols), (1, cols), (4, rows, cols)], name="pairs"
    )(packed, step, change, depth_index, diffusivity, damping, weight)
    (edge,) = call(border_kernel, [(planes, cols)], name="border")(edge, low, high, packed)
    other = lax.ppermute(edge, "lat", swap)
    mixed, fields = call(
        functools.partial(mix_kernel, levels, padded, scale, loops),
        [flat, (loops, 8, rows, cols)],
        scratch=[
            pltpu.VMEM((2, 2 * (rows + 2 * SUB), 8, cols), F32),
            pltpu.VMEM((4, rows, cols), F32),
        ],
        name="mix",
    )(packed, low, high, edge, other, weight, observed, still)
    mine = lax.all_to_all(fields, "loop", 0, 0)
    theirs = lax.ppermute(mine, "lat", swap)
    state_next, gradient, inner = call(
        functools.partial(solve_kernel, levels, scale, blocks),
        [flat, (2, rows, cols), (blocks, 1, cols)],
        scratch=[pltpu.VMEM((2, loops, rows, 2 * cols), F32)],
        vmem=VMEM_BYTES if loops <= 16 else 2 * VMEM_BYTES,
        name="solve",
    )(mine, theirs, mixed, depth_index, step, change, gram)
    inner_all = lax.all_to_all(inner, GRID, 0, 0)
    (direction,) = call(direction_kernel, [(2, rows, cols)], name="direction")(
        inner_all, gradient, step, change
    )
    return (state_next.reshape(2, levels, rows, cols), gradient, direction)


def solution(mesh):
    return jax.shard_map(
        on_device,
        mesh=mesh,
        in_specs=(
            P("members", None, "loop", "lat"),
            P("members", None, "loop", "lat"),
            P(None, "loop", "lat"),
            P("members", "loop", "lat"),
            P("loop", "lat"),
            P("loop", "lat"),
            P("loop", "lat"),
            P("members", None, "loop", "lat"),
            P("members", None, "loop", "lat"),
        ),
        out_specs=(
            P("members", None, "loop", "lat"),
            P("members", "loop", "lat"),
            P("members", "loop", "lat"),
        ),
        check_vma=False,
    )
```

```python
import functools

import jax
import jax.numpy as jnp
from jax import lax
from jax.experimental import pallas as pl
from jax.experimental.pallas import tpu as pltpu
from jax.sharding import PartitionSpec as P

ITERS = 3
SUB = 3
SURFACE_GAIN = 5.0
SLOT = 8
GRID = ("loop", "lat")
VMEM = pl.BlockSpec(memory_space=pltpu.VMEM)
F32 = jnp.float32
VMEM_BYTES = 16 * 1024 * 1024


def round_up(value, to):
    return (value + to - 1) // to * to


def call(kernel, out_shapes, scratch=(), vmem=VMEM_BYTES, name=None):
    return pl.pallas_call(
        kernel,
        out_shape=[jax.ShapeDtypeStruct(shape, F32) for shape in out_shapes],
        out_specs=[VMEM] * len(out_shapes),
        scratch_shapes=list(scratch),
        compiler_params=pltpu.CompilerParams(vmem_limit_bytes=vmem),
        name=name,
    )


def iota(shape, dim):
    return lax.broadcasted_iota(jnp.int32, shape, dim)


def pack_kernel(
    levels, padded, state_hbm, control_hbm, depth_hbm, spread_hbm,
    rows_ref, up_ref, down_ref, state_ref, control_ref, depth_ref, spread_ref, sems,
):
    copies = [
        pltpu.make_async_copy(source, target, sems.at[at])
        for at, (source, target) in enumerate(
            (
                (state_hbm, state_ref),
                (control_hbm, control_ref),
                (depth_hbm, depth_ref),
                (spread_hbm, spread_ref),
            )
        )
    ]
    for copy in copies:
        copy.start()
    for copy in copies:
        copy.wait()
    rows, cols = depth_ref.shape
    depth = depth_ref[...].astype(F32)
    spread = spread_ref[...]
    first = iota((levels, cols), 0) == 0
    rest = jnp.zeros((padded - levels, cols), F32)
    for row in range(rows):
        targets = [rows_ref.at[row]]
        if row < SUB:
            targets.append(down_ref.at[row])
        if row >= rows - SUB:
            targets.append(up_ref.at[row - rows + SUB])
        for tracer in range(2):
            lift = jnp.where(depth[row : row + 1] > 0.5, control_ref[tracer, row : row + 1, :], 0.0)
            value = state_ref[tracer, pl.ds(row, levels, stride=rows), :]
            value = value + jnp.where(first, lift, 0.0)
            for target in targets:
                target[pl.ds(tracer * padded, levels), :] = value
                target[pl.ds(tracer * padded + levels, padded - levels), :] = rest
        for target in targets:
            target[pl.ds(levels, 1), :] = spread[row : row + 1]
            target[pl.ds(levels + 1, 1), :] = depth[row : row + 1]


def edge_of(rows_of, indices, cols, lat):
    lane = iota((1, cols), 1)
    slot = lane // SLOT
    place = lane % SLOT - SUB * lat
    mine = (place >= 0) & (place < SUB)
    total = None
    for index in indices:
        moved = pltpu.roll(rows_of(index), SLOT * index + SUB, 1)
        piece = jnp.where(mine & (slot == index), moved, 0.0)
        total = piece if total is None else total + piece
    return total


def pairs_kernel(
    rows_ref, step_ref, change_ref, depth_ref, spread_ref, damping_ref, weight_ref,
    edge_ref, gram_ref, still_ref,
):
    rows, _, cols = rows_ref.shape
    lat = lax.axis_index("lat")
    edge_ref[...] = edge_of(lambda i: rows_ref[i - SUB], range(SUB, rows + SUB), cols, lat)
    count = step_ref.shape[0]
    lane = iota((1, cols), 1)
    total = jnp.zeros((1, cols), F32)
    at = 2 * count
    for left_ref in (step_ref, change_ref):
        for i in range(count):
            for j in range(i, count):
                value = jnp.sum(left_ref[i] * change_ref[j], axis=(0, 1), keepdims=True)
                total = total + jnp.where(lane == at, value, 0.0)
                at += 1
    gram_ref[...] = total
    depth = depth_ref[...]
    total = jnp.zeros((rows, cols), F32)
    for level in range(weight_ref.shape[0] // rows):
        total = total + jnp.where(level < depth, weight_ref[pl.ds(level * rows, rows), :], 0.0)
    still_ref[0] = 2.0 * total
    still_ref[1] = weight_ref[pl.ds(0, rows), :]
    still_ref[2] = jnp.where(depth > 0, spread_ref[...], 0.0)
    still_ref[3] = damping_ref[...]


def border_kernel(edge_ref, low_ref, high_ref, rows_ref, out_ref):
    cols = edge_ref.shape[-1]
    rows = rows_ref.shape[0]
    lat = lax.axis_index("lat")
    total = edge_ref[...] + edge_of(lambda i: low_ref[i], range(SUB), cols, lat)
    out_ref[...] = total + edge_of(
        lambda i: high_ref[i - rows - SUB], range(rows + SUB, rows + 2 * SUB), cols, lat
    )


def mix_kernel(
    levels, padded, scale, copies,
    rows_ref, low_ref, high_ref, edge_ref, other_ref, weight_ref, observed_ref, still_ref,
    mixed_ref, fields_ref, face_ref, here_ref, there_ref, part_ref,
):
    rows, planes, cols = rows_ref.shape
    lat = lax.axis_index("lat")
    lane = iota((1, cols), 1)
    place = lane % SLOT
    count = rows + 2 * SUB
    level = iota((padded, cols), 0).astype(F32)

    def left(value, by=1):
        return pltpu.roll(value, (cols - by) % cols, 1)

    def right(value, by=1):
        return pltpu.roll(value, by, 1)

    def source(i):
        if i < SUB:
            return low_ref.at[i]
        if i < SUB + rows:
            return rows_ref.at[i - SUB]
        return high_ref.at[i - SUB - rows]

    def face(depth_here, depth_there, spread_here, spread_there):
        opened = level < jnp.minimum(depth_here, depth_there)
        return jnp.where(opened, 0.5 * (spread_here + spread_there), 0.0)

    spread = edge_ref[pl.ds(levels, 1), :] + other_ref[pl.ds(levels, 1), :]
    depth = edge_ref[pl.ds(levels + 1, 1), :] + other_ref[pl.ds(levels + 1, 1), :]
    within = place < 2 * SUB - 1
    col_depth = jnp.minimum(depth, jnp.where(within, left(depth), 0.0))
    col_spread = 0.5 * (spread + left(spread))
    row_depth = jnp.minimum(depth, left(depth, SLOT))
    row_spread = 0.5 * (spread + left(spread, SLOT))

    def strip_face(limit, value):
        return jnp.where(level < limit, value, 0.0)

    to_left = strip_face(right(col_depth), right(col_spread))
    to_right = strip_face(col_depth, col_spread)
    to_above = strip_face(right(row_depth, SLOT), right(row_spread, SLOT))
    to_below = strip_face(row_depth, row_spread)
    out_of_low = place == jnp.where(lat == 0, SUB - 1, SLOT)
    out_of_high = place == jnp.where(lat == 0, SLOT, SUB)
    over_low = jnp.where(out_of_low, to_right, 0.0)
    over_high = jnp.where(out_of_high, to_left, 0.0)
    own_right = jnp.where(place == SUB - 1, 0.0, to_right)
    own_left = jnp.where(place == SUB, 0.0, to_left)
    start = jnp.where(lat == 0, cols - SUB, 0)
    at_border = (lane >= start) & (lane < start + SUB)

    def spread_out(value, east, west):
        before, after = right(value), left(value)
        above, below = right(value, SLOT), left(value, SLOT)
        total = value + east * (after - value) + west * (before - value)
        return total + to_below * (below - value) + to_above * (above - value)

    parts = []
    extras = [None, None]
    for tracer in range(2):
        at = pl.ds(tracer * padded, padded)
        parts.append(edge_ref[at, :] + other_ref[at, :])

    spreads = [source(i)[pl.ds(levels, 1), :] for i in range(count)]
    depths = [source(i)[pl.ds(levels + 1, 1), :] for i in range(count)]
    for i in range(count - 1):
        face_ref[0, i] = face(depths[i], depths[i + 1], spreads[i], spreads[i + 1])
    for i in range(1, count - 1):
        there = jnp.where(lane < cols - 1, left(depths[i]), 0.0)
        face_ref[1, i] = face(depths[i], there, spreads[i], left(spreads[i]))
        there = jnp.where(lane > 0, right(depths[i]), 0.0)
        face_ref[2, i] = face(depths[i], there, spreads[i], right(spreads[i]))

    for sweep in range(1, SUB + 1):
        for tracer in range(2):
            part = parts[tracer]
            across = over_low * (left(part) - part) + over_high * (right(part) - part)
            extra = extras[tracer]
            if extra is not None:
                across = across + spread_out(extra, own_right, own_left)
            extras[tracer] = across
            if sweep < SUB:
                parts[tracer] = spread_out(part, to_right, to_left)
        target = here_ref if sweep % 2 else there_ref
        for i in range(sweep, count - sweep):
            def field(at):
                if sweep == 1:
                    return source(at)
                return (there_ref if sweep % 2 else here_ref).at[at]

            for tracer in range(2):
                at = pl.ds(tracer * padded, padded)
                centre = field(i)[at, :]
                total = centre + face_ref[0, i] * (field(i + 1)[at, :] - centre)
                total = total + face_ref[0, i - 1] * (field(i - 1)[at, :] - centre)
                total = total + face_ref[1, i] * (left(centre) - centre)
                total = total + face_ref[2, i] * (right(centre) - centre)
                target[i, at, :] = total

    target = here_ref if SUB % 2 else there_ref
    for row in range(rows):
        i = row + SUB
        at = pl.ds(row, levels, stride=rows)
        mixed = []
        for tracer in range(2):
            border = jnp.where(at_border, left(extras[tracer], SLOT * i + SUB), 0.0)
            mixed.append((target[i, pl.ds(tracer * padded, padded), :] + border)[:levels])
        wet = level[:levels] < depths[i]
        weight = weight_ref[at, :]
        misfit = []
        for tracer in range(2):
            mixed_ref[tracer, at, :] = mixed[tracer]
            misfit.append(weight * (mixed[tracer] - observed_ref[tracer, at, :]))
        here = pl.ds(row, 1)
        part_ref[0, here, :] = scale * jnp.sum(
            jnp.where(wet, mixed[0] - mixed[1], 0.0), axis=0, keepdims=True
        )
        part_ref[1, here, :] = jnp.sum(
            jnp.where(wet, misfit[1] - misfit[0], 0.0), axis=0, keepdims=True
        )
        part_ref[2, here, :] = misfit[0][0:1]
        part_ref[3, here, :] = misfit[1][0:1]
    for copy in range(copies):
        for field in range(4):
            fields_ref[copy, field] = part_ref[field]
            fields_ref[copy, 4 + field] = still_ref[field]


def solve_kernel(
    levels, scale, copies,
    mine_ref, other_ref, mixed_ref, depth_ref, step_ref, change_ref, gram_ref,
    state_ref, gradient_ref, inner_ref, kept_ref,
):
    loops, _, rows, cols = mine_ref.shape
    height = loops * rows
    width = 2 * cols
    loop = lax.axis_index("loop")
    closed = jnp.where(lax.axis_index("lat") == 0, width - 1, cols - 1)

    def whole(field):
        return jnp.concatenate(
            [
                jnp.concatenate([mine_ref[i, field], other_ref[i, field]], axis=1)
                for i in range(loops)
            ],
            axis=0,
        )

    def around(field):
        parts = []
        for shift in (loops - 1, 0, 1):
            at = lax.rem(loop + shift, loops)
            parts.append(jnp.concatenate([mine_ref[at, field], other_ref[at, field]], axis=1))
        return jnp.concatenate(parts, axis=0)

    def below(value):
        return pltpu.roll(value, value.shape[0] - 1, 0)

    def above(value):
        return pltpu.roll(value, 1, 0)

    def left(value):
        return pltpu.roll(value, width - 1, 1)

    def right(value):
        return pltpu.roll(value, 1, 1)

    def total(value):
        return jnp.sum(value, axis=(0, 1), keepdims=True)

    def faces(spread):
        wet = spread > 0.0
        inside = iota(spread.shape, 1) != closed
        row_face = jnp.where(wet & (below(spread) > 0.0), 0.5 * (spread + below(spread)), 0.0)
        col_face = jnp.where(
            inside & wet & (left(spread) > 0.0), 0.5 * (spread + left(spread)), 0.0
        )
        return row_face, above(row_face), col_face, right(col_face)

    def outflow(value, to_below, to_above, to_right, to_left):
        total = to_right * (value - left(value)) + to_left * (value - right(value))
        return total + to_below * (value - below(value)) + to_above * (value - above(value))

    gained = [SURFACE_GAIN * face for face in faces(whole(6))]
    damping = whole(7)

    def conjugate(rhs):
        residual = rhs
        search = rhs
        solution = None
        norm_now = total(rhs * rhs)
        for sweep in range(ITERS):
            image = damping * search + outflow(search, *gained)
            alpha = norm_now / total(search * image)
            solution = alpha * search if solution is None else solution + alpha * search
            if sweep < ITERS - 1:
                residual = residual - alpha * image
                norm_next = total(residual * residual)
                search = residual + (norm_next / norm_now) * search
                norm_now = norm_next
        return solution

    def keep(slot, value):
        for i in range(loops):
            kept_ref[slot, i] = value[i * rows : (i + 1) * rows]

    def kept_around(slot):
        return jnp.concatenate(
            [kept_ref[slot, lax.rem(loop + shift, loops)] for shift in (loops - 1, 0, 1)], axis=0
        )

    elevation = conjugate(whole(0))
    keep(0, elevation)
    response = conjugate(whole(1) + whole(4) * elevation)
    keep(1, response)

    elevation = kept_around(0)
    spread = around(6)
    sea = spread > 0.0
    lowered = jnp.where(sea, around(5) * elevation, 0.0)
    raised = jnp.where(sea, scale * kept_around(1), 0.0)
    near = faces(spread)
    carried = [around(2) - lowered + raised, around(3) + lowered - raised]
    for sweep in range(SUB):
        carried = [value - outflow(value, *near) for value in carried]
    gradient = [jnp.where(sea, value, 0.0)[rows : 2 * rows, :cols] for value in carried]
    for tracer in range(2):
        gradient_ref[tracer] = gradient[tracer]

    lane = iota((1, cols), 1)
    inner = gram_ref[...]
    count = step_ref.shape[0]
    for index, ref in enumerate((step_ref, change_ref)):
        for i in range(count):
            value = ref[i, pl.ds(0, rows), :] * gradient[0] + ref[i, pl.ds(rows, rows), :] * gradient[1]
            inner = inner + jnp.where(lane == index * count + i, total(value), 0.0)
    inner_ref[...] = jnp.broadcast_to(inner[None], inner_ref.shape)

    depth = depth_ref[...]
    here = elevation[rows : 2 * rows, :cols]
    for level in range(levels):
        at = pl.ds(level * rows, rows)
        change = jnp.where(level < depth, here, 0.0)
        state_ref[0, at, :] = mixed_ref[0, at, :] - change
        state_ref[1, at, :] = mixed_ref[1, at, :] + change


def direction_kernel(inner_ref, gradient_ref, step_ref, change_ref, out_ref):
    count = step_ref.shape[0]
    rows = gradient_ref.shape[1]
    inner = jnp.sum(inner_ref[...], axis=0)

    def scalar(at):
        return inner[:, at : at + 1]

    step_grad = [scalar(i) for i in range(count)]
    change_grad = [scalar(count + i) for i in range(count)]
    at = 2 * count
    step_change = {}
    change_change = {}
    for table in (step_change, change_change):
        for i in range(count):
            for j in range(i, count):
                table[i, j] = table[j, i] = scalar(at)
                at += 1
    gamma = step_change[count - 1, count - 1] / change_change[count - 1, count - 1]
    factors = [None] * count
    for i in range(count - 1, -1, -1):
        factors[i] = step_grad[i] / step_change[i, i]
        for j in range(count):
            if j < i:
                step_grad[j] = step_grad[j] - factors[i] * step_change[j, i]
            change_grad[j] = change_grad[j] - factors[i] * change_change[j, i]
    change_grad = [gamma * value for value in change_grad]
    weights = []
    for i in range(count):
        weights.append(factors[i] - change_grad[i] / step_change[i, i])
        for j in range(i + 1, count):
            change_grad[j] = change_grad[j] + weights[i] * step_change[i, j]
    for tracer in range(2):
        at = pl.ds(tracer * rows, rows)
        value = gradient_ref[tracer]
        for i in range(count - 1, -1, -1):
            value = value - factors[i] * change_ref[i, at, :]
        value = gamma * value
        for i in range(count):
            value = value + weights[i] * step_ref[i, at, :]
        out_ref[tracer] = -value


def on_device(
    state, observed, weight, control, depth_index, diffusivity, damping, history_step, history_change
):
    _, levels, rows, cols = state.shape
    count = history_step.shape[0]
    padded = round_up(levels + 2, 8)
    planes = 2 * padded
    loops = lax.axis_size("loop")
    lats = lax.axis_size("lat")
    blocks = loops * lats
    scale = levels ** (-0.5)
    flat = (2, levels * rows, cols)
    state = state.reshape(flat)
    observed = observed.reshape(flat)
    weight = weight.reshape(flat[1:])
    step = history_step.reshape(count, 2 * rows, cols)
    change = history_change.reshape(count, 2 * rows, cols)

    packed, up, down = pl.pallas_call(
        functools.partial(pack_kernel, levels, padded),
        out_shape=[
            jax.ShapeDtypeStruct(shape, F32)
            for shape in ((rows, planes, cols), (SUB, planes, cols), (SUB, planes, cols))
        ],
        in_specs=[pl.BlockSpec(memory_space=pltpu.HBM)] * 4,
        out_specs=[VMEM] * 3,
        scratch_shapes=[
            pltpu.VMEM(flat, F32),
            pltpu.VMEM((2, rows, cols), F32),
            pltpu.VMEM((rows, cols), jnp.int32),
            pltpu.VMEM((rows, cols), F32),
            pltpu.SemaphoreType.DMA((4,)),
        ],
        compiler_params=pltpu.CompilerParams(vmem_limit_bytes=VMEM_BYTES),
        name="pack",
    )(*(pltpu.with_memory_space_constraint(x, pltpu.HBM) for x in (state, control, depth_index, diffusivity)))
    forward = [(i, (i + 1) % loops) for i in range(loops)]
    backward = [(target, source) for source, target in forward]
    swap = [(0, 1), (1, 0)]
    low = lax.ppermute(up, "loop", forward)
    high = lax.ppermute(down, "loop", backward)
    edge, gram, still = call(
        pairs_kernel, [(planes, cols), (1, cols), (4, rows, cols)], name="pairs"
    )(packed, step, change, depth_index, diffusivity, damping, weight)
    (edge,) = call(border_kernel, [(planes, cols)], name="border")(edge, low, high, packed)
    other = lax.ppermute(edge, "lat", swap)
    mixed, fields = call(
        functools.partial(mix_kernel, levels, padded, scale, loops),
        [flat, (loops, 8, rows, cols)],
        scratch=[
            pltpu.VMEM((3, rows + 2 * SUB, padded, cols), F32),
            pltpu.VMEM((rows + 2 * SUB, planes, cols), F32),
            pltpu.VMEM((rows + 2 * SUB, planes, cols), F32),
            pltpu.VMEM((4, rows, cols), F32),
        ],
        name="mix",
    )(packed, low, high, edge, other, weight, observed, still)
    mine = lax.all_to_all(fields, "loop", 0, 0)
    theirs = lax.ppermute(mine, "lat", swap)
    state_next, gradient, inner = call(
        functools.partial(solve_kernel, levels, scale, blocks),
        [flat, (2, rows, cols), (blocks, 1, cols)],
        scratch=[pltpu.VMEM((2, loops, rows, 2 * cols), F32)],
        vmem=VMEM_BYTES if loops <= 16 else 2 * VMEM_BYTES,
        name="solve",
    )(mine, theirs, mixed, depth_index, step, change, gram)
    inner_all = lax.all_to_all(inner, GRID, 0, 0)
    (direction,) = call(direction_kernel, [(2, rows, cols)], name="direction")(
        inner_all, gradient, step, change
    )
    return (state_next.reshape(2, levels, rows, cols), gradient, direction)


def solution(mesh):
    return jax.shard_map(
        on_device,
        mesh=mesh,
        in_specs=(
            P("members", None, "loop", "lat"),
            P("members", None, "loop", "lat"),
            P(None, "loop", "lat"),
            P("members", "loop", "lat"),
            P("loop", "lat"),
            P("loop", "lat"),
            P("loop", "lat"),
            P("members", None, "loop", "lat"),
            P("members", None, "loop", "lat"),
        ),
        out_specs=(
            P("members", None, "loop", "lat"),
            P("members", "loop", "lat"),
            P("members", "loop", "lat"),
        ),
        check_vma=False,
    )
```

```python
import functools

import jax
import jax.numpy as jnp
from jax import lax
from jax.experimental import pallas as pl
from jax.experimental.pallas import tpu as pltpu
from jax.sharding import PartitionSpec as P

ITERS = 3
SUB = 3
SURFACE_GAIN = 5.0
SLOT = 8
REACH = SUB + 2 * (ITERS - 1)
SHIFT = 5.0
SPAN = 5.0
FUNCTIONALS = 1 + ITERS + ITERS + ITERS * ITERS
GRID = ("loop", "lat")
VMEM = pl.BlockSpec(memory_space=pltpu.VMEM)
F32 = jnp.float32
VMEM_BYTES = 16 * 1024 * 1024


def round_up(value, to):
    return (value + to - 1) // to * to


def call(kernel, out_shapes, scratch=(), vmem=VMEM_BYTES, name=None):
    return pl.pallas_call(
        kernel,
        out_shape=[jax.ShapeDtypeStruct(shape, F32) for shape in out_shapes],
        out_specs=[VMEM] * len(out_shapes),
        scratch_shapes=list(scratch),
        compiler_params=pltpu.CompilerParams(vmem_limit_bytes=vmem),
        name=name,
    )


def iota(shape, dim):
    return lax.broadcasted_iota(jnp.int32, shape, dim)


def pack_kernel(
    levels, padded, *refs
):
    sources, (rows_ref, hist_ref, up_ref, down_ref), targets, sems = (
        refs[:8], refs[8:12], refs[12:20], refs[20]
    )
    copies = [
        pltpu.make_async_copy(source, target, sems.at[at])
        for at, (source, target) in enumerate(zip(sources, targets))
    ]
    for copy in copies:
        copy.start()
    for copy in copies:
        copy.wait()
    state_ref, control_ref, depth_ref, spread_ref, damping_ref, weight_ref, step_ref, change_ref = targets
    rows, cols = depth_ref.shape
    planes = 2 * padded
    count = step_ref.shape[0] // (2 * rows)
    pairs = 2 * count
    near = planes + 2 * pairs
    far = SUB * near
    depth = depth_ref[...].astype(F32)
    spread = spread_ref[...]
    wet = depth > 0.5
    total = jnp.zeros((rows, cols), F32)
    for level in range(levels):
        total = total + jnp.where(level < depth, weight_ref[pl.ds(level * rows, rows), :], 0.0)
    fixed = (
        spread,
        depth,
        damping_ref[...],
        2.0 * total,
        weight_ref[pl.ds(0, rows), :],
        jnp.where(wet, spread, 0.0),
    )
    first = iota((levels, cols), 0) == 0
    rest = jnp.zeros((padded - levels, cols), F32)
    for ref in (up_ref, down_ref):
        ref[pl.ds(ref.shape[0] - 8, 8), :] = jnp.zeros((8, cols), F32)
    for row in range(rows):
        targets = [(rows_ref.at[row], 0, hist_ref.at[row], 0)]
        if row < SUB:
            targets.append((down_ref, row * near, down_ref, row * near + planes))
        if row >= rows - SUB:
            at = (row - rows + SUB) * near
            targets.append((up_ref, at, up_ref, at + planes))
        here = slice(row, row + 1)
        for tracer in range(2):
            lift = jnp.where(wet[here], control_ref[tracer, here, :], 0.0)
            value = state_ref[tracer, pl.ds(row, levels, stride=rows), :]
            value = value + jnp.where(first, lift, 0.0)
            for target, at, _, _ in targets:
                at = at + tracer * padded
                target[pl.ds(at, levels), :] = value
                target[pl.ds(at + levels, padded - levels), :] = rest
        for at, field in enumerate(fixed):
            for target, start, _, _ in targets:
                target[pl.ds(start + levels + at, 1), :] = field[here]
        distant = []
        if SUB <= row < REACH:
            distant.append((down_ref, row - SUB))
        if rows - REACH <= row < rows - SUB:
            distant.append((up_ref, row - rows + REACH))
        for which, ref in enumerate((step_ref, change_ref)):
            both = [ref[pl.ds(tracer * rows + row, count, stride=2 * rows), :] for tracer in range(2)]
            apart = jnp.where(wet[here], both[0] - both[1], 0.0)
            joint = jnp.where(wet[here], both[0] + both[1], 0.0)
            for _, _, target, at in targets:
                target[pl.ds(at + which * count, count), :] = apart
                target[pl.ds(at + pairs + which * count, count), :] = joint
            for target, at in distant:
                target[pl.ds(far + at * pairs + which * count, count), :] = apart
        for target, at in distant:
            target[pl.ds(far + (REACH - SUB) * pairs + at, 1), :] = fixed[5][here]


def edge_of(rows_of, indices, cols, lat):
    lane = iota((1, cols), 1)
    slot = lane // SLOT
    place = lane % SLOT - SUB * lat
    mine = (place >= 0) & (place < SUB)
    total = None
    for index in indices:
        moved = pltpu.roll(rows_of(index), SLOT * index + SUB, 1)
        piece = jnp.where(mine & (slot == index), moved, 0.0)
        total = piece if total is None else total + piece
    return total


def pairs_kernel(rows_ref, step_ref, change_ref, edge_ref, gram_ref):
    rows, _, cols = rows_ref.shape
    lat = lax.axis_index("lat")
    edge_ref[...] = edge_of(lambda i: rows_ref[i - SUB], range(SUB, rows + SUB), cols, lat)
    count = step_ref.shape[0]
    lane = iota((1, cols), 1)
    total = [jnp.zeros((1, cols), F32) for _ in range(count)]
    at = FUNCTIONALS
    for left_ref in (step_ref, change_ref):
        for i in range(count):
            for j in range(i, count):
                value = jnp.sum(left_ref[i] * change_ref[j], axis=(0, 1), keepdims=True)
                total[i] = total[i] + jnp.where(lane == at + j, value, 0.0)
                if i != j:
                    total[j] = total[j] + jnp.where(lane == at + i, value, 0.0)
        at += count
    for i in range(count):
        gram_ref[pl.ds(i, 1), :] = total[i]


def border_layout(planes, rows, pairs):
    tall = rows + 2 * REACH
    short = rows + 2 * SUB
    apart = planes
    joint = apart + tall * pairs
    fields = [joint + short * pairs]
    for size in (tall, short, short, short):
        fields.append(fields[-1] + round_up(size, 8))
    return apart, joint, fields


def border_kernel(levels, edge_ref, low_ref, high_ref, rows_ref, hist_ref, out_ref):
    rows, planes, cols = rows_ref.shape
    pairs = hist_ref.shape[1] // 2
    near = planes + 2 * pairs
    far = SUB * near
    lat = lax.axis_index("lat")
    total = edge_ref[...] + edge_of(
        lambda i: low_ref[pl.ds(i * near, planes), :], range(SUB), cols, lat
    )
    out_ref[pl.ds(0, planes), :] = total + edge_of(
        lambda i: high_ref[pl.ds((i - rows - SUB) * near, planes), :],
        range(rows + SUB, rows + 2 * SUB),
        cols,
        lat,
    )
    apart, joint, fields = border_layout(planes, rows, pairs)
    for start, stop in zip(fields, fields[1:]):
        out_ref[pl.ds(stop - 8, 8), :] = jnp.zeros((8, cols), F32)
    ahead = REACH - SUB
    for i in range(rows + 2 * REACH):
        at = i - REACH
        distant = None
        if at < -SUB:
            distant = (low_ref, i)
        elif at < 0:
            state, here, start = low_ref, low_ref, (at + SUB) * near
        elif at < rows:
            state, here, start = rows_ref.at[at], hist_ref.at[at], 0
        elif at < rows + SUB:
            state, here, start = high_ref, high_ref, (at - rows) * near
        else:
            distant = (high_ref, at - rows - SUB)
        target = pl.ds(apart + i * pairs, pairs)
        if distant is not None:
            ref, at = distant
            out_ref[target, :] = ref[pl.ds(far + at * pairs, pairs), :]
            out_ref[pl.ds(fields[0] + i, 1), :] = ref[pl.ds(far + ahead * pairs + at, 1), :]
            continue
        offset = 0 if 0 <= at < rows else start + planes
        out_ref[target, :] = here[pl.ds(offset, pairs), :]
        out_ref[pl.ds(joint + (i - ahead) * pairs, pairs), :] = here[pl.ds(offset + pairs, pairs), :]
        for field, plane, index in ((0, 5, i), (1, 2, i - ahead), (2, 3, i - ahead), (3, 4, i - ahead)):
            out_ref[pl.ds(fields[field] + index, 1), :] = state[pl.ds(start + levels + plane, 1), :]


def faces_between(here, there, opened=True):
    return jnp.where((here > 0.0) & (there > 0.0) & opened, 0.5 * (here + there), 0.0)


def basis_kernel(planes, rows, pairs, mine_ref, other_ref, out_ref, *work):
    cols = mine_ref.shape[1]
    width = 2 * cols
    apart, joint, fields = border_layout(planes, rows, pairs)
    tall = rows + 2 * REACH
    ahead = REACH - SUB
    opened = iota((1, width), 1) != jnp.where(lax.axis_index("lat") == 0, width - 1, cols - 1)

    def wide(at, size):
        return jnp.concatenate([mine_ref[pl.ds(at, size), :], other_ref[pl.ds(at, size), :]], axis=1)

    def left(value):
        return pltpu.roll(value, width - 1, 1)

    def right(value):
        return pltpu.roll(value, 1, 1)

    spread = [wide(fields[0] + i, 1) for i in range(tall)]
    to_right = [faces_between(value, left(value), opened) for value in spread]
    to_left = [right(value) for value in to_right]
    to_below = [faces_between(spread[i], spread[i + 1]) for i in range(tall - 1)]
    inner = range(ahead, tall - ahead)
    damping = {i: (wide(fields[1] + i - ahead, 1) - SHIFT) * (1.0 / SPAN) for i in inner}
    response_weight = {i: wide(fields[2] + i - ahead, 1) for i in inner}
    weight = {i: wide(fields[3] + i - ahead, 1) for i in inner}
    gain = SURFACE_GAIN / SPAN

    def outflow(get, i):
        value = get(i)
        total = to_right[i] * (value - left(value)) + to_left[i] * (value - right(value))
        total = total + to_below[i] * (value - get(i + 1))
        return value, total + to_below[i - 1] * (value - get(i - 1))

    def mixed(get, ref, reach):
        for i in range(REACH - reach, REACH + rows + reach):
            value, out = outflow(get, i)
            ref[i] = value - out
        return lambda i: ref[i]

    def applied(get, ref, reach):
        for i in range(REACH - reach, REACH + rows + reach):
            value, out = outflow(get, i)
            ref[i] = damping[i] * value + gain * out
        return lambda i: ref[i]

    def keep(slot, get):
        for i in range(rows):
            out_ref[slot, i] = get(i + REACH)[:, :cols]

    def start_apart(i):
        return wide(apart + i * pairs, pairs)

    def start_joint(i):
        return wide(joint + (i - ahead) * pairs, pairs)

    both = (start_apart, start_joint)
    for sweep in range(SUB):
        both = (
            mixed(both[0], work[sweep], REACH - 1 - sweep),
            mixed(both[1], work[SUB + sweep], SUB - 1 - sweep),
        )
    keep(0, both[1])
    reach = REACH - SUB
    powers = [both[0]]
    for power in range(1, ITERS):
        powers.append(applied(powers[-1], work[2 * SUB + power - 1], reach - power))
    for power in range(ITERS):
        keep(1 + power, powers[power])
    reach = ITERS - 1
    slot = 1 + ITERS
    at = 2 * SUB + ITERS - 1
    chains = []
    for factor, power in [(weight, 0)] + [(response_weight, power) for power in range(ITERS)]:
        get = powers[power]
        chains.append(lambda i, factor=factor, get=get: factor[i] * get(i))
    for power in range(1, ITERS):
        for index in range(len(chains)):
            chains[index] = applied(chains[index], work[at], reach - power)
            at += 1
            keep(slot + index * (ITERS - 1) + power - 1, chains[index])


def mix_kernel(
    levels, padded, scale, copies,
    rows_ref, low_ref, high_ref, edge_ref, other_ref, weight_ref, observed_ref, basis_ref, gram_ref,
    mixed_ref, fields_ref, face_ref, here_ref, there_ref, part_ref,
):
    rows, planes, cols = rows_ref.shape
    pairs = basis_ref.shape[2]
    near = planes + 2 * pairs
    lat = lax.axis_index("lat")
    lane = iota((1, cols), 1)
    place = lane % SLOT
    count = rows + 2 * SUB
    level = iota((padded, cols), 0).astype(F32)

    def left(value, by=1):
        return pltpu.roll(value, (cols - by) % cols, 1)

    def right(value, by=1):
        return pltpu.roll(value, by, 1)

    def source(i):
        if i < SUB:
            return low_ref.at[pl.ds(i * near, planes)]
        if i < SUB + rows:
            return rows_ref.at[i - SUB]
        return high_ref.at[pl.ds((i - SUB - rows) * near, planes)]

    def face(depth_here, depth_there, spread_here, spread_there):
        opened = level < jnp.minimum(depth_here, depth_there)
        return jnp.where(opened, 0.5 * (spread_here + spread_there), 0.0)

    spread = edge_ref[pl.ds(levels, 1), :] + other_ref[pl.ds(levels, 1), :]
    depth = edge_ref[pl.ds(levels + 1, 1), :] + other_ref[pl.ds(levels + 1, 1), :]
    within = place < 2 * SUB - 1
    col_depth = jnp.minimum(depth, jnp.where(within, left(depth), 0.0))
    col_spread = 0.5 * (spread + left(spread))
    row_depth = jnp.minimum(depth, left(depth, SLOT))
    row_spread = 0.5 * (spread + left(spread, SLOT))

    def strip_face(limit, value):
        return jnp.where(level < limit, value, 0.0)

    to_left = strip_face(right(col_depth), right(col_spread))
    to_right = strip_face(col_depth, col_spread)
    to_above = strip_face(right(row_depth, SLOT), right(row_spread, SLOT))
    to_below = strip_face(row_depth, row_spread)
    out_of_low = place == jnp.where(lat == 0, SUB - 1, SLOT)
    out_of_high = place == jnp.where(lat == 0, SLOT, SUB)
    over_low = jnp.where(out_of_low, to_right, 0.0)
    over_high = jnp.where(out_of_high, to_left, 0.0)
    own_right = jnp.where(place == SUB - 1, 0.0, to_right)
    own_left = jnp.where(place == SUB, 0.0, to_left)
    start = jnp.where(lat == 0, cols - SUB, 0)
    at_border = (lane >= start) & (lane < start + SUB)

    def spread_out(value, east, west):
        before, after = right(value), left(value)
        above, below = right(value, SLOT), left(value, SLOT)
        total = value + east * (after - value) + west * (before - value)
        return total + to_below * (below - value) + to_above * (above - value)

    parts = []
    extras = [None, None]
    for tracer in range(2):
        at = pl.ds(tracer * padded, padded)
        parts.append(edge_ref[at, :] + other_ref[at, :])

    spreads = [source(i)[pl.ds(levels, 1), :] for i in range(count)]
    depths = [source(i)[pl.ds(levels + 1, 1), :] for i in range(count)]
    for i in range(count - 1):
        face_ref[0, i] = face(depths[i], depths[i + 1], spreads[i], spreads[i + 1])
    for i in range(1, count - 1):
        there = jnp.where(lane < cols - 1, left(depths[i]), 0.0)
        face_ref[1, i] = face(depths[i], there, spreads[i], left(spreads[i]))
        there = jnp.where(lane > 0, right(depths[i]), 0.0)
        face_ref[2, i] = face(depths[i], there, spreads[i], right(spreads[i]))

    for sweep in range(1, SUB + 1):
        for tracer in range(2):
            part = parts[tracer]
            across = over_low * (left(part) - part) + over_high * (right(part) - part)
            extra = extras[tracer]
            if extra is not None:
                across = across + spread_out(extra, own_right, own_left)
            extras[tracer] = across
            if sweep < SUB:
                parts[tracer] = spread_out(part, to_right, to_left)
        target = here_ref if sweep % 2 else there_ref
        for i in range(sweep, count - sweep):
            def field(at):
                if sweep == 1:
                    return source(at)
                return (there_ref if sweep % 2 else here_ref).at[at]

            for tracer in range(2):
                at = pl.ds(tracer * padded, padded)
                centre = field(i)[at, :]
                total = centre + face_ref[0, i] * (field(i + 1)[at, :] - centre)
                total = total + face_ref[0, i - 1] * (field(i - 1)[at, :] - centre)
                total = total + face_ref[1, i] * (left(centre) - centre)
                total = total + face_ref[2, i] * (right(centre) - centre)
                target[i, at, :] = total

    target = here_ref if SUB % 2 else there_ref
    for row in range(rows):
        i = row + SUB
        at = pl.ds(row, levels, stride=rows)
        mixed = []
        for tracer in range(2):
            border = jnp.where(at_border, left(extras[tracer], SLOT * i + SUB), 0.0)
            mixed.append((target[i, pl.ds(tracer * padded, padded), :] + border)[:levels])
        wet = level[:levels] < depths[i]
        weight = weight_ref[at, :]
        misfit = []
        for tracer in range(2):
            mixed_ref[tracer, at, :] = mixed[tracer]
            misfit.append(weight * (mixed[tracer] - observed_ref[tracer, at, :]))
        here = pl.ds(row, 1)
        part_ref[0, here, :] = scale * jnp.sum(
            jnp.where(wet, mixed[0] - mixed[1], 0.0), axis=0, keepdims=True
        )
        part_ref[1, here, :] = jnp.sum(
            jnp.where(wet, misfit[1] - misfit[0], 0.0), axis=0, keepdims=True
        )
        part_ref[2, here, :] = misfit[0][0:1]
        part_ref[3, here, :] = misfit[1][0:1]
    for field, plane in enumerate((3, 4, 5, 2)):
        for row in range(rows):
            part_ref[4 + field, pl.ds(row, 1), :] = rows_ref[row, pl.ds(levels + plane, 1), :]

    sums = [None] * FUNCTIONALS

    def add(at, slot, row, factor):
        value = basis_ref[slot, row] * factor
        sums[at] = value if sums[at] is None else sums[at] + value

    chain = 1 + ITERS
    for row in range(rows):
        here = pl.ds(row, 1)
        get = lambda field: part_ref[field, here, :]
        surface, base = get(0), get(1)
        add(0, 0, row, 0.5 * (get(2) + get(3)))
        add(0, 1, row, 0.5 * (get(2) - get(3)))
        add(1, 1, row, get(5) * surface)
        for power in range(1, ITERS):
            add(1 + power, chain + power - 1, row, surface)
        for j in range(ITERS):
            add(1 + ITERS + j, 1 + j, row, base)
            at = 1 + 2 * ITERS + j * ITERS
            add(at, 1 + j, row, get(4) * surface)
            for power in range(1, ITERS):
                add(at + power, chain + (1 + j) * (ITERS - 1) + power - 1, row, surface)
    half = pairs // 2
    total = gram_ref[...]
    for at in range(FUNCTIONALS):
        value = jnp.sum(sums[at], axis=1, keepdims=True)
        total = total + jnp.where(lane == at, value[:half], 0.0)
        total = total + jnp.where(lane == cols // 2 + at, value[half:], 0.0)
    part_ref[8] = total
    for copy in range(copies):
        fields_ref[copy] = part_ref[...]


def solve_kernel(
    levels, scale,
    mine_ref, other_ref, mixed_ref, depth_ref, step_ref, change_ref,
    state_ref, gradient_ref, direction_ref, kept_ref,
):
    loops, _, rows, cols = mine_ref.shape
    height = loops * rows
    width = 2 * cols
    loop = lax.axis_index("loop")
    closed = jnp.where(lax.axis_index("lat") == 0, width - 1, cols - 1)

    def whole(field):
        return jnp.concatenate(
            [
                jnp.concatenate([mine_ref[i, field], other_ref[i, field]], axis=1)
                for i in range(loops)
            ],
            axis=0,
        )

    def around(field):
        parts = []
        for shift in (loops - 1, 0, 1):
            at = lax.rem(loop + shift, loops)
            parts.append(jnp.concatenate([mine_ref[at, field], other_ref[at, field]], axis=1))
        return jnp.concatenate(parts, axis=0)

    def below(value):
        return pltpu.roll(value, value.shape[0] - 1, 0)

    def above(value):
        return pltpu.roll(value, 1, 0)

    def left(value):
        return pltpu.roll(value, width - 1, 1)

    def right(value):
        return pltpu.roll(value, 1, 1)

    def total(value):
        return jnp.sum(value, axis=(0, 1), keepdims=True)

    def faces(spread):
        row_face = faces_between(spread, below(spread))
        col_face = faces_between(spread, left(spread), iota(spread.shape, 1) != closed)
        return row_face, above(row_face), col_face, right(col_face)

    def outflow(value, to_below, to_above, to_right, to_left):
        total = to_right * (value - left(value)) + to_left * (value - right(value))
        return total + to_below * (value - below(value)) + to_above * (value - above(value))

    gained = [SURFACE_GAIN * face for face in faces(whole(6))]
    damping = whole(7)

    def conjugate(rhs):
        residual = rhs
        search = rhs
        solution = jnp.zeros_like(rhs)
        norm_now = total(rhs * rhs)
        one = jnp.ones((1, 1), F32)
        residual_of = [one]
        search_of = [one]
        solution_of = []
        for sweep in range(ITERS):
            image = damping * search + outflow(search, *gained)
            alpha = norm_now / total(search * image)
            solution = solution + alpha * search
            solution_of = add_up(solution_of, alpha, search_of)
            if sweep < ITERS - 1:
                residual = residual - alpha * image
                norm_next = total(residual * residual)
                beta = norm_next / norm_now
                search = residual + beta * search
                norm_now = norm_next
                image_of = [SHIFT * value for value in search_of]
                image_of = add_up(image_of, SPAN, [None] + search_of)
                residual_of = add_up(residual_of, -alpha, image_of)
                search_of = add_up(residual_of, beta, search_of)
        return solution, solution_of

    def add_up(terms, factor, others):
        result = list(terms) + [None] * (len(others) - len(terms))
        for at, value in enumerate(others):
            if value is not None:
                value = factor * value
                result[at] = value if result[at] is None else result[at] + value
        return result

    def keep(slot, value):
        for i in range(loops):
            kept_ref[slot, i] = value[i * rows : (i + 1) * rows]

    def kept_around(slot):
        return jnp.concatenate(
            [kept_ref[slot, lax.rem(loop + shift, loops)] for shift in (loops - 1, 0, 1)], axis=0
        )

    elevation, elevation_of = conjugate(whole(0))
    keep(0, elevation)
    response, response_of = conjugate(whole(1) + whole(4) * elevation)
    keep(1, response)

    elevation = kept_around(0)
    spread = around(6)
    sea = spread > 0.0
    lowered = jnp.where(sea, around(5) * elevation, 0.0)
    raised = jnp.where(sea, scale * kept_around(1), 0.0)
    near = faces(spread)
    carried = [around(2) - lowered + raised, around(3) + lowered - raised]
    for sweep in range(SUB):
        carried = [value - outflow(value, *near) for value in carried]
    gradient = [jnp.where(sea, value, 0.0)[rows : 2 * rows, :cols] for value in carried]
    for tracer in range(2):
        gradient_ref[tracer] = gradient[tracer]

    count = step_ref.shape[0]
    inner = mine_ref[0, 8]
    for i in range(loops):
        if i:
            inner = inner + mine_ref[i, 8]
        inner = inner + other_ref[i, 8]
    lane = iota((1, cols), 1)
    place = lane % (cols // 2)
    factor = jnp.where(place == 0, 1.0, 0.0)
    for j in range(ITERS):
        factor = jnp.where(place == 1 + j, -elevation_of[j], factor)
        part = scale * response_of[j]
        factor = jnp.where(place == 1 + ITERS + j, part, factor)
        for k in range(ITERS):
            at = 1 + 2 * ITERS + j * ITERS + k
            factor = jnp.where(place == at, part * elevation_of[k], factor)
    products = inner * factor
    step_grad = jnp.sum(jnp.where(lane < cols // 2, products, 0.0), axis=1, keepdims=True)
    change_grad = jnp.sum(jnp.where(lane >= cols // 2, products, 0.0), axis=1, keepdims=True)

    def column(at):
        return inner[:, at : at + 1]

    step_change = [column(FUNCTIONALS + i) for i in range(count)]
    change_change = [column(FUNCTIONALS + count + i) for i in range(count)]
    pick = lambda value, i: value[i : i + 1]
    last = count - 1
    gamma = pick(step_change[last], last) / pick(change_change[last], last)
    rho = [1.0 / pick(step_change[i], i) for i in range(count)]
    factors = [None] * count
    for i in range(count - 1, -1, -1):
        factors[i] = rho[i] * pick(step_grad, i)
        step_grad = step_grad - factors[i] * step_change[i]
        change_grad = change_grad - factors[i] * change_change[i]
    change_grad = gamma * change_grad
    weights = []
    for i in range(count):
        weights.append(factors[i] - rho[i] * pick(change_grad, i))
        change_grad = change_grad + weights[i] * step_change[i]
    factors = [jnp.broadcast_to(value, (rows, cols)) for value in factors]
    weights = [jnp.broadcast_to(value, (rows, cols)) for value in weights]
    for tracer in range(2):
        at = pl.ds(tracer * rows, rows)
        value = gradient[tracer]
        for i in range(count - 1, -1, -1):
            value = value - factors[i] * change_ref[i, at, :]
        value = gamma * value
        for i in range(count):
            value = value + weights[i] * step_ref[i, at, :]
        direction_ref[tracer] = -value

    depth = depth_ref[...]
    here = elevation[rows : 2 * rows, :cols]
    for level in range(levels):
        at = pl.ds(level * rows, rows)
        change = jnp.where(level < depth, here, 0.0)
        state_ref[0, at, :] = mixed_ref[0, at, :] - change
        state_ref[1, at, :] = mixed_ref[1, at, :] + change


def on_device(
    state, observed, weight, control, depth_index, diffusivity, damping, history_step, history_change
):
    _, levels, rows, cols = state.shape
    count = history_step.shape[0]
    padded = round_up(levels + 2, 8)
    planes = 2 * padded
    loops = lax.axis_size("loop")
    lats = lax.axis_size("lat")
    blocks = loops * lats
    scale = levels ** (-0.5)
    flat = (2, levels * rows, cols)
    state = state.reshape(flat)
    observed = observed.reshape(flat)
    weight = weight.reshape(flat[1:])
    step = history_step.reshape(count, 2 * rows, cols)
    change = history_change.reshape(count, 2 * rows, cols)

    pairs = 2 * count
    near = planes + 2 * pairs
    ahead = REACH - SUB
    sent = SUB * near + ahead * pairs + round_up(ahead, 8)
    inputs = (
        state, control, depth_index, diffusivity, damping, weight,
        history_step.reshape(-1, cols), history_change.reshape(-1, cols),
    )
    shapes = ((rows, planes, cols), (rows, 2 * pairs, cols), (sent, cols), (sent, cols))
    packed, hist, up, down = pl.pallas_call(
        functools.partial(pack_kernel, levels, padded),
        out_shape=[jax.ShapeDtypeStruct(shape, F32) for shape in shapes],
        in_specs=[pl.BlockSpec(memory_space=pltpu.HBM)] * len(inputs),
        out_specs=[VMEM] * len(shapes),
        scratch_shapes=[pltpu.VMEM(x.shape, x.dtype) for x in inputs]
        + [pltpu.SemaphoreType.DMA((len(inputs),))],
        compiler_params=pltpu.CompilerParams(vmem_limit_bytes=VMEM_BYTES),
        name="pack",
    )(*(pltpu.with_memory_space_constraint(x, pltpu.HBM) for x in inputs))
    forward = [(i, (i + 1) % loops) for i in range(loops)]
    backward = [(target, source) for source, target in forward]
    swap = [(0, 1), (1, 0)]
    low = lax.ppermute(up, "loop", forward)
    high = lax.ppermute(down, "loop", backward)
    edge, gram = call(pairs_kernel, [(planes, cols), (rows, cols)], name="pairs")(
        packed, step, change
    )
    border = border_layout(planes, rows, pairs)[2][-1]
    (edge,) = call(functools.partial(border_kernel, levels), [(border, cols)], name="border")(
        edge, low, high, packed, hist
    )
    other = lax.ppermute(edge, "lat", swap)
    chains = 1 + ITERS
    buffers = 2 * SUB + ITERS - 1 + chains * (ITERS - 1)
    (basis,) = call(
        functools.partial(basis_kernel, planes, rows, pairs),
        [(1 + ITERS + chains * (ITERS - 1), rows, pairs, cols)],
        scratch=[pltpu.VMEM((rows + 2 * REACH, pairs, 2 * cols), F32)] * buffers,
        name="basis",
    )(edge, other)
    mixed, fields = call(
        functools.partial(mix_kernel, levels, padded, scale, loops),
        [flat, (loops, 9, rows, cols)],
        scratch=[
            pltpu.VMEM((3, rows + 2 * SUB, padded, cols), F32),
            pltpu.VMEM((rows + 2 * SUB, planes, cols), F32),
            pltpu.VMEM((rows + 2 * SUB, planes, cols), F32),
            pltpu.VMEM((9, rows, cols), F32),
        ],
        name="mix",
    )(packed, low, high, edge, other, weight, observed, basis, gram)
    mine = lax.all_to_all(fields, "loop", 0, 0)
    theirs = lax.ppermute(mine, "lat", swap)
    state_next, gradient, direction = call(
        functools.partial(solve_kernel, levels, scale),
        [flat, (2, rows, cols), (2, rows, cols)],
        scratch=[pltpu.VMEM((2, loops, rows, 2 * cols), F32)],
        vmem=VMEM_BYTES if loops <= 16 else 2 * VMEM_BYTES,
        name="solve",
    )(mine, theirs, mixed, depth_index, step, change)
    return (state_next.reshape(2, levels, rows, cols), gradient, direction)


def solution(mesh):
    return jax.shard_map(
        on_device,
        mesh=mesh,
        in_specs=(
            P("members", None, "loop", "lat"),
            P("members", None, "loop", "lat"),
            P(None, "loop", "lat"),
            P("members", "loop", "lat"),
            P("loop", "lat"),
            P("loop", "lat"),
            P("loop", "lat"),
            P("members", None, "loop", "lat"),
            P("members", None, "loop", "lat"),
        ),
        out_specs=(
            P("members", None, "loop", "lat"),
            P("members", "loop", "lat"),
            P("members", "loop", "lat"),
        ),
        check_vma=False,
    )
```

```python
import functools

import jax
import jax.numpy as jnp
from jax import lax
from jax.experimental import pallas as pl
from jax.experimental.pallas import tpu as pltpu
from jax.sharding import PartitionSpec as P

ITERS = 3
SUB = 3
SURFACE_GAIN = 5.0
SLOT = 8
REACH = SUB + 2 * (ITERS - 1)
SHIFT = 5.0
SPAN = 5.0
FUNCTIONALS = 1 + ITERS + ITERS + ITERS * ITERS
GRID = ("loop", "lat")
VMEM = pl.BlockSpec(memory_space=pltpu.VMEM)
F32 = jnp.float32
VMEM_BYTES = 16 * 1024 * 1024


def round_up(value, to):
    return (value + to - 1) // to * to


def call(kernel, out_shapes, scratch=(), vmem=VMEM_BYTES, name=None):
    return pl.pallas_call(
        kernel,
        out_shape=[jax.ShapeDtypeStruct(shape, F32) for shape in out_shapes],
        out_specs=[VMEM] * len(out_shapes),
        scratch_shapes=list(scratch),
        compiler_params=pltpu.CompilerParams(vmem_limit_bytes=vmem),
        name=name,
    )


def iota(shape, dim):
    return lax.broadcasted_iota(jnp.int32, shape, dim)


def state_rows(levels):
    return round_up(2 * levels + 2, 8), levels + 2


def pack_kernel(levels, padded, *refs):
    sources, outs, targets, sems = refs[:6], refs[6:10], refs[10:16], refs[16]
    rows_ref, hist_ref, up_ref, down_ref = outs
    copies = [
        pltpu.make_async_copy(source, target, sems.at[at])
        for at, (source, target) in enumerate(zip(sources, targets))
    ]
    for copy in copies:
        copy.start()
    for copy in copies:
        copy.wait()
    state_ref, control_ref, depth_ref, spread_ref, step_ref, change_ref = targets
    rows, cols = depth_ref.shape
    count = step_ref.shape[0] // (2 * rows)
    pairs = 2 * count
    near, second = state_rows(levels)
    hist = SUB * near
    up_hist_ref = up_ref.at[pl.ds(hist, up_ref.shape[0] - hist)]
    down_hist_ref = down_ref.at[pl.ds(hist, down_ref.shape[0] - hist)]
    far = SUB * 2 * pairs
    depth = depth_ref[...].astype(F32)
    spread = spread_ref[...]
    wet = depth > 0.5
    for row in range(rows):
        here = slice(row, row + 1)
        distant = []
        targets = [(hist_ref.at[row], 0)]
        if row < SUB:
            targets.append((down_hist_ref, row * 2 * pairs))
        elif row < REACH:
            distant.append((down_hist_ref, far + (row - SUB) * pairs))
        if row >= rows - SUB:
            targets.append((up_hist_ref, (row - rows + SUB) * 2 * pairs))
        elif row >= rows - REACH:
            distant.append((up_hist_ref, far + (row - rows + REACH) * pairs))
        for which, ref in enumerate((step_ref, change_ref)):
            both = [ref[pl.ds(tracer * rows + row, count, stride=2 * rows), :] for tracer in range(2)]
            apart = jnp.where(wet[here], both[0] - both[1], 0.0)
            joint = jnp.where(wet[here], both[0] + both[1], 0.0)
            for target, at in targets:
                target[pl.ds(at + which * count, count), :] = apart
                target[pl.ds(at + pairs + which * count, count), :] = joint
            for target, at in distant:
                target[pl.ds(at + which * count, count), :] = apart
    first = iota((levels, cols), 0) == 0
    rest = jnp.zeros((padded - levels, cols), F32)
    fill = jnp.zeros((near - 2 * levels - 2, cols), F32)
    for row in range(rows):
        here = slice(row, row + 1)
        targets = [(rows_ref.at[row], 0, padded)]
        if row < SUB:
            targets.append((down_ref, row * near, second))
        if row >= rows - SUB:
            targets.append((up_ref, (row - rows + SUB) * near, second))
        for tracer in range(2):
            lift = jnp.where(wet[here], control_ref[tracer, here, :], 0.0)
            value = state_ref[tracer, pl.ds(row, levels, stride=rows), :]
            value = value + jnp.where(first, lift, 0.0)
            for target, at, offset in targets:
                target[pl.ds(at + tracer * offset, levels), :] = value
            rows_ref[row, pl.ds(tracer * padded + levels, padded - levels), :] = rest
        for target, at, _ in targets:
            target[pl.ds(at + levels, 1), :] = spread[here]
            target[pl.ds(at + levels + 1, 1), :] = depth[here]
        for target, at, _ in targets[1:]:
            target[pl.ds(at + 2 * levels + 2, near - 2 * levels - 2), :] = fill


def edge_of(rows_of, indices, cols, lat):
    lane = iota((1, cols), 1)
    slot = lane // SLOT
    place = lane % SLOT - SUB * lat
    mine = (place >= 0) & (place < SUB)
    total = None
    for index in indices:
        moved = pltpu.roll(rows_of(index), SLOT * index + SUB, 1)
        piece = jnp.where(mine & (slot == index), moved, 0.0)
        total = piece if total is None else total + piece
    return total


def pairs_kernel(
    rows_ref, step_ref, change_ref, depth_ref, spread_ref, damping_ref, weight_ref,
    edge_ref, still_ref, gram_ref,
):
    rows, _, cols = rows_ref.shape
    lat = lax.axis_index("lat")
    count = step_ref.shape[0]
    lane = iota((1, cols), 1)
    gram = [jnp.zeros((1, cols), F32) for _ in range(count)]
    at = 0
    for left_ref in (step_ref, change_ref):
        for i in range(count):
            for j in range(i, count):
                value = jnp.sum(left_ref[i] * change_ref[j], axis=(0, 1), keepdims=True)
                gram[i] = gram[i] + jnp.where(lane == at + j, value, 0.0)
                if i != j:
                    gram[j] = gram[j] + jnp.where(lane == at + i, value, 0.0)
        at += count
    for i in range(count):
        gram_ref[pl.ds(i, 1), :] = gram[i]
    depth = depth_ref[...]
    total = jnp.zeros((rows, cols), F32)
    for level in range(weight_ref.shape[0] // rows):
        total = total + jnp.where(level < depth, weight_ref[pl.ds(level * rows, rows), :], 0.0)
    fields = (
        jnp.where(depth > 0, spread_ref[...], 0.0),
        damping_ref[...],
        2.0 * total,
        weight_ref[pl.ds(0, rows), :],
        gram_ref[...],
    )
    for copy in range(still_ref.shape[0]):
        for at, field in enumerate(fields):
            still_ref[copy, at] = field
    edge_ref[...] = edge_of(lambda i: rows_ref[i - SUB], range(SUB, rows + SUB), cols, lat)


def faces_between(here, there, opened=True):
    return jnp.where((here > 0.0) & (there > 0.0) & opened, 0.5 * (here + there), 0.0)


def closed_lane(cols):
    return jnp.where(lax.axis_index("lat") == 0, 2 * cols - 1, cols - 1)


def surface_faces(spread, closed):
    height, width = spread.shape
    below = faces_between(spread, pltpu.roll(spread, height - 1, 0))
    right = faces_between(
        spread, pltpu.roll(spread, width - 1, 1), iota(spread.shape, 1) != closed
    )
    return below, pltpu.roll(below, 1, 0), right, pltpu.roll(right, 1, 1)


def gathered(mine_ref, other_ref, field):
    return jnp.concatenate(
        [
            jnp.concatenate([mine_ref[i, field], other_ref[i, field]], axis=1)
            for i in range(mine_ref.shape[0])
        ],
        axis=0,
    )


def gathered_near(mine_ref, other_ref, field):
    loops = mine_ref.shape[0]
    parts = []
    for shift in (loops - 1, 0, 1):
        at = lax.rem(lax.axis_index("loop") + shift, loops)
        parts.append(jnp.concatenate([mine_ref[at, field], other_ref[at, field]], axis=1))
    return jnp.concatenate(parts, axis=0)


def plan_kernel(mine_ref, other_ref, faces_ref, near_ref, plan_ref):
    loops, _, rows, cols = mine_ref.shape
    closed = closed_lane(cols)
    for at, face in enumerate(surface_faces(gathered(mine_ref, other_ref, 0), closed)):
        faces_ref[at] = SURFACE_GAIN * face
    for field in (1, 2):
        faces_ref[3 + field] = gathered(mine_ref, other_ref, field)
    spread = gathered_near(mine_ref, other_ref, 0)
    for at, face in enumerate(surface_faces(spread, closed)):
        near_ref[at] = face
    near_ref[4] = jnp.where(spread > 0.0, gathered_near(mine_ref, other_ref, 3), 0.0)
    near_ref[5] = jnp.where(spread > 0.0, 1.0, 0.0)

    count = plan_ref.shape[0] // 2
    gram = mine_ref[0, 4] + other_ref[0, 4]
    for i in range(1, loops):
        gram = gram + (mine_ref[i, 4] + other_ref[i, 4])
    wide = (count, cols)
    step_change = [jnp.broadcast_to(gram[:, i : i + 1], wide) for i in range(count)]
    change_change = [
        jnp.broadcast_to(gram[:, count + i : count + i + 1], wide) for i in range(count)
    ]
    last = count - 1
    gamma = step_change[last][last:] / change_change[last][last:]
    rho = [1.0 / step_change[i][i : i + 1] for i in range(count)]
    row = iota(wide, 0)
    lane = iota(wide, 1)
    step_grad = jnp.where(lane == row, 1.0, 0.0)
    change_grad = jnp.where(lane == row + count, 1.0, 0.0)
    factors = [None] * count
    for i in range(count - 1, -1, -1):
        factors[i] = rho[i] * step_grad[i : i + 1]
        step_grad = step_grad - factors[i] * step_change[i]
        change_grad = change_grad - factors[i] * change_change[i]
    change_grad = gamma * change_grad
    for i in range(count):
        weight = factors[i] - rho[i] * change_grad[i : i + 1]
        change_grad = change_grad + weight * step_change[i]
        plan_ref[pl.ds(i, 1), :] = -weight
        plan_ref[pl.ds(count + i, 1), :] = gamma * factors[i]
    at = lane[:1] == 2 * count
    plan_ref[pl.ds(0, 1), :] = jnp.where(at, -gamma, plan_ref[pl.ds(0, 1), :])


def halo_kernel(levels, padded, rows, edge_ref, low_ref, high_ref, out_ref, halo_ref):
    planes, cols = out_ref.shape
    lat = lax.axis_index("lat")
    near, second = state_rows(levels)
    rest = jnp.zeros((padded - levels, cols), F32)
    for i in range(2 * SUB):
        ref = low_ref if i < SUB else high_ref
        at = i % SUB * near
        halo_ref[i, pl.ds(levels, padded - levels), :] = rest
        halo_ref[i, pl.ds(padded + levels, padded - levels), :] = rest
        halo_ref[i, pl.ds(0, levels + 2), :] = ref[pl.ds(at, levels + 2), :]
        halo_ref[i, pl.ds(padded, levels), :] = ref[pl.ds(at + second, levels), :]
    total = edge_ref[...] + edge_of(lambda i: halo_ref[i], range(SUB), cols, lat)
    out_ref[...] = total + edge_of(
        lambda i: halo_ref[i - rows], range(rows + SUB, rows + 2 * SUB), cols, lat
    )


def border_kernel(start, low_ref, high_ref, hist_ref, out_ref):
    low_ref = low_ref.at[pl.ds(start, low_ref.shape[0] - start)]
    high_ref = high_ref.at[pl.ds(start, high_ref.shape[0] - start)]
    rows = hist_ref.shape[0]
    pairs = hist_ref.shape[1] // 2
    far = SUB * 2 * pairs
    ahead = REACH - SUB
    joint = (rows + 2 * REACH) * pairs
    for i in range(rows + 2 * REACH):
        at = i - REACH
        target = pl.ds(i * pairs, pairs)
        if at < -SUB:
            out_ref[target, :] = low_ref[pl.ds(far + i * pairs, pairs), :]
            continue
        if at >= rows + SUB:
            out_ref[target, :] = high_ref[pl.ds(far + (at - rows - SUB) * pairs, pairs), :]
            continue
        if at < 0:
            ref, start = low_ref, (at + SUB) * 2 * pairs
        elif at < rows:
            ref, start = hist_ref.at[at], 0
        else:
            ref, start = high_ref, (at - rows) * 2 * pairs
        out_ref[target, :] = ref[pl.ds(start, pairs), :]
        out_ref[pl.ds(joint + (i - ahead) * pairs, pairs), :] = ref[pl.ds(start + pairs, pairs), :]


def basis_kernel(rows, pairs, mine_ref, other_ref, still_ref, still_other_ref, out_ref, *work):
    cols = mine_ref.shape[1]
    width = 2 * cols
    loops = still_ref.shape[0]
    tall = rows + 2 * REACH
    ahead = REACH - SUB
    joint = tall * pairs
    opened = iota((1, width), 1) != closed_lane(cols)

    def wide(at, size):
        return jnp.concatenate([mine_ref[pl.ds(at, size), :], other_ref[pl.ds(at, size), :]], axis=1)

    near = [lax.rem(lax.axis_index("loop") + shift, loops) for shift in (loops - 1, 0, 1)]

    def still(field, i):
        block, row = divmod(i - REACH + rows, rows)
        return jnp.concatenate(
            [
                ref[near[block], field, pl.ds(row, 1), :]
                for ref in (still_ref, still_other_ref)
            ],
            axis=1,
        )

    def left(value):
        return pltpu.roll(value, width - 1, 1)

    def right(value):
        return pltpu.roll(value, 1, 1)

    spread = [still(0, i) for i in range(tall)]
    to_right = [faces_between(value, left(value), opened) for value in spread]
    to_left = [right(value) for value in to_right]
    to_below = [faces_between(spread[i], spread[i + 1]) for i in range(tall - 1)]
    inner = range(ahead, tall - ahead)
    damping = {i: (still(1, i) - SHIFT) * (1.0 / SPAN) for i in inner}
    response_weight = {i: still(2, i) for i in inner}
    weight = {i: still(3, i) for i in inner}
    gain = SURFACE_GAIN / SPAN

    def outflow(get, i):
        value = get(i)
        total = to_right[i] * (value - left(value)) + to_left[i] * (value - right(value))
        total = total + to_below[i] * (value - get(i + 1))
        return value, total + to_below[i - 1] * (value - get(i - 1))

    def mixed(get, ref, reach):
        for i in range(REACH - reach, REACH + rows + reach):
            value, out = outflow(get, i)
            ref[i] = value - out
        return lambda i: ref[i]

    def applied(get, ref, reach):
        for i in range(REACH - reach, REACH + rows + reach):
            value, out = outflow(get, i)
            ref[i] = damping[i] * value + gain * out
        return lambda i: ref[i]

    def keep(slot, get):
        for i in range(rows):
            out_ref[slot, i] = get(i + REACH)[:, :cols]

    def start_apart(i):
        return wide(i * pairs, pairs)

    def start_joint(i):
        return wide(joint + (i - ahead) * pairs, pairs)

    both = (start_apart, start_joint)
    for sweep in range(SUB):
        both = (
            mixed(both[0], work[sweep], REACH - 1 - sweep),
            mixed(both[1], work[SUB + sweep], SUB - 1 - sweep),
        )
    keep(0, both[1])
    reach = REACH - SUB
    powers = [both[0]]
    for power in range(1, ITERS):
        powers.append(applied(powers[-1], work[2 * SUB + power - 1], reach - power))
    for power in range(ITERS):
        keep(1 + power, powers[power])
    reach = ITERS - 1
    slot = 1 + ITERS
    at = 2 * SUB + ITERS - 1
    chains = []
    for factor, power in [(weight, 0)] + [(response_weight, power) for power in range(ITERS)]:
        get = powers[power]
        chains.append(lambda i, factor=factor, get=get: factor[i] * get(i))
    for power in range(1, ITERS):
        for index in range(len(chains)):
            chains[index] = applied(chains[index], work[at], reach - power)
            at += 1
            keep(slot + index * (ITERS - 1) + power - 1, chains[index])


def mix_kernel(
    levels, padded, scale, copies,
    rows_ref, halo_ref, edge_ref, other_ref, weight_ref, observed_ref, basis_ref, still_ref,
    mixed_ref, fields_ref, face_ref, here_ref, there_ref, part_ref,
):
    rows, planes, cols = rows_ref.shape
    pairs = basis_ref.shape[2]
    lat = lax.axis_index("lat")
    lane = iota((1, cols), 1)
    place = lane % SLOT
    count = rows + 2 * SUB
    level = iota((padded, cols), 0).astype(F32)

    def left(value, by=1):
        return pltpu.roll(value, (cols - by) % cols, 1)

    def right(value, by=1):
        return pltpu.roll(value, by, 1)

    def source(i):
        if i < SUB:
            return halo_ref.at[i]
        if i < SUB + rows:
            return rows_ref.at[i - SUB]
        return halo_ref.at[i - rows]

    def face(depth_here, depth_there, spread_here, spread_there):
        opened = level < jnp.minimum(depth_here, depth_there)
        return jnp.where(opened, 0.5 * (spread_here + spread_there), 0.0)

    spread = edge_ref[pl.ds(levels, 1), :] + other_ref[pl.ds(levels, 1), :]
    depth = edge_ref[pl.ds(levels + 1, 1), :] + other_ref[pl.ds(levels + 1, 1), :]
    within = place < 2 * SUB - 1
    col_depth = jnp.minimum(depth, jnp.where(within, left(depth), 0.0))
    col_spread = 0.5 * (spread + left(spread))
    row_depth = jnp.minimum(depth, left(depth, SLOT))
    row_spread = 0.5 * (spread + left(spread, SLOT))

    def strip_face(limit, value):
        return jnp.where(level < limit, value, 0.0)

    to_left = strip_face(right(col_depth), right(col_spread))
    to_right = strip_face(col_depth, col_spread)
    to_above = strip_face(right(row_depth, SLOT), right(row_spread, SLOT))
    to_below = strip_face(row_depth, row_spread)
    out_of_low = place == jnp.where(lat == 0, SUB - 1, SLOT)
    out_of_high = place == jnp.where(lat == 0, SLOT, SUB)
    over_low = jnp.where(out_of_low, to_right, 0.0)
    over_high = jnp.where(out_of_high, to_left, 0.0)
    own_right = jnp.where(place == SUB - 1, 0.0, to_right)
    own_left = jnp.where(place == SUB, 0.0, to_left)
    start = jnp.where(lat == 0, cols - SUB, 0)
    at_border = (lane >= start) & (lane < start + SUB)

    def spread_out(value, east, west):
        before, after = right(value), left(value)
        above, below = right(value, SLOT), left(value, SLOT)
        total = value + east * (after - value) + west * (before - value)
        return total + to_below * (below - value) + to_above * (above - value)

    parts = []
    extras = [None, None]
    for tracer in range(2):
        at = pl.ds(tracer * padded, padded)
        parts.append(edge_ref[at, :] + other_ref[at, :])

    spreads = [source(i)[pl.ds(levels, 1), :] for i in range(count)]
    depths = [source(i)[pl.ds(levels + 1, 1), :] for i in range(count)]
    for i in range(count - 1):
        face_ref[0, i] = face(depths[i], depths[i + 1], spreads[i], spreads[i + 1])
    for i in range(1, count - 1):
        there = jnp.where(lane < cols - 1, left(depths[i]), 0.0)
        face_ref[1, i] = face(depths[i], there, spreads[i], left(spreads[i]))
        there = jnp.where(lane > 0, right(depths[i]), 0.0)
        face_ref[2, i] = face(depths[i], there, spreads[i], right(spreads[i]))

    for sweep in range(1, SUB + 1):
        for tracer in range(2):
            part = parts[tracer]
            across = over_low * (left(part) - part) + over_high * (right(part) - part)
            extra = extras[tracer]
            if extra is not None:
                across = across + spread_out(extra, own_right, own_left)
            extras[tracer] = across
            if sweep < SUB:
                parts[tracer] = spread_out(part, to_right, to_left)
        target = here_ref if sweep % 2 else there_ref
        for i in range(sweep, count - sweep):
            def field(at):
                if sweep == 1:
                    return source(at)
                return (there_ref if sweep % 2 else here_ref).at[at]

            for tracer in range(2):
                at = pl.ds(tracer * padded, padded)
                centre = field(i)[at, :]
                total = centre + face_ref[0, i] * (field(i + 1)[at, :] - centre)
                total = total + face_ref[0, i - 1] * (field(i - 1)[at, :] - centre)
                total = total + face_ref[1, i] * (left(centre) - centre)
                total = total + face_ref[2, i] * (right(centre) - centre)
                target[i, at, :] = total

    target = here_ref if SUB % 2 else there_ref
    for row in range(rows):
        i = row + SUB
        at = pl.ds(row, levels, stride=rows)
        mixed = []
        for tracer in range(2):
            border = jnp.where(at_border, left(extras[tracer], SLOT * i + SUB), 0.0)
            mixed.append((target[i, pl.ds(tracer * padded, padded), :] + border)[:levels])
        wet = level[:levels] < depths[i]
        weight = weight_ref[at, :]
        misfit = []
        for tracer in range(2):
            mixed_ref[tracer, at, :] = mixed[tracer]
            misfit.append(weight * (mixed[tracer] - observed_ref[tracer, at, :]))
        here = pl.ds(row, 1)
        part_ref[0, here, :] = scale * jnp.sum(
            jnp.where(wet, mixed[0] - mixed[1], 0.0), axis=0, keepdims=True
        )
        part_ref[1, here, :] = jnp.sum(
            jnp.where(wet, misfit[1] - misfit[0], 0.0), axis=0, keepdims=True
        )
        part_ref[2, here, :] = misfit[0][0:1]
        part_ref[3, here, :] = misfit[1][0:1]
    sums = [None] * FUNCTIONALS

    def add(at, slot, row, factor):
        value = basis_ref[slot, row] * factor
        sums[at] = value if sums[at] is None else sums[at] + value

    chain = 1 + ITERS
    for row in range(rows):
        here = pl.ds(row, 1)
        get = lambda field: part_ref[field, here, :]
        still = lambda field: still_ref[0, field, here, :]
        surface, base = get(0), get(1)
        add(0, 0, row, 0.5 * (get(2) + get(3)))
        add(0, 1, row, 0.5 * (get(2) - get(3)))
        add(1, 1, row, still(3) * surface)
        for power in range(1, ITERS):
            add(1 + power, chain + power - 1, row, surface)
        for j in range(ITERS):
            add(1 + ITERS + j, 1 + j, row, base)
            at = 1 + 2 * ITERS + j * ITERS
            add(at, 1 + j, row, still(2) * surface)
            for power in range(1, ITERS):
                add(at + power, chain + (1 + j) * (ITERS - 1) + power - 1, row, surface)
    half = pairs // 2
    total = jnp.zeros((half, cols), F32)
    for at in range(FUNCTIONALS):
        value = jnp.sum(sums[at], axis=1, keepdims=True)
        total = total + jnp.where(lane == at, value[:half], 0.0)
        total = total + jnp.where(lane == cols // 2 + at, value[half:], 0.0)
    part_ref[4] = total
    for copy in range(copies):
        fields_ref[copy] = part_ref[...]


def solve_kernel(
    levels, scale,
    mine_ref, other_ref, faces_ref, near_ref, plan_ref, mixed_ref, depth_ref, step_ref, change_ref,
    state_ref, gradient_ref, direction_ref, kept_ref,
):
    loops, _, rows, cols = mine_ref.shape
    loop = lax.axis_index("loop")

    def total(value):
        return jnp.sum(value, axis=(0, 1), keepdims=True)

    def outflow(value, to_below, to_above, to_right, to_left):
        height, width = value.shape
        result = to_right * (value - pltpu.roll(value, width - 1, 1))
        result = result + to_left * (value - pltpu.roll(value, 1, 1))
        result = result + to_below * (value - pltpu.roll(value, height - 1, 0))
        return result + to_above * (value - pltpu.roll(value, 1, 0))

    count = step_ref.shape[0]
    inner = mine_ref[0, 4] + other_ref[0, 4]
    for i in range(1, loops):
        inner = inner + (mine_ref[i, 4] + other_ref[i, 4])
    plan = plan_ref[...]
    shifted = pltpu.roll(inner, cols // 2, 1)
    linear = None
    for i in range(2 * count):
        source = inner if i < count else shifted
        part = plan[:, i : i + 1] * source[i % count : i % count + 1]
        linear = part if linear is None else linear + part
    gamma = plan[:1, 2 * count : 2 * count + 1]

    gained = [faces_ref[i] for i in range(4)]
    damping = faces_ref[4]

    def conjugate(rhs):
        residual = rhs
        search = rhs
        solution = jnp.zeros_like(rhs)
        norm_now = total(rhs * rhs)
        one = jnp.ones((1, 1), F32)
        residual_of = [one]
        search_of = [one]
        solution_of = []
        for sweep in range(ITERS):
            image = damping * search + outflow(search, *gained)
            alpha = norm_now / total(search * image)
            solution = solution + alpha * search
            solution_of = add_up(solution_of, alpha, search_of)
            if sweep < ITERS - 1:
                residual = residual - alpha * image
                norm_next = total(residual * residual)
                beta = norm_next / norm_now
                search = residual + beta * search
                norm_now = norm_next
                image_of = [SHIFT * value for value in search_of]
                image_of = add_up(image_of, SPAN, [None] + search_of)
                residual_of = add_up(residual_of, -alpha, image_of)
                search_of = add_up(residual_of, beta, search_of)
        return solution, solution_of

    def add_up(terms, factor, others):
        result = list(terms) + [None] * (len(others) - len(terms))
        for at, value in enumerate(others):
            if value is not None:
                value = factor * value
                result[at] = value if result[at] is None else result[at] + value
        return result

    def keep(slot, value):
        for i in range(loops):
            kept_ref[slot, i] = value[i * rows : (i + 1) * rows]

    def kept_around(slot):
        return jnp.concatenate(
            [kept_ref[slot, lax.rem(loop + shift, loops)] for shift in (loops - 1, 0, 1)], axis=0
        )

    elevation, elevation_of = conjugate(gathered(mine_ref, other_ref, 0))
    keep(0, elevation)
    pressure = gathered(mine_ref, other_ref, 1) + faces_ref[5] * elevation
    response, response_of = conjugate(pressure)
    keep(1, response)

    lane = iota((1, cols), 1)
    factor = jnp.where(lane == 0, 1.0, 0.0)
    for j in range(ITERS):
        factor = jnp.where(lane == 1 + j, -elevation_of[j], factor)
        part = scale * response_of[j]
        factor = jnp.where(lane == 1 + ITERS + j, part, factor)
        for k in range(ITERS):
            at = 1 + 2 * ITERS + j * ITERS + k
            factor = jnp.where(lane == at, part * elevation_of[k], factor)
    weights = jnp.sum(linear * factor, axis=1, keepdims=True)
    weights = [
        jnp.broadcast_to(weights[i : i + 1], (rows, cols)) for i in range(2 * count)
    ]

    elevation = kept_around(0)
    lowered = near_ref[4] * elevation
    sea = near_ref[5]
    raised = (scale * sea) * kept_around(1)
    near = [near_ref[i] for i in range(4)]
    carried = [
        gathered_near(mine_ref, other_ref, 2) - lowered + raised,
        gathered_near(mine_ref, other_ref, 3) + lowered - raised,
    ]
    for sweep in range(SUB):
        carried = [value - outflow(value, *near) for value in carried]
    for tracer in range(2):
        at = pl.ds(tracer * rows, rows)
        gradient = jnp.where(sea > 0.0, carried[tracer], 0.0)[rows : 2 * rows, :cols]
        gradient_ref[tracer] = gradient
        value = gamma * gradient
        for i in range(count):
            value = value + weights[i] * step_ref[i, at, :]
            value = value + weights[count + i] * change_ref[i, at, :]
        direction_ref[tracer] = value

    depth = depth_ref[...]
    here = elevation[rows : 2 * rows, :cols]
    for level in range(levels):
        at = pl.ds(level * rows, rows)
        change = jnp.where(level < depth, here, 0.0)
        state_ref[0, at, :] = mixed_ref[0, at, :] - change
        state_ref[1, at, :] = mixed_ref[1, at, :] + change


def on_device(
    state, observed, weight, control, depth_index, diffusivity, damping, history_step, history_change
):
    _, levels, rows, cols = state.shape
    count = history_step.shape[0]
    padded = round_up(levels + 2, 8)
    planes = 2 * padded
    loops = lax.axis_size("loop")
    lats = lax.axis_size("lat")
    blocks = loops * lats
    scale = levels ** (-0.5)
    flat = (2, levels * rows, cols)
    state = state.reshape(flat)
    observed = observed.reshape(flat)
    weight = weight.reshape(flat[1:])
    step = history_step.reshape(count, 2 * rows, cols)
    change = history_change.reshape(count, 2 * rows, cols)

    pairs = 2 * count
    inputs = (
        state, control, depth_index, diffusivity,
        history_step.reshape(-1, cols), history_change.reshape(-1, cols),
    )
    states = SUB * state_rows(levels)[0]
    sent = (states + (SUB + REACH) * pairs, cols)
    shapes = ((rows, planes, cols), (rows, 2 * pairs, cols), sent, sent)
    packed, hist, up, down = pl.pallas_call(
        functools.partial(pack_kernel, levels, padded),
        out_shape=[jax.ShapeDtypeStruct(shape, F32) for shape in shapes],
        in_specs=[pl.BlockSpec(memory_space=pltpu.HBM)] * len(inputs),
        out_specs=[VMEM] * len(shapes),
        scratch_shapes=[pltpu.VMEM(x.shape, x.dtype) for x in inputs]
        + [pltpu.SemaphoreType.DMA((len(inputs),))],
        compiler_params=pltpu.CompilerParams(vmem_limit_bytes=VMEM_BYTES),
        name="pack",
    )(*(pltpu.with_memory_space_constraint(x, pltpu.HBM) for x in inputs))
    forward = [(i, (i + 1) % loops) for i in range(loops)]
    backward = [(target, source) for source, target in forward]
    swap = [(0, 1), (1, 0)]
    low = lax.ppermute(up, "loop", forward)
    high = lax.ppermute(down, "loop", backward)
    edge, still, _ = call(
        pairs_kernel, [(planes, cols), (loops, 5, rows, cols), (count, cols)], name="pairs"
    )(packed, step, change, depth_index, diffusivity, damping, weight)
    still_own = still
    still = lax.all_to_all(still, "loop", 0, 0)
    still_other = lax.ppermute(still, "lat", swap)
    height = loops * rows
    large = VMEM_BYTES if loops <= 16 else 2 * VMEM_BYTES
    faces, near, plan = call(
        plan_kernel,
        [(6, height, 2 * cols), (6, 3 * rows, 2 * cols), (pairs, cols)],
        vmem=large,
        name="plan",
    )(still, still_other)
    (border,) = call(
        functools.partial(border_kernel, states),
        [((rows + 2 * REACH + rows + 2 * SUB) * pairs, cols)],
        name="border",
    )(low, high, hist)
    border_other = lax.ppermute(border, "lat", swap)
    chains = 1 + ITERS
    buffers = 2 * SUB + ITERS - 1 + chains * (ITERS - 1)
    (basis,) = call(
        functools.partial(basis_kernel, rows, pairs),
        [(1 + ITERS + chains * (ITERS - 1), rows, pairs, cols)],
        scratch=[pltpu.VMEM((rows + 2 * REACH, pairs, 2 * cols), F32)] * buffers,
        name="basis",
    )(border, border_other, still, still_other)
    edge, halo = call(
        functools.partial(halo_kernel, levels, padded, rows),
        [(planes, cols), (2 * SUB, planes, cols)],
        name="halo",
    )(edge, low, high)
    other = lax.ppermute(edge, "lat", swap)
    mixed, fields = call(
        functools.partial(mix_kernel, levels, padded, scale, loops),
        [flat, (loops, 5, rows, cols)],
        scratch=[
            pltpu.VMEM((3, rows + 2 * SUB, padded, cols), F32),
            pltpu.VMEM((rows + 2 * SUB, planes, cols), F32),
            pltpu.VMEM((rows + 2 * SUB, planes, cols), F32),
            pltpu.VMEM((5, rows, cols), F32),
        ],
        name="mix",
    )(packed, halo, edge, other, weight, observed, basis, still_own)
    mine = lax.all_to_all(fields, "loop", 0, 0)
    theirs = lax.ppermute(mine, "lat", swap)
    state_next, gradient, direction = call(
        functools.partial(solve_kernel, levels, scale),
        [flat, (2, rows, cols), (2, rows, cols)],
        scratch=[pltpu.VMEM((2, loops, rows, 2 * cols), F32)],
        vmem=large,
        name="solve",
    )(mine, theirs, faces, near, plan, mixed, depth_index, step, change)
    return (state_next.reshape(2, levels, rows, cols), gradient, direction)


def solution(mesh):
    return jax.shard_map(
        on_device,
        mesh=mesh,
        in_specs=(
            P("members", None, "loop", "lat"),
            P("members", None, "loop", "lat"),
            P(None, "loop", "lat"),
            P("members", "loop", "lat"),
            P("loop", "lat"),
            P("loop", "lat"),
            P("loop", "lat"),
            P("members", None, "loop", "lat"),
            P("members", None, "loop", "lat"),
        ),
        out_specs=(
            P("members", None, "loop", "lat"),
            P("members", "loop", "lat"),
            P("members", "loop", "lat"),
        ),
        check_vma=False,
    )
```

```python
import functools

import jax
import jax.numpy as jnp
from jax import lax
from jax.experimental import pallas as pl
from jax.experimental.pallas import tpu as pltpu
from jax.sharding import PartitionSpec as P

ITERS = 3
SUB = 3
SURFACE_GAIN = 5.0
SLOT = 8
REACH = SUB + 2 * (ITERS - 1)
SHIFT = 5.0
SPAN = 5.0
FUNCTIONALS = 1 + ITERS + ITERS + ITERS * ITERS
GRID = ("loop", "lat")
VMEM = pl.BlockSpec(memory_space=pltpu.VMEM)
F32 = jnp.float32
VMEM_BYTES = 16 * 1024 * 1024


def round_up(value, to):
    return (value + to - 1) // to * to


def call(kernel, out_shapes, scratch=(), vmem=VMEM_BYTES, name=None):
    return pl.pallas_call(
        kernel,
        out_shape=[jax.ShapeDtypeStruct(shape, F32) for shape in out_shapes],
        out_specs=[VMEM] * len(out_shapes),
        scratch_shapes=list(scratch),
        compiler_params=pltpu.CompilerParams(vmem_limit_bytes=vmem),
        name=name,
    )


def iota(shape, dim):
    return lax.broadcasted_iota(jnp.int32, shape, dim)


def state_rows(levels):
    return round_up(2 * levels + 2, 8), levels + 2


def pack_kernel(levels, padded, *refs):
    sources, outs, targets, sems = refs[:6], refs[6:10], refs[10:16], refs[16]
    rows_ref, hist_ref, up_ref, down_ref = outs
    copies = [
        pltpu.make_async_copy(source, target, sems.at[at])
        for at, (source, target) in enumerate(zip(sources, targets))
    ]
    for copy in copies:
        copy.start()
    for copy in copies:
        copy.wait()
    state_ref, control_ref, depth_ref, spread_ref, step_ref, change_ref = targets
    rows, cols = depth_ref.shape
    count = step_ref.shape[0] // (2 * rows)
    pairs = 2 * count
    near, second = state_rows(levels)
    hist = SUB * near
    up_hist_ref = up_ref.at[pl.ds(hist, up_ref.shape[0] - hist)]
    down_hist_ref = down_ref.at[pl.ds(hist, down_ref.shape[0] - hist)]
    far = SUB * 2 * pairs
    depth = depth_ref[...].astype(F32)
    spread = spread_ref[...]
    wet = depth > 0.5
    for row in range(rows):
        here = slice(row, row + 1)
        distant = []
        targets = [(hist_ref.at[row], 0)]
        if row < SUB:
            targets.append((down_hist_ref, row * 2 * pairs))
        elif row < REACH:
            distant.append((down_hist_ref, far + (row - SUB) * pairs))
        if row >= rows - SUB:
            targets.append((up_hist_ref, (row - rows + SUB) * 2 * pairs))
        elif row >= rows - REACH:
            distant.append((up_hist_ref, far + (row - rows + REACH) * pairs))
        for which, ref in enumerate((step_ref, change_ref)):
            both = [ref[pl.ds(tracer * rows + row, count, stride=2 * rows), :] for tracer in range(2)]
            apart = jnp.where(wet[here], both[0] - both[1], 0.0)
            joint = jnp.where(wet[here], both[0] + both[1], 0.0)
            for target, at in targets:
                target[pl.ds(at + which * count, count), :] = apart
                target[pl.ds(at + pairs + which * count, count), :] = joint
            for target, at in distant:
                target[pl.ds(at + which * count, count), :] = apart
    first = iota((levels, cols), 0) == 0
    rest = jnp.zeros((padded - levels, cols), F32)
    fill = jnp.zeros((near - 2 * levels - 2, cols), F32)
    for row in range(rows):
        here = slice(row, row + 1)
        targets = [(rows_ref.at[row], 0, padded)]
        if row < SUB:
            targets.append((down_ref, row * near, second))
        if row >= rows - SUB:
            targets.append((up_ref, (row - rows + SUB) * near, second))
        for tracer in range(2):
            lift = jnp.where(wet[here], control_ref[tracer, here, :], 0.0)
            value = state_ref[tracer, pl.ds(row, levels, stride=rows), :]
            value = value + jnp.where(first, lift, 0.0)
            for target, at, offset in targets:
                target[pl.ds(at + tracer * offset, levels), :] = value
            rows_ref[row, pl.ds(tracer * padded + levels, padded - levels), :] = rest
        for target, at, _ in targets:
            target[pl.ds(at + levels, 1), :] = spread[here]
            target[pl.ds(at + levels + 1, 1), :] = depth[here]
        for target, at, _ in targets[1:]:
            target[pl.ds(at + 2 * levels + 2, near - 2 * levels - 2), :] = fill


def edge_of(rows_of, indices, cols, lat):
    lane = iota((1, cols), 1)
    slot = lane // SLOT
    place = lane % SLOT - SUB * lat
    mine = (place >= 0) & (place < SUB)
    total = None
    for index in indices:
        moved = pltpu.roll(rows_of(index), SLOT * index + SUB, 1)
        piece = jnp.where(mine & (slot == index), moved, 0.0)
        total = piece if total is None else total + piece
    return total


def pairs_kernel(
    rows_ref, step_ref, change_ref, depth_ref, spread_ref, damping_ref, weight_ref,
    edge_ref, still_ref, own_ref, gram_ref,
):
    rows, _, cols = rows_ref.shape
    lat = lax.axis_index("lat")
    count = step_ref.shape[0]
    lane = iota((1, cols), 1)
    gram = [jnp.zeros((1, cols), F32) for _ in range(count)]
    at = 0
    for left_ref in (step_ref, change_ref):
        for i in range(count):
            for j in range(i, count):
                value = jnp.sum(left_ref[i] * change_ref[j], axis=(0, 1), keepdims=True)
                gram[i] = gram[i] + jnp.where(lane == at + j, value, 0.0)
                if i != j:
                    gram[j] = gram[j] + jnp.where(lane == at + i, value, 0.0)
        at += count
    for i in range(count):
        gram_ref[pl.ds(i, 1), :] = gram[i]
    depth = depth_ref[...]
    total = jnp.zeros((rows, cols), F32)
    for level in range(weight_ref.shape[0] // rows):
        total = total + jnp.where(level < depth, weight_ref[pl.ds(level * rows, rows), :], 0.0)
    fields = (
        jnp.where(depth > 0, spread_ref[...], 0.0),
        damping_ref[...],
        2.0 * total,
        weight_ref[pl.ds(0, rows), :],
        gram_ref[...],
    )
    for at, field in enumerate(fields):
        own_ref[at] = field
        for copy in range(still_ref.shape[0]):
            still_ref[copy, at] = field
    edge_ref[...] = edge_of(lambda i: rows_ref[i - SUB], range(SUB, rows + SUB), cols, lat)


def faces_between(here, there, opened=True):
    return jnp.where((here > 0.0) & (there > 0.0) & opened, 0.5 * (here + there), 0.0)


def closed_lane(cols):
    return jnp.where(lax.axis_index("lat") == 0, 2 * cols - 1, cols - 1)


def surface_faces(spread, closed):
    height, width = spread.shape
    below = faces_between(spread, pltpu.roll(spread, height - 1, 0))
    right = faces_between(
        spread, pltpu.roll(spread, width - 1, 1), iota(spread.shape, 1) != closed
    )
    return below, pltpu.roll(below, 1, 0), right, pltpu.roll(right, 1, 1)


def gathered(mine_ref, other_ref, field):
    return jnp.concatenate(
        [
            jnp.concatenate([mine_ref[i, field], other_ref[i, field]], axis=1)
            for i in range(mine_ref.shape[0])
        ],
        axis=0,
    )


def gathered_near(mine_ref, other_ref, field):
    loops = mine_ref.shape[0]
    parts = []
    for shift in (loops - 1, 0, 1):
        at = lax.rem(lax.axis_index("loop") + shift, loops)
        parts.append(jnp.concatenate([mine_ref[at, field], other_ref[at, field]], axis=1))
    return jnp.concatenate(parts, axis=0)


def plan_kernel(mine_ref, other_ref, faces_ref, near_ref, plan_ref):
    loops, _, rows, cols = mine_ref.shape
    closed = closed_lane(cols)
    for at, face in enumerate(surface_faces(gathered(mine_ref, other_ref, 0), closed)):
        faces_ref[at] = SURFACE_GAIN * face
    for field in (1, 2):
        faces_ref[3 + field] = gathered(mine_ref, other_ref, field)
    spread = gathered_near(mine_ref, other_ref, 0)
    for at, face in enumerate(surface_faces(spread, closed)):
        near_ref[at] = face
    near_ref[4] = jnp.where(spread > 0.0, gathered_near(mine_ref, other_ref, 3), 0.0)
    near_ref[5] = jnp.where(spread > 0.0, 1.0, 0.0)

    count = plan_ref.shape[0] // 2
    gram = mine_ref[0, 4] + other_ref[0, 4]
    for i in range(1, loops):
        gram = gram + (mine_ref[i, 4] + other_ref[i, 4])
    wide = (count, cols)
    step_change = [jnp.broadcast_to(gram[:, i : i + 1], wide) for i in range(count)]
    change_change = [
        jnp.broadcast_to(gram[:, count + i : count + i + 1], wide) for i in range(count)
    ]
    last = count - 1
    gamma = step_change[last][last:] / change_change[last][last:]
    rho = [1.0 / step_change[i][i : i + 1] for i in range(count)]
    row = iota(wide, 0)
    lane = iota(wide, 1)
    step_grad = jnp.where(lane == row, 1.0, 0.0)
    change_grad = jnp.where(lane == row + count, 1.0, 0.0)
    factors = [None] * count
    for i in range(count - 1, -1, -1):
        factors[i] = rho[i] * step_grad[i : i + 1]
        step_grad = step_grad - factors[i] * step_change[i]
        change_grad = change_grad - factors[i] * change_change[i]
    change_grad = gamma * change_grad
    for i in range(count):
        weight = factors[i] - rho[i] * change_grad[i : i + 1]
        change_grad = change_grad + weight * step_change[i]
        plan_ref[pl.ds(i, 1), :] = -weight
        plan_ref[pl.ds(count + i, 1), :] = gamma * factors[i]
    at = lane[:1] == 2 * count
    plan_ref[pl.ds(0, 1), :] = jnp.where(at, -gamma, plan_ref[pl.ds(0, 1), :])


def border_kernel(
    levels, padded, edge_ref, low_ref, high_ref, hist_ref, out_ref, halo_ref
):
    planes, cols = edge_ref.shape
    rows = hist_ref.shape[0]
    pairs = hist_ref.shape[1] // 2
    lat = lax.axis_index("lat")
    near, second = state_rows(levels)
    rest = jnp.zeros((padded - levels, cols), F32)
    for i in range(2 * SUB):
        ref = low_ref if i < SUB else high_ref
        at = i % SUB * near
        halo_ref[i, pl.ds(levels, padded - levels), :] = rest
        halo_ref[i, pl.ds(padded + levels, padded - levels), :] = rest
        halo_ref[i, pl.ds(0, levels + 2), :] = ref[pl.ds(at, levels + 2), :]
        halo_ref[i, pl.ds(padded, levels), :] = ref[pl.ds(at + second, levels), :]
    total = edge_ref[...] + edge_of(lambda i: halo_ref[i], range(SUB), cols, lat)
    out_ref[pl.ds(0, planes), :] = total + edge_of(
        lambda i: halo_ref[i - rows], range(rows + SUB, rows + 2 * SUB), cols, lat
    )
    start = SUB * near
    far = start + SUB * 2 * pairs
    ahead = REACH - SUB
    apart = planes
    joint = apart + (rows + 2 * REACH) * pairs
    for i in range(rows + 2 * REACH):
        at = i - REACH
        target = pl.ds(apart + i * pairs, pairs)
        if at < -SUB:
            out_ref[target, :] = low_ref[pl.ds(far + i * pairs, pairs), :]
            continue
        if at >= rows + SUB:
            out_ref[target, :] = high_ref[pl.ds(far + (at - rows - SUB) * pairs, pairs), :]
            continue
        if at < 0:
            ref, here = low_ref, start + (at + SUB) * 2 * pairs
        elif at < rows:
            ref, here = hist_ref.at[at], 0
        else:
            ref, here = high_ref, start + (at - rows) * 2 * pairs
        out_ref[target, :] = ref[pl.ds(here, pairs), :]
        target = pl.ds(joint + (i - ahead) * pairs, pairs)
        out_ref[target, :] = ref[pl.ds(here + pairs, pairs), :]


def basis_kernel(planes, rows, pairs, mine_ref, other_ref, still_ref, still_other_ref, out_ref, *work):
    cols = mine_ref.shape[1]
    width = 2 * cols
    loops = still_ref.shape[0]
    tall = rows + 2 * REACH
    ahead = REACH - SUB
    apart = planes
    joint = apart + tall * pairs
    opened = iota((1, width), 1) != closed_lane(cols)

    def wide(at, size):
        return jnp.concatenate([mine_ref[pl.ds(at, size), :], other_ref[pl.ds(at, size), :]], axis=1)

    near = [lax.rem(lax.axis_index("loop") + shift, loops) for shift in (loops - 1, 0, 1)]

    def still(field, i):
        block, row = divmod(i - REACH + rows, rows)
        return jnp.concatenate(
            [
                ref[near[block], field, pl.ds(row, 1), :]
                for ref in (still_ref, still_other_ref)
            ],
            axis=1,
        )

    def left(value):
        return pltpu.roll(value, width - 1, 1)

    def right(value):
        return pltpu.roll(value, 1, 1)

    spread = [still(0, i) for i in range(tall)]
    to_right = [faces_between(value, left(value), opened) for value in spread]
    to_left = [right(value) for value in to_right]
    to_below = [faces_between(spread[i], spread[i + 1]) for i in range(tall - 1)]
    inner = range(ahead, tall - ahead)
    damping = {i: (still(1, i) - SHIFT) * (1.0 / SPAN) for i in inner}
    response_weight = {i: still(2, i) for i in inner}
    weight = {i: still(3, i) for i in inner}
    gain = SURFACE_GAIN / SPAN

    def outflow(get, i):
        value = get(i)
        total = to_right[i] * (value - left(value)) + to_left[i] * (value - right(value))
        total = total + to_below[i] * (value - get(i + 1))
        return value, total + to_below[i - 1] * (value - get(i - 1))

    def mixed(get, ref, reach):
        for i in range(REACH - reach, REACH + rows + reach):
            value, out = outflow(get, i)
            ref[i] = value - out
        return lambda i: ref[i]

    def applied(get, ref, reach):
        for i in range(REACH - reach, REACH + rows + reach):
            value, out = outflow(get, i)
            ref[i] = damping[i] * value + gain * out
        return lambda i: ref[i]

    def keep(slot, get):
        for i in range(rows):
            out_ref[slot, i] = get(i + REACH)[:, :cols]

    def start_apart(i):
        return wide(apart + i * pairs, pairs)

    def start_joint(i):
        return wide(joint + (i - ahead) * pairs, pairs)

    both = (start_apart, start_joint)
    for sweep in range(SUB):
        both = (
            mixed(both[0], work[sweep], REACH - 1 - sweep),
            mixed(both[1], work[SUB + sweep], SUB - 1 - sweep),
        )
    keep(0, both[1])
    reach = REACH - SUB
    powers = [both[0]]
    for power in range(1, ITERS):
        powers.append(applied(powers[-1], work[2 * SUB + power - 1], reach - power))
    for power in range(ITERS):
        keep(1 + power, powers[power])
    reach = ITERS - 1
    slot = 1 + ITERS
    at = 2 * SUB + ITERS - 1
    chains = []
    for factor, power in [(weight, 0)] + [(response_weight, power) for power in range(ITERS)]:
        get = powers[power]
        chains.append(lambda i, factor=factor, get=get: factor[i] * get(i))
    for power in range(1, ITERS):
        for index in range(len(chains)):
            chains[index] = applied(chains[index], work[at], reach - power)
            at += 1
            keep(slot + index * (ITERS - 1) + power - 1, chains[index])


def mix_kernel(
    levels, padded, rows_ref, halo_ref, out_ref, face_ref, here_ref, there_ref
):
    rows, _, cols = rows_ref.shape
    lane = iota((1, cols), 1)
    count = rows + 2 * SUB
    level = iota((padded, cols), 0).astype(F32)

    def left(value):
        return pltpu.roll(value, cols - 1, 1)

    def right(value):
        return pltpu.roll(value, 1, 1)

    def source(i):
        if i < SUB:
            return halo_ref.at[i]
        if i < SUB + rows:
            return rows_ref.at[i - SUB]
        return halo_ref.at[i - rows]

    def face(depth_here, depth_there, spread_here, spread_there):
        opened = level < jnp.minimum(depth_here, depth_there)
        return jnp.where(opened, 0.5 * (spread_here + spread_there), 0.0)

    spreads = [source(i)[pl.ds(levels, 1), :] for i in range(count)]
    depths = [source(i)[pl.ds(levels + 1, 1), :] for i in range(count)]
    for i in range(count - 1):
        face_ref[0, i] = face(depths[i], depths[i + 1], spreads[i], spreads[i + 1])
    for i in range(1, count - 1):
        there = jnp.where(lane < cols - 1, left(depths[i]), 0.0)
        face_ref[1, i] = face(depths[i], there, spreads[i], left(spreads[i]))
        there = jnp.where(lane > 0, right(depths[i]), 0.0)
        face_ref[2, i] = face(depths[i], there, spreads[i], right(spreads[i]))

    for sweep in range(1, SUB + 1):
        target = here_ref if sweep % 2 else there_ref
        for i in range(sweep, count - sweep):
            def field(at):
                if sweep == 1:
                    return source(at)
                return (there_ref if sweep % 2 else here_ref).at[at]

            into = out_ref.at[i - SUB] if sweep == SUB else target.at[i]
            for tracer in range(2):
                at = pl.ds(tracer * padded, padded)
                centre = field(i)[at, :]
                total = centre + face_ref[0, i] * (field(i + 1)[at, :] - centre)
                total = total + face_ref[0, i - 1] * (field(i - 1)[at, :] - centre)
                total = total + face_ref[1, i] * (left(centre) - centre)
                total = total + face_ref[2, i] * (right(centre) - centre)
                into[at, :] = total


def fields_kernel(
    levels, padded, scale,
    rows_ref, main_ref, edge_ref, other_ref, weight_ref, observed_ref, basis_ref, still_ref,
    mixed_ref, fields_ref, part_ref,
):
    rows, _, cols = rows_ref.shape
    pairs = basis_ref.shape[2]
    lat = lax.axis_index("lat")
    lane = iota((1, cols), 1)
    place = lane % SLOT
    level = iota((padded, cols), 0).astype(F32)

    def left(value, by=1):
        return pltpu.roll(value, (cols - by) % cols, 1)

    def right(value, by=1):
        return pltpu.roll(value, by, 1)

    spread = edge_ref[pl.ds(levels, 1), :] + other_ref[pl.ds(levels, 1), :]
    depth = edge_ref[pl.ds(levels + 1, 1), :] + other_ref[pl.ds(levels + 1, 1), :]
    within = place < 2 * SUB - 1
    col_depth = jnp.minimum(depth, jnp.where(within, left(depth), 0.0))
    col_spread = 0.5 * (spread + left(spread))
    row_depth = jnp.minimum(depth, left(depth, SLOT))
    row_spread = 0.5 * (spread + left(spread, SLOT))

    def strip_face(limit, value):
        return jnp.where(level < limit, value, 0.0)

    to_left = strip_face(right(col_depth), right(col_spread))
    to_right = strip_face(col_depth, col_spread)
    to_above = strip_face(right(row_depth, SLOT), right(row_spread, SLOT))
    to_below = strip_face(row_depth, row_spread)
    out_of_low = place == jnp.where(lat == 0, SUB - 1, SLOT)
    out_of_high = place == jnp.where(lat == 0, SLOT, SUB)
    over_low = jnp.where(out_of_low, to_right, 0.0)
    over_high = jnp.where(out_of_high, to_left, 0.0)
    own_right = jnp.where(place == SUB - 1, 0.0, to_right)
    own_left = jnp.where(place == SUB, 0.0, to_left)
    start = jnp.where(lat == 0, cols - SUB, 0)
    at_border = (lane >= start) & (lane < start + SUB)

    def spread_out(value, east, west):
        before, after = right(value), left(value)
        above, below = right(value, SLOT), left(value, SLOT)
        total = value + east * (after - value) + west * (before - value)
        return total + to_below * (below - value) + to_above * (above - value)

    parts = []
    extras = [None, None]
    for tracer in range(2):
        at = pl.ds(tracer * padded, padded)
        parts.append(edge_ref[at, :] + other_ref[at, :])

    for sweep in range(1, SUB + 1):
        for tracer in range(2):
            part = parts[tracer]
            across = over_low * (left(part) - part) + over_high * (right(part) - part)
            extra = extras[tracer]
            if extra is not None:
                across = across + spread_out(extra, own_right, own_left)
            extras[tracer] = across
            if sweep < SUB:
                parts[tracer] = spread_out(part, to_right, to_left)

    for row in range(rows):
        i = row + SUB
        at = pl.ds(row, levels, stride=rows)
        mixed = []
        for tracer in range(2):
            border = jnp.where(at_border, left(extras[tracer], SLOT * i + SUB), 0.0)
            mixed.append((main_ref[row, pl.ds(tracer * padded, padded), :] + border)[:levels])
        wet = level[:levels] < rows_ref[row, pl.ds(levels + 1, 1), :]
        weight = weight_ref[at, :]
        misfit = []
        for tracer in range(2):
            mixed_ref[tracer, at, :] = mixed[tracer]
            misfit.append(weight * (mixed[tracer] - observed_ref[tracer, at, :]))
        here = pl.ds(row, 1)
        part_ref[0, here, :] = scale * jnp.sum(
            jnp.where(wet, mixed[0] - mixed[1], 0.0), axis=0, keepdims=True
        )
        part_ref[1, here, :] = jnp.sum(
            jnp.where(wet, misfit[1] - misfit[0], 0.0), axis=0, keepdims=True
        )
        part_ref[2, here, :] = misfit[0][0:1]
        part_ref[3, here, :] = misfit[1][0:1]
    sums = [None] * FUNCTIONALS

    def add(at, slot, row, factor):
        value = basis_ref[slot, row] * factor
        sums[at] = value if sums[at] is None else sums[at] + value

    chain = 1 + ITERS
    for row in range(rows):
        here = pl.ds(row, 1)
        get = lambda field: part_ref[field, here, :]
        still = lambda field: still_ref[field, here, :]
        surface, base = get(0), get(1)
        add(0, 0, row, 0.5 * (get(2) + get(3)))
        add(0, 1, row, 0.5 * (get(2) - get(3)))
        add(1, 1, row, still(3) * surface)
        for power in range(1, ITERS):
            add(1 + power, chain + power - 1, row, surface)
        for j in range(ITERS):
            add(1 + ITERS + j, 1 + j, row, base)
            at = 1 + 2 * ITERS + j * ITERS
            add(at, 1 + j, row, still(2) * surface)
            for power in range(1, ITERS):
                add(at + power, chain + (1 + j) * (ITERS - 1) + power - 1, row, surface)
    half = pairs // 2
    total = jnp.zeros((half, cols), F32)
    for at in range(FUNCTIONALS):
        value = jnp.sum(sums[at], axis=1, keepdims=True)
        total = total + jnp.where(lane == at, value[:half], 0.0)
        total = total + jnp.where(lane == cols // 2 + at, value[half:], 0.0)
    part_ref[4] = total
    for copy in range(fields_ref.shape[0]):
        fields_ref[copy] = part_ref[...]


def solve_kernel(
    levels, scale,
    mine_ref, other_ref, faces_ref, near_ref, plan_ref, mixed_ref, depth_ref, step_ref, change_ref,
    state_ref, gradient_ref, direction_ref, kept_ref,
):
    loops, _, rows, cols = mine_ref.shape
    loop = lax.axis_index("loop")

    def total(value):
        return jnp.sum(value, axis=(0, 1), keepdims=True)

    def outflow(value, to_below, to_above, to_right, to_left):
        height, width = value.shape
        result = to_right * (value - pltpu.roll(value, width - 1, 1))
        result = result + to_left * (value - pltpu.roll(value, 1, 1))
        result = result + to_below * (value - pltpu.roll(value, height - 1, 0))
        return result + to_above * (value - pltpu.roll(value, 1, 0))

    count = step_ref.shape[0]
    inner = mine_ref[0, 4] + other_ref[0, 4]
    for i in range(1, loops):
        inner = inner + (mine_ref[i, 4] + other_ref[i, 4])
    plan = plan_ref[...]
    shifted = pltpu.roll(inner, cols // 2, 1)
    linear = None
    for i in range(2 * count):
        source = inner if i < count else shifted
        part = plan[:, i : i + 1] * source[i % count : i % count + 1]
        linear = part if linear is None else linear + part
    gamma = plan[:1, 2 * count : 2 * count + 1]

    gained = [faces_ref[i] for i in range(4)]
    damping = faces_ref[4]

    def conjugate(rhs):
        residual = rhs
        search = rhs
        solution = jnp.zeros_like(rhs)
        norm_now = total(rhs * rhs)
        one = jnp.ones((1, 1), F32)
        residual_of = [one]
        search_of = [one]
        solution_of = []
        for sweep in range(ITERS):
            image = damping * search + outflow(search, *gained)
            alpha = norm_now / total(search * image)
            solution = solution + alpha * search
            solution_of = add_up(solution_of, alpha, search_of)
            if sweep < ITERS - 1:
                residual = residual - alpha * image
                norm_next = total(residual * residual)
                beta = norm_next / norm_now
                search = residual + beta * search
                norm_now = norm_next
                image_of = [SHIFT * value for value in search_of]
                image_of = add_up(image_of, SPAN, [None] + search_of)
                residual_of = add_up(residual_of, -alpha, image_of)
                search_of = add_up(residual_of, beta, search_of)
        return solution, solution_of

    def add_up(terms, factor, others):
        result = list(terms) + [None] * (len(others) - len(terms))
        for at, value in enumerate(others):
            if value is not None:
                value = factor * value
                result[at] = value if result[at] is None else result[at] + value
        return result

    def keep(slot, value):
        for i in range(loops):
            kept_ref[slot, i] = value[i * rows : (i + 1) * rows]

    def kept_around(slot):
        return jnp.concatenate(
            [kept_ref[slot, lax.rem(loop + shift, loops)] for shift in (loops - 1, 0, 1)], axis=0
        )

    elevation, elevation_of = conjugate(gathered(mine_ref, other_ref, 0))
    keep(0, elevation)
    pressure = gathered(mine_ref, other_ref, 1) + faces_ref[5] * elevation
    response, response_of = conjugate(pressure)
    keep(1, response)

    lane = iota((1, cols), 1)
    factor = jnp.where(lane == 0, 1.0, 0.0)
    for j in range(ITERS):
        factor = jnp.where(lane == 1 + j, -elevation_of[j], factor)
        part = scale * response_of[j]
        factor = jnp.where(lane == 1 + ITERS + j, part, factor)
        for k in range(ITERS):
            at = 1 + 2 * ITERS + j * ITERS + k
            factor = jnp.where(lane == at, part * elevation_of[k], factor)
    weights = jnp.sum(linear * factor, axis=1, keepdims=True)
    weights = [
        jnp.broadcast_to(weights[i : i + 1], (rows, cols)) for i in range(2 * count)
    ]

    elevation = kept_around(0)
    lowered = near_ref[4] * elevation
    sea = near_ref[5]
    raised = (scale * sea) * kept_around(1)
    near = [near_ref[i] for i in range(4)]
    carried = [
        gathered_near(mine_ref, other_ref, 2) - lowered + raised,
        gathered_near(mine_ref, other_ref, 3) + lowered - raised,
    ]
    for sweep in range(SUB):
        carried = [value - outflow(value, *near) for value in carried]
    for tracer in range(2):
        at = pl.ds(tracer * rows, rows)
        gradient = jnp.where(sea > 0.0, carried[tracer], 0.0)[rows : 2 * rows, :cols]
        gradient_ref[tracer] = gradient
        value = gamma * gradient
        for i in range(count):
            value = value + weights[i] * step_ref[i, at, :]
            value = value + weights[count + i] * change_ref[i, at, :]
        direction_ref[tracer] = value

    depth = depth_ref[...]
    here = elevation[rows : 2 * rows, :cols]
    for level in range(levels):
        at = pl.ds(level * rows, rows)
        change = jnp.where(level < depth, here, 0.0)
        state_ref[0, at, :] = mixed_ref[0, at, :] - change
        state_ref[1, at, :] = mixed_ref[1, at, :] + change


def on_device(
    state, observed, weight, control, depth_index, diffusivity, damping, history_step, history_change
):
    _, levels, rows, cols = state.shape
    count = history_step.shape[0]
    padded = round_up(levels + 2, 8)
    planes = 2 * padded
    loops = lax.axis_size("loop")
    lats = lax.axis_size("lat")
    blocks = loops * lats
    scale = levels ** (-0.5)
    flat = (2, levels * rows, cols)
    state = state.reshape(flat)
    observed = observed.reshape(flat)
    weight = weight.reshape(flat[1:])
    step = history_step.reshape(count, 2 * rows, cols)
    change = history_change.reshape(count, 2 * rows, cols)

    pairs = 2 * count
    inputs = (
        state, control, depth_index, diffusivity,
        history_step.reshape(-1, cols), history_change.reshape(-1, cols),
    )
    states = SUB * state_rows(levels)[0]
    sent = (states + (SUB + REACH) * pairs, cols)
    shapes = ((rows, planes, cols), (rows, 2 * pairs, cols), sent, sent)
    packed, hist, up, down = pl.pallas_call(
        functools.partial(pack_kernel, levels, padded),
        out_shape=[jax.ShapeDtypeStruct(shape, F32) for shape in shapes],
        in_specs=[pl.BlockSpec(memory_space=pltpu.HBM)] * len(inputs),
        out_specs=[VMEM] * len(shapes),
        scratch_shapes=[pltpu.VMEM(x.shape, x.dtype) for x in inputs]
        + [pltpu.SemaphoreType.DMA((len(inputs),))],
        compiler_params=pltpu.CompilerParams(vmem_limit_bytes=VMEM_BYTES),
        name="pack",
    )(*(pltpu.with_memory_space_constraint(x, pltpu.HBM) for x in inputs))
    forward = [(i, (i + 1) % loops) for i in range(loops)]
    backward = [(target, source) for source, target in forward]
    swap = [(0, 1), (1, 0)]
    low = lax.ppermute(up, "loop", forward)
    high = lax.ppermute(down, "loop", backward)
    edge, still, still_own, _ = call(
        pairs_kernel,
        [(planes, cols), (loops, 5, rows, cols), (5, rows, cols), (count, cols)],
        name="pairs",
    )(packed, step, change, depth_index, diffusivity, damping, weight)
    still = lax.all_to_all(still, "loop", 0, 0)
    still_other = lax.ppermute(still, "lat", swap)
    height = loops * rows
    large = VMEM_BYTES if loops <= 16 else 2 * VMEM_BYTES
    faces, near, plan = call(
        plan_kernel,
        [(6, height, 2 * cols), (6, 3 * rows, 2 * cols), (pairs, cols)],
        vmem=large,
        name="plan",
    )(still, still_other)
    swapped = planes + (rows + 2 * REACH + rows + 2 * SUB) * pairs
    border, halo = call(
        functools.partial(border_kernel, levels, padded),
        [(swapped, cols), (2 * SUB, planes, cols)],
        name="border",
    )(edge, low, high, hist)
    other = lax.ppermute(border, "lat", swap)
    tall = rows + 2 * SUB
    (mixed,) = call(
        functools.partial(mix_kernel, levels, padded),
        [(rows, planes, cols)],
        scratch=[pltpu.VMEM((3, tall, padded, cols), F32)]
        + [pltpu.VMEM((tall, planes, cols), F32)] * 2,
        name="mix",
    )(packed, halo)
    chains = 1 + ITERS
    buffers = 2 * SUB + ITERS - 1 + chains * (ITERS - 1)
    (basis,) = call(
        functools.partial(basis_kernel, planes, rows, pairs),
        [(1 + ITERS + chains * (ITERS - 1), rows, pairs, cols)],
        scratch=[pltpu.VMEM((rows + 2 * REACH, pairs, 2 * cols), F32)] * buffers,
        name="basis",
    )(border, other, still, still_other)
    mixed, fields = call(
        functools.partial(fields_kernel, levels, padded, scale),
        [flat, (loops, 5, rows, cols)],
        scratch=[pltpu.VMEM((5, rows, cols), F32)],
        name="fields",
    )(packed, mixed, border, other, weight, observed, basis, still_own)
    mine = lax.all_to_all(fields, "loop", 0, 0)
    theirs = lax.ppermute(mine, "lat", swap)
    state_next, gradient, direction = call(
        functools.partial(solve_kernel, levels, scale),
        [flat, (2, rows, cols), (2, rows, cols)],
        scratch=[pltpu.VMEM((2, loops, rows, 2 * cols), F32)],
        vmem=large,
        name="solve",
    )(mine, theirs, faces, near, plan, mixed, depth_index, step, change)
    return (state_next.reshape(2, levels, rows, cols), gradient, direction)


def solution(mesh):
    return jax.shard_map(
        on_device,
        mesh=mesh,
        in_specs=(
            P("members", None, "loop", "lat"),
            P("members", None, "loop", "lat"),
            P(None, "loop", "lat"),
            P("members", "loop", "lat"),
            P("loop", "lat"),
            P("loop", "lat"),
            P("loop", "lat"),
            P("members", None, "loop", "lat"),
            P("members", None, "loop", "lat"),
        ),
        out_specs=(
            P("members", None, "loop", "lat"),
            P("members", "loop", "lat"),
            P("members", "loop", "lat"),
        ),
        check_vma=False,
    )
```

```python
import functools

import jax
import jax.numpy as jnp
from jax import lax
from jax.experimental import pallas as pl
from jax.experimental.pallas import tpu as pltpu
from jax.sharding import PartitionSpec as P

ITERS = 3
SUB = 3
SURFACE_GAIN = 5.0
SLOT = 8
REACH = SUB + 2 * (ITERS - 1)
SHIFT = 5.0
SPAN = 5.0
FUNCTIONALS = 1 + ITERS + ITERS + ITERS * ITERS
GRID = ("loop", "lat")
VMEM = pl.BlockSpec(memory_space=pltpu.VMEM)
F32 = jnp.float32
VMEM_BYTES = 16 * 1024 * 1024


def round_up(value, to):
    return (value + to - 1) // to * to


def call(kernel, out_shapes, scratch=(), vmem=VMEM_BYTES, name=None):
    return pl.pallas_call(
        kernel,
        out_shape=[jax.ShapeDtypeStruct(shape, F32) for shape in out_shapes],
        out_specs=[VMEM] * len(out_shapes),
        scratch_shapes=list(scratch),
        compiler_params=pltpu.CompilerParams(vmem_limit_bytes=vmem),
        name=name,
    )


def iota(shape, dim):
    return lax.broadcasted_iota(jnp.int32, shape, dim)


def row_layout(levels, pairs):
    second = levels + 2
    surface = second + levels
    return surface + 5, second, surface, pairs + 3


def pack_kernel(levels, padded, *refs):
    sources, outs, targets, sems = refs[:9], refs[9:13], refs[13:22], refs[22]
    rows_ref, hist_ref, up_ref, down_ref = outs
    rows, cols = targets[2].shape
    copies = []
    for at, (source, target) in enumerate(zip(sources, targets)):
        if at == 8:
            source = source.at[:, pl.ds(0, rows), :]
        copies.append(pltpu.make_async_copy(source, target, sems.at[at]))
    for copy in copies:
        copy.start()
    for copy in copies[2:]:
        copy.wait()
    (
        state_ref, control_ref, depth_ref, spread_ref, step_ref, change_ref, damping_ref, weight_ref,
        observed_ref,
    ) = targets
    count = step_ref.shape[0] // (2 * rows)
    pairs = 2 * count
    near, second, surface, distant = row_layout(levels, pairs)
    hist = SUB * near
    far = hist + SUB * pairs
    depth = depth_ref[...].astype(F32)
    spread = spread_ref[...]
    wet = depth > 0.5
    total = jnp.zeros((rows, cols), F32)
    for level in range(levels):
        total = total + jnp.where(level < depth, weight_ref[pl.ds(level * rows, rows), :], 0.0)
    fields = [
        damping_ref[...],
        2.0 * total,
        weight_ref[pl.ds(0, rows), :],
        observed_ref[0],
        observed_ref[1],
    ]
    for ref in (up_ref, down_ref):
        ref[pl.ds(ref.shape[0] - 8, 8), :] = jnp.zeros((8, cols), F32)

    def near_of(row):
        if row < SUB:
            return [(down_ref, row)]
        return [(up_ref, row - rows + SUB)] if row >= rows - SUB else []

    def far_of(row):
        result = []
        if SUB <= row < REACH:
            result.append((down_ref, far + (row - SUB) * distant))
        if rows - REACH <= row < rows - SUB:
            result.append((up_ref, far + (row - rows + REACH) * distant))
        return result

    for row in range(rows):
        here = slice(row, row + 1)
        targets = [(hist_ref.at[row], 0)]
        targets += [(ref, hist + at * pairs) for ref, at in near_of(row)] + far_of(row)
        for which, ref in enumerate((step_ref, change_ref)):
            both = [ref[pl.ds(tracer * rows + row, count, stride=2 * rows), :] for tracer in range(2)]
            apart = jnp.where(wet[here], both[0] - both[1], 0.0)
            for target, at in targets:
                target[pl.ds(at + which * count, count), :] = apart
        for target, at in far_of(row):
            target[pl.ds(at + pairs, 1), :] = jnp.where(wet[here], spread[here], 0.0)
        for target, at in near_of(row):
            for field in range(5):
                target[pl.ds(at * near + surface + field, 1), :] = fields[field][here]
    for copy in copies[:2]:
        copy.wait()
    first = iota((levels, cols), 0) == 0
    rest = jnp.zeros((padded - levels, cols), F32)
    for row in range(rows):
        here = slice(row, row + 1)
        targets = [(rows_ref.at[row], 0, padded)]
        targets += [(ref, at * near, second) for ref, at in near_of(row)]
        for tracer in range(2):
            lift = jnp.where(wet[here], control_ref[tracer, here, :], 0.0)
            value = state_ref[tracer, pl.ds(row, levels, stride=rows), :]
            value = value + jnp.where(first, lift, 0.0)
            for target, at, offset in targets:
                target[pl.ds(at + tracer * offset, levels), :] = value
            for target, at in far_of(row):
                target[pl.ds(at + pairs + 1 + tracer, 1), :] = value[0:1]
            rows_ref[row, pl.ds(tracer * padded + levels, padded - levels), :] = rest
        for target, at, _ in targets:
            target[pl.ds(at + levels, 1), :] = spread[here]
            target[pl.ds(at + levels + 1, 1), :] = depth[here]
        for field in range(4):
            rows_ref[row, pl.ds(levels + 2 + field, 1), :] = fields[field][here]
        rows_ref[row, pl.ds(padded + levels, 1), :] = fields[4][here]


def edge_of(rows_of, indices, cols, lat):
    lane = iota((1, cols), 1)
    slot = lane // SLOT
    place = lane % SLOT - SUB * lat
    mine = (place >= 0) & (place < SUB)
    total = None
    for index in indices:
        moved = pltpu.roll(rows_of(index), SLOT * index + SUB, 1)
        piece = jnp.where(mine & (slot == index), moved, 0.0)
        total = piece if total is None else total + piece
    return total


def pairs_kernel(levels, rows_ref, step_ref, change_ref, edge_ref, still_ref, depth_ref, gram_ref):
    rows, _, cols = rows_ref.shape
    lat = lax.axis_index("lat")
    count = step_ref.shape[0]
    lane = iota((1, cols), 1)
    gram = [jnp.zeros((1, cols), F32) for _ in range(count)]
    at = 0
    for left_ref in (step_ref, change_ref):
        for i in range(count):
            for j in range(i, count):
                value = jnp.sum(left_ref[i] * change_ref[j], axis=(0, 1), keepdims=True)
                gram[i] = gram[i] + jnp.where(lane == at + j, value, 0.0)
                if i != j:
                    gram[j] = gram[j] + jnp.where(lane == at + i, value, 0.0)
        at += count
    for i in range(count):
        gram_ref[3, pl.ds(i, 1), :] = gram[i]
    for row in range(rows):
        plane = lambda at: rows_ref[row, pl.ds(levels + at, 1), :]
        here = pl.ds(row, 1)
        depth_ref[here, :] = plane(1)
        gram_ref[0, here, :] = jnp.where(plane(1) > 0.5, plane(0), 0.0)
        gram_ref[1, here, :] = plane(2)
        gram_ref[2, here, :] = plane(3)
    for copy in range(still_ref.shape[0]):
        still_ref[copy] = gram_ref[...]
    edge_ref[...] = edge_of(lambda i: rows_ref[i - SUB], range(SUB, rows + SUB), cols, lat)


def faces_between(here, there, opened=True):
    return jnp.where((here > 0.0) & (there > 0.0) & opened, 0.5 * (here + there), 0.0)


def closed_lane(cols):
    return jnp.where(lax.axis_index("lat") == 0, 2 * cols - 1, cols - 1)


def surface_faces(spread, closed):
    height, width = spread.shape
    below = faces_between(spread, pltpu.roll(spread, height - 1, 0))
    right = faces_between(
        spread, pltpu.roll(spread, width - 1, 1), iota(spread.shape, 1) != closed
    )
    return below, pltpu.roll(below, 1, 0), right, pltpu.roll(right, 1, 1)


def gathered(mine_ref, other_ref, field):
    return jnp.concatenate(
        [
            jnp.concatenate([mine_ref[i, field], other_ref[i, field]], axis=1)
            for i in range(mine_ref.shape[0])
        ],
        axis=0,
    )


def surface_outflow(value, to_below, to_above, to_right, to_left):
    height, width = value.shape
    result = to_right * (value - pltpu.roll(value, width - 1, 1))
    result = result + to_left * (value - pltpu.roll(value, 1, 1))
    result = result + to_below * (value - pltpu.roll(value, height - 1, 0))
    return result + to_above * (value - pltpu.roll(value, 1, 0))


def plan_kernel(mine_ref, other_ref, faces_ref, plan_ref):
    loops, _, rows, cols = mine_ref.shape
    closed = closed_lane(cols)
    for at, face in enumerate(surface_faces(gathered(mine_ref, other_ref, 0), closed)):
        faces_ref[at] = SURFACE_GAIN * face
    for field in (1, 2):
        faces_ref[3 + field] = gathered(mine_ref, other_ref, field)
    count = plan_ref.shape[0] // 2
    gram = mine_ref[0, 3] + other_ref[0, 3]
    for i in range(1, loops):
        gram = gram + (mine_ref[i, 3] + other_ref[i, 3])
    wide = (count, cols)
    step_change = [jnp.broadcast_to(gram[:, i : i + 1], wide) for i in range(count)]
    change_change = [
        jnp.broadcast_to(gram[:, count + i : count + i + 1], wide) for i in range(count)
    ]
    last = count - 1
    gamma = step_change[last][last:] / change_change[last][last:]
    rho = [1.0 / step_change[i][i : i + 1] for i in range(count)]
    row = iota(wide, 0)
    lane = iota(wide, 1)
    step_grad = jnp.where(lane == row, 1.0, 0.0)
    change_grad = jnp.where(lane == row + count, 1.0, 0.0)
    factors = [None] * count
    for i in range(count - 1, -1, -1):
        factors[i] = rho[i] * step_grad[i : i + 1]
        step_grad = step_grad - factors[i] * step_change[i]
        change_grad = change_grad - factors[i] * change_change[i]
    change_grad = gamma * change_grad
    for i in range(count):
        weight = factors[i] - rho[i] * change_grad[i : i + 1]
        change_grad = change_grad + weight * step_change[i]
        plan_ref[pl.ds(i, 1), :] = -weight
        plan_ref[pl.ds(count + i, 1), :] = gamma * factors[i]
    at = lane[:1] == 2 * count
    plan_ref[pl.ds(0, 1), :] = jnp.where(at, -gamma, plan_ref[pl.ds(0, 1), :])


def border_kernel(
    levels, padded, edge_ref, low_ref, high_ref, rows_ref, hist_ref, out_ref, halo_ref
):
    planes, cols = edge_ref.shape
    rows, pairs, _ = hist_ref.shape
    lat = lax.axis_index("lat")
    near, second, surface, distant = row_layout(levels, pairs)
    hist = SUB * near
    far = hist + SUB * pairs
    rest = jnp.zeros((padded - levels, cols), F32)
    for i in range(2 * SUB):
        ref = low_ref if i < SUB else high_ref
        at = i % SUB * near
        halo_ref[i, pl.ds(levels, padded - levels), :] = rest
        halo_ref[i, pl.ds(padded + levels, padded - levels), :] = rest
        halo_ref[i, pl.ds(0, levels + 2), :] = ref[pl.ds(at, levels + 2), :]
        halo_ref[i, pl.ds(padded, levels), :] = ref[pl.ds(at + second, levels), :]
    total = edge_ref[...] + edge_of(lambda i: halo_ref[i], range(SUB), cols, lat)
    out_ref[pl.ds(0, planes), :] = total + edge_of(
        lambda i: halo_ref[i - rows], range(rows + SUB, rows + 2 * SUB), cols, lat
    )
    tall = 3 * rows
    fields = planes + (rows + 2 * REACH) * pairs
    out_ref[pl.ds(fields, 8 * tall), :] = jnp.zeros((8 * tall, cols), F32)
    for at in range(-REACH, rows + REACH):
        if 0 <= at < rows:
            ref, apart = hist_ref.at[at], 0
        elif -SUB <= at < rows + SUB:
            ref, index = (low_ref, at + SUB) if at < 0 else (high_ref, at - rows)
            apart = hist + index * pairs
        else:
            ref, index = (low_ref, at + REACH) if at < 0 else (high_ref, at - rows - SUB)
            apart = far + index * distant
        out_ref[pl.ds(planes + (at + REACH) * pairs, pairs), :] = ref[pl.ds(apart, pairs), :]
        if 0 <= at < rows:
            ref = rows_ref.at[at]
            places = {0: levels, 6: 0, 7: padded, 5: padded + levels}
            places.update({1 + field: levels + 2 + field for field in range(4)})
            limit = levels + 1
        elif -SUB <= at < rows + SUB:
            start = index * near
            places = {0: start + levels, 6: start, 7: start + second}
            places.update({1 + field: start + surface + field for field in range(5)})
            limit = start + levels + 1
        else:
            places = {0: apart + pairs, 6: apart + pairs + 1, 7: apart + pairs + 2}
            limit = None
        for field, place in places.items():
            value = ref[pl.ds(place, 1), :]
            if field == 0 and limit is not None:
                value = jnp.where(ref[pl.ds(limit, 1), :] > 0.5, value, 0.0)
            out_ref[pl.ds(fields + field * tall + at + rows, 1), :] = value


def basis_kernel(
    planes, rows, pairs, mine_ref, other_ref, step_ref, change_ref, _,
    out_ref, near_ref, base_ref, first_ref, *work
):
    cols = mine_ref.shape[1]
    width = 2 * cols
    tall = rows + 2 * REACH
    ahead = REACH - SUB
    high = 3 * rows
    apart = planes
    fields = apart + tall * pairs
    closed = closed_lane(cols)
    opened = iota((1, width), 1) != closed

    def wide(at, size):
        return jnp.concatenate([mine_ref[pl.ds(at, size), :], other_ref[pl.ds(at, size), :]], axis=1)

    def left(value):
        return pltpu.roll(value, width - 1, 1)

    def right(value):
        return pltpu.roll(value, 1, 1)

    def field(at):
        return wide(fields + at * high, high)

    def field_row(at, i):
        return wide(fields + at * high + i - REACH + rows, 1)

    faces = surface_faces(field(0), closed)
    for at in range(4):
        near_ref[at] = faces[at]
    sea = jnp.where(field(0) > 0.0, 1.0, 0.0)
    weight = field(3)
    near_ref[4] = weight * sea
    near_ref[5] = sea
    value = [field(6), field(7)]
    for sweep in range(SUB):
        value = [part - surface_outflow(part, *faces) for part in value]
    value = [weight * (value[0] - field(4)), weight * (value[1] - field(5))]
    for sweep in range(SUB):
        value = [part - surface_outflow(part, *faces) for part in value]
    base = [(part * sea)[rows : 2 * rows, :cols] for part in value]
    for tracer in range(2):
        base_ref[tracer] = base[tracer]
    lane = iota((1, cols), 1)
    for i in range(pairs // 2):
        total = jnp.zeros((1, cols), F32)
        for at, ref in ((0, step_ref), (cols // 2, change_ref)):
            part = ref[i, pl.ds(0, rows), :] * base[0] + ref[i, pl.ds(rows, rows), :] * base[1]
            part = jnp.sum(part, axis=(0, 1), keepdims=True)
            total = total + jnp.where(lane == at, part, 0.0)
        first_ref[pl.ds(i, 1), :] = total

    spread = [field_row(0, i) for i in range(tall)]
    to_right = [faces_between(value, left(value), opened) for value in spread]
    to_left = [right(value) for value in to_right]
    to_below = [faces_between(spread[i], spread[i + 1]) for i in range(tall - 1)]
    inner = range(ahead, tall - ahead)
    damping = {i: (field_row(1, i) - SHIFT) * (1.0 / SPAN) for i in inner}
    response_weight = {i: field_row(2, i) for i in inner}
    weight = {i: field_row(3, i) for i in inner}
    gain = SURFACE_GAIN / SPAN

    def outflow(get, i):
        value = get(i)
        total = to_right[i] * (value - left(value)) + to_left[i] * (value - right(value))
        total = total + to_below[i] * (value - get(i + 1))
        return value, total + to_below[i - 1] * (value - get(i - 1))

    def mixed(get, ref, reach):
        for i in range(REACH - reach, REACH + rows + reach):
            value, out = outflow(get, i)
            ref[i] = value - out
        return lambda i: ref[i]

    def applied(get, ref, reach):
        for i in range(REACH - reach, REACH + rows + reach):
            value, out = outflow(get, i)
            ref[i] = damping[i] * value + gain * out
        return lambda i: ref[i]

    def keep(slot, get):
        for i in range(rows):
            out_ref[slot, i] = get(i + REACH)[:, :cols]

    def start_apart(i):
        return wide(apart + i * pairs, pairs)

    get = start_apart
    for sweep in range(SUB):
        get = mixed(get, work[sweep], REACH - 1 - sweep)
    reach = REACH - SUB
    powers = [get]
    for power in range(1, ITERS):
        powers.append(applied(powers[-1], work[SUB + power - 1], reach - power))
    for power in range(ITERS):
        keep(power, powers[power])
    reach = ITERS - 1
    slot = ITERS
    at = SUB + ITERS - 1
    chains = []
    for factor, power in [(weight, 0)] + [(response_weight, power) for power in range(ITERS)]:
        get = powers[power]
        chains.append(lambda i, factor=factor, get=get: factor[i] * get(i))
    for power in range(1, ITERS):
        for index in range(len(chains)):
            chains[index] = applied(chains[index], work[at], reach - power)
            at += 1
            keep(slot + index * (ITERS - 1) + power - 1, chains[index])


def mix_kernel(
    levels, padded, rows_ref, halo_ref, out_ref, face_ref, here_ref, there_ref
):
    rows, _, cols = rows_ref.shape
    lane = iota((1, cols), 1)
    count = rows + 2 * SUB
    level = iota((padded, cols), 0).astype(F32)

    def left(value):
        return pltpu.roll(value, cols - 1, 1)

    def right(value):
        return pltpu.roll(value, 1, 1)

    def source(i):
        if i < SUB:
            return halo_ref.at[i]
        if i < SUB + rows:
            return rows_ref.at[i - SUB]
        return halo_ref.at[i - rows]

    def face(depth_here, depth_there, spread_here, spread_there):
        opened = level < jnp.minimum(depth_here, depth_there)
        return jnp.where(opened, 0.5 * (spread_here + spread_there), 0.0)

    spreads = [source(i)[pl.ds(levels, 1), :] for i in range(count)]
    depths = [source(i)[pl.ds(levels + 1, 1), :] for i in range(count)]
    for i in range(count - 1):
        face_ref[0, i] = face(depths[i], depths[i + 1], spreads[i], spreads[i + 1])
    for i in range(1, count - 1):
        there = jnp.where(lane < cols - 1, left(depths[i]), 0.0)
        face_ref[1, i] = face(depths[i], there, spreads[i], left(spreads[i]))
        there = jnp.where(lane > 0, right(depths[i]), 0.0)
        face_ref[2, i] = face(depths[i], there, spreads[i], right(spreads[i]))

    for sweep in range(1, SUB + 1):
        target = here_ref if sweep % 2 else there_ref
        for i in range(sweep, count - sweep):
            def field(at):
                if sweep == 1:
                    return source(at)
                return (there_ref if sweep % 2 else here_ref).at[at]

            into = out_ref.at[i - SUB] if sweep == SUB else target.at[i]
            for tracer in range(2):
                at = pl.ds(tracer * padded, padded)
                centre = field(i)[at, :]
                total = centre + face_ref[0, i] * (field(i + 1)[at, :] - centre)
                total = total + face_ref[0, i - 1] * (field(i - 1)[at, :] - centre)
                total = total + face_ref[1, i] * (left(centre) - centre)
                total = total + face_ref[2, i] * (right(centre) - centre)
                into[at, :] = total


def fields_kernel(
    levels, padded, scale,
    rows_ref, main_ref, edge_ref, other_ref, weight_ref, observed_ref, basis_ref, first_ref,
    mixed_ref, fields_ref, part_ref,
):
    rows, _, cols = rows_ref.shape
    pairs = basis_ref.shape[2]
    lat = lax.axis_index("lat")
    lane = iota((1, cols), 1)
    place = lane % SLOT
    level = iota((padded, cols), 0).astype(F32)

    def left(value, by=1):
        return pltpu.roll(value, (cols - by) % cols, 1)

    def right(value, by=1):
        return pltpu.roll(value, by, 1)

    spread = edge_ref[pl.ds(levels, 1), :] + other_ref[pl.ds(levels, 1), :]
    depth = edge_ref[pl.ds(levels + 1, 1), :] + other_ref[pl.ds(levels + 1, 1), :]
    within = place < 2 * SUB - 1
    col_depth = jnp.minimum(depth, jnp.where(within, left(depth), 0.0))
    col_spread = 0.5 * (spread + left(spread))
    row_depth = jnp.minimum(depth, left(depth, SLOT))
    row_spread = 0.5 * (spread + left(spread, SLOT))

    def strip_face(limit, value):
        return jnp.where(level < limit, value, 0.0)

    to_left = strip_face(right(col_depth), right(col_spread))
    to_right = strip_face(col_depth, col_spread)
    to_above = strip_face(right(row_depth, SLOT), right(row_spread, SLOT))
    to_below = strip_face(row_depth, row_spread)
    out_of_low = place == jnp.where(lat == 0, SUB - 1, SLOT)
    out_of_high = place == jnp.where(lat == 0, SLOT, SUB)
    over_low = jnp.where(out_of_low, to_right, 0.0)
    over_high = jnp.where(out_of_high, to_left, 0.0)
    own_right = jnp.where(place == SUB - 1, 0.0, to_right)
    own_left = jnp.where(place == SUB, 0.0, to_left)
    start = jnp.where(lat == 0, cols - SUB, 0)
    at_border = (lane >= start) & (lane < start + SUB)

    def spread_out(value, east, west):
        before, after = right(value), left(value)
        above, below = right(value, SLOT), left(value, SLOT)
        total = value + east * (after - value) + west * (before - value)
        return total + to_below * (below - value) + to_above * (above - value)

    parts = []
    extras = [None, None]
    for tracer in range(2):
        at = pl.ds(tracer * padded, padded)
        parts.append(edge_ref[at, :] + other_ref[at, :])

    for sweep in range(1, SUB + 1):
        for tracer in range(2):
            part = parts[tracer]
            across = over_low * (left(part) - part) + over_high * (right(part) - part)
            extra = extras[tracer]
            if extra is not None:
                across = across + spread_out(extra, own_right, own_left)
            extras[tracer] = across
            if sweep < SUB:
                parts[tracer] = spread_out(part, to_right, to_left)

    for row in range(rows):
        i = row + SUB
        at = pl.ds(row, levels, stride=rows)
        mixed = []
        for tracer in range(2):
            border = jnp.where(at_border, left(extras[tracer], SLOT * i + SUB), 0.0)
            mixed.append((main_ref[row, pl.ds(tracer * padded, padded), :] + border)[:levels])
        wet = level[:levels] < rows_ref[row, pl.ds(levels + 1, 1), :]
        weight = weight_ref[at, :]
        misfit = []
        for tracer in range(2):
            mixed_ref[tracer, at, :] = mixed[tracer]
            misfit.append(weight * (mixed[tracer] - observed_ref[tracer, at, :]))
        here = pl.ds(row, 1)
        part_ref[0, here, :] = scale * jnp.sum(
            jnp.where(wet, mixed[0] - mixed[1], 0.0), axis=0, keepdims=True
        )
        part_ref[1, here, :] = jnp.sum(
            jnp.where(wet, misfit[1] - misfit[0], 0.0), axis=0, keepdims=True
        )
    sums = [None] * FUNCTIONALS

    def add(at, slot, row, factor):
        value = basis_ref[slot, row] * factor
        sums[at] = value if sums[at] is None else sums[at] + value

    for row in range(rows):
        here = pl.ds(row, 1)
        surface, base = part_ref[0, here, :], part_ref[1, here, :]
        fixed = lambda plane: rows_ref[row, pl.ds(levels + plane, 1), :]
        add(1, 0, row, fixed(4) * surface)
        for power in range(1, ITERS):
            add(1 + power, ITERS + power - 1, row, surface)
        for j in range(ITERS):
            add(1 + ITERS + j, j, row, base)
            at = 1 + 2 * ITERS + j * ITERS
            add(at, j, row, fixed(3) * surface)
            for power in range(1, ITERS):
                add(at + power, ITERS + (1 + j) * (ITERS - 1) + power - 1, row, surface)
    half = pairs // 2
    total = first_ref[...]
    for at in range(1, FUNCTIONALS):
        value = jnp.sum(sums[at], axis=1, keepdims=True)
        total = total + jnp.where(lane == at, value[:half], 0.0)
        total = total + jnp.where(lane == cols // 2 + at, value[half:], 0.0)
    part_ref[2] = total
    for copy in range(fields_ref.shape[0]):
        fields_ref[copy] = part_ref[...]


def solve_kernel(
    levels, scale,
    mine_ref, other_ref, faces_ref, near_ref, base_ref, plan_ref, mixed_ref, depth_ref, step_ref,
    change_ref, state_ref, gradient_ref, direction_ref, kept_ref,
):
    loops, _, rows, cols = mine_ref.shape
    loop = lax.axis_index("loop")

    def total(value):
        parts = [
            value[i * rows : (i + 1) * rows, j * cols : (j + 1) * cols]
            for i in range(loops)
            for j in range(2)
        ]
        while len(parts) > 1:
            half = (len(parts) + 1) // 2
            parts = [a + b for a, b in zip(parts, parts[half:])] + parts[len(parts) - half : half]
        return jnp.sum(jnp.sum(parts[0], axis=1, keepdims=True), axis=0, keepdims=True)

    count = step_ref.shape[0]
    inner = mine_ref[0, 2] + other_ref[0, 2]
    for i in range(1, loops):
        inner = inner + (mine_ref[i, 2] + other_ref[i, 2])
    plan = plan_ref[...]
    shifted = pltpu.roll(inner, cols // 2, 1)
    linear = None
    for i in range(2 * count):
        source = inner if i < count else shifted
        part = plan[:, i : i + 1] * source[i % count : i % count + 1]
        linear = part if linear is None else linear + part
    gamma = plan[:1, 2 * count : 2 * count + 1]

    gained = [faces_ref[i] for i in range(4)]
    damping = faces_ref[4]

    def conjugate(rhs):
        residual = rhs
        search = rhs
        solution = jnp.zeros_like(rhs)
        norm_now = total(rhs * rhs)
        one = jnp.ones((1, 1), F32)
        residual_of = [one]
        search_of = [one]
        solution_of = []
        for sweep in range(ITERS):
            image = damping * search + surface_outflow(search, *gained)
            alpha = norm_now / total(search * image)
            solution = solution + alpha * search
            solution_of = add_up(solution_of, alpha, search_of)
            if sweep < ITERS - 1:
                residual = residual - alpha * image
                norm_next = total(residual * residual)
                beta = norm_next / norm_now
                search = residual + beta * search
                norm_now = norm_next
                image_of = [SHIFT * value for value in search_of]
                image_of = add_up(image_of, SPAN, [None] + search_of)
                residual_of = add_up(residual_of, -alpha, image_of)
                search_of = add_up(residual_of, beta, search_of)
        return solution, solution_of

    def add_up(terms, factor, others):
        result = list(terms) + [None] * (len(others) - len(terms))
        for at, value in enumerate(others):
            if value is not None:
                value = factor * value
                result[at] = value if result[at] is None else result[at] + value
        return result

    def near(slot, value):
        for i in range(loops):
            kept_ref[slot, i] = value[i * rows : (i + 1) * rows]
        return jnp.concatenate(
            [kept_ref[slot, lax.rem(loop + shift, loops)] for shift in (loops - 1, 0, 1)], axis=0
        )

    elevation, elevation_of = conjugate(gathered(mine_ref, other_ref, 0))
    pressure = gathered(mine_ref, other_ref, 1) + faces_ref[5] * elevation
    elevation = near(0, elevation)
    depth = depth_ref[...]
    here = elevation[rows : 2 * rows, :cols]
    for level in range(levels):
        at = pl.ds(level * rows, rows)
        change = jnp.where(level < depth, here, 0.0)
        state_ref[0, at, :] = mixed_ref[0, at, :] - change
        state_ref[1, at, :] = mixed_ref[1, at, :] + change
    response, response_of = conjugate(pressure)
    response = near(1, response)

    lane = iota((1, cols), 1)
    factor = jnp.where(lane == 0, 1.0, 0.0)
    for j in range(ITERS):
        factor = jnp.where(lane == 1 + j, -elevation_of[j], factor)
        part = scale * response_of[j]
        factor = jnp.where(lane == 1 + ITERS + j, part, factor)
        for k in range(ITERS):
            at = 1 + 2 * ITERS + j * ITERS + k
            factor = jnp.where(lane == at, part * elevation_of[k], factor)
    weights = jnp.sum(linear * factor, axis=1, keepdims=True)
    weights = [
        jnp.broadcast_to(weights[i : i + 1], (rows, cols)) for i in range(2 * count)
    ]

    sea = near_ref[5]
    carried = near_ref[4] * elevation - (scale * sea) * response
    faces = [near_ref[i] for i in range(4)]
    for sweep in range(SUB):
        carried = carried - surface_outflow(carried, *faces)
    carried = (sea * carried)[rows : 2 * rows, :cols]
    for tracer in range(2):
        at = pl.ds(tracer * rows, rows)
        gradient = base_ref[tracer] - carried if tracer == 0 else base_ref[tracer] + carried
        gradient_ref[tracer] = gradient
        value = gamma * gradient
        for i in range(count):
            value = value + weights[i] * step_ref[i, at, :]
            value = value + weights[count + i] * change_ref[i, at, :]
        direction_ref[tracer] = value


def on_device(
    state, observed, weight, control, depth_index, diffusivity, damping, history_step, history_change
):
    _, levels, rows, cols = state.shape
    count = history_step.shape[0]
    padded = round_up(levels + 6, 8)
    planes = 2 * padded
    loops = lax.axis_size("loop")
    lats = lax.axis_size("lat")
    blocks = loops * lats
    scale = levels ** (-0.5)
    flat = (2, levels * rows, cols)
    state = state.reshape(flat)
    observed = observed.reshape(flat)
    weight = weight.reshape(flat[1:])
    step = history_step.reshape(count, 2 * rows, cols)
    change = history_change.reshape(count, 2 * rows, cols)

    pairs = 2 * count
    inputs = (
        state, control, depth_index, diffusivity,
        history_step.reshape(-1, cols), history_change.reshape(-1, cols), damping, weight, observed,
    )
    held = [x.shape for x in inputs[:-1]] + [(2, rows, cols)]
    near, _, _, distant = row_layout(levels, pairs)
    sent = (round_up(SUB * (near + pairs) + (REACH - SUB) * distant, 8), cols)
    shapes = ((rows, planes, cols), (rows, pairs, cols), sent, sent)
    packed, hist, up, down = pl.pallas_call(
        functools.partial(pack_kernel, levels, padded),
        out_shape=[jax.ShapeDtypeStruct(shape, F32) for shape in shapes],
        in_specs=[pl.BlockSpec(memory_space=pltpu.HBM)] * len(inputs),
        out_specs=[VMEM] * len(shapes),
        scratch_shapes=[pltpu.VMEM(shape, x.dtype) for shape, x in zip(held, inputs)]
        + [pltpu.SemaphoreType.DMA((len(inputs),))],
        compiler_params=pltpu.CompilerParams(vmem_limit_bytes=VMEM_BYTES),
        name="pack",
    )(*(pltpu.with_memory_space_constraint(x, pltpu.HBM) for x in inputs))
    forward = [(i, (i + 1) % loops) for i in range(loops)]
    backward = [(target, source) for source, target in forward]
    swap = [(0, 1), (1, 0)]
    low = lax.ppermute(up, "loop", forward)
    high = lax.ppermute(down, "loop", backward)
    edge, still, depth, _ = call(
        functools.partial(pairs_kernel, levels),
        [(planes, cols), (loops, 4, rows, cols), (rows, cols), (4, rows, cols)],
        name="pairs",
    )(packed, step, change)
    still = lax.all_to_all(still, "loop", 0, 0)
    still_other = lax.ppermute(still, "lat", swap)
    height = loops * rows
    large = VMEM_BYTES if loops <= 16 else 2 * VMEM_BYTES
    faces, plan = call(
        plan_kernel, [(6, height, 2 * cols), (pairs, cols)], vmem=large, name="plan"
    )(still, still_other)
    swapped = planes + (rows + 2 * REACH) * pairs + 8 * 3 * rows
    border, halo = call(
        functools.partial(border_kernel, levels, padded),
        [(swapped, cols), (2 * SUB, planes, cols)],
        name="border",
    )(edge, low, high, packed, hist)
    other = lax.ppermute(border, "lat", swap)
    tall = rows + 2 * SUB
    (mixed,) = call(
        functools.partial(mix_kernel, levels, padded),
        [(rows, planes, cols)],
        scratch=[pltpu.VMEM((3, tall, padded, cols), F32)]
        + [pltpu.VMEM((tall, planes, cols), F32)] * 2,
        name="mix",
    )(packed, halo)
    chains = 1 + ITERS
    buffers = SUB + ITERS - 1 + chains * (ITERS - 1)
    shapes = (
        (ITERS + chains * (ITERS - 1), rows, pairs, cols),
        (6, 3 * rows, 2 * cols),
        (2, rows, cols),
        (count, cols),
    )
    basis, around, base, first = pl.pallas_call(
        functools.partial(basis_kernel, planes, rows, pairs),
        out_shape=[jax.ShapeDtypeStruct(shape, F32) for shape in shapes],
        in_specs=[VMEM] * 4 + [pl.BlockSpec(memory_space=pl.ANY)],
        out_specs=[VMEM] * len(shapes),
        scratch_shapes=[pltpu.VMEM((rows + 2 * REACH, pairs, 2 * cols), F32)] * buffers,
        compiler_params=pltpu.CompilerParams(vmem_limit_bytes=VMEM_BYTES),
        name="basis",
    )(border, other, step, change, still_other)
    mixed, fields = call(
        functools.partial(fields_kernel, levels, padded, scale),
        [flat, (loops, 3, rows, cols)],
        scratch=[pltpu.VMEM((3, rows, cols), F32)],
        name="fields",
    )(packed, mixed, border, other, weight, observed, basis, first)
    mine = lax.all_to_all(fields, "loop", 0, 0)
    theirs = lax.ppermute(mine, "lat", swap)
    shapes = (flat, (2, rows, cols), (2, rows, cols))
    state_next, gradient, direction = call(
        functools.partial(solve_kernel, levels, scale),
        shapes,
        scratch=[pltpu.VMEM((2, loops, rows, 2 * cols), F32)],
        vmem=large,
        name="solve",
    )(mine, theirs, faces, around, base, plan, mixed, depth, step, change)
    return (state_next.reshape(2, levels, rows, cols), gradient, direction)


def solution(mesh):
    return jax.shard_map(
        on_device,
        mesh=mesh,
        in_specs=(
            P("members", None, "loop", "lat"),
            P("members", None, "loop", "lat"),
            P(None, "loop", "lat"),
            P("members", "loop", "lat"),
            P("loop", "lat"),
            P("loop", "lat"),
            P("loop", "lat"),
            P("members", None, "loop", "lat"),
            P("members", None, "loop", "lat"),
        ),
        out_specs=(
            P("members", None, "loop", "lat"),
            P("members", "loop", "lat"),
            P("members", "loop", "lat"),
        ),
        check_vma=False,
    )
```

```python
import functools

import jax
import jax.numpy as jnp
from jax import lax
from jax.experimental import pallas as pl
from jax.experimental.pallas import tpu as pltpu
from jax.sharding import PartitionSpec as P

ITERS = 3
SUB = 3
SURFACE_GAIN = 5.0
SLOT = 8
WIDE_SLOT = 16
REACH = SUB + 2 * (ITERS - 1)
SHIFT = 5.0
SPAN = 5.0
FUNCTIONALS = 1 + ITERS + ITERS + ITERS * ITERS
GRID = ("loop", "lat")
VMEM = pl.BlockSpec(memory_space=pltpu.VMEM)
F32 = jnp.float32
VMEM_BYTES = 16 * 1024 * 1024


def round_up(value, to):
    return (value + to - 1) // to * to


def call(kernel, out_shapes, scratch=(), vmem=VMEM_BYTES, name=None):
    return pl.pallas_call(
        kernel,
        out_shape=[jax.ShapeDtypeStruct(shape, F32) for shape in out_shapes],
        out_specs=[VMEM] * len(out_shapes),
        scratch_shapes=list(scratch),
        compiler_params=pltpu.CompilerParams(vmem_limit_bytes=vmem),
        name=name,
    )


def iota(shape, dim):
    return lax.broadcasted_iota(jnp.int32, shape, dim)


def state_rows(levels):
    return 2 * levels + 2, levels + 2


def hist_rows(pairs):
    return pairs + 8, pairs + 3


def pack_kernel(levels, padded, *refs):
    sources, outs, targets, sems = refs[:9], refs[9:15], refs[15:24], refs[24]
    rows_ref, hist_ref = outs[:2]
    rows, cols = targets[2].shape
    copies = []
    for at, (source, target) in enumerate(zip(sources, targets)):
        if at == 8:
            source = source.at[:, pl.ds(0, rows), :]
        copies.append(pltpu.make_async_copy(source, target, sems.at[at]))
    for copy in copies:
        copy.start()
    for copy in copies[2:]:
        copy.wait()
    (
        state_ref, control_ref, depth_ref, spread_ref, step_ref, change_ref, damping_ref, weight_ref,
        observed_ref,
    ) = targets
    count = step_ref.shape[0] // (2 * rows)
    pairs = 2 * count
    near, second = state_rows(levels)
    close, distant = hist_rows(pairs)
    depth = depth_ref[...].astype(F32)
    spread = spread_ref[...]
    wet = depth > 0.5
    total = jnp.zeros((rows, cols), F32)
    for level in range(levels):
        total = total + jnp.where(level < depth, weight_ref[pl.ds(level * rows, rows), :], 0.0)
    fields = [
        damping_ref[...],
        2.0 * total,
        weight_ref[pl.ds(0, rows), :],
        observed_ref[0],
        observed_ref[1],
    ]
    for row in range(rows):
        here = slice(row, row + 1)
        for which, ref in enumerate((step_ref, change_ref)):
            both = [ref[pl.ds(tracer * rows + row, count, stride=2 * rows), :] for tracer in range(2)]
            apart = jnp.where(wet[here], both[0] - both[1], 0.0)
            hist_ref[row, pl.ds(which * count, count), :] = apart
    for copy in copies[:2]:
        copy.wait()
    first = iota((levels, cols), 0) == 0
    rest = jnp.zeros((padded - levels, cols), F32)
    for row in range(rows):
        here = slice(row, row + 1)
        for tracer in range(2):
            lift = jnp.where(wet[here], control_ref[tracer, here, :], 0.0)
            value = state_ref[tracer, pl.ds(row, levels, stride=rows), :]
            value = value + jnp.where(first, lift, 0.0)
            rows_ref[row, pl.ds(tracer * padded, levels), :] = value
            rows_ref[row, pl.ds(tracer * padded + levels, padded - levels), :] = rest
        for field, value in enumerate([spread, depth] + fields[:4]):
            rows_ref[row, pl.ds(levels + field, 1), :] = value[here]
        rows_ref[row, pl.ds(padded + levels, 1), :] = fields[4][here]

    even = lax.rem(lax.axis_index("loop"), 2) == 0

    def put(refs, at, upper, lower):
        here = pl.ds(at, upper.shape[0])
        refs[0][here, :] = jnp.where(even, upper, lower)
        refs[1][here, :] = jnp.where(even, lower, upper)

    def fill(refs, last):
        if last < refs[0].shape[0]:
            rest = jnp.zeros((refs[0].shape[0] - last, cols), F32)
            put(refs, last, rest, rest)

    masked = jnp.where(wet, spread, 0.0)
    for at in range(REACH):
        far = at < REACH - SUB
        index = at if far else at - (REACH - SUB)
        upper = rows - REACH + at if far else rows - SUB + index
        lower = SUB + index if far else index
        start = SUB * close + index * distant if far else index * close
        put(outs[2:4], start, hist_ref[upper], hist_ref[lower])
        start = start + pairs
        put(outs[2:4], start, masked[upper : upper + 1], masked[lower : lower + 1])
        for tracer in range(2):
            here = pl.ds(tracer * padded, 1)
            put(outs[2:4], start + 1 + tracer, rows_ref[upper, here, :], rows_ref[lower, here, :])
        if not far:
            here = pl.ds(levels + 2, 4)
            put(outs[2:4], start + 3, rows_ref[upper, here, :], rows_ref[lower, here, :])
            here = pl.ds(padded + levels, 1)
            put(outs[2:4], start + 7, rows_ref[upper, here, :], rows_ref[lower, here, :])
    fill(outs[2:4], SUB * close + (REACH - SUB) * distant)
    for at in range(SUB):
        upper, lower = rows - SUB + at, at
        for start, size, place in ((0, levels + 2, 0), (padded, levels, second)):
            here = pl.ds(start, size)
            put(outs[4:6], at * near + place, rows_ref[upper, here, :], rows_ref[lower, here, :])
    fill(outs[4:6], SUB * near)


def edge_of(rows_of, indices, cols, lat):
    lane = iota((1, cols), 1)
    slot = lane // SLOT
    place = lane % SLOT - SUB * lat
    mine = (place >= 0) & (place < SUB)
    total = None
    for index in indices:
        moved = pltpu.roll(rows_of(index), SLOT * index + SUB, 1)
        piece = jnp.where(mine & (slot == index), moved, 0.0)
        total = piece if total is None else total + piece
    return total


def pairs_kernel(levels, rows_ref, step_ref, change_ref, edge_ref, depth_ref, fixed_ref):
    rows, _, cols = rows_ref.shape
    lat = lax.axis_index("lat")
    count = step_ref.shape[0]
    lane = iota((1, cols), 1)
    gram = [jnp.zeros((1, cols), F32) for _ in range(count)]
    at = FUNCTIONALS
    for left_ref in (step_ref, change_ref):
        for i in range(count):
            for j in range(i, count):
                value = jnp.sum(left_ref[i] * change_ref[j], axis=(0, 1), keepdims=True)
                gram[i] = gram[i] + jnp.where(lane == at + j, value, 0.0)
                if i != j:
                    gram[j] = gram[j] + jnp.where(lane == at + i, value, 0.0)
        at += count
    for i in range(count):
        fixed_ref[3, pl.ds(i, 1), :] = gram[i]
    for row in range(rows):
        plane = lambda at: rows_ref[row, pl.ds(levels + at, 1), :]
        here = pl.ds(row, 1)
        depth_ref[here, :] = plane(1)
        fixed_ref[0, here, :] = jnp.where(plane(1) > 0.5, plane(0), 0.0)
        fixed_ref[1, here, :] = plane(2)
        fixed_ref[2, here, :] = plane(3)
    edge_ref[...] = edge_of(lambda i: rows_ref[i - SUB], range(SUB, rows + SUB), cols, lat)


def faces_between(here, there, opened=True):
    return jnp.where((here > 0.0) & (there > 0.0) & opened, 0.5 * (here + there), 0.0)


def closed_lane(cols):
    return jnp.where(lax.axis_index("lat") == 0, 2 * cols - 1, cols - 1)


def surface_faces(spread, closed):
    height, width = spread.shape
    below = faces_between(spread, pltpu.roll(spread, height - 1, 0))
    right = faces_between(
        spread, pltpu.roll(spread, width - 1, 1), iota(spread.shape, 1) != closed
    )
    return below, pltpu.roll(below, 1, 0), right, pltpu.roll(right, 1, 1)


def gathered(mine_ref, other_ref, field):
    return jnp.concatenate(
        [
            jnp.concatenate([mine_ref[i, field], other_ref[i, field]], axis=1)
            for i in range(mine_ref.shape[0])
        ],
        axis=0,
    )


def surface_outflow(value, to_below, to_above, to_right, to_left):
    height, width = value.shape
    result = to_right * (value - pltpu.roll(value, width - 1, 1))
    result = result + to_left * (value - pltpu.roll(value, 1, 1))
    result = result + to_below * (value - pltpu.roll(value, height - 1, 0))
    return result + to_above * (value - pltpu.roll(value, 1, 0))


def plan_kernel(mine_ref, other_ref, faces_ref, plan_ref):
    loops, _, rows, cols = mine_ref.shape
    closed = closed_lane(cols)
    for at, face in enumerate(surface_faces(gathered(mine_ref, other_ref, 3), closed)):
        faces_ref[at] = SURFACE_GAIN * face
    for field in (4, 5):
        faces_ref[field] = gathered(mine_ref, other_ref, field)
    count = plan_ref.shape[0] // 2
    gram = mine_ref[0, 2] + other_ref[0, 2]
    for i in range(1, loops):
        gram = gram + (mine_ref[i, 2] + other_ref[i, 2])
    wide = (count, cols)
    tables = [
        jnp.broadcast_to(gram[:, i : i + 1], wide)
        for i in range(FUNCTIONALS, FUNCTIONALS + 2 * count)
    ]
    step_change, change_change = tables[:count], tables[count:]
    last = count - 1
    gamma = step_change[last][last:] / change_change[last][last:]
    rho = [1.0 / step_change[i][i : i + 1] for i in range(count)]
    row = iota(wide, 0)
    lane = iota(wide, 1)
    step_grad = jnp.where(lane == row, 1.0, 0.0)
    change_grad = jnp.where(lane == row + count, 1.0, 0.0)
    factors = [None] * count
    for i in range(count - 1, -1, -1):
        factors[i] = rho[i] * step_grad[i : i + 1]
        step_grad = step_grad - factors[i] * step_change[i]
        change_grad = change_grad - factors[i] * change_change[i]
    change_grad = gamma * change_grad
    for i in range(count):
        weight = factors[i] - rho[i] * change_grad[i : i + 1]
        change_grad = change_grad + weight * step_change[i]
        plan_ref[pl.ds(i, 1), :] = -weight
        plan_ref[pl.ds(count + i, 1), :] = gamma * factors[i]
    at = lane[:1] == 2 * count
    plan_ref[pl.ds(0, 1), :] = jnp.where(at, -gamma, plan_ref[pl.ds(0, 1), :])


def received(first_ref, second_ref):
    even = lax.rem(lax.axis_index("loop"), 2) == 0

    def low(at, size):
        here = pl.ds(at, size)
        return jnp.where(even, second_ref[here, :], first_ref[here, :])

    def high(at, size):
        here = pl.ds(at, size)
        return jnp.where(even, first_ref[here, :], second_ref[here, :])

    return low, high


def halo_kernel(levels, padded, rows, edge_ref, first_ref, second_ref, _, out_ref, halo_ref):
    planes, cols = edge_ref.shape
    lat = lax.axis_index("lat")
    near, second = state_rows(levels)
    rest = jnp.zeros((padded - levels, cols), F32)
    low, high = received(first_ref, second_ref)
    for i in range(2 * SUB):
        get = low if i < SUB else high
        at = i % SUB * near
        halo_ref[i, pl.ds(levels, padded - levels), :] = rest
        halo_ref[i, pl.ds(padded + levels, padded - levels), :] = rest
        halo_ref[i, pl.ds(0, levels + 2), :] = get(at, levels + 2)
        halo_ref[i, pl.ds(padded, levels), :] = get(at + second, levels)
    total = edge_ref[...] + edge_of(lambda i: halo_ref[i], range(SUB), cols, lat)
    out_ref[...] = total + edge_of(
        lambda i: halo_ref[i - rows], range(rows + SUB, rows + 2 * SUB), cols, lat
    )


def border_kernel(levels, padded, first_ref, second_ref, rows_ref, hist_ref, out_ref, swap_ref):
    rows, pairs, cols = hist_ref.shape
    close, distant = hist_rows(pairs)
    low, high = received(first_ref, second_ref)
    tall = 3 * rows
    fields = (rows + 2 * REACH) * pairs
    out_ref[pl.ds(fields, 8 * tall), :] = jnp.zeros((8 * tall, cols), F32)
    lane = iota((1, cols), 1)
    place = lane % WIDE_SLOT - REACH * lax.axis_index("lat")
    sent = (place >= 0) & (place < REACH)
    slots = cols // WIDE_SLOT
    groups = [None] * slot_groups(rows, cols)
    for at in range(-REACH, rows + REACH):
        get = low if at < 0 else high
        if 0 <= at < rows:
            own = rows_ref.at[at]
            get = lambda place, size: own[pl.ds(place, size), :]
            apart = hist_ref[at]
            places = {0: levels, 6: 0, 7: padded, 5: padded + levels}
            places.update({1 + field: levels + 2 + field for field in range(4)})
        elif -SUB <= at < rows + SUB:
            start = (at + SUB if at < 0 else at - rows) * close
            apart = get(start, pairs)
            start = start + pairs
            places = {0: start, 6: start + 1, 7: start + 2}
            places.update({1 + field: start + 3 + field for field in range(5)})
        else:
            start = SUB * close + (at + REACH if at < 0 else at - rows - SUB) * distant
            apart = get(start, pairs)
            start = start + pairs
            places = {0: start, 6: start + 1, 7: start + 2}
        out_ref[pl.ds((at + REACH) * pairs, pairs), :] = apart
        group, slot = divmod(at + REACH, slots)
        moved = pltpu.roll(apart, WIDE_SLOT * slot + REACH, 1)
        moved = jnp.where(sent & (lane // WIDE_SLOT == slot), moved, 0.0)
        groups[group] = moved if groups[group] is None else groups[group] + moved
        for field, place in places.items():
            value = get(place, 1)
            if field == 0 and 0 <= at < rows:
                value = jnp.where(get(levels + 1, 1) > 0.5, value, 0.0)
            out_ref[pl.ds(fields + field * tall + at + rows, 1), :] = value
    for at, group in enumerate(groups):
        swap_ref[pl.ds(at * pairs, pairs), :] = group
    swap_ref[pl.ds(len(groups) * pairs, 8 * tall), :] = out_ref[pl.ds(fields, 8 * tall), :]


def slot_groups(rows, cols):
    slots = cols // WIDE_SLOT
    return (rows + 2 * REACH + slots - 1) // slots


def basis_kernel(
    rows, pairs, mine_ref, other_ref, step_ref, change_ref,
    out_ref, near_ref, base_ref, first_ref, *work
):
    cols = mine_ref.shape[1]
    width = 2 * cols
    tall = rows + 2 * REACH
    ahead = REACH - SUB
    high = 3 * rows
    fields = tall * pairs
    closed = closed_lane(cols)
    opened = iota((1, width), 1) != closed
    slots = cols // WIDE_SLOT
    other_fields = slot_groups(rows, cols) * pairs
    lane = iota((1, cols), 1)
    start = jnp.where(lax.axis_index("lat") == 0, 0, cols - REACH)
    at_border = (lane >= start) & (lane < start + REACH)

    def wide(at, size):
        there = pl.ds(at - fields + other_fields, size)
        return jnp.concatenate([mine_ref[pl.ds(at, size), :], other_ref[there, :]], axis=1)

    def left(value):
        return pltpu.roll(value, width - 1, 1)

    def right(value):
        return pltpu.roll(value, 1, 1)

    def field(at):
        return wide(fields + at * high, high)

    def field_row(at, i):
        return wide(fields + at * high + i - REACH + rows, 1)

    faces = surface_faces(field(0), closed)
    for at in range(4):
        near_ref[at] = faces[at]
    sea = jnp.where(field(0) > 0.0, 1.0, 0.0)
    weight = field(3)
    near_ref[4] = weight * sea
    near_ref[5] = sea
    value = [field(6), field(7)]
    for sweep in range(SUB):
        value = [part - surface_outflow(part, *faces) for part in value]
    value = [weight * (value[0] - field(4)), weight * (value[1] - field(5))]
    for sweep in range(SUB):
        value = [part - surface_outflow(part, *faces) for part in value]
    base = [(part * sea)[rows : 2 * rows, :cols] for part in value]
    for tracer in range(2):
        base_ref[tracer] = base[tracer]
    for i in range(pairs // 2):
        total = jnp.zeros((1, cols), F32)
        for at, ref in ((0, step_ref), (cols // 2, change_ref)):
            part = ref[i, pl.ds(0, rows), :] * base[0] + ref[i, pl.ds(rows, rows), :] * base[1]
            part = jnp.sum(part, axis=(0, 1), keepdims=True)
            total = total + jnp.where(lane == at, part, 0.0)
        first_ref[pl.ds(i, 1), :] = total

    spread = [field_row(0, i) for i in range(tall)]
    to_right = [faces_between(value, left(value), opened) for value in spread]
    to_left = [right(value) for value in to_right]
    to_below = [faces_between(spread[i], spread[i + 1]) for i in range(tall - 1)]
    inner = range(ahead, tall - ahead)
    damping = {i: (field_row(1, i) - SHIFT) * (1.0 / SPAN) for i in inner}
    response_weight = {i: field_row(2, i) for i in inner}
    weight = {i: field_row(3, i) for i in inner}
    gain = SURFACE_GAIN / SPAN

    def outflow(get, i):
        value = get(i)
        total = to_right[i] * (value - left(value)) + to_left[i] * (value - right(value))
        total = total + to_below[i] * (value - get(i + 1))
        return value, total + to_below[i - 1] * (value - get(i - 1))

    def mixed(get, ref, reach):
        for i in range(REACH - reach, REACH + rows + reach):
            value, out = outflow(get, i)
            ref[i] = value - out
        return lambda i: ref[i]

    def applied(get, ref, reach):
        for i in range(REACH - reach, REACH + rows + reach):
            value, out = outflow(get, i)
            ref[i] = damping[i] * value + gain * out
        return lambda i: ref[i]

    def keep(slot, get):
        for i in range(rows):
            out_ref[slot, i] = get(i + REACH)[:, :cols]

    for i in range(tall):
        group, slot = divmod(i, slots)
        there = other_ref[pl.ds(group * pairs, pairs), :]
        there = pltpu.roll(there, (cols - WIDE_SLOT * slot - REACH) % cols, 1)
        work[-1][i, :, :cols] = mine_ref[pl.ds(i * pairs, pairs), :]
        work[-1][i, :, cols:] = jnp.where(at_border, there, 0.0)
    get = lambda i: work[-1][i]
    for sweep in range(SUB):
        get = mixed(get, work[sweep], REACH - 1 - sweep)
    reach = REACH - SUB
    powers = [get]
    for power in range(1, ITERS):
        powers.append(applied(powers[-1], work[SUB + power - 1], reach - power))
    for power in range(ITERS):
        keep(power, powers[power])
    reach = ITERS - 1
    slot = ITERS
    at = SUB + ITERS - 1
    chains = []
    for factor, power in [(weight, 0)] + [(response_weight, power) for power in range(ITERS)]:
        get = powers[power]
        chains.append(lambda i, factor=factor, get=get: factor[i] * get(i))
    for power in range(1, ITERS):
        for index in range(len(chains)):
            chains[index] = applied(chains[index], work[at], reach - power)
            at += 1
            keep(slot + index * (ITERS - 1) + power - 1, chains[index])


def mix_kernel(
    levels, padded, rows_ref, halo_ref, out_ref, face_ref, here_ref, there_ref
):
    rows, _, cols = rows_ref.shape
    lane = iota((1, cols), 1)
    count = rows + 2 * SUB
    level = iota((padded, cols), 0).astype(F32)

    def left(value):
        return pltpu.roll(value, cols - 1, 1)

    def right(value):
        return pltpu.roll(value, 1, 1)

    def source(i):
        if i < SUB:
            return halo_ref.at[i]
        if i < SUB + rows:
            return rows_ref.at[i - SUB]
        return halo_ref.at[i - rows]

    def face(depth_here, depth_there, spread_here, spread_there):
        opened = level < jnp.minimum(depth_here, depth_there)
        return jnp.where(opened, 0.5 * (spread_here + spread_there), 0.0)

    spreads = [source(i)[pl.ds(levels, 1), :] for i in range(count)]
    depths = [source(i)[pl.ds(levels + 1, 1), :] for i in range(count)]
    for i in range(count - 1):
        face_ref[0, i] = face(depths[i], depths[i + 1], spreads[i], spreads[i + 1])
    for i in range(1, count - 1):
        there = jnp.where(lane < cols - 1, left(depths[i]), 0.0)
        face_ref[1, i] = face(depths[i], there, spreads[i], left(spreads[i]))
        there = jnp.where(lane > 0, right(depths[i]), 0.0)
        face_ref[2, i] = face(depths[i], there, spreads[i], right(spreads[i]))

    for sweep in range(1, SUB + 1):
        target = here_ref if sweep % 2 else there_ref
        for i in range(sweep, count - sweep):
            def field(at):
                if sweep == 1:
                    return source(at)
                return (there_ref if sweep % 2 else here_ref).at[at]

            into = out_ref.at[i - SUB] if sweep == SUB else target.at[i]
            for tracer in range(2):
                at = pl.ds(tracer * padded, padded)
                centre = field(i)[at, :]
                total = centre + face_ref[0, i] * (field(i + 1)[at, :] - centre)
                total = total + face_ref[0, i - 1] * (field(i - 1)[at, :] - centre)
                total = total + face_ref[1, i] * (left(centre) - centre)
                total = total + face_ref[2, i] * (right(centre) - centre)
                into[at, :] = total


def fields_kernel(
    levels, padded, scale,
    rows_ref, main_ref, edge_ref, other_ref, weight_ref, observed_ref, basis_ref, first_ref, fixed_ref,
    mixed_ref, fields_ref, part_ref,
):
    rows, _, cols = rows_ref.shape
    pairs = basis_ref.shape[2]
    lat = lax.axis_index("lat")
    lane = iota((1, cols), 1)
    place = lane % SLOT
    level = iota((padded, cols), 0).astype(F32)

    def left(value, by=1):
        return pltpu.roll(value, (cols - by) % cols, 1)

    def right(value, by=1):
        return pltpu.roll(value, by, 1)

    spread = edge_ref[pl.ds(levels, 1), :] + other_ref[pl.ds(levels, 1), :]
    depth = edge_ref[pl.ds(levels + 1, 1), :] + other_ref[pl.ds(levels + 1, 1), :]
    within = place < 2 * SUB - 1
    col_depth = jnp.minimum(depth, jnp.where(within, left(depth), 0.0))
    col_spread = 0.5 * (spread + left(spread))
    row_depth = jnp.minimum(depth, left(depth, SLOT))
    row_spread = 0.5 * (spread + left(spread, SLOT))

    def strip_face(limit, value):
        return jnp.where(level < limit, value, 0.0)

    to_left = strip_face(right(col_depth), right(col_spread))
    to_right = strip_face(col_depth, col_spread)
    to_above = strip_face(right(row_depth, SLOT), right(row_spread, SLOT))
    to_below = strip_face(row_depth, row_spread)
    out_of_low = place == jnp.where(lat == 0, SUB - 1, SLOT)
    out_of_high = place == jnp.where(lat == 0, SLOT, SUB)
    over_low = jnp.where(out_of_low, to_right, 0.0)
    over_high = jnp.where(out_of_high, to_left, 0.0)
    own_right = jnp.where(place == SUB - 1, 0.0, to_right)
    own_left = jnp.where(place == SUB, 0.0, to_left)
    start = jnp.where(lat == 0, cols - SUB, 0)
    at_border = (lane >= start) & (lane < start + SUB)

    def spread_out(value, east, west):
        before, after = right(value), left(value)
        above, below = right(value, SLOT), left(value, SLOT)
        total = value + east * (after - value) + west * (before - value)
        return total + to_below * (below - value) + to_above * (above - value)

    parts = []
    extras = [None, None]
    for tracer in range(2):
        at = pl.ds(tracer * padded, padded)
        parts.append(edge_ref[at, :] + other_ref[at, :])

    for sweep in range(1, SUB + 1):
        for tracer in range(2):
            part = parts[tracer]
            across = over_low * (left(part) - part) + over_high * (right(part) - part)
            extra = extras[tracer]
            if extra is not None:
                across = across + spread_out(extra, own_right, own_left)
            extras[tracer] = across
            if sweep < SUB:
                parts[tracer] = spread_out(part, to_right, to_left)

    for row in range(rows):
        i = row + SUB
        at = pl.ds(row, levels, stride=rows)
        mixed = []
        for tracer in range(2):
            border = jnp.where(at_border, left(extras[tracer], SLOT * i + SUB), 0.0)
            mixed.append((main_ref[row, pl.ds(tracer * padded, padded), :] + border)[:levels])
        wet = level[:levels] < rows_ref[row, pl.ds(levels + 1, 1), :]
        weight = weight_ref[at, :]
        misfit = []
        for tracer in range(2):
            mixed_ref[tracer, at, :] = mixed[tracer]
            misfit.append(weight * (mixed[tracer] - observed_ref[tracer, at, :]))
        here = pl.ds(row, 1)
        part_ref[0, here, :] = scale * jnp.sum(
            jnp.where(wet, mixed[0] - mixed[1], 0.0), axis=0, keepdims=True
        )
        part_ref[1, here, :] = jnp.sum(
            jnp.where(wet, misfit[1] - misfit[0], 0.0), axis=0, keepdims=True
        )
    sums = [None] * FUNCTIONALS

    def add(at, slot, row, factor):
        value = basis_ref[slot, row] * factor
        sums[at] = value if sums[at] is None else sums[at] + value

    for row in range(rows):
        here = pl.ds(row, 1)
        surface, base = part_ref[0, here, :], part_ref[1, here, :]
        fixed = lambda plane: rows_ref[row, pl.ds(levels + plane, 1), :]
        add(1, 0, row, fixed(4) * surface)
        for power in range(1, ITERS):
            add(1 + power, ITERS + power - 1, row, surface)
        for j in range(ITERS):
            add(1 + ITERS + j, j, row, base)
            at = 1 + 2 * ITERS + j * ITERS
            add(at, j, row, fixed(3) * surface)
            for power in range(1, ITERS):
                add(at + power, ITERS + (1 + j) * (ITERS - 1) + power - 1, row, surface)
    half = pairs // 2
    total = first_ref[...] + fixed_ref[3]
    for at in range(1, FUNCTIONALS):
        value = jnp.sum(sums[at], axis=1, keepdims=True)
        total = total + jnp.where(lane == at, value[:half], 0.0)
        total = total + jnp.where(lane == cols // 2 + at, value[half:], 0.0)
    part_ref[2] = total
    for field in range(3):
        part_ref[3 + field] = fixed_ref[field]
    for copy in range(fields_ref.shape[0]):
        fields_ref[copy] = part_ref[...]


def solve_kernel(
    levels, scale,
    mine_ref, other_ref, faces_ref, near_ref, base_ref, plan_ref, mixed_ref, depth_ref, step_ref,
    change_ref, state_ref, gradient_ref, direction_ref, kept_ref,
):
    loops, _, rows, cols = mine_ref.shape
    loop = lax.axis_index("loop")

    def total(value):
        parts = [
            value[i * rows : (i + 1) * rows, j * cols : (j + 1) * cols]
            for i in range(loops)
            for j in range(2)
        ]
        while len(parts) > 1:
            half = (len(parts) + 1) // 2
            parts = [a + b for a, b in zip(parts, parts[half:])] + parts[len(parts) - half : half]
        return jnp.sum(jnp.sum(parts[0], axis=1, keepdims=True), axis=0, keepdims=True)

    count = step_ref.shape[0]
    inner = mine_ref[0, 2] + other_ref[0, 2]
    for i in range(1, loops):
        inner = inner + (mine_ref[i, 2] + other_ref[i, 2])
    plan = plan_ref[...]
    shifted = pltpu.roll(inner, cols // 2, 1)
    linear = None
    for i in range(2 * count):
        source = inner if i < count else shifted
        part = plan[:, i : i + 1] * source[i % count : i % count + 1]
        linear = part if linear is None else linear + part
    gamma = plan[:1, 2 * count : 2 * count + 1]

    gained = [faces_ref[i] for i in range(4)]
    damping = faces_ref[4]

    def conjugate(rhs):
        residual = rhs
        search = rhs
        solution = jnp.zeros_like(rhs)
        norm_now = total(rhs * rhs)
        one = jnp.ones((1, 1), F32)
        residual_of = [one]
        search_of = [one]
        solution_of = []
        for sweep in range(ITERS):
            image = damping * search + surface_outflow(search, *gained)
            alpha = norm_now / total(search * image)
            solution = solution + alpha * search
            solution_of = add_up(solution_of, alpha, search_of)
            if sweep < ITERS - 1:
                residual = residual - alpha * image
                norm_next = total(residual * residual)
                beta = norm_next / norm_now
                search = residual + beta * search
                norm_now = norm_next
                image_of = [SHIFT * value for value in search_of]
                image_of = add_up(image_of, SPAN, [None] + search_of)
                residual_of = add_up(residual_of, -alpha, image_of)
                search_of = add_up(residual_of, beta, search_of)
        return solution, solution_of

    def add_up(terms, factor, others):
        result = list(terms) + [None] * (len(others) - len(terms))
        for at, value in enumerate(others):
            if value is not None:
                value = factor * value
                result[at] = value if result[at] is None else result[at] + value
        return result

    def near(slot, value):
        for i in range(loops):
            kept_ref[slot, i] = value[i * rows : (i + 1) * rows]
        return jnp.concatenate(
            [kept_ref[slot, lax.rem(loop + shift, loops)] for shift in (loops - 1, 0, 1)], axis=0
        )

    elevation, elevation_of = conjugate(gathered(mine_ref, other_ref, 0))
    pressure = gathered(mine_ref, other_ref, 1) + faces_ref[5] * elevation
    elevation = near(0, elevation)
    depth = depth_ref[...]
    here = elevation[rows : 2 * rows, :cols]
    for level in range(levels):
        at = pl.ds(level * rows, rows)
        change = jnp.where(level < depth, here, 0.0)
        state_ref[0, at, :] = mixed_ref[0, at, :] - change
        state_ref[1, at, :] = mixed_ref[1, at, :] + change
    response, response_of = conjugate(pressure)
    response = near(1, response)

    lane = iota((1, cols), 1)
    factor = jnp.where(lane == 0, 1.0, 0.0)
    for j in range(ITERS):
        factor = jnp.where(lane == 1 + j, -elevation_of[j], factor)
        part = scale * response_of[j]
        factor = jnp.where(lane == 1 + ITERS + j, part, factor)
        for k in range(ITERS):
            at = 1 + 2 * ITERS + j * ITERS + k
            factor = jnp.where(lane == at, part * elevation_of[k], factor)
    weights = jnp.sum(linear * factor, axis=1, keepdims=True)
    weights = [
        jnp.broadcast_to(weights[i : i + 1], (rows, cols)) for i in range(2 * count)
    ]

    sea = near_ref[5]
    carried = near_ref[4] * elevation - (scale * sea) * response
    faces = [near_ref[i] for i in range(4)]
    for sweep in range(SUB):
        carried = carried - surface_outflow(carried, *faces)
    carried = (sea * carried)[rows : 2 * rows, :cols]
    for tracer in range(2):
        at = pl.ds(tracer * rows, rows)
        gradient = base_ref[tracer] - carried if tracer == 0 else base_ref[tracer] + carried
        gradient_ref[tracer] = gradient
        value = gamma * gradient
        for i in range(count):
            value = value + weights[i] * step_ref[i, at, :]
            value = value + weights[count + i] * change_ref[i, at, :]
        direction_ref[tracer] = value


def on_device(
    state, observed, weight, control, depth_index, diffusivity, damping, history_step, history_change
):
    _, levels, rows, cols = state.shape
    count = history_step.shape[0]
    padded = round_up(levels + 6, 8)
    planes = 2 * padded
    loops = lax.axis_size("loop")
    lats = lax.axis_size("lat")
    blocks = loops * lats
    scale = levels ** (-0.5)
    flat = (2, levels * rows, cols)
    state = state.reshape(flat)
    observed = observed.reshape(flat)
    weight = weight.reshape(flat[1:])
    step = history_step.reshape(count, 2 * rows, cols)
    change = history_change.reshape(count, 2 * rows, cols)

    pairs = 2 * count
    inputs = (
        state, control, depth_index, diffusivity,
        history_step.reshape(-1, cols), history_change.reshape(-1, cols), damping, weight, observed,
    )
    held = [x.shape for x in inputs[:-1]] + [(2, rows, cols)]
    close, distant = hist_rows(pairs)
    sent_hist = (round_up(SUB * close + (REACH - SUB) * distant, 8), cols)
    sent = (round_up(SUB * state_rows(levels)[0], 8), cols)
    shapes = ((rows, planes, cols), (rows, pairs, cols), sent_hist, sent_hist, sent, sent)
    packed, hist, first_hist, second_hist, first, second = pl.pallas_call(
        functools.partial(pack_kernel, levels, padded),
        out_shape=[jax.ShapeDtypeStruct(shape, F32) for shape in shapes],
        in_specs=[pl.BlockSpec(memory_space=pltpu.HBM)] * len(inputs),
        out_specs=[VMEM] * len(shapes),
        scratch_shapes=[pltpu.VMEM(shape, x.dtype) for shape, x in zip(held, inputs)]
        + [pltpu.SemaphoreType.DMA((len(inputs),))],
        compiler_params=pltpu.CompilerParams(vmem_limit_bytes=VMEM_BYTES),
        name="pack",
    )(*(pltpu.with_memory_space_constraint(x, pltpu.HBM) for x in inputs))
    partner = [(i, i ^ 1) for i in range(loops)]
    following = [(i, (i - 1 + 2 * (i % 2)) % loops) for i in range(loops)]
    swap = [(0, 1), (1, 0)]
    first_hist = lax.ppermute(first_hist, "loop", partner)
    second_hist = lax.ppermute(second_hist, "loop", following)
    first = lax.ppermute(first, "loop", partner)
    second = lax.ppermute(second, "loop", following)
    edge, depth, fixed = call(
        functools.partial(pairs_kernel, levels),
        [(planes, cols), (rows, cols), (4, rows, cols)],
        name="pairs",
    )(packed, step, change)
    height = loops * rows
    large = VMEM_BYTES if loops <= 16 else 2 * VMEM_BYTES
    fields = 8 * 3 * rows
    border, border_other = call(
        functools.partial(border_kernel, levels, padded),
        [
            ((rows + 2 * REACH) * pairs + fields, cols),
            (slot_groups(rows, cols) * pairs + fields, cols),
        ],
        name="border",
    )(first_hist, second_hist, packed, hist)
    border_other = lax.ppermute(border_other, "lat", swap)
    chains = 1 + ITERS
    buffers = SUB + ITERS + chains * (ITERS - 1)
    shapes = (
        (ITERS + chains * (ITERS - 1), rows, pairs, cols),
        (6, 3 * rows, 2 * cols),
        (2, rows, cols),
        (count, cols),
    )
    basis, around, base, near_start = pl.pallas_call(
        functools.partial(basis_kernel, rows, pairs),
        out_shape=[jax.ShapeDtypeStruct(shape, F32) for shape in shapes],
        in_specs=[VMEM] * 4,
        out_specs=[VMEM] * len(shapes),
        scratch_shapes=[pltpu.VMEM((rows + 2 * REACH, pairs, 2 * cols), F32)] * buffers,
        compiler_params=pltpu.CompilerParams(vmem_limit_bytes=VMEM_BYTES),
        name="basis",
    )(border, border_other, step, change)
    edge, halo = call(
        functools.partial(halo_kernel, levels, padded, rows),
        [(planes, cols), (2 * SUB, planes, cols)],
        name="halo",
    )(edge, first, second, near_start)
    other = lax.ppermute(edge, "lat", swap)
    tall = rows + 2 * SUB
    (mixed,) = call(
        functools.partial(mix_kernel, levels, padded),
        [(rows, planes, cols)],
        scratch=[pltpu.VMEM((3, tall, padded, cols), F32)]
        + [pltpu.VMEM((tall, planes, cols), F32)] * 2,
        name="mix",
    )(packed, halo)
    mixed, fields = call(
        functools.partial(fields_kernel, levels, padded, scale),
        [flat, (loops, 6, rows, cols)],
        scratch=[pltpu.VMEM((6, rows, cols), F32)],
        name="fields",
    )(packed, mixed, edge, other, weight, observed, basis, near_start, fixed)
    mine = lax.all_to_all(fields, "loop", 0, 0)
    theirs = lax.ppermute(mine, "lat", swap)
    faces, plan = call(
        plan_kernel, [(6, height, 2 * cols), (pairs, cols)], vmem=large, name="plan"
    )(mine, theirs)
    shapes = (flat, (2, rows, cols), (2, rows, cols))
    state_next, gradient, direction = call(
        functools.partial(solve_kernel, levels, scale),
        shapes,
        scratch=[pltpu.VMEM((2, loops, rows, 2 * cols), F32)],
        vmem=large,
        name="solve",
    )(mine, theirs, faces, around, base, plan, mixed, depth, step, change)
    return (state_next.reshape(2, levels, rows, cols), gradient, direction)


def solution(mesh):
    return jax.shard_map(
        on_device,
        mesh=mesh,
        in_specs=(
            P("members", None, "loop", "lat"),
            P("members", None, "loop", "lat"),
            P(None, "loop", "lat"),
            P("members", "loop", "lat"),
            P("loop", "lat"),
            P("loop", "lat"),
            P("loop", "lat"),
            P("members", None, "loop", "lat"),
            P("members", None, "loop", "lat"),
        ),
        out_specs=(
            P("members", None, "loop", "lat"),
            P("members", "loop", "lat"),
            P("members", "loop", "lat"),
        ),
        check_vma=False,
    )
```

```python
import functools

import jax
import jax.numpy as jnp
from jax import lax
from jax.experimental import pallas as pl
from jax.experimental.pallas import tpu as pltpu
from jax.sharding import PartitionSpec as P

ITERS = 3
SUB = 3
SURFACE_GAIN = 5.0
SLOT = 8
WIDE_SLOT = 16
FOLD = SLOT * SUB
SWAP_ROWS = 240
REACH = SUB + 2 * (ITERS - 1)
SHIFT = 5.0
SPAN = 5.0
FUNCTIONALS = 1 + ITERS + ITERS + ITERS * ITERS
GRID = ("loop", "lat")
VMEM = pl.BlockSpec(memory_space=pltpu.VMEM)
F32 = jnp.float32
VMEM_BYTES = 16 * 1024 * 1024


def round_up(value, to):
    return (value + to - 1) // to * to


def call(kernel, out_shapes, scratch=(), vmem=VMEM_BYTES, name=None):
    return pl.pallas_call(
        kernel,
        out_shape=[jax.ShapeDtypeStruct(shape, F32) for shape in out_shapes],
        out_specs=[VMEM] * len(out_shapes),
        scratch_shapes=list(scratch),
        compiler_params=pltpu.CompilerParams(vmem_limit_bytes=vmem),
        name=name,
    )


def iota(shape, dim):
    return lax.broadcasted_iota(jnp.int32, shape, dim)


def state_rows(levels):
    return 2 * levels + 2, levels + 2


def hist_rows(pairs):
    return pairs + 8, pairs + 3


def pack_kernel(levels, padded, *refs):
    sources, outs, targets, sems = refs[:9], refs[9:15], refs[15:24], refs[24]
    rows_ref, hist_ref = outs[:2]
    rows, cols = targets[2].shape
    copies = []
    for at, (source, target) in enumerate(zip(sources, targets)):
        if at == 8:
            source = source.at[:, pl.ds(0, rows), :]
        copies.append(pltpu.make_async_copy(source, target, sems.at[at]))
    for copy in copies:
        copy.start()
    for copy in copies[2:]:
        copy.wait()
    (
        state_ref, control_ref, depth_ref, spread_ref, step_ref, change_ref, damping_ref, weight_ref,
        observed_ref,
    ) = targets
    count = step_ref.shape[0] // (2 * rows)
    pairs = 2 * count
    near, second = state_rows(levels)
    close, distant = hist_rows(pairs)
    depth = depth_ref[...].astype(F32)
    spread = spread_ref[...]
    wet = depth > 0.5
    total = jnp.zeros((rows, cols), F32)
    for level in range(levels):
        total = total + jnp.where(level < depth, weight_ref[pl.ds(level * rows, rows), :], 0.0)
    fields = [
        damping_ref[...],
        2.0 * total,
        weight_ref[pl.ds(0, rows), :],
        observed_ref[0],
        observed_ref[1],
    ]
    for row in range(rows):
        here = slice(row, row + 1)
        for which, ref in enumerate((step_ref, change_ref)):
            both = [ref[pl.ds(tracer * rows + row, count, stride=2 * rows), :] for tracer in range(2)]
            apart = jnp.where(wet[here], both[0] - both[1], 0.0)
            hist_ref[row, pl.ds(which * count, count), :] = apart
    for copy in copies[:2]:
        copy.wait()
    first = iota((levels, cols), 0) == 0
    rest = jnp.zeros((padded - levels, cols), F32)
    for row in range(rows):
        here = slice(row, row + 1)
        for tracer in range(2):
            lift = jnp.where(wet[here], control_ref[tracer, here, :], 0.0)
            value = state_ref[tracer, pl.ds(row, levels, stride=rows), :]
            value = value + jnp.where(first, lift, 0.0)
            rows_ref[row, pl.ds(tracer * padded, levels), :] = value
            rows_ref[row, pl.ds(tracer * padded + levels, padded - levels), :] = rest
        for field, value in enumerate([spread, depth] + fields[:4]):
            rows_ref[row, pl.ds(levels + field, 1), :] = value[here]
        rows_ref[row, pl.ds(padded + levels, 1), :] = fields[4][here]

    even = lax.rem(lax.axis_index("loop"), 2) == 0

    def put(refs, at, upper, lower):
        here = pl.ds(at, upper.shape[0])
        refs[0][here, :] = jnp.where(even, upper, lower)
        refs[1][here, :] = jnp.where(even, lower, upper)

    def fill(refs, last):
        if last < refs[0].shape[0]:
            rest = jnp.zeros((refs[0].shape[0] - last, cols), F32)
            put(refs, last, rest, rest)

    masked = jnp.where(wet, spread, 0.0)
    for at in range(REACH):
        far = at < REACH - SUB
        index = at if far else at - (REACH - SUB)
        upper = rows - REACH + at if far else rows - SUB + index
        lower = SUB + index if far else index
        start = SUB * close + index * distant if far else index * close
        put(outs[2:4], start, hist_ref[upper], hist_ref[lower])
        start = start + pairs
        put(outs[2:4], start, masked[upper : upper + 1], masked[lower : lower + 1])
        for tracer in range(2):
            here = pl.ds(tracer * padded, 1)
            put(outs[2:4], start + 1 + tracer, rows_ref[upper, here, :], rows_ref[lower, here, :])
        if not far:
            here = pl.ds(levels + 2, 4)
            put(outs[2:4], start + 3, rows_ref[upper, here, :], rows_ref[lower, here, :])
            here = pl.ds(padded + levels, 1)
            put(outs[2:4], start + 7, rows_ref[upper, here, :], rows_ref[lower, here, :])
    last = SUB * close + (REACH - SUB) * distant
    folds = outs[2].shape[0] - FOLD
    if last < folds:
        rest = jnp.zeros((folds - last, cols), F32)
        put(outs[2:4], last, rest, rest)
    lat = lax.axis_index("lat")
    put(
        outs[2:4],
        folds,
        folded(edge_of(lambda i: rows_ref[rows - SUB + i], range(SUB), cols, lat)),
        folded(edge_of(lambda i: rows_ref[i], range(SUB), cols, lat)),
    )
    for at in range(SUB):
        upper, lower = rows - SUB + at, at
        for start, size, place in ((0, levels + 2, 0), (padded, levels, second)):
            here = pl.ds(start, size)
            put(outs[4:6], at * near + place, rows_ref[upper, here, :], rows_ref[lower, here, :])
    fill(outs[4:6], SUB * near)


def edge_of(rows_of, indices, cols, lat):
    lane = iota((1, cols), 1)
    slot = lane // SLOT
    place = lane % SLOT - SUB * lat
    mine = (place >= 0) & (place < SUB)
    total = None
    for index in indices:
        moved = pltpu.roll(rows_of(index), SLOT * index + SUB, 1)
        piece = jnp.where(mine & (slot == index), moved, 0.0)
        total = piece if total is None else total + piece
    return total


def folded(edge):
    planes, cols = edge.shape
    total = None
    for at, start in enumerate(range(0, planes, FOLD)):
        size = min(FOLD, planes - start)
        part = pltpu.roll(edge[start : start + size], FOLD * at, 1)
        if size < FOLD:
            part = jnp.concatenate([part, jnp.zeros((FOLD - size, cols), F32)], axis=0)
        total = part if total is None else total + part
    return total


def unfolded(fold, planes, lane_at):
    cols = fold.shape[1]
    lane = iota((1, cols), 1)
    here = (lane >= lane_at) & (lane < lane_at + FOLD)
    parts = []
    for at, start in enumerate(range(0, planes, FOLD)):
        part = pltpu.roll(fold, (lane_at - FOLD * at) % cols, 1)
        parts.append(jnp.where(here, part, 0.0)[: min(FOLD, planes - start)])
    return jnp.concatenate(parts, axis=0)


def level_face(levels, depth_here, depth_there, spread_here, spread_there):
    opened = levels < jnp.minimum(depth_here, depth_there)
    return jnp.where(opened, 0.5 * (spread_here + spread_there), 0.0)


def side_faces(level, depth, spread):
    cols = depth.shape[1]
    lane = iota((1, cols), 1)
    result = []
    for by, inside in ((cols - 1, lane < cols - 1), (1, lane > 0)):
        there = jnp.where(inside, pltpu.roll(depth, by, 1), 0.0)
        result.append(level_face(level, depth, there, spread, pltpu.roll(spread, by, 1)))
    return result


def mixed_row(get, faces, i, at):
    below, above, right, left = faces
    centre = get(i)[at, :]
    cols = centre.shape[1]
    total = centre + below * (get(i + 1)[at, :] - centre)
    total = total + above * (get(i - 1)[at, :] - centre)
    total = total + right * (pltpu.roll(centre, cols - 1, 1) - centre)
    return total + left * (pltpu.roll(centre, 1, 1) - centre)


def pairs_kernel(
    levels, padded, rows_ref, step_ref, change_ref, edge_ref, depth_ref, fixed_ref, face_ref, inner_ref
):
    rows, _, cols = rows_ref.shape
    level = iota((padded, cols), 0).astype(F32)
    spreads = [rows_ref[i, pl.ds(levels, 1), :] for i in range(rows)]
    depths = [rows_ref[i, pl.ds(levels + 1, 1), :] for i in range(rows)]
    for i in range(rows):
        if i + 1 < rows:
            face_ref[0, i] = level_face(level, depths[i], depths[i + 1], spreads[i], spreads[i + 1])
        face_ref[1, i], face_ref[2, i] = side_faces(level, depths[i], spreads[i])
    face_ref[0, rows - 1] = jnp.zeros((padded, cols), F32)
    for sweep in range(SUB):
        source = rows_ref if sweep == 0 else inner_ref.at[sweep - 1]
        for i in range(rows):
            for tracer in range(2):
                at = pl.ds(tracer * padded, padded)
                if sweep < i < rows - 1 - sweep:
                    faces = face_ref[0, i], face_ref[0, i - 1], face_ref[1, i], face_ref[2, i]
                    inner_ref[sweep, i, at, :] = mixed_row(lambda j: source.at[j], faces, i, at)
                else:
                    inner_ref[sweep, i, at, :] = jnp.zeros((padded, cols), F32)
    lat = lax.axis_index("lat")
    count = step_ref.shape[0]
    lane = iota((1, cols), 1)
    gram = [jnp.zeros((1, cols), F32) for _ in range(count)]
    at = FUNCTIONALS
    for left_ref in (step_ref, change_ref):
        for i in range(count):
            for j in range(i, count):
                value = jnp.sum(left_ref[i] * change_ref[j], axis=(0, 1), keepdims=True)
                gram[i] = gram[i] + jnp.where(lane == at + j, value, 0.0)
                if i != j:
                    gram[j] = gram[j] + jnp.where(lane == at + i, value, 0.0)
        at += count
    for i in range(count):
        fixed_ref[3, pl.ds(i, 1), :] = gram[i]
    for row in range(rows):
        plane = lambda at: rows_ref[row, pl.ds(levels + at, 1), :]
        here = pl.ds(row, 1)
        depth_ref[here, :] = plane(1)
        fixed_ref[0, here, :] = jnp.where(plane(1) > 0.5, plane(0), 0.0)
        fixed_ref[1, here, :] = plane(2)
        fixed_ref[2, here, :] = plane(3)
    edge_ref[...] = edge_of(lambda i: rows_ref[i - SUB], range(SUB, rows + SUB), cols, lat)


def faces_between(here, there, opened=True):
    return jnp.where((here > 0.0) & (there > 0.0) & opened, 0.5 * (here + there), 0.0)


def closed_lane(cols):
    return jnp.where(lax.axis_index("lat") == 0, 2 * cols - 1, cols - 1)


def surface_faces(spread, closed):
    height, width = spread.shape
    below = faces_between(spread, pltpu.roll(spread, height - 1, 0))
    right = faces_between(
        spread, pltpu.roll(spread, width - 1, 1), iota(spread.shape, 1) != closed
    )
    return below, pltpu.roll(below, 1, 0), right, pltpu.roll(right, 1, 1)


def gathered(mine_ref, other_ref, field):
    return jnp.concatenate(
        [
            jnp.concatenate([mine_ref[i, field], other_ref[i, field]], axis=1)
            for i in range(mine_ref.shape[0])
        ],
        axis=0,
    )


def surface_outflow(value, to_below, to_above, to_right, to_left):
    height, width = value.shape
    result = to_right * (value - pltpu.roll(value, width - 1, 1))
    result = result + to_left * (value - pltpu.roll(value, 1, 1))
    result = result + to_below * (value - pltpu.roll(value, height - 1, 0))
    return result + to_above * (value - pltpu.roll(value, 1, 0))


def plan_kernel(mine_ref, other_ref, faces_ref, plan_ref):
    loops, _, rows, cols = mine_ref.shape
    closed = closed_lane(cols)
    for at, face in enumerate(surface_faces(gathered(mine_ref, other_ref, 3), closed)):
        faces_ref[at] = SURFACE_GAIN * face
    for field in (4, 5):
        faces_ref[field] = gathered(mine_ref, other_ref, field)
    count = plan_ref.shape[0] // 2
    gram = mine_ref[0, 2] + other_ref[0, 2]
    for i in range(1, loops):
        gram = gram + (mine_ref[i, 2] + other_ref[i, 2])
    wide = (count, cols)
    tables = [
        jnp.broadcast_to(gram[:, i : i + 1], wide)
        for i in range(FUNCTIONALS, FUNCTIONALS + 2 * count)
    ]
    step_change, change_change = tables[:count], tables[count:]
    last = count - 1
    gamma = step_change[last][last:] / change_change[last][last:]
    rho = [1.0 / step_change[i][i : i + 1] for i in range(count)]
    row = iota(wide, 0)
    lane = iota(wide, 1)
    step_grad = jnp.where(lane == row, 1.0, 0.0)
    change_grad = jnp.where(lane == row + count, 1.0, 0.0)
    factors = [None] * count
    for i in range(count - 1, -1, -1):
        factors[i] = rho[i] * step_grad[i : i + 1]
        step_grad = step_grad - factors[i] * step_change[i]
        change_grad = change_grad - factors[i] * change_change[i]
    change_grad = gamma * change_grad
    for i in range(count):
        weight = factors[i] - rho[i] * change_grad[i : i + 1]
        change_grad = change_grad + weight * step_change[i]
        plan_ref[pl.ds(i, 1), :] = -weight
        plan_ref[pl.ds(count + i, 1), :] = gamma * factors[i]
    at = lane[:1] == 2 * count
    plan_ref[pl.ds(0, 1), :] = jnp.where(at, -gamma, plan_ref[pl.ds(0, 1), :])


def received(first_ref, second_ref):
    even = lax.rem(lax.axis_index("loop"), 2) == 0

    def low(at, size):
        here = pl.ds(at, size)
        return jnp.where(even, second_ref[here, :], first_ref[here, :])

    def high(at, size):
        here = pl.ds(at, size)
        return jnp.where(even, first_ref[here, :], second_ref[here, :])

    return low, high


def border_kernel(
    levels, padded, edge_ref, first_ref, second_ref, rows_ref, hist_ref, out_ref, swap_ref
):
    rows, pairs, cols = hist_ref.shape
    close, distant = hist_rows(pairs)
    low, high = received(first_ref, second_ref)
    tall = 3 * rows
    fields = (rows + 2 * REACH) * pairs
    out_ref[pl.ds(fields, 8 * tall), :] = jnp.zeros((8 * tall, cols), F32)
    lane = iota((1, cols), 1)
    place = lane % WIDE_SLOT - REACH * lax.axis_index("lat")
    sent = (place >= 0) & (place < REACH)
    slots = cols // WIDE_SLOT
    groups = [None] * slot_groups(rows, cols)
    for at in range(-REACH, rows + REACH):
        get = low if at < 0 else high
        if 0 <= at < rows:
            own = rows_ref.at[at]
            get = lambda place, size: own[pl.ds(place, size), :]
            apart = hist_ref[at]
            places = {0: levels, 6: 0, 7: padded, 5: padded + levels}
            places.update({1 + field: levels + 2 + field for field in range(4)})
        elif -SUB <= at < rows + SUB:
            start = (at + SUB if at < 0 else at - rows) * close
            apart = get(start, pairs)
            start = start + pairs
            places = {0: start, 6: start + 1, 7: start + 2}
            places.update({1 + field: start + 3 + field for field in range(5)})
        else:
            start = SUB * close + (at + REACH if at < 0 else at - rows - SUB) * distant
            apart = get(start, pairs)
            start = start + pairs
            places = {0: start, 6: start + 1, 7: start + 2}
        out_ref[pl.ds((at + REACH) * pairs, pairs), :] = apart
        group, slot = divmod(at + REACH, slots)
        moved = pltpu.roll(apart, WIDE_SLOT * slot + REACH, 1)
        moved = jnp.where(sent & (lane // WIDE_SLOT == slot), moved, 0.0)
        groups[group] = moved if groups[group] is None else groups[group] + moved
        for field, place in places.items():
            value = get(place, 1)
            if field == 0 and 0 <= at < rows:
                value = jnp.where(get(levels + 1, 1) > 0.5, value, 0.0)
            out_ref[pl.ds(fields + field * tall + at + rows, 1), :] = value
    for at, group in enumerate(groups):
        swap_ref[pl.ds(at * pairs, pairs), :] = group
    total = None
    for field in range(8):
        moved = pltpu.roll(
            out_ref[pl.ds(fields + field * tall, tall), :], WIDE_SLOT * field + REACH, 1
        )
        moved = jnp.where(sent & (lane // WIDE_SLOT == field), moved, 0.0)
        total = moved if total is None else total + moved
    at = len(groups) * pairs
    swap_ref[pl.ds(at, tall), :] = total
    at = at + tall
    planes = edge_ref.shape[0]
    folds = first_ref.shape[0] - FOLD
    before = unfolded(low(folds, FOLD), planes, 0)
    after = unfolded(high(folds, FOLD), planes, SLOT * (rows + SUB))
    swap_ref[pl.ds(at, planes), :] = edge_ref[...] + (before + after)
    at = at + planes
    if at < swap_ref.shape[0]:
        swap_ref[pl.ds(at, swap_ref.shape[0] - at), :] = jnp.zeros(
            (swap_ref.shape[0] - at, cols), F32
        )


def slot_groups(rows, cols):
    slots = cols // WIDE_SLOT
    return (rows + 2 * REACH + slots - 1) // slots


def basis_kernel(
    rows, pairs, mine_ref, other_ref, step_ref, change_ref,
    out_ref, near_ref, base_ref, first_ref, *work
):
    cols = mine_ref.shape[1]
    width = 2 * cols
    tall = rows + 2 * REACH
    ahead = REACH - SUB
    high = 3 * rows
    fields = tall * pairs
    closed = closed_lane(cols)
    opened = iota((1, width), 1) != closed
    slots = cols // WIDE_SLOT
    other_fields = slot_groups(rows, cols) * pairs
    beside_ref = work[-2]
    lane = iota((1, cols), 1)
    start = jnp.where(lax.axis_index("lat") == 0, 0, cols - REACH)
    at_border = (lane >= start) & (lane < start + REACH)

    packed = other_ref[pl.ds(other_fields, high), :]
    for at in range(8):
        there = pltpu.roll(packed, (cols - WIDE_SLOT * at - REACH) % cols, 1)
        beside_ref[pl.ds(at * high, high), :] = jnp.where(at_border, there, 0.0)

    def wide(at, size):
        there = pl.ds(at - fields, size)
        return jnp.concatenate([mine_ref[pl.ds(at, size), :], beside_ref[there, :]], axis=1)

    def left(value):
        return pltpu.roll(value, width - 1, 1)

    def right(value):
        return pltpu.roll(value, 1, 1)

    def field(at):
        return wide(fields + at * high, high)

    def field_row(at, i):
        return wide(fields + at * high + i - REACH + rows, 1)

    faces = surface_faces(field(0), closed)
    for at in range(4):
        near_ref[at] = faces[at]
    sea = jnp.where(field(0) > 0.0, 1.0, 0.0)
    weight = field(3)
    near_ref[4] = weight * sea
    near_ref[5] = sea
    value = [field(6), field(7)]
    for sweep in range(SUB):
        value = [part - surface_outflow(part, *faces) for part in value]
    value = [weight * (value[0] - field(4)), weight * (value[1] - field(5))]
    for sweep in range(SUB):
        value = [part - surface_outflow(part, *faces) for part in value]
    base = [(part * sea)[rows : 2 * rows, :cols] for part in value]
    for tracer in range(2):
        base_ref[tracer] = base[tracer]
    for i in range(pairs // 2):
        total = jnp.zeros((1, cols), F32)
        for at, ref in ((0, step_ref), (cols // 2, change_ref)):
            part = ref[i, pl.ds(0, rows), :] * base[0] + ref[i, pl.ds(rows, rows), :] * base[1]
            part = jnp.sum(part, axis=(0, 1), keepdims=True)
            total = total + jnp.where(lane == at, part, 0.0)
        first_ref[pl.ds(i, 1), :] = total

    spread = [field_row(0, i) for i in range(tall)]
    to_right = [faces_between(value, left(value), opened) for value in spread]
    to_left = [right(value) for value in to_right]
    to_below = [faces_between(spread[i], spread[i + 1]) for i in range(tall - 1)]
    inner = range(ahead, tall - ahead)
    damping = {i: (field_row(1, i) - SHIFT) * (1.0 / SPAN) for i in inner}
    response_weight = {i: field_row(2, i) for i in inner}
    weight = {i: field_row(3, i) for i in inner}
    gain = SURFACE_GAIN / SPAN

    def outflow(get, i):
        value = get(i)
        total = to_right[i] * (value - left(value)) + to_left[i] * (value - right(value))
        total = total + to_below[i] * (value - get(i + 1))
        return value, total + to_below[i - 1] * (value - get(i - 1))

    def mixed(get, ref, reach):
        for i in range(REACH - reach, REACH + rows + reach):
            value, out = outflow(get, i)
            ref[i] = value - out
        return lambda i: ref[i]

    def applied(get, ref, reach):
        for i in range(REACH - reach, REACH + rows + reach):
            value, out = outflow(get, i)
            ref[i] = damping[i] * value + gain * out
        return lambda i: ref[i]

    def keep(slot, get):
        for i in range(rows):
            out_ref[slot, i] = get(i + REACH)[:, :cols]

    for i in range(tall):
        group, slot = divmod(i, slots)
        there = other_ref[pl.ds(group * pairs, pairs), :]
        there = pltpu.roll(there, (cols - WIDE_SLOT * slot - REACH) % cols, 1)
        work[-1][i, :, :cols] = mine_ref[pl.ds(i * pairs, pairs), :]
        work[-1][i, :, cols:] = jnp.where(at_border, there, 0.0)
    get = lambda i: work[-1][i]
    for sweep in range(SUB):
        get = mixed(get, work[sweep], REACH - 1 - sweep)
    reach = REACH - SUB
    powers = [get]
    for power in range(1, ITERS):
        powers.append(applied(powers[-1], work[SUB + power - 1], reach - power))
    for power in range(ITERS):
        keep(power, powers[power])
    reach = ITERS - 1
    slot = ITERS
    at = SUB + ITERS - 1
    chains = []
    for factor, power in [(weight, 0)] + [(response_weight, power) for power in range(ITERS)]:
        get = powers[power]
        chains.append(lambda i, factor=factor, get=get: factor[i] * get(i))
    for power in range(1, ITERS):
        for index in range(len(chains)):
            chains[index] = applied(chains[index], work[at], reach - power)
            at += 1
            keep(slot + index * (ITERS - 1) + power - 1, chains[index])


def mix_kernel(
    levels, padded, rows_ref, first_ref, second_ref, own_face_ref, inner_ref, _,
    out_ref, face_ref, outer_ref, halo_ref
):
    rows, _, cols = rows_ref.shape
    count = rows + 2 * SUB
    near, second = state_rows(levels)
    rest = jnp.zeros((padded - levels, cols), F32)
    low, high = received(first_ref, second_ref)
    for i in range(2 * SUB):
        get = low if i < SUB else high
        at = i % SUB * near
        halo_ref[i, pl.ds(levels, padded - levels), :] = rest
        halo_ref[i, pl.ds(padded + levels, padded - levels), :] = rest
        halo_ref[i, pl.ds(0, levels + 2), :] = get(at, levels + 2)
        halo_ref[i, pl.ds(padded, levels), :] = get(at + second, levels)
    level = iota((padded, cols), 0).astype(F32)

    def state_row(i):
        if i < SUB:
            return halo_ref.at[i]
        return rows_ref.at[i - SUB] if i < SUB + rows else halo_ref.at[i - rows]

    def face(kind, i):
        last = SUB + rows - (1 if kind == 0 else 0)
        return own_face_ref[kind, i - SUB] if SUB <= i < last else face_ref[kind, i]

    spreads = [state_row(i)[pl.ds(levels, 1), :] for i in range(count)]
    depths = [state_row(i)[pl.ds(levels + 1, 1), :] for i in range(count)]
    for i in range(count - 1):
        if not SUB <= i < SUB + rows - 1:
            face_ref[0, i] = level_face(level, depths[i], depths[i + 1], spreads[i], spreads[i + 1])
        if i > 0 and not SUB <= i < SUB + rows:
            face_ref[1, i], face_ref[2, i] = side_faces(level, depths[i], spreads[i])

    def after(sweep):
        def get(i):
            if sweep == 0:
                return state_row(i)
            if SUB + sweep <= i < SUB + rows - sweep:
                return inner_ref.at[sweep - 1, i - SUB]
            return outer_ref.at[sweep - 1, i]

        return get

    for sweep in range(1, SUB + 1):
        for i in range(sweep, count - sweep):
            done = SUB + sweep <= i < SUB + rows - sweep
            if done and sweep < SUB:
                continue
            into = out_ref.at[i - SUB] if sweep == SUB else outer_ref.at[sweep - 1, i]
            for tracer in range(2):
                at = pl.ds(tracer * padded, padded)
                if done:
                    into[at, :] = inner_ref[sweep - 1, i - SUB, at, :]
                else:
                    faces = face(0, i), face(0, i - 1), face(1, i), face(2, i)
                    into[at, :] = mixed_row(after(sweep - 1), faces, i, at)


def hold_kernel(weight_hbm, observed_hbm, weight_ref, observed_ref, sems):
    copies = [
        pltpu.make_async_copy(weight_hbm, weight_ref, sems.at[0]),
        pltpu.make_async_copy(observed_hbm, observed_ref, sems.at[1]),
    ]
    for copy in copies:
        copy.start()
    for copy in copies:
        copy.wait()


def strip_kernel(levels, padded, edge_at, mine_ref, other_ref, _, out_ref):
    cols = mine_ref.shape[1]
    planes = 2 * padded
    edge_ref = mine_ref.at[pl.ds(edge_at, planes)]
    other_ref = other_ref.at[pl.ds(edge_at, planes)]
    lat = lax.axis_index("lat")
    lane = iota((1, cols), 1)
    place = lane % SLOT
    level = iota((padded, cols), 0).astype(F32)

    def left(value, by=1):
        return pltpu.roll(value, (cols - by) % cols, 1)

    def right(value, by=1):
        return pltpu.roll(value, by, 1)

    spread = edge_ref[pl.ds(levels, 1), :] + other_ref[pl.ds(levels, 1), :]
    depth = edge_ref[pl.ds(levels + 1, 1), :] + other_ref[pl.ds(levels + 1, 1), :]
    within = place < 2 * SUB - 1
    col_depth = jnp.minimum(depth, jnp.where(within, left(depth), 0.0))
    col_spread = 0.5 * (spread + left(spread))
    row_depth = jnp.minimum(depth, left(depth, SLOT))
    row_spread = 0.5 * (spread + left(spread, SLOT))

    def strip_face(limit, value):
        return jnp.where(level < limit, value, 0.0)

    to_left = strip_face(right(col_depth), right(col_spread))
    to_right = strip_face(col_depth, col_spread)
    to_above = strip_face(right(row_depth, SLOT), right(row_spread, SLOT))
    to_below = strip_face(row_depth, row_spread)
    out_of_low = place == jnp.where(lat == 0, SUB - 1, SLOT)
    out_of_high = place == jnp.where(lat == 0, SLOT, SUB)
    over_low = jnp.where(out_of_low, to_right, 0.0)
    over_high = jnp.where(out_of_high, to_left, 0.0)
    own_right = jnp.where(place == SUB - 1, 0.0, to_right)
    own_left = jnp.where(place == SUB, 0.0, to_left)

    def spread_out(value, east, west):
        before, after = right(value), left(value)
        above, below = right(value, SLOT), left(value, SLOT)
        total = value + east * (after - value) + west * (before - value)
        return total + to_below * (below - value) + to_above * (above - value)

    parts = []
    extras = [None, None]
    for tracer in range(2):
        at = pl.ds(tracer * padded, padded)
        parts.append(edge_ref[at, :] + other_ref[at, :])

    for sweep in range(1, SUB + 1):
        for tracer in range(2):
            part = parts[tracer]
            across = over_low * (left(part) - part) + over_high * (right(part) - part)
            extra = extras[tracer]
            if extra is not None:
                across = across + spread_out(extra, own_right, own_left)
            extras[tracer] = across
            if sweep < SUB:
                parts[tracer] = spread_out(part, to_right, to_left)

    for tracer in range(2):
        out_ref[pl.ds(tracer * padded, padded), :] = extras[tracer]


def fields_kernel(
    levels, padded, scale,
    rows_ref, main_ref, extra_ref, weight_ref, observed_ref, basis_ref, first_ref, fixed_ref,
    mixed_ref, fields_ref, part_ref,
):
    rows, _, cols = rows_ref.shape
    pairs = basis_ref.shape[2]
    lat = lax.axis_index("lat")
    lane = iota((1, cols), 1)
    place = lane % SLOT
    level = iota((padded, cols), 0).astype(F32)

    def left(value, by=1):
        return pltpu.roll(value, (cols - by) % cols, 1)

    def right(value, by=1):
        return pltpu.roll(value, by, 1)

    start = jnp.where(lat == 0, cols - SUB, 0)
    at_border = (lane >= start) & (lane < start + SUB)

    for row in range(rows):
        i = row + SUB
        at = pl.ds(row, levels, stride=rows)
        mixed = []
        for tracer in range(2):
            border = jnp.where(at_border, left(extra_ref[pl.ds(tracer * padded, padded), :], SLOT * i + SUB), 0.0)
            mixed.append((main_ref[row, pl.ds(tracer * padded, padded), :] + border)[:levels])
        wet = level[:levels] < rows_ref[row, pl.ds(levels + 1, 1), :]
        weight = weight_ref[at, :]
        misfit = []
        for tracer in range(2):
            mixed_ref[tracer, at, :] = mixed[tracer]
            misfit.append(weight * (mixed[tracer] - observed_ref[tracer, at, :]))
        here = pl.ds(row, 1)
        part_ref[0, here, :] = scale * jnp.sum(
            jnp.where(wet, mixed[0] - mixed[1], 0.0), axis=0, keepdims=True
        )
        part_ref[1, here, :] = jnp.sum(
            jnp.where(wet, misfit[1] - misfit[0], 0.0), axis=0, keepdims=True
        )
    sums = [None] * FUNCTIONALS

    def add(at, slot, row, factor):
        value = basis_ref[slot, row] * factor
        sums[at] = value if sums[at] is None else sums[at] + value

    for row in range(rows):
        here = pl.ds(row, 1)
        surface, base = part_ref[0, here, :], part_ref[1, here, :]
        fixed = lambda plane: rows_ref[row, pl.ds(levels + plane, 1), :]
        add(1, 0, row, fixed(4) * surface)
        for power in range(1, ITERS):
            add(1 + power, ITERS + power - 1, row, surface)
        for j in range(ITERS):
            add(1 + ITERS + j, j, row, base)
            at = 1 + 2 * ITERS + j * ITERS
            add(at, j, row, fixed(3) * surface)
            for power in range(1, ITERS):
                add(at + power, ITERS + (1 + j) * (ITERS - 1) + power - 1, row, surface)
    half = pairs // 2
    total = first_ref[...] + fixed_ref[3]
    for at in range(1, FUNCTIONALS):
        value = jnp.sum(sums[at], axis=1, keepdims=True)
        total = total + jnp.where(lane == at, value[:half], 0.0)
        total = total + jnp.where(lane == cols // 2 + at, value[half:], 0.0)
    part_ref[2] = total
    for field in range(3):
        part_ref[3 + field] = fixed_ref[field]
    for copy in range(fields_ref.shape[0]):
        fields_ref[copy] = part_ref[...]


def solve_kernel(
    levels, scale,
    mine_ref, other_ref, faces_ref, near_ref, base_ref, plan_ref, mixed_ref, depth_ref, step_ref,
    change_ref, state_ref, gradient_ref, direction_ref, kept_ref,
):
    loops, _, rows, cols = mine_ref.shape
    loop = lax.axis_index("loop")

    def total(value):
        parts = [
            value[i * rows : (i + 1) * rows, j * cols : (j + 1) * cols]
            for i in range(loops)
            for j in range(2)
        ]
        while len(parts) > 1:
            half = (len(parts) + 1) // 2
            parts = [a + b for a, b in zip(parts, parts[half:])] + parts[len(parts) - half : half]
        return jnp.sum(jnp.sum(parts[0], axis=1, keepdims=True), axis=0, keepdims=True)

    count = step_ref.shape[0]
    inner = mine_ref[0, 2] + other_ref[0, 2]
    for i in range(1, loops):
        inner = inner + (mine_ref[i, 2] + other_ref[i, 2])
    plan = plan_ref[...]
    shifted = pltpu.roll(inner, cols // 2, 1)
    linear = None
    for i in range(2 * count):
        source = inner if i < count else shifted
        part = plan[:, i : i + 1] * source[i % count : i % count + 1]
        linear = part if linear is None else linear + part
    gamma = plan[:1, 2 * count : 2 * count + 1]

    gained = [faces_ref[i] for i in range(4)]
    damping = faces_ref[4]

    def conjugate(rhs):
        residual = rhs
        search = rhs
        solution = jnp.zeros_like(rhs)
        norm_now = total(rhs * rhs)
        one = jnp.ones((1, 1), F32)
        residual_of = [one]
        search_of = [one]
        solution_of = []
        for sweep in range(ITERS):
            image = damping * search + surface_outflow(search, *gained)
            alpha = norm_now / total(search * image)
            solution = solution + alpha * search
            solution_of = add_up(solution_of, alpha, search_of)
            if sweep < ITERS - 1:
                residual = residual - alpha * image
                norm_next = total(residual * residual)
                beta = norm_next / norm_now
                search = residual + beta * search
                norm_now = norm_next
                image_of = [SHIFT * value for value in search_of]
                image_of = add_up(image_of, SPAN, [None] + search_of)
                residual_of = add_up(residual_of, -alpha, image_of)
                search_of = add_up(residual_of, beta, search_of)
        return solution, solution_of

    def add_up(terms, factor, others):
        result = list(terms) + [None] * (len(others) - len(terms))
        for at, value in enumerate(others):
            if value is not None:
                value = factor * value
                result[at] = value if result[at] is None else result[at] + value
        return result

    def near(slot, value):
        for i in range(loops):
            kept_ref[slot, i] = value[i * rows : (i + 1) * rows]
        return jnp.concatenate(
            [kept_ref[slot, lax.rem(loop + shift, loops)] for shift in (loops - 1, 0, 1)], axis=0
        )

    elevation, elevation_of = conjugate(gathered(mine_ref, other_ref, 0))
    pressure = gathered(mine_ref, other_ref, 1) + faces_ref[5] * elevation
    elevation = near(0, elevation)
    depth = depth_ref[...]
    here = elevation[rows : 2 * rows, :cols]
    for level in range(levels):
        at = pl.ds(level * rows, rows)
        change = jnp.where(level < depth, here, 0.0)
        state_ref[0, at, :] = mixed_ref[0, at, :] - change
        state_ref[1, at, :] = mixed_ref[1, at, :] + change
    response, response_of = conjugate(pressure)
    response = near(1, response)

    lane = iota((1, cols), 1)
    factor = jnp.where(lane == 0, 1.0, 0.0)
    for j in range(ITERS):
        factor = jnp.where(lane == 1 + j, -elevation_of[j], factor)
        part = scale * response_of[j]
        factor = jnp.where(lane == 1 + ITERS + j, part, factor)
        for k in range(ITERS):
            at = 1 + 2 * ITERS + j * ITERS + k
            factor = jnp.where(lane == at, part * elevation_of[k], factor)
    weights = jnp.sum(linear * factor, axis=1, keepdims=True)
    weights = [
        jnp.broadcast_to(weights[i : i + 1], (rows, cols)) for i in range(2 * count)
    ]

    sea = near_ref[5]
    carried = near_ref[4] * elevation - (scale * sea) * response
    faces = [near_ref[i] for i in range(4)]
    for sweep in range(SUB):
        carried = carried - surface_outflow(carried, *faces)
    carried = (sea * carried)[rows : 2 * rows, :cols]
    for tracer in range(2):
        at = pl.ds(tracer * rows, rows)
        gradient = base_ref[tracer] - carried if tracer == 0 else base_ref[tracer] + carried
        gradient_ref[tracer] = gradient
        value = gamma * gradient
        for i in range(count):
            value = value + weights[i] * step_ref[i, at, :]
            value = value + weights[count + i] * change_ref[i, at, :]
        direction_ref[tracer] = value


def on_device(
    state, observed, weight, control, depth_index, diffusivity, damping, history_step, history_change
):
    _, levels, rows, cols = state.shape
    count = history_step.shape[0]
    padded = round_up(levels + 6, 8)
    planes = 2 * padded
    loops = lax.axis_size("loop")
    lats = lax.axis_size("lat")
    blocks = loops * lats
    scale = levels ** (-0.5)
    flat = (2, levels * rows, cols)
    state = state.reshape(flat)
    observed = observed.reshape(flat)
    weight = weight.reshape(flat[1:])
    step = history_step.reshape(count, 2 * rows, cols)
    change = history_change.reshape(count, 2 * rows, cols)

    pairs = 2 * count
    inputs = (
        state, control, depth_index, diffusivity,
        history_step.reshape(-1, cols), history_change.reshape(-1, cols), damping, weight, observed,
    )
    held = [x.shape for x in inputs[:-1]] + [(2, rows, cols)]
    close, distant = hist_rows(pairs)
    sent_hist = (round_up(SUB * close + (REACH - SUB) * distant, 8) + FOLD, cols)
    sent = (round_up(SUB * state_rows(levels)[0], 8), cols)
    shapes = ((rows, planes, cols), (rows, pairs, cols), sent_hist, sent_hist, sent, sent)
    packed, hist, first_hist, second_hist, first, second = pl.pallas_call(
        functools.partial(pack_kernel, levels, padded),
        out_shape=[jax.ShapeDtypeStruct(shape, F32) for shape in shapes],
        in_specs=[pl.BlockSpec(memory_space=pltpu.HBM)] * len(inputs),
        out_specs=[VMEM] * len(shapes),
        scratch_shapes=[pltpu.VMEM(shape, x.dtype) for shape, x in zip(held, inputs)]
        + [pltpu.SemaphoreType.DMA((len(inputs),))],
        compiler_params=pltpu.CompilerParams(vmem_limit_bytes=VMEM_BYTES),
        name="pack",
    )(*(pltpu.with_memory_space_constraint(x, pltpu.HBM) for x in inputs))
    partner = [(i, i ^ 1) for i in range(loops)]
    following = [(i, (i - 1 + 2 * (i % 2)) % loops) for i in range(loops)]
    swap = [(0, 1), (1, 0)]
    first_hist = lax.ppermute(first_hist, "loop", partner)
    second_hist = lax.ppermute(second_hist, "loop", following)
    first = lax.ppermute(first, "loop", partner)
    second = lax.ppermute(second, "loop", following)
    edge, depth, fixed, own_face, inner = call(
        functools.partial(pairs_kernel, levels, padded),
        [
            (planes, cols), (rows, cols), (4, rows, cols), (3, rows, padded, cols),
            (SUB, rows, planes, cols),
        ],
        name="pairs",
    )(packed, step, change)
    height = loops * rows
    large = VMEM_BYTES if loops <= 16 else 2 * VMEM_BYTES
    fields = 8 * 3 * rows
    fields = 8 * 3 * rows
    edge_at = slot_groups(rows, cols) * pairs + 3 * rows
    border, border_mine = call(
        functools.partial(border_kernel, levels, padded),
        [((rows + 2 * REACH) * pairs + fields, cols), (max(SWAP_ROWS, edge_at + planes), cols)],
        name="border",
    )(edge, first_hist, second_hist, packed, hist)
    border_other = lax.ppermute(border_mine, "lat", swap)
    held_weight, held_observed = pl.pallas_call(
        hold_kernel,
        out_shape=[jax.ShapeDtypeStruct(x.shape, F32) for x in (weight, observed)],
        in_specs=[pl.BlockSpec(memory_space=pltpu.HBM)] * 2,
        out_specs=[VMEM] * 2,
        scratch_shapes=[pltpu.SemaphoreType.DMA((2,))],
        compiler_params=pltpu.CompilerParams(vmem_limit_bytes=VMEM_BYTES),
        name="hold",
    )(*(pltpu.with_memory_space_constraint(x, pltpu.HBM) for x in (weight, observed)))
    (extra,) = pl.pallas_call(
        functools.partial(strip_kernel, levels, padded, edge_at),
        out_shape=[jax.ShapeDtypeStruct((planes, cols), F32)],
        in_specs=[VMEM] * 2 + [pl.BlockSpec(memory_space=pl.ANY)],
        out_specs=[VMEM],
        compiler_params=pltpu.CompilerParams(vmem_limit_bytes=VMEM_BYTES),
        name="strip",
    )(border_mine, border_other, held_weight)
    fields_height = fields
    chains = 1 + ITERS
    buffers = SUB + ITERS + chains * (ITERS - 1)
    shapes = (
        (ITERS + chains * (ITERS - 1), rows, pairs, cols),
        (6, 3 * rows, 2 * cols),
        (2, rows, cols),
        (count, cols),
    )
    basis, around, base, near_start = pl.pallas_call(
        functools.partial(basis_kernel, rows, pairs),
        out_shape=[jax.ShapeDtypeStruct(shape, F32) for shape in shapes],
        in_specs=[VMEM] * 4,
        out_specs=[VMEM] * len(shapes),
        scratch_shapes=[pltpu.VMEM((rows + 2 * REACH, pairs, 2 * cols), F32)] * (buffers - 1)
        + [
            pltpu.VMEM((fields_height, cols), F32),
            pltpu.VMEM((rows + 2 * REACH, pairs, 2 * cols), F32),
        ],
        compiler_params=pltpu.CompilerParams(vmem_limit_bytes=VMEM_BYTES),
        name="basis",
    )(border, border_other, step, change)
    tall = rows + 2 * SUB
    (mixed,) = call(
        functools.partial(mix_kernel, levels, padded),
        [(rows, planes, cols)],
        scratch=[
            pltpu.VMEM((3, tall, padded, cols), F32),
            pltpu.VMEM((SUB - 1, tall, planes, cols), F32),
            pltpu.VMEM((2 * SUB, planes, cols), F32),
        ],
        name="mix",
    )(packed, first, second, own_face, inner, near_start)
    mixed, fields = call(
        functools.partial(fields_kernel, levels, padded, scale),
        [flat, (loops, 6, rows, cols)],
        scratch=[pltpu.VMEM((6, rows, cols), F32)],
        name="fields",
    )(packed, mixed, extra, held_weight, held_observed, basis, near_start, fixed)
    mine = lax.all_to_all(fields, "loop", 0, 0)
    theirs = lax.ppermute(mine, "lat", swap)
    faces, plan = call(
        plan_kernel, [(6, height, 2 * cols), (pairs, cols)], vmem=large, name="plan"
    )(mine, theirs)
    shapes = (flat, (2, rows, cols), (2, rows, cols))
    state_next, gradient, direction = call(
        functools.partial(solve_kernel, levels, scale),
        shapes,
        scratch=[pltpu.VMEM((2, loops, rows, 2 * cols), F32)],
        vmem=large,
        name="solve",
    )(mine, theirs, faces, around, base, plan, mixed, depth, step, change)
    return (state_next.reshape(2, levels, rows, cols), gradient, direction)


def solution(mesh):
    return jax.shard_map(
        on_device,
        mesh=mesh,
        in_specs=(
            P("members", None, "loop", "lat"),
            P("members", None, "loop", "lat"),
            P(None, "loop", "lat"),
            P("members", "loop", "lat"),
            P("loop", "lat"),
            P("loop", "lat"),
            P("loop", "lat"),
            P("members", None, "loop", "lat"),
            P("members", None, "loop", "lat"),
        ),
        out_specs=(
            P("members", None, "loop", "lat"),
            P("members", "loop", "lat"),
            P("members", "loop", "lat"),
        ),
        check_vma=False,
    )
```

```python
import functools

import jax
import jax.numpy as jnp
from jax import lax
from jax.experimental import pallas as pl
from jax.experimental.pallas import tpu as pltpu
from jax.sharding import PartitionSpec as P

ITERS = 3
SUB = 3
SURFACE_GAIN = 5.0
SLOT = 8
WIDE_SLOT = 16
FOLD = SLOT * SUB
SWAP_ROWS = 240
REACH = SUB + 2 * (ITERS - 1)
SHIFT = 5.0
SPAN = 5.0
FUNCTIONALS = 1 + ITERS + ITERS + ITERS * ITERS
GRID = ("loop", "lat")
VMEM = pl.BlockSpec(memory_space=pltpu.VMEM)
F32 = jnp.float32
VMEM_BYTES = 16 * 1024 * 1024


def round_up(value, to):
    return (value + to - 1) // to * to


def call(kernel, out_shapes, scratch=(), vmem=VMEM_BYTES, name=None):
    return pl.pallas_call(
        kernel,
        out_shape=[jax.ShapeDtypeStruct(shape, F32) for shape in out_shapes],
        out_specs=[VMEM] * len(out_shapes),
        scratch_shapes=list(scratch),
        compiler_params=pltpu.CompilerParams(vmem_limit_bytes=vmem),
        name=name,
    )


def iota(shape, dim):
    return lax.broadcasted_iota(jnp.int32, shape, dim)


def state_rows(levels):
    return 2 * levels + 2, levels + 2


def hist_rows(pairs):
    return pairs + 8, pairs + 3


def pack_kernel(levels, padded, *refs):
    sources, outs, targets, sems = refs[:9], refs[9:15], refs[15:22], refs[22]
    rows_ref, hist_ref = outs[:2]
    targets = targets[:4] + outs[4:6] + targets[4:]
    rows, cols = targets[2].shape
    copies = []
    for at, (source, target) in enumerate(zip(sources, targets)):
        if at == 8:
            source = source.at[:, pl.ds(0, rows), :]
        copies.append(pltpu.make_async_copy(source, target, sems.at[at]))
    for copy in copies:
        copy.start()
    for copy in copies[2:]:
        copy.wait()
    (
        state_ref, control_ref, depth_ref, spread_ref, step_ref, change_ref, damping_ref, weight_ref,
        observed_ref,
    ) = targets
    count = step_ref.shape[0] // (2 * rows)
    pairs = 2 * count
    close, distant = hist_rows(pairs)
    depth = depth_ref[...].astype(F32)
    spread = spread_ref[...]
    wet = depth > 0.5
    total = jnp.zeros((rows, cols), F32)
    for level in range(levels):
        total = total + jnp.where(level < depth, weight_ref[pl.ds(level * rows, rows), :], 0.0)
    fields = [
        damping_ref[...],
        2.0 * total,
        weight_ref[pl.ds(0, rows), :],
        observed_ref[0],
        observed_ref[1],
    ]
    for row in range(rows):
        here = slice(row, row + 1)
        for which, ref in enumerate((step_ref, change_ref)):
            both = [ref[pl.ds(tracer * rows + row, count, stride=2 * rows), :] for tracer in range(2)]
            apart = jnp.where(wet[here], both[0] - both[1], 0.0)
            hist_ref[row, pl.ds(which * count, count), :] = apart
    for copy in copies[:2]:
        copy.wait()
    first = iota((levels, cols), 0) == 0
    rest = jnp.zeros((padded - levels, cols), F32)
    for row in range(rows):
        here = slice(row, row + 1)
        for tracer in range(2):
            lift = jnp.where(wet[here], control_ref[tracer, here, :], 0.0)
            value = state_ref[tracer, pl.ds(row, levels, stride=rows), :]
            value = value + jnp.where(first, lift, 0.0)
            rows_ref[row, pl.ds(tracer * padded, levels), :] = value
            rows_ref[row, pl.ds(tracer * padded + levels, padded - levels), :] = rest
        for field, value in enumerate([spread, depth] + fields[:4]):
            rows_ref[row, pl.ds(levels + field, 1), :] = value[here]
        rows_ref[row, pl.ds(padded + levels, 1), :] = fields[4][here]

    even = lax.rem(lax.axis_index("loop"), 2) == 0

    def put(refs, at, upper, lower):
        here = pl.ds(at, upper.shape[0])
        refs[0][here, :] = jnp.where(even, upper, lower)
        refs[1][here, :] = jnp.where(even, lower, upper)

    masked = jnp.where(wet, spread, 0.0)
    for at in range(REACH):
        far = at < REACH - SUB
        index = at if far else at - (REACH - SUB)
        upper = rows - REACH + at if far else rows - SUB + index
        lower = SUB + index if far else index
        start = SUB * close + index * distant if far else index * close
        put(outs[2:4], start, hist_ref[upper], hist_ref[lower])
        start = start + pairs
        put(outs[2:4], start, masked[upper : upper + 1], masked[lower : lower + 1])
        for tracer in range(2):
            here = pl.ds(tracer * padded, 1)
            put(outs[2:4], start + 1 + tracer, rows_ref[upper, here, :], rows_ref[lower, here, :])
        if not far:
            here = pl.ds(levels + 2, 4)
            put(outs[2:4], start + 3, rows_ref[upper, here, :], rows_ref[lower, here, :])
            here = pl.ds(padded + levels, 1)
            put(outs[2:4], start + 7, rows_ref[upper, here, :], rows_ref[lower, here, :])
    last = SUB * close + (REACH - SUB) * distant
    folds = outs[2].shape[0] - FOLD
    if last < folds:
        rest = jnp.zeros((folds - last, cols), F32)
        put(outs[2:4], last, rest, rest)
    lat = lax.axis_index("lat")
    put(
        outs[2:4],
        folds,
        folded(edge_of(lambda i: rows_ref[rows - SUB + i], range(SUB), cols, lat)),
        folded(edge_of(lambda i: rows_ref[i], range(SUB), cols, lat)),
    )


def edge_of(rows_of, indices, cols, lat):
    lane = iota((1, cols), 1)
    slot = lane // SLOT
    place = lane % SLOT - SUB * lat
    mine = (place >= 0) & (place < SUB)
    total = None
    for index in indices:
        moved = pltpu.roll(rows_of(index), SLOT * index + SUB, 1)
        piece = jnp.where(mine & (slot == index), moved, 0.0)
        total = piece if total is None else total + piece
    return total


def folded(edge):
    planes, cols = edge.shape
    total = None
    for at, start in enumerate(range(0, planes, FOLD)):
        size = min(FOLD, planes - start)
        part = pltpu.roll(edge[start : start + size], FOLD * at, 1)
        if size < FOLD:
            part = jnp.concatenate([part, jnp.zeros((FOLD - size, cols), F32)], axis=0)
        total = part if total is None else total + part
    return total


def unfolded(fold, planes, lane_at):
    cols = fold.shape[1]
    lane = iota((1, cols), 1)
    here = (lane >= lane_at) & (lane < lane_at + FOLD)
    parts = []
    for at, start in enumerate(range(0, planes, FOLD)):
        part = pltpu.roll(fold, (lane_at - FOLD * at) % cols, 1)
        parts.append(jnp.where(here, part, 0.0)[: min(FOLD, planes - start)])
    return jnp.concatenate(parts, axis=0)


def level_face(levels, depth_here, depth_there, spread_here, spread_there):
    opened = levels < jnp.minimum(depth_here, depth_there)
    return jnp.where(opened, 0.5 * (spread_here + spread_there), 0.0)


def side_faces(level, depth, spread):
    cols = depth.shape[1]
    lane = iota((1, cols), 1)
    result = []
    for by, inside in ((cols - 1, lane < cols - 1), (1, lane > 0)):
        there = jnp.where(inside, pltpu.roll(depth, by, 1), 0.0)
        result.append(level_face(level, depth, there, spread, pltpu.roll(spread, by, 1)))
    return result


def mixed_row(get, faces, i, at):
    below, above, right, left = faces
    centre = get(i)[at, :]
    cols = centre.shape[1]
    total = centre + below * (get(i + 1)[at, :] - centre)
    total = total + above * (get(i - 1)[at, :] - centre)
    total = total + right * (pltpu.roll(centre, cols - 1, 1) - centre)
    return total + left * (pltpu.roll(centre, 1, 1) - centre)


def pairs_kernel(
    levels, padded, rows_ref, step_ref, change_ref,
    first_ref, second_ref, edge_ref, depth_ref, fixed_ref, face_ref, inner_ref,
):
    rows, _, cols = rows_ref.shape
    even = lax.rem(lax.axis_index("loop"), 2) == 0
    near, second = state_rows(levels)

    def put(at, upper, lower):
        here = pl.ds(at, upper.shape[0])
        first_ref[here, :] = jnp.where(even, upper, lower)
        second_ref[here, :] = jnp.where(even, lower, upper)

    for i in range(SUB):
        for start, size, place in ((0, levels + 2, 0), (padded, levels, second)):
            here = pl.ds(start, size)
            put(i * near + place, rows_ref[rows - SUB + i, here, :], rows_ref[i, here, :])
    if SUB * near < first_ref.shape[0]:
        rest = jnp.zeros((first_ref.shape[0] - SUB * near, cols), F32)
        put(SUB * near, rest, rest)
    level = iota((padded, cols), 0).astype(F32)
    spreads = [rows_ref[i, pl.ds(levels, 1), :] for i in range(rows)]
    depths = [rows_ref[i, pl.ds(levels + 1, 1), :] for i in range(rows)]
    for i in range(rows):
        if i + 1 < rows:
            face_ref[0, i] = level_face(level, depths[i], depths[i + 1], spreads[i], spreads[i + 1])
        face_ref[1, i], face_ref[2, i] = side_faces(level, depths[i], spreads[i])
    face_ref[0, rows - 1] = jnp.zeros((padded, cols), F32)
    for sweep in range(SUB):
        source = rows_ref if sweep == 0 else inner_ref.at[sweep - 1]
        for i in range(rows):
            for tracer in range(2):
                at = pl.ds(tracer * padded, padded)
                if sweep < i < rows - 1 - sweep:
                    faces = face_ref[0, i], face_ref[0, i - 1], face_ref[1, i], face_ref[2, i]
                    inner_ref[sweep, i, at, :] = mixed_row(lambda j: source.at[j], faces, i, at)
                else:
                    inner_ref[sweep, i, at, :] = jnp.zeros((padded, cols), F32)
    lat = lax.axis_index("lat")
    count = step_ref.shape[0]
    lane = iota((1, cols), 1)
    gram = [jnp.zeros((1, cols), F32) for _ in range(count)]
    at = FUNCTIONALS
    for left_ref in (step_ref, change_ref):
        for i in range(count):
            for j in range(i, count):
                value = jnp.sum(left_ref[i] * change_ref[j], axis=(0, 1), keepdims=True)
                gram[i] = gram[i] + jnp.where(lane == at + j, value, 0.0)
                if i != j:
                    gram[j] = gram[j] + jnp.where(lane == at + i, value, 0.0)
        at += count
    for i in range(count):
        fixed_ref[3, pl.ds(i, 1), :] = gram[i]
    for row in range(rows):
        plane = lambda at: rows_ref[row, pl.ds(levels + at, 1), :]
        here = pl.ds(row, 1)
        depth_ref[here, :] = plane(1)
        fixed_ref[0, here, :] = jnp.where(plane(1) > 0.5, plane(0), 0.0)
        fixed_ref[1, here, :] = plane(2)
        fixed_ref[2, here, :] = plane(3)
    edge_ref[...] = edge_of(lambda i: rows_ref[i - SUB], range(SUB, rows + SUB), cols, lat)


def faces_between(here, there, opened=True):
    return jnp.where((here > 0.0) & (there > 0.0) & opened, 0.5 * (here + there), 0.0)


def closed_lane(cols):
    return jnp.where(lax.axis_index("lat") == 0, 2 * cols - 1, cols - 1)


def surface_faces(spread, closed):
    height, width = spread.shape
    below = faces_between(spread, pltpu.roll(spread, height - 1, 0))
    right = faces_between(
        spread, pltpu.roll(spread, width - 1, 1), iota(spread.shape, 1) != closed
    )
    return below, pltpu.roll(below, 1, 0), right, pltpu.roll(right, 1, 1)


def gathered(mine_ref, other_ref, field):
    return jnp.concatenate(
        [
            jnp.concatenate([mine_ref[i, field], other_ref[i, field]], axis=1)
            for i in range(mine_ref.shape[0])
        ],
        axis=0,
    )


def surface_outflow(value, to_below, to_above, to_right, to_left):
    height, width = value.shape
    result = to_right * (value - pltpu.roll(value, width - 1, 1))
    result = result + to_left * (value - pltpu.roll(value, 1, 1))
    result = result + to_below * (value - pltpu.roll(value, height - 1, 0))
    return result + to_above * (value - pltpu.roll(value, 1, 0))


def plan_kernel(mine_ref, other_ref, faces_ref, plan_ref):
    loops, _, rows, cols = mine_ref.shape
    closed = closed_lane(cols)
    for at, face in enumerate(surface_faces(gathered(mine_ref, other_ref, 3), closed)):
        faces_ref[at] = SURFACE_GAIN * face
    for field in (4, 5):
        faces_ref[field] = gathered(mine_ref, other_ref, field)
    count = plan_ref.shape[0] // 2
    gram = mine_ref[0, 2] + other_ref[0, 2]
    for i in range(1, loops):
        gram = gram + (mine_ref[i, 2] + other_ref[i, 2])
    wide = (count, cols)
    tables = [
        jnp.broadcast_to(gram[:, i : i + 1], wide)
        for i in range(FUNCTIONALS, FUNCTIONALS + 2 * count)
    ]
    step_change, change_change = tables[:count], tables[count:]
    last = count - 1
    gamma = step_change[last][last:] / change_change[last][last:]
    rho = [1.0 / step_change[i][i : i + 1] for i in range(count)]
    row = iota(wide, 0)
    lane = iota(wide, 1)
    step_grad = jnp.where(lane == row, 1.0, 0.0)
    change_grad = jnp.where(lane == row + count, 1.0, 0.0)
    factors = [None] * count
    for i in range(count - 1, -1, -1):
        factors[i] = rho[i] * step_grad[i : i + 1]
        step_grad = step_grad - factors[i] * step_change[i]
        change_grad = change_grad - factors[i] * change_change[i]
    change_grad = gamma * change_grad
    for i in range(count):
        weight = factors[i] - rho[i] * change_grad[i : i + 1]
        change_grad = change_grad + weight * step_change[i]
        plan_ref[pl.ds(i, 1), :] = -weight
        plan_ref[pl.ds(count + i, 1), :] = gamma * factors[i]
    at = lane[:1] == 2 * count
    plan_ref[pl.ds(0, 1), :] = jnp.where(at, -gamma, plan_ref[pl.ds(0, 1), :])


def received(first_ref, second_ref):
    even = lax.rem(lax.axis_index("loop"), 2) == 0

    def low(at, size):
        here = pl.ds(at, size)
        return jnp.where(even, second_ref[here, :], first_ref[here, :])

    def high(at, size):
        here = pl.ds(at, size)
        return jnp.where(even, first_ref[here, :], second_ref[here, :])

    return low, high


def border_kernel(
    levels, padded, edge_ref, first_ref, second_ref, rows_ref, hist_ref, out_ref, swap_ref
):
    rows, pairs, cols = hist_ref.shape
    close, distant = hist_rows(pairs)
    low, high = received(first_ref, second_ref)
    tall = 3 * rows
    fields = (rows + 2 * REACH) * pairs
    out_ref[pl.ds(fields, 8 * tall), :] = jnp.zeros((8 * tall, cols), F32)
    lane = iota((1, cols), 1)
    place = lane % WIDE_SLOT - REACH * lax.axis_index("lat")
    sent = (place >= 0) & (place < REACH)
    slots = cols // WIDE_SLOT
    groups = [None] * slot_groups(rows, cols)
    for at in range(-REACH, rows + REACH):
        get = low if at < 0 else high
        if 0 <= at < rows:
            own = rows_ref.at[at]
            get = lambda place, size: own[pl.ds(place, size), :]
            apart = hist_ref[at]
            places = {0: levels, 6: 0, 7: padded, 5: padded + levels}
            places.update({1 + field: levels + 2 + field for field in range(4)})
        elif -SUB <= at < rows + SUB:
            start = (at + SUB if at < 0 else at - rows) * close
            apart = get(start, pairs)
            start = start + pairs
            places = {0: start, 6: start + 1, 7: start + 2}
            places.update({1 + field: start + 3 + field for field in range(5)})
        else:
            start = SUB * close + (at + REACH if at < 0 else at - rows - SUB) * distant
            apart = get(start, pairs)
            start = start + pairs
            places = {0: start, 6: start + 1, 7: start + 2}
        out_ref[pl.ds((at + REACH) * pairs, pairs), :] = apart
        group, slot = divmod(at + REACH, slots)
        moved = pltpu.roll(apart, WIDE_SLOT * slot + REACH, 1)
        moved = jnp.where(sent & (lane // WIDE_SLOT == slot), moved, 0.0)
        groups[group] = moved if groups[group] is None else groups[group] + moved
        for field, place in places.items():
            value = get(place, 1)
            if field == 0 and 0 <= at < rows:
                value = jnp.where(get(levels + 1, 1) > 0.5, value, 0.0)
            out_ref[pl.ds(fields + field * tall + at + rows, 1), :] = value
    for at, group in enumerate(groups):
        swap_ref[pl.ds(at * pairs, pairs), :] = group
    total = None
    for field in range(8):
        moved = pltpu.roll(
            out_ref[pl.ds(fields + field * tall, tall), :], WIDE_SLOT * field + REACH, 1
        )
        moved = jnp.where(sent & (lane // WIDE_SLOT == field), moved, 0.0)
        total = moved if total is None else total + moved
    at = len(groups) * pairs
    swap_ref[pl.ds(at, tall), :] = total
    at = at + tall
    planes = edge_ref.shape[0]
    folds = first_ref.shape[0] - FOLD
    before = unfolded(low(folds, FOLD), planes, 0)
    after = unfolded(high(folds, FOLD), planes, SLOT * (rows + SUB))
    swap_ref[pl.ds(at, planes), :] = edge_ref[...] + (before + after)
    at = at + planes
    if at < swap_ref.shape[0]:
        swap_ref[pl.ds(at, swap_ref.shape[0] - at), :] = jnp.zeros(
            (swap_ref.shape[0] - at, cols), F32
        )


def slot_groups(rows, cols):
    slots = cols // WIDE_SLOT
    return (rows + 2 * REACH + slots - 1) // slots


def basis_kernel(
    rows, pairs, mine_ref, other_ref, step_ref, change_ref,
    out_ref, near_ref, base_ref, first_ref, *work
):
    cols = mine_ref.shape[1]
    width = 2 * cols
    tall = rows + 2 * REACH
    ahead = REACH - SUB
    high = 3 * rows
    fields = tall * pairs
    closed = closed_lane(cols)
    opened = iota((1, width), 1) != closed
    slots = cols // WIDE_SLOT
    other_fields = slot_groups(rows, cols) * pairs
    beside_ref = work[-2]
    lane = iota((1, cols), 1)
    start = jnp.where(lax.axis_index("lat") == 0, 0, cols - REACH)
    at_border = (lane >= start) & (lane < start + REACH)

    packed = other_ref[pl.ds(other_fields, high), :]
    for at in range(8):
        there = pltpu.roll(packed, (cols - WIDE_SLOT * at - REACH) % cols, 1)
        beside_ref[pl.ds(at * high, high), :] = jnp.where(at_border, there, 0.0)

    def wide(at, size):
        there = pl.ds(at - fields, size)
        return jnp.concatenate([mine_ref[pl.ds(at, size), :], beside_ref[there, :]], axis=1)

    def left(value):
        return pltpu.roll(value, width - 1, 1)

    def right(value):
        return pltpu.roll(value, 1, 1)

    def field(at):
        return wide(fields + at * high, high)

    def field_row(at, i):
        return wide(fields + at * high + i - REACH + rows, 1)

    faces = surface_faces(field(0), closed)
    for at in range(4):
        near_ref[at] = faces[at]
    sea = jnp.where(field(0) > 0.0, 1.0, 0.0)
    weight = field(3)
    near_ref[4] = weight * sea
    near_ref[5] = sea
    value = [field(6), field(7)]
    for sweep in range(SUB):
        value = [part - surface_outflow(part, *faces) for part in value]
    value = [weight * (value[0] - field(4)), weight * (value[1] - field(5))]
    for sweep in range(SUB):
        value = [part - surface_outflow(part, *faces) for part in value]
    base = [(part * sea)[rows : 2 * rows, :cols] for part in value]
    for tracer in range(2):
        base_ref[tracer] = base[tracer]
    for i in range(pairs // 2):
        total = jnp.zeros((1, cols), F32)
        for at, ref in ((0, step_ref), (cols // 2, change_ref)):
            part = ref[i, pl.ds(0, rows), :] * base[0] + ref[i, pl.ds(rows, rows), :] * base[1]
            part = jnp.sum(part, axis=(0, 1), keepdims=True)
            total = total + jnp.where(lane == at, part, 0.0)
        first_ref[pl.ds(i, 1), :] = total

    spread = [field_row(0, i) for i in range(tall)]
    to_right = [faces_between(value, left(value), opened) for value in spread]
    to_left = [right(value) for value in to_right]
    to_below = [faces_between(spread[i], spread[i + 1]) for i in range(tall - 1)]
    inner = range(ahead, tall - ahead)
    damping = {i: (field_row(1, i) - SHIFT) * (1.0 / SPAN) for i in inner}
    response_weight = {i: field_row(2, i) for i in inner}
    weight = {i: field_row(3, i) for i in inner}
    gain = SURFACE_GAIN / SPAN

    def outflow(get, i):
        value = get(i)
        total = to_right[i] * (value - left(value)) + to_left[i] * (value - right(value))
        total = total + to_below[i] * (value - get(i + 1))
        return value, total + to_below[i - 1] * (value - get(i - 1))

    def mixed(get, ref, reach):
        for i in range(REACH - reach, REACH + rows + reach):
            value, out = outflow(get, i)
            ref[i] = value - out
        return lambda i: ref[i]

    def applied(get, ref, reach):
        for i in range(REACH - reach, REACH + rows + reach):
            value, out = outflow(get, i)
            ref[i] = damping[i] * value + gain * out
        return lambda i: ref[i]

    def keep(slot, get):
        for i in range(rows):
            out_ref[slot, i] = get(i + REACH)[:, :cols]

    for i in range(tall):
        group, slot = divmod(i, slots)
        there = other_ref[pl.ds(group * pairs, pairs), :]
        there = pltpu.roll(there, (cols - WIDE_SLOT * slot - REACH) % cols, 1)
        work[-1][i, :, :cols] = mine_ref[pl.ds(i * pairs, pairs), :]
        work[-1][i, :, cols:] = jnp.where(at_border, there, 0.0)
    get = lambda i: work[-1][i]
    for sweep in range(SUB):
        get = mixed(get, work[sweep], REACH - 1 - sweep)
    reach = REACH - SUB
    powers = [get]
    for power in range(1, ITERS):
        powers.append(applied(powers[-1], work[SUB + power - 1], reach - power))
    for power in range(ITERS):
        keep(power, powers[power])
    reach = ITERS - 1
    slot = ITERS
    at = SUB + ITERS - 1
    chains = []
    for factor, power in [(weight, 0)] + [(response_weight, power) for power in range(ITERS)]:
        get = powers[power]
        chains.append(lambda i, factor=factor, get=get: factor[i] * get(i))
    for power in range(1, ITERS):
        for index in range(len(chains)):
            chains[index] = applied(chains[index], work[at], reach - power)
            at += 1
            keep(slot + index * (ITERS - 1) + power - 1, chains[index])


def mix_kernel(
    levels, padded, rows_ref, first_ref, second_ref, own_face_ref, inner_ref, _,
    out_ref, face_ref, outer_ref, halo_ref
):
    rows, _, cols = rows_ref.shape
    count = rows + 2 * SUB
    near, second = state_rows(levels)
    rest = jnp.zeros((padded - levels, cols), F32)
    low, high = received(first_ref, second_ref)
    for i in range(2 * SUB):
        get = low if i < SUB else high
        at = i % SUB * near
        halo_ref[i, pl.ds(levels, padded - levels), :] = rest
        halo_ref[i, pl.ds(padded + levels, padded - levels), :] = rest
        halo_ref[i, pl.ds(0, levels + 2), :] = get(at, levels + 2)
        halo_ref[i, pl.ds(padded, levels), :] = get(at + second, levels)
    level = iota((padded, cols), 0).astype(F32)

    def state_row(i):
        if i < SUB:
            return halo_ref.at[i]
        return rows_ref.at[i - SUB] if i < SUB + rows else halo_ref.at[i - rows]

    def face(kind, i):
        last = SUB + rows - (1 if kind == 0 else 0)
        return own_face_ref[kind, i - SUB] if SUB <= i < last else face_ref[kind, i]

    spreads = [state_row(i)[pl.ds(levels, 1), :] for i in range(count)]
    depths = [state_row(i)[pl.ds(levels + 1, 1), :] for i in range(count)]
    for i in range(count - 1):
        if not SUB <= i < SUB + rows - 1:
            face_ref[0, i] = level_face(level, depths[i], depths[i + 1], spreads[i], spreads[i + 1])
        if i > 0 and not SUB <= i < SUB + rows:
            face_ref[1, i], face_ref[2, i] = side_faces(level, depths[i], spreads[i])

    def after(sweep):
        def get(i):
            if sweep == 0:
                return state_row(i)
            if SUB + sweep <= i < SUB + rows - sweep:
                return inner_ref.at[sweep - 1, i - SUB]
            return outer_ref.at[sweep - 1, i]

        return get

    for sweep in range(1, SUB + 1):
        for i in range(sweep, count - sweep):
            done = SUB + sweep <= i < SUB + rows - sweep
            if done and sweep < SUB:
                continue
            into = out_ref.at[i - SUB] if sweep == SUB else outer_ref.at[sweep - 1, i]
            for tracer in range(2):
                at = pl.ds(tracer * padded, padded)
                if done:
                    into[at, :] = inner_ref[sweep - 1, i - SUB, at, :]
                else:
                    faces = face(0, i), face(0, i - 1), face(1, i), face(2, i)
                    into[at, :] = mixed_row(after(sweep - 1), faces, i, at)


def hold_kernel(weight_hbm, observed_hbm, weight_ref, observed_ref, sems):
    copies = [
        pltpu.make_async_copy(weight_hbm, weight_ref, sems.at[0]),
        pltpu.make_async_copy(observed_hbm, observed_ref, sems.at[1]),
    ]
    for copy in copies:
        copy.start()
    for copy in copies:
        copy.wait()


def strip_kernel(levels, padded, edge_at, mine_ref, other_ref, _, out_ref):
    cols = mine_ref.shape[1]
    planes = 2 * padded
    edge_ref = mine_ref.at[pl.ds(edge_at, planes)]
    other_ref = other_ref.at[pl.ds(edge_at, planes)]
    lat = lax.axis_index("lat")
    lane = iota((1, cols), 1)
    place = lane % SLOT
    level = iota((padded, cols), 0).astype(F32)

    def left(value, by=1):
        return pltpu.roll(value, (cols - by) % cols, 1)

    def right(value, by=1):
        return pltpu.roll(value, by, 1)

    spread = edge_ref[pl.ds(levels, 1), :] + other_ref[pl.ds(levels, 1), :]
    depth = edge_ref[pl.ds(levels + 1, 1), :] + other_ref[pl.ds(levels + 1, 1), :]
    within = place < 2 * SUB - 1
    col_depth = jnp.minimum(depth, jnp.where(within, left(depth), 0.0))
    col_spread = 0.5 * (spread + left(spread))
    row_depth = jnp.minimum(depth, left(depth, SLOT))
    row_spread = 0.5 * (spread + left(spread, SLOT))

    def strip_face(limit, value):
        return jnp.where(level < limit, value, 0.0)

    to_left = strip_face(right(col_depth), right(col_spread))
    to_right = strip_face(col_depth, col_spread)
    to_above = strip_face(right(row_depth, SLOT), right(row_spread, SLOT))
    to_below = strip_face(row_depth, row_spread)
    out_of_low = place == jnp.where(lat == 0, SUB - 1, SLOT)
    out_of_high = place == jnp.where(lat == 0, SLOT, SUB)
    over_low = jnp.where(out_of_low, to_right, 0.0)
    over_high = jnp.where(out_of_high, to_left, 0.0)
    own_right = jnp.where(place == SUB - 1, 0.0, to_right)
    own_left = jnp.where(place == SUB, 0.0, to_left)

    def spread_out(value, east, west):
        before, after = right(value), left(value)
        above, below = right(value, SLOT), left(value, SLOT)
        total = value + east * (after - value) + west * (before - value)
        return total + to_below * (below - value) + to_above * (above - value)

    parts = []
    extras = [None, None]
    for tracer in range(2):
        at = pl.ds(tracer * padded, padded)
        parts.append(edge_ref[at, :] + other_ref[at, :])

    for sweep in range(1, SUB + 1):
        for tracer in range(2):
            part = parts[tracer]
            across = over_low * (left(part) - part) + over_high * (right(part) - part)
            extra = extras[tracer]
            if extra is not None:
                across = across + spread_out(extra, own_right, own_left)
            extras[tracer] = across
            if sweep < SUB:
                parts[tracer] = spread_out(part, to_right, to_left)

    for tracer in range(2):
        out_ref[pl.ds(tracer * padded, padded), :] = extras[tracer]


def fields_kernel(
    levels, padded, scale,
    rows_ref, main_ref, extra_ref, weight_ref, observed_ref, basis_ref, first_ref, fixed_ref,
    mixed_ref, fields_ref, part_ref,
):
    rows, _, cols = rows_ref.shape
    pairs = basis_ref.shape[2]
    lat = lax.axis_index("lat")
    lane = iota((1, cols), 1)
    place = lane % SLOT
    level = iota((padded, cols), 0).astype(F32)

    def left(value, by=1):
        return pltpu.roll(value, (cols - by) % cols, 1)

    def right(value, by=1):
        return pltpu.roll(value, by, 1)

    start = jnp.where(lat == 0, cols - SUB, 0)
    at_border = (lane >= start) & (lane < start + SUB)

    for row in range(rows):
        i = row + SUB
        at = pl.ds(row, levels, stride=rows)
        mixed = []
        for tracer in range(2):
            border = jnp.where(at_border, left(extra_ref[pl.ds(tracer * padded, padded), :], SLOT * i + SUB), 0.0)
            mixed.append((main_ref[row, pl.ds(tracer * padded, padded), :] + border)[:levels])
        wet = level[:levels] < rows_ref[row, pl.ds(levels + 1, 1), :]
        weight = weight_ref[at, :]
        misfit = []
        for tracer in range(2):
            mixed_ref[tracer, at, :] = mixed[tracer]
            misfit.append(weight * (mixed[tracer] - observed_ref[tracer, at, :]))
        here = pl.ds(row, 1)
        part_ref[0, here, :] = scale * jnp.sum(
            jnp.where(wet, mixed[0] - mixed[1], 0.0), axis=0, keepdims=True
        )
        part_ref[1, here, :] = jnp.sum(
            jnp.where(wet, misfit[1] - misfit[0], 0.0), axis=0, keepdims=True
        )
    sums = [None] * FUNCTIONALS

    def add(at, slot, row, factor):
        value = basis_ref[slot, row] * factor
        sums[at] = value if sums[at] is None else sums[at] + value

    for row in range(rows):
        here = pl.ds(row, 1)
        surface, base = part_ref[0, here, :], part_ref[1, here, :]
        fixed = lambda plane: rows_ref[row, pl.ds(levels + plane, 1), :]
        add(1, 0, row, fixed(4) * surface)
        for power in range(1, ITERS):
            add(1 + power, ITERS + power - 1, row, surface)
        for j in range(ITERS):
            add(1 + ITERS + j, j, row, base)
            at = 1 + 2 * ITERS + j * ITERS
            add(at, j, row, fixed(3) * surface)
            for power in range(1, ITERS):
                add(at + power, ITERS + (1 + j) * (ITERS - 1) + power - 1, row, surface)
    half = pairs // 2
    total = first_ref[...] + fixed_ref[3]
    for at in range(1, FUNCTIONALS):
        value = jnp.sum(sums[at], axis=1, keepdims=True)
        total = total + jnp.where(lane == at, value[:half], 0.0)
        total = total + jnp.where(lane == cols // 2 + at, value[half:], 0.0)
    part_ref[2] = total
    for field in range(3):
        part_ref[3 + field] = fixed_ref[field]
    for copy in range(fields_ref.shape[0]):
        fields_ref[copy] = part_ref[...]


def solve_kernel(
    levels, scale,
    mine_ref, other_ref, faces_ref, near_ref, base_ref, plan_ref, mixed_ref, depth_ref, step_ref,
    change_ref, state_ref, gradient_ref, direction_ref, kept_ref,
):
    loops, _, rows, cols = mine_ref.shape
    loop = lax.axis_index("loop")

    def total(value):
        parts = [
            value[i * rows : (i + 1) * rows, j * cols : (j + 1) * cols]
            for i in range(loops)
            for j in range(2)
        ]
        while len(parts) > 1:
            half = (len(parts) + 1) // 2
            parts = [a + b for a, b in zip(parts, parts[half:])] + parts[len(parts) - half : half]
        return jnp.sum(jnp.sum(parts[0], axis=1, keepdims=True), axis=0, keepdims=True)

    count = step_ref.shape[0]
    inner = mine_ref[0, 2] + other_ref[0, 2]
    for i in range(1, loops):
        inner = inner + (mine_ref[i, 2] + other_ref[i, 2])
    plan = plan_ref[...]
    shifted = pltpu.roll(inner, cols // 2, 1)
    linear = None
    for i in range(2 * count):
        source = inner if i < count else shifted
        part = plan[:, i : i + 1] * source[i % count : i % count + 1]
        linear = part if linear is None else linear + part
    gamma = plan[:1, 2 * count : 2 * count + 1]

    gained = [faces_ref[i] for i in range(4)]
    damping = faces_ref[4]

    def conjugate(rhs):
        residual = rhs
        search = rhs
        solution = jnp.zeros_like(rhs)
        norm_now = total(rhs * rhs)
        one = jnp.ones((1, 1), F32)
        residual_of = [one]
        search_of = [one]
        solution_of = []
        for sweep in range(ITERS):
            image = damping * search + surface_outflow(search, *gained)
            alpha = norm_now / total(search * image)
            solution = solution + alpha * search
            solution_of = add_up(solution_of, alpha, search_of)
            if sweep < ITERS - 1:
                residual = residual - alpha * image
                norm_next = total(residual * residual)
                beta = norm_next / norm_now
                search = residual + beta * search
                norm_now = norm_next
                image_of = [SHIFT * value for value in search_of]
                image_of = add_up(image_of, SPAN, [None] + search_of)
                residual_of = add_up(residual_of, -alpha, image_of)
                search_of = add_up(residual_of, beta, search_of)
        return solution, solution_of

    def add_up(terms, factor, others):
        result = list(terms) + [None] * (len(others) - len(terms))
        for at, value in enumerate(others):
            if value is not None:
                value = factor * value
                result[at] = value if result[at] is None else result[at] + value
        return result

    def near(slot, value):
        for i in range(loops):
            kept_ref[slot, i] = value[i * rows : (i + 1) * rows]
        return jnp.concatenate(
            [kept_ref[slot, lax.rem(loop + shift, loops)] for shift in (loops - 1, 0, 1)], axis=0
        )

    elevation, elevation_of = conjugate(gathered(mine_ref, other_ref, 0))
    pressure = gathered(mine_ref, other_ref, 1) + faces_ref[5] * elevation
    elevation = near(0, elevation)
    depth = depth_ref[...]
    here = elevation[rows : 2 * rows, :cols]
    for level in range(levels):
        at = pl.ds(level * rows, rows)
        change = jnp.where(level < depth, here, 0.0)
        state_ref[0, at, :] = mixed_ref[0, at, :] - change
        state_ref[1, at, :] = mixed_ref[1, at, :] + change
    response, response_of = conjugate(pressure)
    response = near(1, response)

    lane = iota((1, cols), 1)
    factor = jnp.where(lane == 0, 1.0, 0.0)
    for j in range(ITERS):
        factor = jnp.where(lane == 1 + j, -elevation_of[j], factor)
        part = scale * response_of[j]
        factor = jnp.where(lane == 1 + ITERS + j, part, factor)
        for k in range(ITERS):
            at = 1 + 2 * ITERS + j * ITERS + k
            factor = jnp.where(lane == at, part * elevation_of[k], factor)
    weights = jnp.sum(linear * factor, axis=1, keepdims=True)
    weights = [
        jnp.broadcast_to(weights[i : i + 1], (rows, cols)) for i in range(2 * count)
    ]

    sea = near_ref[5]
    carried = near_ref[4] * elevation - (scale * sea) * response
    faces = [near_ref[i] for i in range(4)]
    for sweep in range(SUB):
        carried = carried - surface_outflow(carried, *faces)
    carried = (sea * carried)[rows : 2 * rows, :cols]
    for tracer in range(2):
        at = pl.ds(tracer * rows, rows)
        gradient = base_ref[tracer] - carried if tracer == 0 else base_ref[tracer] + carried
        gradient_ref[tracer] = gradient
        value = gamma * gradient
        for i in range(count):
            value = value + weights[i] * step_ref[i, at, :]
            value = value + weights[count + i] * change_ref[i, at, :]
        direction_ref[tracer] = value


def on_device(
    state, observed, weight, control, depth_index, diffusivity, damping, history_step, history_change
):
    _, levels, rows, cols = state.shape
    count = history_step.shape[0]
    padded = round_up(levels + 6, 8)
    planes = 2 * padded
    loops = lax.axis_size("loop")
    lats = lax.axis_size("lat")
    blocks = loops * lats
    scale = levels ** (-0.5)
    flat = (2, levels * rows, cols)
    state = state.reshape(flat)
    observed = observed.reshape(flat)
    weight = weight.reshape(flat[1:])

    pairs = 2 * count
    inputs = (
        state, control, depth_index, diffusivity,
        history_step.reshape(-1, cols), history_change.reshape(-1, cols), damping, weight, observed,
    )
    held = [x.shape for x in inputs[:-1]] + [(2, rows, cols)]
    close, distant = hist_rows(pairs)
    sent_hist = (round_up(SUB * close + (REACH - SUB) * distant, 8) + FOLD, cols)
    sent = (round_up(SUB * state_rows(levels)[0], 8), cols)
    stored = (2 * count * rows, cols)
    shapes = ((rows, planes, cols), (rows, pairs, cols), sent_hist, sent_hist, stored, stored)
    packed, hist, first_hist, second_hist, step, change = pl.pallas_call(
        functools.partial(pack_kernel, levels, padded),
        out_shape=[jax.ShapeDtypeStruct(shape, F32) for shape in shapes],
        in_specs=[pl.BlockSpec(memory_space=pltpu.HBM)] * len(inputs),
        out_specs=[VMEM] * len(shapes),
        scratch_shapes=[
            pltpu.VMEM(shape, x.dtype) for at, (shape, x) in enumerate(zip(held, inputs)) if at not in (4, 5)
        ]
        + [pltpu.SemaphoreType.DMA((len(inputs),))],
        compiler_params=pltpu.CompilerParams(vmem_limit_bytes=VMEM_BYTES),
        name="pack",
    )(*(pltpu.with_memory_space_constraint(x, pltpu.HBM) for x in inputs))
    partner = [(i, i ^ 1) for i in range(loops)]
    following = [(i, (i - 1 + 2 * (i % 2)) % loops) for i in range(loops)]
    swap = [(0, 1), (1, 0)]
    first_hist = lax.ppermute(first_hist, "loop", partner)
    step = step.reshape(count, 2 * rows, cols)
    change = change.reshape(count, 2 * rows, cols)
    second_hist = lax.ppermute(second_hist, "loop", following)
    first, second, edge, depth, fixed, own_face, inner = call(
        functools.partial(pairs_kernel, levels, padded),
        [
            sent, sent, (planes, cols), (rows, cols), (4, rows, cols), (3, rows, padded, cols),
            (SUB, rows, planes, cols),
        ],
        name="pairs",
    )(packed, step, change)
    first = lax.ppermute(first, "loop", partner)
    second = lax.ppermute(second, "loop", following)
    height = loops * rows
    large = VMEM_BYTES if loops <= 16 else 2 * VMEM_BYTES
    fields = 8 * 3 * rows
    fields = 8 * 3 * rows
    edge_at = slot_groups(rows, cols) * pairs + 3 * rows
    border, border_mine = call(
        functools.partial(border_kernel, levels, padded),
        [((rows + 2 * REACH) * pairs + fields, cols), (max(SWAP_ROWS, edge_at + planes), cols)],
        name="border",
    )(edge, first_hist, second_hist, packed, hist)
    border_other = lax.ppermute(border_mine, "lat", swap)
    held_weight, held_observed = pl.pallas_call(
        hold_kernel,
        out_shape=[jax.ShapeDtypeStruct(x.shape, F32) for x in (weight, observed)],
        in_specs=[pl.BlockSpec(memory_space=pltpu.HBM)] * 2,
        out_specs=[VMEM] * 2,
        scratch_shapes=[pltpu.SemaphoreType.DMA((2,))],
        compiler_params=pltpu.CompilerParams(vmem_limit_bytes=VMEM_BYTES),
        name="hold",
    )(*(pltpu.with_memory_space_constraint(x, pltpu.HBM) for x in (weight, observed)))
    (extra,) = pl.pallas_call(
        functools.partial(strip_kernel, levels, padded, edge_at),
        out_shape=[jax.ShapeDtypeStruct((planes, cols), F32)],
        in_specs=[VMEM] * 2 + [pl.BlockSpec(memory_space=pl.ANY)],
        out_specs=[VMEM],
        compiler_params=pltpu.CompilerParams(vmem_limit_bytes=VMEM_BYTES),
        name="strip",
    )(border_mine, border_other, held_weight)
    fields_height = fields
    chains = 1 + ITERS
    buffers = SUB + ITERS + chains * (ITERS - 1)
    shapes = (
        (ITERS + chains * (ITERS - 1), rows, pairs, cols),
        (6, 3 * rows, 2 * cols),
        (2, rows, cols),
        (count, cols),
    )
    basis, around, base, near_start = pl.pallas_call(
        functools.partial(basis_kernel, rows, pairs),
        out_shape=[jax.ShapeDtypeStruct(shape, F32) for shape in shapes],
        in_specs=[VMEM] * 4,
        out_specs=[VMEM] * len(shapes),
        scratch_shapes=[pltpu.VMEM((rows + 2 * REACH, pairs, 2 * cols), F32)] * (buffers - 1)
        + [
            pltpu.VMEM((fields_height, cols), F32),
            pltpu.VMEM((rows + 2 * REACH, pairs, 2 * cols), F32),
        ],
        compiler_params=pltpu.CompilerParams(vmem_limit_bytes=VMEM_BYTES),
        name="basis",
    )(border, border_other, step, change)
    tall = rows + 2 * SUB
    (mixed,) = call(
        functools.partial(mix_kernel, levels, padded),
        [(rows, planes, cols)],
        scratch=[
            pltpu.VMEM((3, tall, padded, cols), F32),
            pltpu.VMEM((SUB - 1, tall, planes, cols), F32),
            pltpu.VMEM((2 * SUB, planes, cols), F32),
        ],
        name="mix",
    )(packed, first, second, own_face, inner, near_start)
    mixed, fields = call(
        functools.partial(fields_kernel, levels, padded, scale),
        [flat, (loops, 6, rows, cols)],
        scratch=[pltpu.VMEM((6, rows, cols), F32)],
        name="fields",
    )(packed, mixed, extra, held_weight, held_observed, basis, near_start, fixed)
    mine = lax.all_to_all(fields, "loop", 0, 0)
    theirs = lax.ppermute(mine, "lat", swap)
    faces, plan = call(
        plan_kernel, [(6, height, 2 * cols), (pairs, cols)], vmem=large, name="plan"
    )(mine, theirs)
    shapes = (flat, (2, rows, cols), (2, rows, cols))
    state_next, gradient, direction = call(
        functools.partial(solve_kernel, levels, scale),
        shapes,
        scratch=[pltpu.VMEM((2, loops, rows, 2 * cols), F32)],
        vmem=large,
        name="solve",
    )(mine, theirs, faces, around, base, plan, mixed, depth, step, change)
    return (state_next.reshape(2, levels, rows, cols), gradient, direction)


def solution(mesh):
    return jax.shard_map(
        on_device,
        mesh=mesh,
        in_specs=(
            P("members", None, "loop", "lat"),
            P("members", None, "loop", "lat"),
            P(None, "loop", "lat"),
            P("members", "loop", "lat"),
            P("loop", "lat"),
            P("loop", "lat"),
            P("loop", "lat"),
            P("members", None, "loop", "lat"),
            P("members", None, "loop", "lat"),
        ),
        out_specs=(
            P("members", None, "loop", "lat"),
            P("members", "loop", "lat"),
            P("members", "loop", "lat"),
        ),
        check_vma=False,
    )
```

```python
import functools

import jax
import jax.numpy as jnp
from jax import lax
from jax.experimental import pallas as pl
from jax.experimental.pallas import tpu as pltpu
from jax.sharding import PartitionSpec as P

ITERS = 3
SUB = 3
SURFACE_GAIN = 5.0
SLOT = 8
WIDE_SLOT = 16
FOLD = SLOT * SUB
SWAP_ROWS = 240
REACH = SUB + 2 * (ITERS - 1)
SHIFT = 5.0
SPAN = 5.0
FUNCTIONALS = 1 + ITERS + ITERS + ITERS * ITERS
GRID = ("loop", "lat")
VMEM = pl.BlockSpec(memory_space=pltpu.VMEM)
F32 = jnp.float32
VMEM_BYTES = 16 * 1024 * 1024


def round_up(value, to):
    return (value + to - 1) // to * to


def call(kernel, out_shapes, scratch=(), vmem=VMEM_BYTES, name=None):
    return pl.pallas_call(
        kernel,
        out_shape=[jax.ShapeDtypeStruct(shape, F32) for shape in out_shapes],
        out_specs=[VMEM] * len(out_shapes),
        scratch_shapes=list(scratch),
        compiler_params=pltpu.CompilerParams(vmem_limit_bytes=vmem),
        name=name,
    )


def iota(shape, dim):
    return lax.broadcasted_iota(jnp.int32, shape, dim)


def state_rows(levels):
    return 2 * (levels - 1), levels - 1


def hist_rows(pairs):
    return pairs + 9, pairs + 3


def pack_kernel(levels, padded, *refs):
    sources, outs, targets, sems = refs[:9], refs[9:15], refs[15:22], refs[22]
    rows_ref, hist_ref = outs[:2]
    targets = targets[:4] + outs[4:6] + targets[4:]
    rows, cols = targets[2].shape
    copies = []
    for at, (source, target) in enumerate(zip(sources, targets)):
        if at == 8:
            source = source.at[:, pl.ds(0, rows), :]
        copies.append(pltpu.make_async_copy(source, target, sems.at[at]))
    for copy in copies:
        copy.start()
    for copy in copies[2:]:
        copy.wait()
    (
        state_ref, control_ref, depth_ref, spread_ref, step_ref, change_ref, damping_ref, weight_ref,
        observed_ref,
    ) = targets
    count = step_ref.shape[0] // (2 * rows)
    pairs = 2 * count
    close, distant = hist_rows(pairs)
    depth = depth_ref[...].astype(F32)
    spread = spread_ref[...]
    wet = depth > 0.5
    total = jnp.zeros((rows, cols), F32)
    for level in range(levels):
        total = total + jnp.where(level < depth, weight_ref[pl.ds(level * rows, rows), :], 0.0)
    fields = [
        damping_ref[...],
        2.0 * total,
        weight_ref[pl.ds(0, rows), :],
        observed_ref[0],
        observed_ref[1],
    ]
    for row in range(rows):
        here = slice(row, row + 1)
        for which, ref in enumerate((step_ref, change_ref)):
            both = [ref[pl.ds(tracer * rows + row, count, stride=2 * rows), :] for tracer in range(2)]
            apart = jnp.where(wet[here], both[0] - both[1], 0.0)
            hist_ref[row, pl.ds(which * count, count), :] = apart
    for copy in copies[:2]:
        copy.wait()
    first = iota((levels, cols), 0) == 0
    rest = jnp.zeros((padded - levels, cols), F32)
    for row in range(rows):
        here = slice(row, row + 1)
        for tracer in range(2):
            lift = jnp.where(wet[here], control_ref[tracer, here, :], 0.0)
            value = state_ref[tracer, pl.ds(row, levels, stride=rows), :]
            value = value + jnp.where(first, lift, 0.0)
            rows_ref[row, pl.ds(tracer * padded, levels), :] = value
            rows_ref[row, pl.ds(tracer * padded + levels, padded - levels), :] = rest
        for field, value in enumerate([spread, depth] + fields[:4]):
            rows_ref[row, pl.ds(levels + field, 1), :] = value[here]
        rows_ref[row, pl.ds(padded + levels, 1), :] = fields[4][here]

    even = lax.rem(lax.axis_index("loop"), 2) == 0

    def put(refs, at, upper, lower):
        here = pl.ds(at, upper.shape[0])
        refs[0][here, :] = jnp.where(even, upper, lower)
        refs[1][here, :] = jnp.where(even, lower, upper)

    masked = jnp.where(wet, spread, 0.0)
    for at in range(REACH):
        far = at < REACH - SUB
        index = at if far else at - (REACH - SUB)
        upper = rows - REACH + at if far else rows - SUB + index
        lower = SUB + index if far else index
        start = SUB * close + index * distant if far else index * close
        put(outs[2:4], start, hist_ref[upper], hist_ref[lower])
        start = start + pairs
        kind = masked if far else spread
        put(outs[2:4], start, kind[upper : upper + 1], kind[lower : lower + 1])
        for tracer in range(2):
            here = pl.ds(tracer * padded, 1)
            put(outs[2:4], start + 1 + tracer, rows_ref[upper, here, :], rows_ref[lower, here, :])
        if not far:
            here = pl.ds(levels + 2, 4)
            put(outs[2:4], start + 3, rows_ref[upper, here, :], rows_ref[lower, here, :])
            here = pl.ds(padded + levels, 1)
            put(outs[2:4], start + 7, rows_ref[upper, here, :], rows_ref[lower, here, :])
            put(outs[2:4], start + 8, depth[upper : upper + 1], depth[lower : lower + 1])
    last = SUB * close + (REACH - SUB) * distant
    folds = outs[2].shape[0] - FOLD
    if last < folds:
        rest = jnp.zeros((folds - last, cols), F32)
        put(outs[2:4], last, rest, rest)
    lat = lax.axis_index("lat")
    put(
        outs[2:4],
        folds,
        folded(edge_of(lambda i: rows_ref[rows - SUB + i], range(SUB), cols, lat)),
        folded(edge_of(lambda i: rows_ref[i], range(SUB), cols, lat)),
    )


def edge_of(rows_of, indices, cols, lat):
    lane = iota((1, cols), 1)
    slot = lane // SLOT
    place = lane % SLOT - SUB * lat
    mine = (place >= 0) & (place < SUB)
    total = None
    for index in indices:
        moved = pltpu.roll(rows_of(index), SLOT * index + SUB, 1)
        piece = jnp.where(mine & (slot == index), moved, 0.0)
        total = piece if total is None else total + piece
    return total


def folded(edge):
    planes, cols = edge.shape
    total = None
    for at, start in enumerate(range(0, planes, FOLD)):
        size = min(FOLD, planes - start)
        part = pltpu.roll(edge[start : start + size], FOLD * at, 1)
        if size < FOLD:
            part = jnp.concatenate([part, jnp.zeros((FOLD - size, cols), F32)], axis=0)
        total = part if total is None else total + part
    return total


def unfolded(fold, planes, lane_at):
    cols = fold.shape[1]
    lane = iota((1, cols), 1)
    here = (lane >= lane_at) & (lane < lane_at + FOLD)
    parts = []
    for at, start in enumerate(range(0, planes, FOLD)):
        part = pltpu.roll(fold, (lane_at - FOLD * at) % cols, 1)
        parts.append(jnp.where(here, part, 0.0)[: min(FOLD, planes - start)])
    return jnp.concatenate(parts, axis=0)


def level_face(levels, depth_here, depth_there, spread_here, spread_there):
    opened = levels < jnp.minimum(depth_here, depth_there)
    return jnp.where(opened, 0.5 * (spread_here + spread_there), 0.0)


def side_faces(level, depth, spread):
    cols = depth.shape[1]
    lane = iota((1, cols), 1)
    result = []
    for by, inside in ((cols - 1, lane < cols - 1), (1, lane > 0)):
        there = jnp.where(inside, pltpu.roll(depth, by, 1), 0.0)
        result.append(level_face(level, depth, there, spread, pltpu.roll(spread, by, 1)))
    return result


def mixed_row(get, faces, i, at):
    below, above, right, left = faces
    centre = get(i)[at, :]
    cols = centre.shape[1]
    total = centre + below * (get(i + 1)[at, :] - centre)
    total = total + above * (get(i - 1)[at, :] - centre)
    total = total + right * (pltpu.roll(centre, cols - 1, 1) - centre)
    return total + left * (pltpu.roll(centre, 1, 1) - centre)


def pairs_kernel(
    levels, padded, rows_ref, step_ref, change_ref,
    first_ref, second_ref, edge_ref, depth_ref, fixed_ref, face_ref, inner_ref,
):
    rows, _, cols = rows_ref.shape
    even = lax.rem(lax.axis_index("loop"), 2) == 0
    near, second = state_rows(levels)

    def put(at, upper, lower):
        here = pl.ds(at, upper.shape[0])
        first_ref[here, :] = jnp.where(even, upper, lower)
        second_ref[here, :] = jnp.where(even, lower, upper)

    for i in range(SUB):
        for start, size, place in ((1, levels - 1, 0), (padded + 1, levels - 1, second)):
            here = pl.ds(start, size)
            put(i * near + place, rows_ref[rows - SUB + i, here, :], rows_ref[i, here, :])
    if SUB * near < first_ref.shape[0]:
        rest = jnp.zeros((first_ref.shape[0] - SUB * near, cols), F32)
        put(SUB * near, rest, rest)
    level = iota((padded, cols), 0).astype(F32)
    spreads = [rows_ref[i, pl.ds(levels, 1), :] for i in range(rows)]
    depths = [rows_ref[i, pl.ds(levels + 1, 1), :] for i in range(rows)]
    for i in range(rows):
        if i + 1 < rows:
            face_ref[0, i] = level_face(level, depths[i], depths[i + 1], spreads[i], spreads[i + 1])
        face_ref[1, i], face_ref[2, i] = side_faces(level, depths[i], spreads[i])
    face_ref[0, rows - 1] = jnp.zeros((padded, cols), F32)
    for sweep in range(SUB):
        source = rows_ref if sweep == 0 else inner_ref.at[sweep - 1]
        for i in range(rows):
            for tracer in range(2):
                at = pl.ds(tracer * padded, padded)
                if sweep < i < rows - 1 - sweep:
                    faces = face_ref[0, i], face_ref[0, i - 1], face_ref[1, i], face_ref[2, i]
                    inner_ref[sweep, i, at, :] = mixed_row(lambda j: source.at[j], faces, i, at)
                else:
                    inner_ref[sweep, i, at, :] = jnp.zeros((padded, cols), F32)
    lat = lax.axis_index("lat")
    count = step_ref.shape[0]
    lane = iota((1, cols), 1)
    gram = [jnp.zeros((1, cols), F32) for _ in range(count)]
    at = FUNCTIONALS
    for left_ref in (step_ref, change_ref):
        for i in range(count):
            for j in range(i, count):
                value = jnp.sum(left_ref[i] * change_ref[j], axis=(0, 1), keepdims=True)
                gram[i] = gram[i] + jnp.where(lane == at + j, value, 0.0)
                if i != j:
                    gram[j] = gram[j] + jnp.where(lane == at + i, value, 0.0)
        at += count
    for i in range(count):
        fixed_ref[3, pl.ds(i, 1), :] = gram[i]
    for row in range(rows):
        plane = lambda at: rows_ref[row, pl.ds(levels + at, 1), :]
        here = pl.ds(row, 1)
        depth_ref[here, :] = plane(1)
        fixed_ref[0, here, :] = jnp.where(plane(1) > 0.5, plane(0), 0.0)
        fixed_ref[1, here, :] = plane(2)
        fixed_ref[2, here, :] = plane(3)
    edge_ref[...] = edge_of(lambda i: rows_ref[i - SUB], range(SUB, rows + SUB), cols, lat)


def faces_between(here, there, opened=True):
    return jnp.where((here > 0.0) & (there > 0.0) & opened, 0.5 * (here + there), 0.0)


def closed_lane(cols):
    return jnp.where(lax.axis_index("lat") == 0, 2 * cols - 1, cols - 1)


def surface_faces(spread, closed):
    height, width = spread.shape
    below = faces_between(spread, pltpu.roll(spread, height - 1, 0))
    right = faces_between(
        spread, pltpu.roll(spread, width - 1, 1), iota(spread.shape, 1) != closed
    )
    return below, pltpu.roll(below, 1, 0), right, pltpu.roll(right, 1, 1)


def gathered(mine_ref, other_ref, field):
    return jnp.concatenate(
        [
            jnp.concatenate([mine_ref[i, field], other_ref[i, field]], axis=1)
            for i in range(mine_ref.shape[0])
        ],
        axis=0,
    )


def surface_outflow(value, to_below, to_above, to_right, to_left):
    height, width = value.shape
    result = to_right * (value - pltpu.roll(value, width - 1, 1))
    result = result + to_left * (value - pltpu.roll(value, 1, 1))
    result = result + to_below * (value - pltpu.roll(value, height - 1, 0))
    return result + to_above * (value - pltpu.roll(value, 1, 0))


def plan_kernel(mine_ref, other_ref, faces_ref, plan_ref):
    loops, _, rows, cols = mine_ref.shape
    closed = closed_lane(cols)
    for at, face in enumerate(surface_faces(gathered(mine_ref, other_ref, 3), closed)):
        faces_ref[at] = SURFACE_GAIN * face
    for field in (4, 5):
        faces_ref[field] = gathered(mine_ref, other_ref, field)
    count = plan_ref.shape[0] // 2
    gram = mine_ref[0, 2] + other_ref[0, 2]
    for i in range(1, loops):
        gram = gram + (mine_ref[i, 2] + other_ref[i, 2])
    wide = (count, cols)
    tables = [
        jnp.broadcast_to(gram[:, i : i + 1], wide)
        for i in range(FUNCTIONALS, FUNCTIONALS + 2 * count)
    ]
    step_change, change_change = tables[:count], tables[count:]
    last = count - 1
    gamma = step_change[last][last:] / change_change[last][last:]
    rho = [1.0 / step_change[i][i : i + 1] for i in range(count)]
    row = iota(wide, 0)
    lane = iota(wide, 1)
    step_grad = jnp.where(lane == row, 1.0, 0.0)
    change_grad = jnp.where(lane == row + count, 1.0, 0.0)
    factors = [None] * count
    for i in range(count - 1, -1, -1):
        factors[i] = rho[i] * step_grad[i : i + 1]
        step_grad = step_grad - factors[i] * step_change[i]
        change_grad = change_grad - factors[i] * change_change[i]
    change_grad = gamma * change_grad
    for i in range(count):
        weight = factors[i] - rho[i] * change_grad[i : i + 1]
        change_grad = change_grad + weight * step_change[i]
        plan_ref[pl.ds(i, 1), :] = -weight
        plan_ref[pl.ds(count + i, 1), :] = gamma * factors[i]
    at = lane[:1] == 2 * count
    plan_ref[pl.ds(0, 1), :] = jnp.where(at, -gamma, plan_ref[pl.ds(0, 1), :])


def received(first_ref, second_ref):
    even = lax.rem(lax.axis_index("loop"), 2) == 0

    def low(at, size):
        here = pl.ds(at, size)
        return jnp.where(even, second_ref[here, :], first_ref[here, :])

    def high(at, size):
        here = pl.ds(at, size)
        return jnp.where(even, first_ref[here, :], second_ref[here, :])

    return low, high


def border_kernel(
    levels, padded, edge_ref, first_ref, second_ref, rows_ref, hist_ref, out_ref, swap_ref
):
    rows, pairs, cols = hist_ref.shape
    close, distant = hist_rows(pairs)
    low, high = received(first_ref, second_ref)
    tall = 3 * rows
    fields = (rows + 2 * REACH) * pairs
    out_ref[pl.ds(fields, 8 * tall), :] = jnp.zeros((8 * tall, cols), F32)
    lane = iota((1, cols), 1)
    place = lane % WIDE_SLOT - REACH * lax.axis_index("lat")
    sent = (place >= 0) & (place < REACH)
    slots = cols // WIDE_SLOT
    groups = [None] * slot_groups(rows, cols)
    for at in range(-REACH, rows + REACH):
        get = low if at < 0 else high
        limit = None
        if 0 <= at < rows:
            own = rows_ref.at[at]
            limit = levels + 1
            get = lambda place, size: own[pl.ds(place, size), :]
            apart = hist_ref[at]
            places = {0: levels, 6: 0, 7: padded, 5: padded + levels}
            places.update({1 + field: levels + 2 + field for field in range(4)})
        elif -SUB <= at < rows + SUB:
            start = (at + SUB if at < 0 else at - rows) * close
            apart = get(start, pairs)
            start = start + pairs
            places = {0: start, 6: start + 1, 7: start + 2}
            places.update({1 + field: start + 3 + field for field in range(5)})
            limit = start + 8
        else:
            start = SUB * close + (at + REACH if at < 0 else at - rows - SUB) * distant
            apart = get(start, pairs)
            start = start + pairs
            places = {0: start, 6: start + 1, 7: start + 2}
        out_ref[pl.ds((at + REACH) * pairs, pairs), :] = apart
        group, slot = divmod(at + REACH, slots)
        moved = pltpu.roll(apart, WIDE_SLOT * slot + REACH, 1)
        moved = jnp.where(sent & (lane // WIDE_SLOT == slot), moved, 0.0)
        groups[group] = moved if groups[group] is None else groups[group] + moved
        for field, place in places.items():
            value = get(place, 1)
            if field == 0 and limit is not None:
                value = jnp.where(get(limit, 1) > 0.5, value, 0.0)
            out_ref[pl.ds(fields + field * tall + at + rows, 1), :] = value
    for at, group in enumerate(groups):
        swap_ref[pl.ds(at * pairs, pairs), :] = group
    total = None
    for field in range(8):
        moved = pltpu.roll(
            out_ref[pl.ds(fields + field * tall, tall), :], WIDE_SLOT * field + REACH, 1
        )
        moved = jnp.where(sent & (lane // WIDE_SLOT == field), moved, 0.0)
        total = moved if total is None else total + moved
    at = len(groups) * pairs
    swap_ref[pl.ds(at, tall), :] = total
    at = at + tall
    planes = edge_ref.shape[0]
    folds = first_ref.shape[0] - FOLD
    before = unfolded(low(folds, FOLD), planes, 0)
    after = unfolded(high(folds, FOLD), planes, SLOT * (rows + SUB))
    swap_ref[pl.ds(at, planes), :] = edge_ref[...] + (before + after)
    at = at + planes
    if at < swap_ref.shape[0]:
        swap_ref[pl.ds(at, swap_ref.shape[0] - at), :] = jnp.zeros(
            (swap_ref.shape[0] - at, cols), F32
        )


def slot_groups(rows, cols):
    slots = cols // WIDE_SLOT
    return (rows + 2 * REACH + slots - 1) // slots


def basis_kernel(
    rows, pairs, mine_ref, other_ref, step_ref, change_ref,
    out_ref, near_ref, base_ref, first_ref, *work
):
    cols = mine_ref.shape[1]
    width = 2 * cols
    tall = rows + 2 * REACH
    ahead = REACH - SUB
    high = 3 * rows
    fields = tall * pairs
    closed = closed_lane(cols)
    opened = iota((1, width), 1) != closed
    slots = cols // WIDE_SLOT
    other_fields = slot_groups(rows, cols) * pairs
    beside_ref = work[-2]
    lane = iota((1, cols), 1)
    start = jnp.where(lax.axis_index("lat") == 0, 0, cols - REACH)
    at_border = (lane >= start) & (lane < start + REACH)

    packed = other_ref[pl.ds(other_fields, high), :]
    for at in range(8):
        there = pltpu.roll(packed, (cols - WIDE_SLOT * at - REACH) % cols, 1)
        beside_ref[pl.ds(at * high, high), :] = jnp.where(at_border, there, 0.0)

    def wide(at, size):
        there = pl.ds(at - fields, size)
        return jnp.concatenate([mine_ref[pl.ds(at, size), :], beside_ref[there, :]], axis=1)

    def left(value):
        return pltpu.roll(value, width - 1, 1)

    def right(value):
        return pltpu.roll(value, 1, 1)

    def field(at):
        return wide(fields + at * high, high)

    def field_row(at, i):
        return wide(fields + at * high + i - REACH + rows, 1)

    faces = surface_faces(field(0), closed)
    for at in range(4):
        near_ref[at] = faces[at]
    sea = jnp.where(field(0) > 0.0, 1.0, 0.0)
    weight = field(3)
    near_ref[4] = weight * sea
    near_ref[5] = sea
    value = [field(6), field(7)]
    for sweep in range(SUB):
        value = [part - surface_outflow(part, *faces) for part in value]
    value = [weight * (value[0] - field(4)), weight * (value[1] - field(5))]
    for sweep in range(SUB):
        value = [part - surface_outflow(part, *faces) for part in value]
    base = [(part * sea)[rows : 2 * rows, :cols] for part in value]
    for tracer in range(2):
        base_ref[tracer] = base[tracer]
    for i in range(pairs // 2):
        total = jnp.zeros((1, cols), F32)
        for at, ref in ((0, step_ref), (cols // 2, change_ref)):
            part = ref[i, pl.ds(0, rows), :] * base[0] + ref[i, pl.ds(rows, rows), :] * base[1]
            part = jnp.sum(part, axis=(0, 1), keepdims=True)
            total = total + jnp.where(lane == at, part, 0.0)
        first_ref[pl.ds(i, 1), :] = total

    spread = [field_row(0, i) for i in range(tall)]
    to_right = [faces_between(value, left(value), opened) for value in spread]
    to_left = [right(value) for value in to_right]
    to_below = [faces_between(spread[i], spread[i + 1]) for i in range(tall - 1)]
    inner = range(ahead, tall - ahead)
    damping = {i: (field_row(1, i) - SHIFT) * (1.0 / SPAN) for i in inner}
    response_weight = {i: field_row(2, i) for i in inner}
    weight = {i: field_row(3, i) for i in inner}
    gain = SURFACE_GAIN / SPAN

    def outflow(get, i):
        value = get(i)
        total = to_right[i] * (value - left(value)) + to_left[i] * (value - right(value))
        total = total + to_below[i] * (value - get(i + 1))
        return value, total + to_below[i - 1] * (value - get(i - 1))

    def mixed(get, ref, reach):
        for i in range(REACH - reach, REACH + rows + reach):
            value, out = outflow(get, i)
            ref[i] = value - out
        return lambda i: ref[i]

    def applied(get, ref, reach):
        for i in range(REACH - reach, REACH + rows + reach):
            value, out = outflow(get, i)
            ref[i] = damping[i] * value + gain * out
        return lambda i: ref[i]

    def keep(slot, get):
        for i in range(rows):
            out_ref[slot, i] = get(i + REACH)[:, :cols]

    for i in range(tall):
        group, slot = divmod(i, slots)
        there = other_ref[pl.ds(group * pairs, pairs), :]
        there = pltpu.roll(there, (cols - WIDE_SLOT * slot - REACH) % cols, 1)
        work[-1][i, :, :cols] = mine_ref[pl.ds(i * pairs, pairs), :]
        work[-1][i, :, cols:] = jnp.where(at_border, there, 0.0)
    get = lambda i: work[-1][i]
    for sweep in range(SUB):
        get = mixed(get, work[sweep], REACH - 1 - sweep)
    reach = REACH - SUB
    powers = [get]
    for power in range(1, ITERS):
        powers.append(applied(powers[-1], work[SUB + power - 1], reach - power))
    for power in range(ITERS):
        keep(power, powers[power])
    reach = ITERS - 1
    slot = ITERS
    at = SUB + ITERS - 1
    chains = []
    for factor, power in [(weight, 0)] + [(response_weight, power) for power in range(ITERS)]:
        get = powers[power]
        chains.append(lambda i, factor=factor, get=get: factor[i] * get(i))
    for power in range(1, ITERS):
        for index in range(len(chains)):
            chains[index] = applied(chains[index], work[at], reach - power)
            at += 1
            keep(slot + index * (ITERS - 1) + power - 1, chains[index])


def mix_kernel(
    levels, padded, pairs, rows_ref, first_ref, second_ref, first_hist_ref, second_hist_ref,
    own_face_ref, inner_ref, _, out_ref, face_ref, outer_ref, halo_ref
):
    rows, _, cols = rows_ref.shape
    count = rows + 2 * SUB
    near, second = state_rows(levels)
    rest = jnp.zeros((padded - levels, cols), F32)
    close, _ = hist_rows(pairs)
    state_of = received(first_ref, second_ref)
    hist_of = received(first_hist_ref, second_hist_ref)
    for i in range(2 * SUB):
        at = i % SUB * near
        start = i % SUB * close + pairs
        state, hist = state_of[i // SUB], hist_of[i // SUB]
        halo_ref[i, pl.ds(levels, padded - levels), :] = rest
        halo_ref[i, pl.ds(padded + levels, padded - levels), :] = rest
        halo_ref[i, pl.ds(0, 1), :] = hist(start + 1, 1)
        halo_ref[i, pl.ds(1, levels - 1), :] = state(at, levels - 1)
        halo_ref[i, pl.ds(levels, 1), :] = hist(start, 1)
        halo_ref[i, pl.ds(levels + 1, 1), :] = hist(start + 8, 1)
        halo_ref[i, pl.ds(padded, 1), :] = hist(start + 2, 1)
        halo_ref[i, pl.ds(padded + 1, levels - 1), :] = state(at + second, levels - 1)
    level = iota((padded, cols), 0).astype(F32)

    def state_row(i):
        if i < SUB:
            return halo_ref.at[i]
        return rows_ref.at[i - SUB] if i < SUB + rows else halo_ref.at[i - rows]

    def face(kind, i):
        last = SUB + rows - (1 if kind == 0 else 0)
        return own_face_ref[kind, i - SUB] if SUB <= i < last else face_ref[kind, i]

    spreads = [state_row(i)[pl.ds(levels, 1), :] for i in range(count)]
    depths = [state_row(i)[pl.ds(levels + 1, 1), :] for i in range(count)]
    for i in range(count - 1):
        if not SUB <= i < SUB + rows - 1:
            face_ref[0, i] = level_face(level, depths[i], depths[i + 1], spreads[i], spreads[i + 1])
        if i > 0 and not SUB <= i < SUB + rows:
            face_ref[1, i], face_ref[2, i] = side_faces(level, depths[i], spreads[i])

    def after(sweep):
        def get(i):
            if sweep == 0:
                return state_row(i)
            if SUB + sweep <= i < SUB + rows - sweep:
                return inner_ref.at[sweep - 1, i - SUB]
            return outer_ref.at[sweep - 1, i]

        return get

    for sweep in range(1, SUB + 1):
        for i in range(sweep, count - sweep):
            done = SUB + sweep <= i < SUB + rows - sweep
            if done and sweep < SUB:
                continue
            into = out_ref.at[i - SUB] if sweep == SUB else outer_ref.at[sweep - 1, i]
            for tracer in range(2):
                at = pl.ds(tracer * padded, padded)
                if done:
                    into[at, :] = inner_ref[sweep - 1, i - SUB, at, :]
                else:
                    faces = face(0, i), face(0, i - 1), face(1, i), face(2, i)
                    into[at, :] = mixed_row(after(sweep - 1), faces, i, at)


def hold_kernel(weight_hbm, observed_hbm, weight_ref, observed_ref, sems):
    copies = [
        pltpu.make_async_copy(weight_hbm, weight_ref, sems.at[0]),
        pltpu.make_async_copy(observed_hbm, observed_ref, sems.at[1]),
    ]
    for copy in copies:
        copy.start()
    for copy in copies:
        copy.wait()


def strip_kernel(levels, padded, edge_at, mine_ref, other_ref, _, out_ref):
    cols = mine_ref.shape[1]
    planes = 2 * padded
    edge_ref = mine_ref.at[pl.ds(edge_at, planes)]
    other_ref = other_ref.at[pl.ds(edge_at, planes)]
    lat = lax.axis_index("lat")
    lane = iota((1, cols), 1)
    place = lane % SLOT
    level = iota((padded, cols), 0).astype(F32)

    def left(value, by=1):
        return pltpu.roll(value, (cols - by) % cols, 1)

    def right(value, by=1):
        return pltpu.roll(value, by, 1)

    spread = edge_ref[pl.ds(levels, 1), :] + other_ref[pl.ds(levels, 1), :]
    depth = edge_ref[pl.ds(levels + 1, 1), :] + other_ref[pl.ds(levels + 1, 1), :]
    within = place < 2 * SUB - 1
    col_depth = jnp.minimum(depth, jnp.where(within, left(depth), 0.0))
    col_spread = 0.5 * (spread + left(spread))
    row_depth = jnp.minimum(depth, left(depth, SLOT))
    row_spread = 0.5 * (spread + left(spread, SLOT))

    def strip_face(limit, value):
        return jnp.where(level < limit, value, 0.0)

    to_left = strip_face(right(col_depth), right(col_spread))
    to_right = strip_face(col_depth, col_spread)
    to_above = strip_face(right(row_depth, SLOT), right(row_spread, SLOT))
    to_below = strip_face(row_depth, row_spread)
    out_of_low = place == jnp.where(lat == 0, SUB - 1, SLOT)
    out_of_high = place == jnp.where(lat == 0, SLOT, SUB)
    over_low = jnp.where(out_of_low, to_right, 0.0)
    over_high = jnp.where(out_of_high, to_left, 0.0)
    own_right = jnp.where(place == SUB - 1, 0.0, to_right)
    own_left = jnp.where(place == SUB, 0.0, to_left)

    def spread_out(value, east, west):
        before, after = right(value), left(value)
        above, below = right(value, SLOT), left(value, SLOT)
        total = value + east * (after - value) + west * (before - value)
        return total + to_below * (below - value) + to_above * (above - value)

    parts = []
    extras = [None, None]
    for tracer in range(2):
        at = pl.ds(tracer * padded, padded)
        parts.append(edge_ref[at, :] + other_ref[at, :])

    for sweep in range(1, SUB + 1):
        for tracer in range(2):
            part = parts[tracer]
            across = over_low * (left(part) - part) + over_high * (right(part) - part)
            extra = extras[tracer]
            if extra is not None:
                across = across + spread_out(extra, own_right, own_left)
            extras[tracer] = across
            if sweep < SUB:
                parts[tracer] = spread_out(part, to_right, to_left)

    for tracer in range(2):
        out_ref[pl.ds(tracer * padded, padded), :] = extras[tracer]


def fields_kernel(
    levels, padded, scale,
    rows_ref, main_ref, extra_ref, weight_ref, observed_ref, basis_ref, first_ref, fixed_ref,
    mixed_ref, fields_ref, part_ref,
):
    rows, _, cols = rows_ref.shape
    pairs = basis_ref.shape[2]
    lat = lax.axis_index("lat")
    lane = iota((1, cols), 1)
    place = lane % SLOT
    level = iota((padded, cols), 0).astype(F32)

    def left(value, by=1):
        return pltpu.roll(value, (cols - by) % cols, 1)

    def right(value, by=1):
        return pltpu.roll(value, by, 1)

    start = jnp.where(lat == 0, cols - SUB, 0)
    at_border = (lane >= start) & (lane < start + SUB)

    for row in range(rows):
        i = row + SUB
        at = pl.ds(row, levels, stride=rows)
        mixed = []
        for tracer in range(2):
            border = jnp.where(at_border, left(extra_ref[pl.ds(tracer * padded, padded), :], SLOT * i + SUB), 0.0)
            mixed.append((main_ref[row, pl.ds(tracer * padded, padded), :] + border)[:levels])
        wet = level[:levels] < rows_ref[row, pl.ds(levels + 1, 1), :]
        weight = weight_ref[at, :]
        misfit = []
        for tracer in range(2):
            mixed_ref[tracer, at, :] = mixed[tracer]
            misfit.append(weight * (mixed[tracer] - observed_ref[tracer, at, :]))
        here = pl.ds(row, 1)
        part_ref[0, here, :] = scale * jnp.sum(
            jnp.where(wet, mixed[0] - mixed[1], 0.0), axis=0, keepdims=True
        )
        part_ref[1, here, :] = jnp.sum(
            jnp.where(wet, misfit[1] - misfit[0], 0.0), axis=0, keepdims=True
        )
    sums = [None] * FUNCTIONALS

    def add(at, slot, row, factor):
        value = basis_ref[slot, row] * factor
        sums[at] = value if sums[at] is None else sums[at] + value

    for row in range(rows):
        here = pl.ds(row, 1)
        surface, base = part_ref[0, here, :], part_ref[1, here, :]
        fixed = lambda plane: rows_ref[row, pl.ds(levels + plane, 1), :]
        add(1, 0, row, fixed(4) * surface)
        for power in range(1, ITERS):
            add(1 + power, ITERS + power - 1, row, surface)
        for j in range(ITERS):
            add(1 + ITERS + j, j, row, base)
            at = 1 + 2 * ITERS + j * ITERS
            add(at, j, row, fixed(3) * surface)
            for power in range(1, ITERS):
                add(at + power, ITERS + (1 + j) * (ITERS - 1) + power - 1, row, surface)
    half = pairs // 2
    total = first_ref[...] + fixed_ref[3]
    for at in range(1, FUNCTIONALS):
        value = jnp.sum(sums[at], axis=1, keepdims=True)
        total = total + jnp.where(lane == at, value[:half], 0.0)
        total = total + jnp.where(lane == cols // 2 + at, value[half:], 0.0)
    part_ref[2] = total
    for field in range(3):
        part_ref[3 + field] = fixed_ref[field]
    for copy in range(fields_ref.shape[0]):
        fields_ref[copy] = part_ref[...]


def solve_kernel(
    levels, scale,
    mine_ref, other_ref, faces_ref, near_ref, base_ref, plan_ref, mixed_ref, depth_ref, step_ref,
    change_ref, state_ref, gradient_ref, direction_ref, kept_ref,
):
    loops, _, rows, cols = mine_ref.shape
    loop = lax.axis_index("loop")

    def total(value):
        parts = [
            value[i * rows : (i + 1) * rows, j * cols : (j + 1) * cols]
            for i in range(loops)
            for j in range(2)
        ]
        while len(parts) > 1:
            half = (len(parts) + 1) // 2
            parts = [a + b for a, b in zip(parts, parts[half:])] + parts[len(parts) - half : half]
        return jnp.sum(jnp.sum(parts[0], axis=1, keepdims=True), axis=0, keepdims=True)

    count = step_ref.shape[0]
    inner = mine_ref[0, 2] + other_ref[0, 2]
    for i in range(1, loops):
        inner = inner + (mine_ref[i, 2] + other_ref[i, 2])
    plan = plan_ref[...]
    shifted = pltpu.roll(inner, cols // 2, 1)
    linear = None
    for i in range(2 * count):
        source = inner if i < count else shifted
        part = plan[:, i : i + 1] * source[i % count : i % count + 1]
        linear = part if linear is None else linear + part
    gamma = plan[:1, 2 * count : 2 * count + 1]

    gained = [faces_ref[i] for i in range(4)]
    damping = faces_ref[4]

    def conjugate(rhs):
        residual = rhs
        search = rhs
        solution = jnp.zeros_like(rhs)
        norm_now = total(rhs * rhs)
        one = jnp.ones((1, 1), F32)
        residual_of = [one]
        search_of = [one]
        solution_of = []
        for sweep in range(ITERS):
            image = damping * search + surface_outflow(search, *gained)
            alpha = norm_now / total(search * image)
            solution = solution + alpha * search
            solution_of = add_up(solution_of, alpha, search_of)
            if sweep < ITERS - 1:
                residual = residual - alpha * image
                norm_next = total(residual * residual)
                beta = norm_next / norm_now
                search = residual + beta * search
                norm_now = norm_next
                image_of = [SHIFT * value for value in search_of]
                image_of = add_up(image_of, SPAN, [None] + search_of)
                residual_of = add_up(residual_of, -alpha, image_of)
                search_of = add_up(residual_of, beta, search_of)
        return solution, solution_of

    def add_up(terms, factor, others):
        result = list(terms) + [None] * (len(others) - len(terms))
        for at, value in enumerate(others):
            if value is not None:
                value = factor * value
                result[at] = value if result[at] is None else result[at] + value
        return result

    def near(slot, value):
        for i in range(loops):
            kept_ref[slot, i] = value[i * rows : (i + 1) * rows]
        return jnp.concatenate(
            [kept_ref[slot, lax.rem(loop + shift, loops)] for shift in (loops - 1, 0, 1)], axis=0
        )

    elevation, elevation_of = conjugate(gathered(mine_ref, other_ref, 0))
    pressure = gathered(mine_ref, other_ref, 1) + faces_ref[5] * elevation
    elevation = near(0, elevation)
    depth = depth_ref[...]
    here = elevation[rows : 2 * rows, :cols]
    for level in range(levels):
        at = pl.ds(level * rows, rows)
        change = jnp.where(level < depth, here, 0.0)
        state_ref[0, at, :] = mixed_ref[0, at, :] - change
        state_ref[1, at, :] = mixed_ref[1, at, :] + change
    response, response_of = conjugate(pressure)
    response = near(1, response)

    lane = iota((1, cols), 1)
    factor = jnp.where(lane == 0, 1.0, 0.0)
    for j in range(ITERS):
        factor = jnp.where(lane == 1 + j, -elevation_of[j], factor)
        part = scale * response_of[j]
        factor = jnp.where(lane == 1 + ITERS + j, part, factor)
        for k in range(ITERS):
            at = 1 + 2 * ITERS + j * ITERS + k
            factor = jnp.where(lane == at, part * elevation_of[k], factor)
    weights = jnp.sum(linear * factor, axis=1, keepdims=True)
    weights = [
        jnp.broadcast_to(weights[i : i + 1], (rows, cols)) for i in range(2 * count)
    ]

    sea = near_ref[5]
    carried = near_ref[4] * elevation - (scale * sea) * response
    faces = [near_ref[i] for i in range(4)]
    for sweep in range(SUB):
        carried = carried - surface_outflow(carried, *faces)
    carried = (sea * carried)[rows : 2 * rows, :cols]
    for tracer in range(2):
        at = pl.ds(tracer * rows, rows)
        gradient = base_ref[tracer] - carried if tracer == 0 else base_ref[tracer] + carried
        gradient_ref[tracer] = gradient
        value = gamma * gradient
        for i in range(count):
            value = value + weights[i] * step_ref[i, at, :]
            value = value + weights[count + i] * change_ref[i, at, :]
        direction_ref[tracer] = value


def on_device(
    state, observed, weight, control, depth_index, diffusivity, damping, history_step, history_change
):
    _, levels, rows, cols = state.shape
    count = history_step.shape[0]
    padded = round_up(levels + 6, 8)
    planes = 2 * padded
    loops = lax.axis_size("loop")
    lats = lax.axis_size("lat")
    blocks = loops * lats
    scale = levels ** (-0.5)
    flat = (2, levels * rows, cols)
    state = state.reshape(flat)
    observed = observed.reshape(flat)
    weight = weight.reshape(flat[1:])

    pairs = 2 * count
    inputs = (
        state, control, depth_index, diffusivity,
        history_step.reshape(-1, cols), history_change.reshape(-1, cols), damping, weight, observed,
    )
    held = [x.shape for x in inputs[:-1]] + [(2, rows, cols)]
    close, distant = hist_rows(pairs)
    sent_hist = (round_up(SUB * close + (REACH - SUB) * distant, 8) + FOLD, cols)
    sent = (round_up(SUB * state_rows(levels)[0], 8), cols)
    stored = (2 * count * rows, cols)
    shapes = ((rows, planes, cols), (rows, pairs, cols), sent_hist, sent_hist, stored, stored)
    packed, hist, first_hist, second_hist, step, change = pl.pallas_call(
        functools.partial(pack_kernel, levels, padded),
        out_shape=[jax.ShapeDtypeStruct(shape, F32) for shape in shapes],
        in_specs=[pl.BlockSpec(memory_space=pltpu.HBM)] * len(inputs),
        out_specs=[VMEM] * len(shapes),
        scratch_shapes=[
            pltpu.VMEM(shape, x.dtype) for at, (shape, x) in enumerate(zip(held, inputs)) if at not in (4, 5)
        ]
        + [pltpu.SemaphoreType.DMA((len(inputs),))],
        compiler_params=pltpu.CompilerParams(vmem_limit_bytes=VMEM_BYTES),
        name="pack",
    )(*(pltpu.with_memory_space_constraint(x, pltpu.HBM) for x in inputs))
    partner = [(i, i ^ 1) for i in range(loops)]
    following = [(i, (i - 1 + 2 * (i % 2)) % loops) for i in range(loops)]
    swap = [(0, 1), (1, 0)]
    first_hist = lax.ppermute(first_hist, "loop", partner)
    step = step.reshape(count, 2 * rows, cols)
    change = change.reshape(count, 2 * rows, cols)
    second_hist = lax.ppermute(second_hist, "loop", following)
    first, second, edge, depth, fixed, own_face, inner = call(
        functools.partial(pairs_kernel, levels, padded),
        [
            sent, sent, (planes, cols), (rows, cols), (4, rows, cols), (3, rows, padded, cols),
            (SUB, rows, planes, cols),
        ],
        name="pairs",
    )(packed, step, change)
    first = lax.ppermute(first, "loop", partner)
    second = lax.ppermute(second, "loop", following)
    height = loops * rows
    large = VMEM_BYTES if loops <= 16 else 2 * VMEM_BYTES
    fields = 8 * 3 * rows
    fields = 8 * 3 * rows
    edge_at = slot_groups(rows, cols) * pairs + 3 * rows
    border, border_mine = call(
        functools.partial(border_kernel, levels, padded),
        [((rows + 2 * REACH) * pairs + fields, cols), (max(SWAP_ROWS, edge_at + planes), cols)],
        name="border",
    )(edge, first_hist, second_hist, packed, hist)
    border_other = lax.ppermute(border_mine, "lat", swap)
    held_weight, held_observed = pl.pallas_call(
        hold_kernel,
        out_shape=[jax.ShapeDtypeStruct(x.shape, F32) for x in (weight, observed)],
        in_specs=[pl.BlockSpec(memory_space=pltpu.HBM)] * 2,
        out_specs=[VMEM] * 2,
        scratch_shapes=[pltpu.SemaphoreType.DMA((2,))],
        compiler_params=pltpu.CompilerParams(vmem_limit_bytes=VMEM_BYTES),
        name="hold",
    )(*(pltpu.with_memory_space_constraint(x, pltpu.HBM) for x in (weight, observed)))
    (extra,) = pl.pallas_call(
        functools.partial(strip_kernel, levels, padded, edge_at),
        out_shape=[jax.ShapeDtypeStruct((planes, cols), F32)],
        in_specs=[VMEM] * 2 + [pl.BlockSpec(memory_space=pl.ANY)],
        out_specs=[VMEM],
        compiler_params=pltpu.CompilerParams(vmem_limit_bytes=VMEM_BYTES),
        name="strip",
    )(border_mine, border_other, held_weight)
    fields_height = fields
    chains = 1 + ITERS
    buffers = SUB + ITERS + chains * (ITERS - 1)
    shapes = (
        (ITERS + chains * (ITERS - 1), rows, pairs, cols),
        (6, 3 * rows, 2 * cols),
        (2, rows, cols),
        (count, cols),
    )
    basis, around, base, near_start = pl.pallas_call(
        functools.partial(basis_kernel, rows, pairs),
        out_shape=[jax.ShapeDtypeStruct(shape, F32) for shape in shapes],
        in_specs=[VMEM] * 4,
        out_specs=[VMEM] * len(shapes),
        scratch_shapes=[pltpu.VMEM((rows + 2 * REACH, pairs, 2 * cols), F32)] * (buffers - 1)
        + [
            pltpu.VMEM((fields_height, cols), F32),
            pltpu.VMEM((rows + 2 * REACH, pairs, 2 * cols), F32),
        ],
        compiler_params=pltpu.CompilerParams(vmem_limit_bytes=VMEM_BYTES),
        name="basis",
    )(border, border_other, step, change)
    tall = rows + 2 * SUB
    (mixed,) = call(
        functools.partial(mix_kernel, levels, padded, pairs),
        [(rows, planes, cols)],
        scratch=[
            pltpu.VMEM((3, tall, padded, cols), F32),
            pltpu.VMEM((SUB - 1, tall, planes, cols), F32),
            pltpu.VMEM((2 * SUB, planes, cols), F32),
        ],
        name="mix",
    )(packed, first, second, first_hist, second_hist, own_face, inner, near_start)
    mixed, fields = call(
        functools.partial(fields_kernel, levels, padded, scale),
        [flat, (loops, 6, rows, cols)],
        scratch=[pltpu.VMEM((6, rows, cols), F32)],
        name="fields",
    )(packed, mixed, extra, held_weight, held_observed, basis, near_start, fixed)
    mine = lax.all_to_all(fields, "loop", 0, 0)
    theirs = lax.ppermute(mine, "lat", swap)
    faces, plan = call(
        plan_kernel, [(6, height, 2 * cols), (pairs, cols)], vmem=large, name="plan"
    )(mine, theirs)
    shapes = (flat, (2, rows, cols), (2, rows, cols))
    state_next, gradient, direction = call(
        functools.partial(solve_kernel, levels, scale),
        shapes,
        scratch=[pltpu.VMEM((2, loops, rows, 2 * cols), F32)],
        vmem=large,
        name="solve",
    )(mine, theirs, faces, around, base, plan, mixed, depth, step, change)
    return (state_next.reshape(2, levels, rows, cols), gradient, direction)


def solution(mesh):
    return jax.shard_map(
        on_device,
        mesh=mesh,
        in_specs=(
            P("members", None, "loop", "lat"),
            P("members", None, "loop", "lat"),
            P(None, "loop", "lat"),
            P("members", "loop", "lat"),
            P("loop", "lat"),
            P("loop", "lat"),
            P("loop", "lat"),
            P("members", None, "loop", "lat"),
            P("members", None, "loop", "lat"),
        ),
        out_specs=(
            P("members", None, "loop", "lat"),
            P("members", "loop", "lat"),
            P("members", "loop", "lat"),
        ),
        check_vma=False,
    )
```

```python
import functools

import jax
import jax.numpy as jnp
from jax import lax
from jax.experimental import pallas as pl
from jax.experimental.pallas import tpu as pltpu
from jax.sharding import PartitionSpec as P

ITERS = 3
SUB = 3
SURFACE_GAIN = 5.0
SLOT = 8
WIDE_SLOT = 16
FOLD = SLOT * SUB
SWAP_ROWS = 240
REACH = SUB + 2 * (ITERS - 1)
SHIFT = 5.0
SPAN = 5.0
FUNCTIONALS = 1 + ITERS + ITERS + ITERS * ITERS
GRID = ("loop", "lat")
VMEM = pl.BlockSpec(memory_space=pltpu.VMEM)
F32 = jnp.float32
VMEM_BYTES = 16 * 1024 * 1024


def round_up(value, to):
    return (value + to - 1) // to * to


def call(kernel, out_shapes, scratch=(), vmem=VMEM_BYTES, name=None):
    return pl.pallas_call(
        kernel,
        out_shape=[jax.ShapeDtypeStruct(shape, F32) for shape in out_shapes],
        out_specs=[VMEM] * len(out_shapes),
        scratch_shapes=list(scratch),
        compiler_params=pltpu.CompilerParams(vmem_limit_bytes=vmem),
        name=name,
    )


def iota(shape, dim):
    return lax.broadcasted_iota(jnp.int32, shape, dim)


def state_rows(levels):
    return 2 * (levels - 1), levels - 1


def hist_rows(pairs):
    return pairs + 9, pairs + 3


def pack_kernel(levels, padded, *refs):
    sources, outs, targets, sems = refs[:9], refs[9:15], refs[15:22], refs[22]
    rows_ref, hist_ref = outs[:2]
    targets = targets[:4] + outs[4:6] + targets[4:]
    rows, cols = targets[2].shape
    copies = []
    for at, (source, target) in enumerate(zip(sources, targets)):
        if at == 0:
            target = target.at[:, pl.ds(0, source.shape[1]), :]
        if at == 8:
            source = source.at[:, pl.ds(0, rows), :]
        copies.append(pltpu.make_async_copy(source, target, sems.at[at]))
    for copy in copies:
        copy.start()
    for copy in copies[2:]:
        copy.wait()
    (
        state_ref, control_ref, depth_ref, spread_ref, step_ref, change_ref, damping_ref, weight_ref,
        observed_ref,
    ) = targets
    count = step_ref.shape[0] // (2 * rows)
    pairs = 2 * count
    close, distant = hist_rows(pairs)
    depth = depth_ref[...].astype(F32)
    spread = spread_ref[...]
    wet = depth > 0.5
    total = jnp.zeros((rows, cols), F32)
    for level in range(levels):
        total = total + jnp.where(level < depth, weight_ref[pl.ds(level * rows, rows), :], 0.0)
    fields = [
        damping_ref[...],
        2.0 * total,
        weight_ref[pl.ds(0, rows), :],
        observed_ref[0],
        observed_ref[1],
    ]
    for row in range(rows):
        here = slice(row, row + 1)
        for which, ref in enumerate((step_ref, change_ref)):
            both = [ref[pl.ds(tracer * rows + row, count, stride=2 * rows), :] for tracer in range(2)]
            apart = jnp.where(wet[here], both[0] - both[1], 0.0)
            hist_ref[row, pl.ds(which * count, count), :] = apart
    for copy in copies[:2]:
        copy.wait()
    first = iota((levels, cols), 0) == 0
    rest = jnp.zeros((padded - levels, cols), F32)
    for row in range(rows):
        here = slice(row, row + 1)
        for tracer in range(2):
            lift = jnp.where(wet[here], control_ref[tracer, here, :], 0.0)
            value = state_ref[tracer, pl.ds(row, levels, stride=rows), :]
            value = value + jnp.where(first, lift, 0.0)
            rows_ref[row, pl.ds(tracer * padded, levels), :] = value
            rows_ref[row, pl.ds(tracer * padded + levels, padded - levels), :] = rest
        for field, value in enumerate([spread, depth] + fields[:4]):
            rows_ref[row, pl.ds(levels + field, 1), :] = value[here]
        rows_ref[row, pl.ds(padded + levels, 1), :] = fields[4][here]

    even = lax.rem(lax.axis_index("loop"), 2) == 0

    def put(refs, at, upper, lower):
        here = pl.ds(at, upper.shape[0])
        refs[0][here, :] = jnp.where(even, upper, lower)
        refs[1][here, :] = jnp.where(even, lower, upper)

    masked = jnp.where(wet, spread, 0.0)
    for at in range(REACH):
        far = at < REACH - SUB
        index = at if far else at - (REACH - SUB)
        upper = rows - REACH + at if far else rows - SUB + index
        lower = SUB + index if far else index
        start = SUB * close + index * distant if far else index * close
        put(outs[2:4], start, hist_ref[upper], hist_ref[lower])
        start = start + pairs
        kind = masked if far else spread
        put(outs[2:4], start, kind[upper : upper + 1], kind[lower : lower + 1])
        for tracer in range(2):
            here = pl.ds(tracer * padded, 1)
            put(outs[2:4], start + 1 + tracer, rows_ref[upper, here, :], rows_ref[lower, here, :])
        if not far:
            here = pl.ds(levels + 2, 4)
            put(outs[2:4], start + 3, rows_ref[upper, here, :], rows_ref[lower, here, :])
            here = pl.ds(padded + levels, 1)
            put(outs[2:4], start + 7, rows_ref[upper, here, :], rows_ref[lower, here, :])
            put(outs[2:4], start + 8, depth[upper : upper + 1], depth[lower : lower + 1])
    last = SUB * close + (REACH - SUB) * distant
    folds = outs[2].shape[0] - FOLD
    if last < folds:
        rest = jnp.zeros((folds - last, cols), F32)
        put(outs[2:4], last, rest, rest)
    lat = lax.axis_index("lat")
    put(
        outs[2:4],
        folds,
        folded(edge_of(lambda i: rows_ref[rows - SUB + i], range(SUB), cols, lat)),
        folded(edge_of(lambda i: rows_ref[i], range(SUB), cols, lat)),
    )


def edge_of(rows_of, indices, cols, lat):
    lane = iota((1, cols), 1)
    slot = lane // SLOT
    place = lane % SLOT - SUB * lat
    mine = (place >= 0) & (place < SUB)
    total = None
    for index in indices:
        moved = pltpu.roll(rows_of(index), SLOT * index + SUB, 1)
        piece = jnp.where(mine & (slot == index), moved, 0.0)
        total = piece if total is None else total + piece
    return total


def folded(edge):
    planes, cols = edge.shape
    total = None
    for at, start in enumerate(range(0, planes, FOLD)):
        size = min(FOLD, planes - start)
        part = pltpu.roll(edge[start : start + size], FOLD * at, 1)
        if size < FOLD:
            part = jnp.concatenate([part, jnp.zeros((FOLD - size, cols), F32)], axis=0)
        total = part if total is None else total + part
    return total


def unfolded(fold, planes, lane_at):
    cols = fold.shape[1]
    lane = iota((1, cols), 1)
    here = (lane >= lane_at) & (lane < lane_at + FOLD)
    parts = []
    for at, start in enumerate(range(0, planes, FOLD)):
        part = pltpu.roll(fold, (lane_at - FOLD * at) % cols, 1)
        parts.append(jnp.where(here, part, 0.0)[: min(FOLD, planes - start)])
    return jnp.concatenate(parts, axis=0)


def level_face(levels, depth_here, depth_there, spread_here, spread_there):
    opened = levels < jnp.minimum(depth_here, depth_there)
    return jnp.where(opened, 0.5 * (spread_here + spread_there), 0.0)


def side_faces(level, depth, spread):
    cols = depth.shape[1]
    lane = iota((1, cols), 1)
    result = []
    for by, inside in ((cols - 1, lane < cols - 1), (1, lane > 0)):
        there = jnp.where(inside, pltpu.roll(depth, by, 1), 0.0)
        result.append(level_face(level, depth, there, spread, pltpu.roll(spread, by, 1)))
    return result


def mixed_row(get, faces, i, at):
    below, above, right, left = faces
    centre = get(i)[at, :]
    cols = centre.shape[1]
    total = centre + below * (get(i + 1)[at, :] - centre)
    total = total + above * (get(i - 1)[at, :] - centre)
    total = total + right * (pltpu.roll(centre, cols - 1, 1) - centre)
    return total + left * (pltpu.roll(centre, 1, 1) - centre)


def pairs_kernel(
    levels, padded, rows_ref, step_ref, change_ref,
    first_ref, second_ref, edge_ref, depth_ref, fixed_ref, face_ref, inner_ref,
):
    rows, _, cols = rows_ref.shape
    even = lax.rem(lax.axis_index("loop"), 2) == 0
    near, second = state_rows(levels)

    def put(at, upper, lower):
        here = pl.ds(at, upper.shape[0])
        first_ref[here, :] = jnp.where(even, upper, lower)
        second_ref[here, :] = jnp.where(even, lower, upper)

    for i in range(SUB):
        for start, size, place in ((1, levels - 1, 0), (padded + 1, levels - 1, second)):
            here = pl.ds(start, size)
            put(i * near + place, rows_ref[rows - SUB + i, here, :], rows_ref[i, here, :])
    if SUB * near < first_ref.shape[0]:
        rest = jnp.zeros((first_ref.shape[0] - SUB * near, cols), F32)
        put(SUB * near, rest, rest)
    level = iota((padded, cols), 0).astype(F32)
    spreads = [rows_ref[i, pl.ds(levels, 1), :] for i in range(rows)]
    depths = [rows_ref[i, pl.ds(levels + 1, 1), :] for i in range(rows)]
    for i in range(rows):
        if i + 1 < rows:
            face_ref[0, i] = level_face(level, depths[i], depths[i + 1], spreads[i], spreads[i + 1])
        face_ref[1, i], face_ref[2, i] = side_faces(level, depths[i], spreads[i])
    face_ref[0, rows - 1] = jnp.zeros((padded, cols), F32)
    for sweep in range(SUB):
        source = rows_ref if sweep == 0 else inner_ref.at[sweep - 1]
        for i in range(rows):
            for tracer in range(2):
                at = pl.ds(tracer * padded, padded)
                if sweep < i < rows - 1 - sweep:
                    faces = face_ref[0, i], face_ref[0, i - 1], face_ref[1, i], face_ref[2, i]
                    inner_ref[sweep, i, at, :] = mixed_row(lambda j: source.at[j], faces, i, at)
                else:
                    inner_ref[sweep, i, at, :] = jnp.zeros((padded, cols), F32)
    lat = lax.axis_index("lat")
    count = step_ref.shape[0]
    lane = iota((1, cols), 1)
    gram = [jnp.zeros((1, cols), F32) for _ in range(count)]
    at = FUNCTIONALS
    for left_ref in (step_ref, change_ref):
        for i in range(count):
            for j in range(i, count):
                value = jnp.sum(left_ref[i] * change_ref[j], axis=(0, 1), keepdims=True)
                gram[i] = gram[i] + jnp.where(lane == at + j, value, 0.0)
                if i != j:
                    gram[j] = gram[j] + jnp.where(lane == at + i, value, 0.0)
        at += count
    for i in range(count):
        fixed_ref[3, pl.ds(i, 1), :] = gram[i]
    for row in range(rows):
        plane = lambda at: rows_ref[row, pl.ds(levels + at, 1), :]
        here = pl.ds(row, 1)
        depth_ref[here, :] = plane(1)
        fixed_ref[0, here, :] = jnp.where(plane(1) > 0.5, plane(0), 0.0)
        fixed_ref[1, here, :] = plane(2)
        fixed_ref[2, here, :] = plane(3)
    edge_ref[...] = edge_of(lambda i: rows_ref[i - SUB], range(SUB, rows + SUB), cols, lat)


def faces_between(here, there, opened=True):
    return jnp.where((here > 0.0) & (there > 0.0) & opened, 0.5 * (here + there), 0.0)


def closed_lane(cols):
    return jnp.where(lax.axis_index("lat") == 0, 2 * cols - 1, cols - 1)


def surface_faces(spread, closed):
    height, width = spread.shape
    below = faces_between(spread, pltpu.roll(spread, height - 1, 0))
    right = faces_between(
        spread, pltpu.roll(spread, width - 1, 1), iota(spread.shape, 1) != closed
    )
    return below, pltpu.roll(below, 1, 0), right, pltpu.roll(right, 1, 1)


def gathered(mine_ref, other_ref, field):
    return jnp.concatenate(
        [
            jnp.concatenate([mine_ref[i, field], other_ref[i, field]], axis=1)
            for i in range(mine_ref.shape[0])
        ],
        axis=0,
    )


def surface_outflow(value, to_below, to_above, to_right, to_left):
    height, width = value.shape
    result = to_right * (value - pltpu.roll(value, width - 1, 1))
    result = result + to_left * (value - pltpu.roll(value, 1, 1))
    result = result + to_below * (value - pltpu.roll(value, height - 1, 0))
    return result + to_above * (value - pltpu.roll(value, 1, 0))


def plan_kernel(mine_ref, other_ref, faces_ref, plan_ref):
    loops, _, rows, cols = mine_ref.shape
    closed = closed_lane(cols)
    for at, face in enumerate(surface_faces(gathered(mine_ref, other_ref, 3), closed)):
        faces_ref[at] = SURFACE_GAIN * face
    for field in (4, 5):
        faces_ref[field] = gathered(mine_ref, other_ref, field)
    count = plan_ref.shape[0] // 2
    gram = mine_ref[0, 2] + other_ref[0, 2]
    for i in range(1, loops):
        gram = gram + (mine_ref[i, 2] + other_ref[i, 2])
    wide = (count, cols)
    tables = [
        jnp.broadcast_to(gram[:, i : i + 1], wide)
        for i in range(FUNCTIONALS, FUNCTIONALS + 2 * count)
    ]
    step_change, change_change = tables[:count], tables[count:]
    last = count - 1
    gamma = step_change[last][last:] / change_change[last][last:]
    rho = [1.0 / step_change[i][i : i + 1] for i in range(count)]
    row = iota(wide, 0)
    lane = iota(wide, 1)
    step_grad = jnp.where(lane == row, 1.0, 0.0)
    change_grad = jnp.where(lane == row + count, 1.0, 0.0)
    factors = [None] * count
    for i in range(count - 1, -1, -1):
        factors[i] = rho[i] * step_grad[i : i + 1]
        step_grad = step_grad - factors[i] * step_change[i]
        change_grad = change_grad - factors[i] * change_change[i]
    change_grad = gamma * change_grad
    for i in range(count):
        weight = factors[i] - rho[i] * change_grad[i : i + 1]
        change_grad = change_grad + weight * step_change[i]
        plan_ref[pl.ds(i, 1), :] = -weight
        plan_ref[pl.ds(count + i, 1), :] = gamma * factors[i]
    at = lane[:1] == 2 * count
    plan_ref[pl.ds(0, 1), :] = jnp.where(at, -gamma, plan_ref[pl.ds(0, 1), :])


def received(first_ref, second_ref):
    even = lax.rem(lax.axis_index("loop"), 2) == 0

    def low(at, size):
        here = pl.ds(at, size)
        return jnp.where(even, second_ref[here, :], first_ref[here, :])

    def high(at, size):
        here = pl.ds(at, size)
        return jnp.where(even, first_ref[here, :], second_ref[here, :])

    return low, high


def border_kernel(
    levels, padded, edge_ref, first_ref, second_ref, rows_ref, hist_ref, out_ref, swap_ref
):
    rows, pairs, cols = hist_ref.shape
    close, distant = hist_rows(pairs)
    low, high = received(first_ref, second_ref)
    tall = 3 * rows
    fields = (rows + 2 * REACH) * pairs
    out_ref[pl.ds(fields, 8 * tall), :] = jnp.zeros((8 * tall, cols), F32)
    lane = iota((1, cols), 1)
    place = lane % WIDE_SLOT - REACH * lax.axis_index("lat")
    sent = (place >= 0) & (place < REACH)
    slots = cols // WIDE_SLOT
    groups = [None] * slot_groups(rows, cols)
    for at in range(-REACH, rows + REACH):
        get = low if at < 0 else high
        limit = None
        if 0 <= at < rows:
            own = rows_ref.at[at]
            limit = levels + 1
            get = lambda place, size: own[pl.ds(place, size), :]
            apart = hist_ref[at]
            places = {0: levels, 6: 0, 7: padded, 5: padded + levels}
            places.update({1 + field: levels + 2 + field for field in range(4)})
        elif -SUB <= at < rows + SUB:
            start = (at + SUB if at < 0 else at - rows) * close
            apart = get(start, pairs)
            start = start + pairs
            places = {0: start, 6: start + 1, 7: start + 2}
            places.update({1 + field: start + 3 + field for field in range(5)})
            limit = start + 8
        else:
            start = SUB * close + (at + REACH if at < 0 else at - rows - SUB) * distant
            apart = get(start, pairs)
            start = start + pairs
            places = {0: start, 6: start + 1, 7: start + 2}
        out_ref[pl.ds((at + REACH) * pairs, pairs), :] = apart
        group, slot = divmod(at + REACH, slots)
        moved = pltpu.roll(apart, WIDE_SLOT * slot + REACH, 1)
        moved = jnp.where(sent & (lane // WIDE_SLOT == slot), moved, 0.0)
        groups[group] = moved if groups[group] is None else groups[group] + moved
        for field, place in places.items():
            value = get(place, 1)
            if field == 0 and limit is not None:
                value = jnp.where(get(limit, 1) > 0.5, value, 0.0)
            out_ref[pl.ds(fields + field * tall + at + rows, 1), :] = value
    for at, group in enumerate(groups):
        swap_ref[pl.ds(at * pairs, pairs), :] = group
    total = None
    for field in range(8):
        moved = pltpu.roll(
            out_ref[pl.ds(fields + field * tall, tall), :], WIDE_SLOT * field + REACH, 1
        )
        moved = jnp.where(sent & (lane // WIDE_SLOT == field), moved, 0.0)
        total = moved if total is None else total + moved
    at = len(groups) * pairs
    swap_ref[pl.ds(at, tall), :] = total
    at = at + tall
    planes = edge_ref.shape[0]
    folds = first_ref.shape[0] - FOLD
    before = unfolded(low(folds, FOLD), planes, 0)
    after = unfolded(high(folds, FOLD), planes, SLOT * (rows + SUB))
    swap_ref[pl.ds(at, planes), :] = edge_ref[...] + (before + after)
    at = at + planes
    if at < swap_ref.shape[0]:
        swap_ref[pl.ds(at, swap_ref.shape[0] - at), :] = jnp.zeros(
            (swap_ref.shape[0] - at, cols), F32
        )


def slot_groups(rows, cols):
    slots = cols // WIDE_SLOT
    return (rows + 2 * REACH + slots - 1) // slots


def basis_kernel(
    rows, pairs, mine_ref, other_ref, step_ref, change_ref,
    out_ref, near_ref, base_ref, first_ref, *work
):
    cols = mine_ref.shape[1]
    width = 2 * cols
    tall = rows + 2 * REACH
    ahead = REACH - SUB
    high = 3 * rows
    fields = tall * pairs
    closed = closed_lane(cols)
    opened = iota((1, width), 1) != closed
    slots = cols // WIDE_SLOT
    other_fields = slot_groups(rows, cols) * pairs
    beside_ref = work[-2]
    lane = iota((1, cols), 1)
    start = jnp.where(lax.axis_index("lat") == 0, 0, cols - REACH)
    at_border = (lane >= start) & (lane < start + REACH)

    packed = other_ref[pl.ds(other_fields, high), :]
    for at in range(8):
        there = pltpu.roll(packed, (cols - WIDE_SLOT * at - REACH) % cols, 1)
        beside_ref[pl.ds(at * high, high), :] = jnp.where(at_border, there, 0.0)

    def wide(at, size):
        there = pl.ds(at - fields, size)
        return jnp.concatenate([mine_ref[pl.ds(at, size), :], beside_ref[there, :]], axis=1)

    def left(value):
        return pltpu.roll(value, width - 1, 1)

    def right(value):
        return pltpu.roll(value, 1, 1)

    def field(at):
        return wide(fields + at * high, high)

    def field_row(at, i):
        return wide(fields + at * high + i - REACH + rows, 1)

    faces = surface_faces(field(0), closed)
    for at in range(4):
        near_ref[at] = faces[at]
    sea = jnp.where(field(0) > 0.0, 1.0, 0.0)
    weight = field(3)
    near_ref[4] = weight * sea
    near_ref[5] = sea
    value = [field(6), field(7)]
    for sweep in range(SUB):
        value = [part - surface_outflow(part, *faces) for part in value]
    value = [weight * (value[0] - field(4)), weight * (value[1] - field(5))]
    for sweep in range(SUB):
        value = [part - surface_outflow(part, *faces) for part in value]
    base = [(part * sea)[rows : 2 * rows, :cols] for part in value]
    for tracer in range(2):
        base_ref[tracer] = base[tracer]
    for i in range(pairs // 2):
        total = jnp.zeros((1, cols), F32)
        for at, ref in ((0, step_ref), (cols // 2, change_ref)):
            part = ref[i, pl.ds(0, rows), :] * base[0] + ref[i, pl.ds(rows, rows), :] * base[1]
            part = jnp.sum(part, axis=(0, 1), keepdims=True)
            total = total + jnp.where(lane == at, part, 0.0)
        first_ref[pl.ds(i, 1), :] = total

    spread = [field_row(0, i) for i in range(tall)]
    to_right = [faces_between(value, left(value), opened) for value in spread]
    to_left = [right(value) for value in to_right]
    to_below = [faces_between(spread[i], spread[i + 1]) for i in range(tall - 1)]
    inner = range(ahead, tall - ahead)
    damping = {i: (field_row(1, i) - SHIFT) * (1.0 / SPAN) for i in inner}
    response_weight = {i: field_row(2, i) for i in inner}
    weight = {i: field_row(3, i) for i in inner}
    gain = SURFACE_GAIN / SPAN

    def outflow(get, i):
        value = get(i)
        total = to_right[i] * (value - left(value)) + to_left[i] * (value - right(value))
        total = total + to_below[i] * (value - get(i + 1))
        return value, total + to_below[i - 1] * (value - get(i - 1))

    def mixed(get, ref, reach):
        for i in range(REACH - reach, REACH + rows + reach):
            value, out = outflow(get, i)
            ref[i] = value - out
        return lambda i: ref[i]

    def applied(get, ref, reach):
        for i in range(REACH - reach, REACH + rows + reach):
            value, out = outflow(get, i)
            ref[i] = damping[i] * value + gain * out
        return lambda i: ref[i]

    def keep(slot, get):
        for i in range(rows):
            out_ref[slot, i] = get(i + REACH)[:, :cols]

    for i in range(tall):
        group, slot = divmod(i, slots)
        there = other_ref[pl.ds(group * pairs, pairs), :]
        there = pltpu.roll(there, (cols - WIDE_SLOT * slot - REACH) % cols, 1)
        work[-1][i, :, :cols] = mine_ref[pl.ds(i * pairs, pairs), :]
        work[-1][i, :, cols:] = jnp.where(at_border, there, 0.0)
    get = lambda i: work[-1][i]
    for sweep in range(SUB):
        get = mixed(get, work[sweep], REACH - 1 - sweep)
    reach = REACH - SUB
    powers = [get]
    for power in range(1, ITERS):
        powers.append(applied(powers[-1], work[SUB + power - 1], reach - power))
    for power in range(ITERS):
        keep(power, powers[power])
    reach = ITERS - 1
    slot = ITERS
    at = SUB + ITERS - 1
    chains = []
    for factor, power in [(weight, 0)] + [(response_weight, power) for power in range(ITERS)]:
        get = powers[power]
        chains.append(lambda i, factor=factor, get=get: factor[i] * get(i))
    for power in range(1, ITERS):
        for index in range(len(chains)):
            chains[index] = applied(chains[index], work[at], reach - power)
            at += 1
            keep(slot + index * (ITERS - 1) + power - 1, chains[index])


def mix_kernel(
    levels, padded, pairs, rows_ref, first_ref, second_ref, first_hist_ref, second_hist_ref,
    own_face_ref, inner_ref, _, out_ref, face_ref, outer_ref, halo_ref
):
    rows, _, cols = rows_ref.shape
    count = rows + 2 * SUB
    near, second = state_rows(levels)
    rest = jnp.zeros((padded - levels, cols), F32)
    close, _ = hist_rows(pairs)
    state_of = received(first_ref, second_ref)
    hist_of = received(first_hist_ref, second_hist_ref)
    for i in range(2 * SUB):
        at = i % SUB * near
        start = i % SUB * close + pairs
        state, hist = state_of[i // SUB], hist_of[i // SUB]
        halo_ref[i, pl.ds(levels, padded - levels), :] = rest
        halo_ref[i, pl.ds(padded + levels, padded - levels), :] = rest
        halo_ref[i, pl.ds(0, 1), :] = hist(start + 1, 1)
        halo_ref[i, pl.ds(1, levels - 1), :] = state(at, levels - 1)
        halo_ref[i, pl.ds(levels, 1), :] = hist(start, 1)
        halo_ref[i, pl.ds(levels + 1, 1), :] = hist(start + 8, 1)
        halo_ref[i, pl.ds(padded, 1), :] = hist(start + 2, 1)
        halo_ref[i, pl.ds(padded + 1, levels - 1), :] = state(at + second, levels - 1)
    level = iota((padded, cols), 0).astype(F32)

    def state_row(i):
        if i < SUB:
            return halo_ref.at[i]
        return rows_ref.at[i - SUB] if i < SUB + rows else halo_ref.at[i - rows]

    def face(kind, i):
        last = SUB + rows - (1 if kind == 0 else 0)
        return own_face_ref[kind, i - SUB] if SUB <= i < last else face_ref[kind, i]

    spreads = [state_row(i)[pl.ds(levels, 1), :] for i in range(count)]
    depths = [state_row(i)[pl.ds(levels + 1, 1), :] for i in range(count)]
    for i in range(count - 1):
        if not SUB <= i < SUB + rows - 1:
            face_ref[0, i] = level_face(level, depths[i], depths[i + 1], spreads[i], spreads[i + 1])
        if i > 0 and not SUB <= i < SUB + rows:
            face_ref[1, i], face_ref[2, i] = side_faces(level, depths[i], spreads[i])

    def after(sweep):
        def get(i):
            if sweep == 0:
                return state_row(i)
            if SUB + sweep <= i < SUB + rows - sweep:
                return inner_ref.at[sweep - 1, i - SUB]
            return outer_ref.at[sweep - 1, i]

        return get

    for sweep in range(1, SUB + 1):
        for i in range(sweep, count - sweep):
            done = SUB + sweep <= i < SUB + rows - sweep
            if done and sweep < SUB:
                continue
            into = out_ref.at[i - SUB] if sweep == SUB else outer_ref.at[sweep - 1, i]
            for tracer in range(2):
                at = pl.ds(tracer * padded, padded)
                if done:
                    into[at, :] = inner_ref[sweep - 1, i - SUB, at, :]
                else:
                    faces = face(0, i), face(0, i - 1), face(1, i), face(2, i)
                    into[at, :] = mixed_row(after(sweep - 1), faces, i, at)


def hold_kernel(weight_hbm, observed_hbm, weight_ref, observed_ref, sems):
    size = weight_hbm.shape[0]
    copies = [
        pltpu.make_async_copy(weight_hbm, weight_ref.at[pl.ds(0, size), :], sems.at[0]),
        pltpu.make_async_copy(observed_hbm, observed_ref.at[:, pl.ds(0, size), :], sems.at[1]),
    ]
    for copy in copies:
        copy.start()
    for copy in copies:
        copy.wait()


def strip_kernel(levels, padded, edge_at, mine_ref, other_ref, _, out_ref):
    cols = mine_ref.shape[1]
    planes = 2 * padded
    edge_ref = mine_ref.at[pl.ds(edge_at, planes)]
    other_ref = other_ref.at[pl.ds(edge_at, planes)]
    lat = lax.axis_index("lat")
    lane = iota((1, cols), 1)
    place = lane % SLOT
    level = iota((padded, cols), 0).astype(F32)

    def left(value, by=1):
        return pltpu.roll(value, (cols - by) % cols, 1)

    def right(value, by=1):
        return pltpu.roll(value, by, 1)

    spread = edge_ref[pl.ds(levels, 1), :] + other_ref[pl.ds(levels, 1), :]
    depth = edge_ref[pl.ds(levels + 1, 1), :] + other_ref[pl.ds(levels + 1, 1), :]
    within = place < 2 * SUB - 1
    col_depth = jnp.minimum(depth, jnp.where(within, left(depth), 0.0))
    col_spread = 0.5 * (spread + left(spread))
    row_depth = jnp.minimum(depth, left(depth, SLOT))
    row_spread = 0.5 * (spread + left(spread, SLOT))

    def strip_face(limit, value):
        return jnp.where(level < limit, value, 0.0)

    to_left = strip_face(right(col_depth), right(col_spread))
    to_right = strip_face(col_depth, col_spread)
    to_above = strip_face(right(row_depth, SLOT), right(row_spread, SLOT))
    to_below = strip_face(row_depth, row_spread)
    out_of_low = place == jnp.where(lat == 0, SUB - 1, SLOT)
    out_of_high = place == jnp.where(lat == 0, SLOT, SUB)
    over_low = jnp.where(out_of_low, to_right, 0.0)
    over_high = jnp.where(out_of_high, to_left, 0.0)
    own_right = jnp.where(place == SUB - 1, 0.0, to_right)
    own_left = jnp.where(place == SUB, 0.0, to_left)

    def spread_out(value, east, west):
        before, after = right(value), left(value)
        above, below = right(value, SLOT), left(value, SLOT)
        total = value + east * (after - value) + west * (before - value)
        return total + to_below * (below - value) + to_above * (above - value)

    parts = []
    extras = [None, None]
    for tracer in range(2):
        at = pl.ds(tracer * padded, padded)
        parts.append(edge_ref[at, :] + other_ref[at, :])

    for sweep in range(1, SUB + 1):
        for tracer in range(2):
            part = parts[tracer]
            across = over_low * (left(part) - part) + over_high * (right(part) - part)
            extra = extras[tracer]
            if extra is not None:
                across = across + spread_out(extra, own_right, own_left)
            extras[tracer] = across
            if sweep < SUB:
                parts[tracer] = spread_out(part, to_right, to_left)

    for tracer in range(2):
        out_ref[pl.ds(tracer * padded, padded), :] = extras[tracer]


def fields_kernel(
    levels, padded, scale,
    rows_ref, main_ref, extra_ref, weight_ref, observed_ref, basis_ref, first_ref, fixed_ref,
    mixed_ref, fields_ref, part_ref,
):
    rows, _, cols = rows_ref.shape
    pairs = basis_ref.shape[2]
    lat = lax.axis_index("lat")
    lane = iota((1, cols), 1)
    place = lane % SLOT
    level = iota((padded, cols), 0).astype(F32)

    def left(value, by=1):
        return pltpu.roll(value, (cols - by) % cols, 1)

    def right(value, by=1):
        return pltpu.roll(value, by, 1)

    start = jnp.where(lat == 0, cols - SUB, 0)
    at_border = (lane >= start) & (lane < start + SUB)

    for row in range(rows):
        i = row + SUB
        at = pl.ds(row, levels, stride=rows)
        mixed = []
        for tracer in range(2):
            border = jnp.where(at_border, left(extra_ref[pl.ds(tracer * padded, padded), :], SLOT * i + SUB), 0.0)
            mixed.append((main_ref[row, pl.ds(tracer * padded, padded), :] + border)[:levels])
        wet = level[:levels] < rows_ref[row, pl.ds(levels + 1, 1), :]
        weight = weight_ref[at, :]
        misfit = []
        for tracer in range(2):
            mixed_ref[tracer, at, :] = mixed[tracer]
            misfit.append(weight * (mixed[tracer] - observed_ref[tracer, at, :]))
        here = pl.ds(row, 1)
        part_ref[0, here, :] = scale * jnp.sum(
            jnp.where(wet, mixed[0] - mixed[1], 0.0), axis=0, keepdims=True
        )
        part_ref[1, here, :] = jnp.sum(
            jnp.where(wet, misfit[1] - misfit[0], 0.0), axis=0, keepdims=True
        )
    sums = [None] * FUNCTIONALS

    def add(at, slot, row, factor):
        value = basis_ref[slot, row] * factor
        sums[at] = value if sums[at] is None else sums[at] + value

    for row in range(rows):
        here = pl.ds(row, 1)
        surface, base = part_ref[0, here, :], part_ref[1, here, :]
        fixed = lambda plane: rows_ref[row, pl.ds(levels + plane, 1), :]
        add(1, 0, row, fixed(4) * surface)
        for power in range(1, ITERS):
            add(1 + power, ITERS + power - 1, row, surface)
        for j in range(ITERS):
            add(1 + ITERS + j, j, row, base)
            at = 1 + 2 * ITERS + j * ITERS
            add(at, j, row, fixed(3) * surface)
            for power in range(1, ITERS):
                add(at + power, ITERS + (1 + j) * (ITERS - 1) + power - 1, row, surface)
    half = pairs // 2
    total = first_ref[...] + fixed_ref[3]
    for at in range(1, FUNCTIONALS):
        value = jnp.sum(sums[at], axis=1, keepdims=True)
        total = total + jnp.where(lane == at, value[:half], 0.0)
        total = total + jnp.where(lane == cols // 2 + at, value[half:], 0.0)
    part_ref[2] = total
    for field in range(3):
        part_ref[3 + field] = fixed_ref[field]
    for copy in range(fields_ref.shape[0]):
        fields_ref[copy] = part_ref[...]


def solve_kernel(
    levels, scale,
    mine_ref, other_ref, faces_ref, near_ref, base_ref, plan_ref, mixed_ref, depth_ref, step_ref,
    change_ref, state_ref, gradient_ref, direction_ref, kept_ref,
):
    loops, _, rows, cols = mine_ref.shape
    loop = lax.axis_index("loop")

    def total(value):
        parts = [
            value[i * rows : (i + 1) * rows, j * cols : (j + 1) * cols]
            for i in range(loops)
            for j in range(2)
        ]
        while len(parts) > 1:
            half = (len(parts) + 1) // 2
            parts = [a + b for a, b in zip(parts, parts[half:])] + parts[len(parts) - half : half]
        return jnp.sum(jnp.sum(parts[0], axis=1, keepdims=True), axis=0, keepdims=True)

    count = step_ref.shape[0]
    inner = mine_ref[0, 2] + other_ref[0, 2]
    for i in range(1, loops):
        inner = inner + (mine_ref[i, 2] + other_ref[i, 2])
    plan = plan_ref[...]
    shifted = pltpu.roll(inner, cols // 2, 1)
    linear = None
    for i in range(2 * count):
        source = inner if i < count else shifted
        part = plan[:, i : i + 1] * source[i % count : i % count + 1]
        linear = part if linear is None else linear + part
    gamma = plan[:1, 2 * count : 2 * count + 1]

    gained = [faces_ref[i] for i in range(4)]
    damping = faces_ref[4]

    def conjugate(rhs):
        residual = rhs
        search = rhs
        solution = jnp.zeros_like(rhs)
        norm_now = total(rhs * rhs)
        one = jnp.ones((1, 1), F32)
        residual_of = [one]
        search_of = [one]
        solution_of = []
        for sweep in range(ITERS):
            image = damping * search + surface_outflow(search, *gained)
            alpha = norm_now / total(search * image)
            solution = solution + alpha * search
            solution_of = add_up(solution_of, alpha, search_of)
            if sweep < ITERS - 1:
                residual = residual - alpha * image
                norm_next = total(residual * residual)
                beta = norm_next / norm_now
                search = residual + beta * search
                norm_now = norm_next
                image_of = [SHIFT * value for value in search_of]
                image_of = add_up(image_of, SPAN, [None] + search_of)
                residual_of = add_up(residual_of, -alpha, image_of)
                search_of = add_up(residual_of, beta, search_of)
        return solution, solution_of

    def add_up(terms, factor, others):
        result = list(terms) + [None] * (len(others) - len(terms))
        for at, value in enumerate(others):
            if value is not None:
                value = factor * value
                result[at] = value if result[at] is None else result[at] + value
        return result

    def near(slot, value):
        for i in range(loops):
            kept_ref[slot, i] = value[i * rows : (i + 1) * rows]
        return jnp.concatenate(
            [kept_ref[slot, lax.rem(loop + shift, loops)] for shift in (loops - 1, 0, 1)], axis=0
        )

    elevation, elevation_of = conjugate(gathered(mine_ref, other_ref, 0))
    pressure = gathered(mine_ref, other_ref, 1) + faces_ref[5] * elevation
    elevation = near(0, elevation)
    depth = depth_ref[...]
    here = elevation[rows : 2 * rows, :cols]
    for level in range(levels):
        at = pl.ds(level * rows, rows)
        change = jnp.where(level < depth, here, 0.0)
        state_ref[0, at, :] = mixed_ref[0, at, :] - change
        state_ref[1, at, :] = mixed_ref[1, at, :] + change
    response, response_of = conjugate(pressure)
    response = near(1, response)

    lane = iota((1, cols), 1)
    factor = jnp.where(lane == 0, 1.0, 0.0)
    for j in range(ITERS):
        factor = jnp.where(lane == 1 + j, -elevation_of[j], factor)
        part = scale * response_of[j]
        factor = jnp.where(lane == 1 + ITERS + j, part, factor)
        for k in range(ITERS):
            at = 1 + 2 * ITERS + j * ITERS + k
            factor = jnp.where(lane == at, part * elevation_of[k], factor)
    weights = jnp.sum(linear * factor, axis=1, keepdims=True)
    weights = [
        jnp.broadcast_to(weights[i : i + 1], (rows, cols)) for i in range(2 * count)
    ]

    sea = near_ref[5]
    carried = near_ref[4] * elevation - (scale * sea) * response
    faces = [near_ref[i] for i in range(4)]
    for sweep in range(SUB):
        carried = carried - surface_outflow(carried, *faces)
    carried = (sea * carried)[rows : 2 * rows, :cols]
    for tracer in range(2):
        at = pl.ds(tracer * rows, rows)
        gradient = base_ref[tracer] - carried if tracer == 0 else base_ref[tracer] + carried
        gradient_ref[tracer] = gradient
        value = gamma * gradient
        for i in range(count):
            value = value + weights[i] * step_ref[i, at, :]
            value = value + weights[count + i] * change_ref[i, at, :]
        direction_ref[tracer] = value


def on_device(
    state, observed, weight, control, depth_index, diffusivity, damping, history_step, history_change
):
    _, levels, rows, cols = state.shape
    count = history_step.shape[0]
    padded = round_up(levels + 6, 8)
    planes = 2 * padded
    loops = lax.axis_size("loop")
    lats = lax.axis_size("lat")
    blocks = loops * lats
    scale = levels ** (-0.5)
    flat = (2, levels * rows, cols)
    state = state.reshape(flat)
    observed = observed.reshape(flat)
    weight = weight.reshape(flat[1:])

    pairs = 2 * count
    inputs = (
        state, control, depth_index, diffusivity,
        history_step.reshape(-1, cols), history_change.reshape(-1, cols), damping, weight, observed,
    )
    whole = round_up(levels, 8) * rows
    held = [(2, whole, cols)] + [x.shape for x in inputs[1:-1]] + [(2, rows, cols)]
    close, distant = hist_rows(pairs)
    sent_hist = (round_up(SUB * close + (REACH - SUB) * distant, 8) + FOLD, cols)
    sent = (round_up(SUB * state_rows(levels)[0], 8), cols)
    stored = (2 * count * rows, cols)
    shapes = ((rows, planes, cols), (rows, pairs, cols), sent_hist, sent_hist, stored, stored)
    packed, hist, first_hist, second_hist, step, change = pl.pallas_call(
        functools.partial(pack_kernel, levels, padded),
        out_shape=[jax.ShapeDtypeStruct(shape, F32) for shape in shapes],
        in_specs=[pl.BlockSpec(memory_space=pltpu.HBM)] * len(inputs),
        out_specs=[VMEM] * len(shapes),
        scratch_shapes=[
            pltpu.VMEM(shape, x.dtype) for at, (shape, x) in enumerate(zip(held, inputs)) if at not in (4, 5)
        ]
        + [pltpu.SemaphoreType.DMA((len(inputs),))],
        compiler_params=pltpu.CompilerParams(vmem_limit_bytes=VMEM_BYTES),
        name="pack",
    )(*(pltpu.with_memory_space_constraint(x, pltpu.HBM) for x in inputs))
    partner = [(i, i ^ 1) for i in range(loops)]
    following = [(i, (i - 1 + 2 * (i % 2)) % loops) for i in range(loops)]
    swap = [(0, 1), (1, 0)]
    first_hist = lax.ppermute(first_hist, "loop", partner)
    step = step.reshape(count, 2 * rows, cols)
    change = change.reshape(count, 2 * rows, cols)
    second_hist = lax.ppermute(second_hist, "loop", following)
    first, second, edge, depth, fixed, own_face, inner = call(
        functools.partial(pairs_kernel, levels, padded),
        [
            sent, sent, (planes, cols), (rows, cols), (4, rows, cols), (3, rows, padded, cols),
            (SUB, rows, planes, cols),
        ],
        name="pairs",
    )(packed, step, change)
    first = lax.ppermute(first, "loop", partner)
    second = lax.ppermute(second, "loop", following)
    height = loops * rows
    large = VMEM_BYTES if loops <= 16 else 2 * VMEM_BYTES
    fields = 8 * 3 * rows
    fields = 8 * 3 * rows
    edge_at = slot_groups(rows, cols) * pairs + 3 * rows
    border, border_mine = call(
        functools.partial(border_kernel, levels, padded),
        [((rows + 2 * REACH) * pairs + fields, cols), (max(SWAP_ROWS, edge_at + planes), cols)],
        name="border",
    )(edge, first_hist, second_hist, packed, hist)
    border_other = lax.ppermute(border_mine, "lat", swap)
    held_weight, held_observed = pl.pallas_call(
        hold_kernel,
        out_shape=[jax.ShapeDtypeStruct(shape, F32) for shape in ((whole, cols), (2, whole, cols))],
        in_specs=[pl.BlockSpec(memory_space=pltpu.HBM)] * 2,
        out_specs=[VMEM] * 2,
        scratch_shapes=[pltpu.SemaphoreType.DMA((2,))],
        compiler_params=pltpu.CompilerParams(vmem_limit_bytes=VMEM_BYTES),
        name="hold",
    )(*(pltpu.with_memory_space_constraint(x, pltpu.HBM) for x in (weight, observed)))
    (extra,) = pl.pallas_call(
        functools.partial(strip_kernel, levels, padded, edge_at),
        out_shape=[jax.ShapeDtypeStruct((planes, cols), F32)],
        in_specs=[VMEM] * 2 + [pl.BlockSpec(memory_space=pl.ANY)],
        out_specs=[VMEM],
        compiler_params=pltpu.CompilerParams(vmem_limit_bytes=VMEM_BYTES),
        name="strip",
    )(border_mine, border_other, held_weight)
    fields_height = fields
    chains = 1 + ITERS
    buffers = SUB + ITERS + chains * (ITERS - 1)
    shapes = (
        (ITERS + chains * (ITERS - 1), rows, pairs, cols),
        (6, 3 * rows, 2 * cols),
        (2, rows, cols),
        (count, cols),
    )
    basis, around, base, near_start = pl.pallas_call(
        functools.partial(basis_kernel, rows, pairs),
        out_shape=[jax.ShapeDtypeStruct(shape, F32) for shape in shapes],
        in_specs=[VMEM] * 4,
        out_specs=[VMEM] * len(shapes),
        scratch_shapes=[pltpu.VMEM((rows + 2 * REACH, pairs, 2 * cols), F32)] * (buffers - 1)
        + [
            pltpu.VMEM((fields_height, cols), F32),
            pltpu.VMEM((rows + 2 * REACH, pairs, 2 * cols), F32),
        ],
        compiler_params=pltpu.CompilerParams(vmem_limit_bytes=VMEM_BYTES),
        name="basis",
    )(border, border_other, step, change)
    tall = rows + 2 * SUB
    (mixed,) = call(
        functools.partial(mix_kernel, levels, padded, pairs),
        [(rows, planes, cols)],
        scratch=[
            pltpu.VMEM((3, tall, padded, cols), F32),
            pltpu.VMEM((SUB - 1, tall, planes, cols), F32),
            pltpu.VMEM((2 * SUB, planes, cols), F32),
        ],
        name="mix",
    )(packed, first, second, first_hist, second_hist, own_face, inner, near_start)
    mixed, fields = call(
        functools.partial(fields_kernel, levels, padded, scale),
        [(2, whole, cols), (loops, 6, rows, cols)],
        scratch=[pltpu.VMEM((6, rows, cols), F32)],
        name="fields",
    )(packed, mixed, extra, held_weight, held_observed, basis, near_start, fixed)
    mine = lax.all_to_all(fields, "loop", 0, 0)
    theirs = lax.ppermute(mine, "lat", swap)
    faces, plan = call(
        plan_kernel, [(6, height, 2 * cols), (pairs, cols)], vmem=large, name="plan"
    )(mine, theirs)
    shapes = (flat, (2, rows, cols), (2, rows, cols))
    state_next, gradient, direction = call(
        functools.partial(solve_kernel, levels, scale),
        shapes,
        scratch=[pltpu.VMEM((2, loops, rows, 2 * cols), F32)],
        vmem=large,
        name="solve",
    )(mine, theirs, faces, around, base, plan, mixed, depth, step, change)
    return (state_next.reshape(2, levels, rows, cols), gradient, direction)


def solution(mesh):
    return jax.shard_map(
        on_device,
        mesh=mesh,
        in_specs=(
            P("members", None, "loop", "lat"),
            P("members", None, "loop", "lat"),
            P(None, "loop", "lat"),
            P("members", "loop", "lat"),
            P("loop", "lat"),
            P("loop", "lat"),
            P("loop", "lat"),
            P("members", None, "loop", "lat"),
            P("members", None, "loop", "lat"),
        ),
        out_specs=(
            P("members", None, "loop", "lat"),
            P("members", "loop", "lat"),
            P("members", "loop", "lat"),
        ),
        check_vma=False,
    )
```

```python
import functools

import jax
import jax.numpy as jnp
from jax import lax
from jax.experimental import pallas as pl
from jax.experimental.pallas import tpu as pltpu
from jax.sharding import PartitionSpec as P

ITERS = 3
SUB = 3
SURFACE_GAIN = 5.0
SLOT = 8
WIDE_SLOT = 16
FOLD = SLOT * SUB
SWAP_ROWS = 240
REACH = SUB + 2 * (ITERS - 1)
SHIFT = 5.0
SPAN = 5.0
FUNCTIONALS = 1 + ITERS + ITERS + ITERS * ITERS
GRID = ("loop", "lat")
VMEM = pl.BlockSpec(memory_space=pltpu.VMEM)
F32 = jnp.float32
VMEM_BYTES = 16 * 1024 * 1024


def round_up(value, to):
    return (value + to - 1) // to * to


def call(kernel, out_shapes, scratch=(), vmem=VMEM_BYTES, name=None):
    return pl.pallas_call(
        kernel,
        out_shape=[jax.ShapeDtypeStruct(shape, F32) for shape in out_shapes],
        out_specs=[VMEM] * len(out_shapes),
        scratch_shapes=list(scratch),
        compiler_params=pltpu.CompilerParams(vmem_limit_bytes=vmem),
        name=name,
    )


def iota(shape, dim):
    return lax.broadcasted_iota(jnp.int32, shape, dim)


def state_rows(levels):
    return 2 * (levels - 1), levels - 1


def hist_rows(pairs):
    return pairs + 9, pairs + 3


def pack_kernel(levels, padded, *refs):
    sources, outs, targets, sems = refs[:9], refs[9:15], refs[15:22], refs[22]
    rows_ref, hist_ref = outs[:2]
    targets = targets[:4] + outs[4:6] + targets[4:]
    rows, cols = targets[2].shape
    copies = []
    for at, (source, target) in enumerate(zip(sources, targets)):
        if at == 0:
            target = target.at[:, pl.ds(0, source.shape[1]), :]
        if at == 8:
            source = source.at[:, pl.ds(0, rows), :]
        copies.append(pltpu.make_async_copy(source, target, sems.at[at]))
    for copy in copies:
        copy.start()
    for copy in copies[2:]:
        copy.wait()
    (
        state_ref, control_ref, depth_ref, spread_ref, step_ref, change_ref, damping_ref, weight_ref,
        observed_ref,
    ) = targets
    count = step_ref.shape[0] // (2 * rows)
    pairs = 2 * count
    close, distant = hist_rows(pairs)
    depth = depth_ref[...].astype(F32)
    spread = spread_ref[...]
    wet = depth > 0.5
    total = jnp.zeros((rows, cols), F32)
    for level in range(levels):
        total = total + jnp.where(level < depth, weight_ref[pl.ds(level * rows, rows), :], 0.0)
    fields = [
        damping_ref[...],
        2.0 * total,
        weight_ref[pl.ds(0, rows), :],
        observed_ref[0],
        observed_ref[1],
    ]
    for row in range(rows):
        here = slice(row, row + 1)
        for which, ref in enumerate((step_ref, change_ref)):
            both = [ref[pl.ds(tracer * rows + row, count, stride=2 * rows), :] for tracer in range(2)]
            apart = jnp.where(wet[here], both[0] - both[1], 0.0)
            hist_ref[row, pl.ds(which * count, count), :] = apart
    for copy in copies[:2]:
        copy.wait()
    first = iota((levels, cols), 0) == 0
    rest = jnp.zeros((padded - levels, cols), F32)
    for row in range(rows):
        here = slice(row, row + 1)
        for tracer in range(2):
            lift = jnp.where(wet[here], control_ref[tracer, here, :], 0.0)
            value = state_ref[tracer, pl.ds(row, levels, stride=rows), :]
            value = value + jnp.where(first, lift, 0.0)
            rows_ref[row, pl.ds(tracer * padded, levels), :] = value
            rows_ref[row, pl.ds(tracer * padded + levels, padded - levels), :] = rest
        for field, value in enumerate([spread, depth] + fields[:4]):
            rows_ref[row, pl.ds(levels + field, 1), :] = value[here]
        rows_ref[row, pl.ds(padded + levels, 1), :] = fields[4][here]

    even = lax.rem(lax.axis_index("loop"), 2) == 0

    def put(refs, at, upper, lower):
        here = pl.ds(at, upper.shape[0])
        refs[0][here, :] = jnp.where(even, upper, lower)
        refs[1][here, :] = jnp.where(even, lower, upper)

    masked = jnp.where(wet, spread, 0.0)
    for at in range(REACH):
        far = at < REACH - SUB
        index = at if far else at - (REACH - SUB)
        upper = rows - REACH + at if far else rows - SUB + index
        lower = SUB + index if far else index
        start = SUB * close + index * distant if far else index * close
        put(outs[2:4], start, hist_ref[upper], hist_ref[lower])
        start = start + pairs
        kind = masked if far else spread
        put(outs[2:4], start, kind[upper : upper + 1], kind[lower : lower + 1])
        for tracer in range(2):
            here = pl.ds(tracer * padded, 1)
            put(outs[2:4], start + 1 + tracer, rows_ref[upper, here, :], rows_ref[lower, here, :])
        if not far:
            here = pl.ds(levels + 2, 4)
            put(outs[2:4], start + 3, rows_ref[upper, here, :], rows_ref[lower, here, :])
            here = pl.ds(padded + levels, 1)
            put(outs[2:4], start + 7, rows_ref[upper, here, :], rows_ref[lower, here, :])
            put(outs[2:4], start + 8, depth[upper : upper + 1], depth[lower : lower + 1])
    last = SUB * close + (REACH - SUB) * distant
    folds = outs[2].shape[0] - FOLD
    if last < folds:
        rest = jnp.zeros((folds - last, cols), F32)
        put(outs[2:4], last, rest, rest)
    lat = lax.axis_index("lat")
    put(
        outs[2:4],
        folds,
        folded(edge_of(lambda i: rows_ref[rows - SUB + i], range(SUB), cols, lat)),
        folded(edge_of(lambda i: rows_ref[i], range(SUB), cols, lat)),
    )


def edge_of(rows_of, indices, cols, lat):
    lane = iota((1, cols), 1)
    slot = lane // SLOT
    place = lane % SLOT - SUB * lat
    mine = (place >= 0) & (place < SUB)
    total = None
    for index in indices:
        moved = pltpu.roll(rows_of(index), SLOT * index + SUB, 1)
        piece = jnp.where(mine & (slot == index), moved, 0.0)
        total = piece if total is None else total + piece
    return total


def folded(edge):
    planes, cols = edge.shape
    total = None
    for at, start in enumerate(range(0, planes, FOLD)):
        size = min(FOLD, planes - start)
        part = pltpu.roll(edge[start : start + size], FOLD * at, 1)
        if size < FOLD:
            part = jnp.concatenate([part, jnp.zeros((FOLD - size, cols), F32)], axis=0)
        total = part if total is None else total + part
    return total


def unfolded(fold, planes, lane_at):
    cols = fold.shape[1]
    lane = iota((1, cols), 1)
    here = (lane >= lane_at) & (lane < lane_at + FOLD)
    parts = []
    for at, start in enumerate(range(0, planes, FOLD)):
        part = pltpu.roll(fold, (lane_at - FOLD * at) % cols, 1)
        parts.append(jnp.where(here, part, 0.0)[: min(FOLD, planes - start)])
    return jnp.concatenate(parts, axis=0)


def level_face(levels, depth_here, depth_there, spread_here, spread_there):
    opened = levels < jnp.minimum(depth_here, depth_there)
    return jnp.where(opened, 0.5 * (spread_here + spread_there), 0.0)


def side_faces(level, depth, spread):
    cols = depth.shape[1]
    lane = iota((1, cols), 1)
    result = []
    for by, inside in ((cols - 1, lane < cols - 1), (1, lane > 0)):
        there = jnp.where(inside, pltpu.roll(depth, by, 1), 0.0)
        result.append(level_face(level, depth, there, spread, pltpu.roll(spread, by, 1)))
    return result


def mixed_row(get, faces, i, at):
    below, above, right, left = faces
    centre = get(i)[at, :]
    cols = centre.shape[1]
    total = centre + below * (get(i + 1)[at, :] - centre)
    total = total + above * (get(i - 1)[at, :] - centre)
    total = total + right * (pltpu.roll(centre, cols - 1, 1) - centre)
    return total + left * (pltpu.roll(centre, 1, 1) - centre)


def pairs_kernel(
    levels, padded, rows_ref, step_ref, change_ref,
    first_ref, second_ref, edge_ref, depth_ref, fixed_ref, face_ref, inner_ref,
):
    rows, _, cols = rows_ref.shape
    even = lax.rem(lax.axis_index("loop"), 2) == 0
    near, second = state_rows(levels)

    def put(at, upper, lower):
        here = pl.ds(at, upper.shape[0])
        first_ref[here, :] = jnp.where(even, upper, lower)
        second_ref[here, :] = jnp.where(even, lower, upper)

    for i in range(SUB):
        for start, size, place in ((1, levels - 1, 0), (padded + 1, levels - 1, second)):
            here = pl.ds(start, size)
            put(i * near + place, rows_ref[rows - SUB + i, here, :], rows_ref[i, here, :])
    if SUB * near < first_ref.shape[0]:
        rest = jnp.zeros((first_ref.shape[0] - SUB * near, cols), F32)
        put(SUB * near, rest, rest)
    level = iota((padded, cols), 0).astype(F32)
    spreads = [rows_ref[i, pl.ds(levels, 1), :] for i in range(rows)]
    depths = [rows_ref[i, pl.ds(levels + 1, 1), :] for i in range(rows)]
    for i in range(rows):
        if i + 1 < rows:
            face_ref[0, i] = level_face(level, depths[i], depths[i + 1], spreads[i], spreads[i + 1])
        face_ref[1, i], face_ref[2, i] = side_faces(level, depths[i], spreads[i])
    face_ref[0, rows - 1] = jnp.zeros((padded, cols), F32)
    for sweep in range(SUB):
        source = rows_ref if sweep == 0 else inner_ref.at[sweep - 1]
        for i in range(rows):
            for tracer in range(2):
                at = pl.ds(tracer * padded, padded)
                if sweep < i < rows - 1 - sweep:
                    faces = face_ref[0, i], face_ref[0, i - 1], face_ref[1, i], face_ref[2, i]
                    inner_ref[sweep, i, at, :] = mixed_row(lambda j: source.at[j], faces, i, at)
                else:
                    inner_ref[sweep, i, at, :] = jnp.zeros((padded, cols), F32)
    lat = lax.axis_index("lat")
    count = step_ref.shape[0]
    lane = iota((1, cols), 1)
    gram = [jnp.zeros((1, cols), F32) for _ in range(count)]
    at = FUNCTIONALS
    for left_ref in (step_ref, change_ref):
        for i in range(count):
            for j in range(i, count):
                value = jnp.sum(left_ref[i] * change_ref[j], axis=(0, 1), keepdims=True)
                gram[i] = gram[i] + jnp.where(lane == at + j, value, 0.0)
                if i != j:
                    gram[j] = gram[j] + jnp.where(lane == at + i, value, 0.0)
        at += count
    for i in range(count):
        fixed_ref[3, pl.ds(i, 1), :] = gram[i]
    for row in range(rows):
        plane = lambda at: rows_ref[row, pl.ds(levels + at, 1), :]
        here = pl.ds(row, 1)
        depth_ref[here, :] = plane(1)
        fixed_ref[0, here, :] = jnp.where(plane(1) > 0.5, plane(0), 0.0)
        fixed_ref[1, here, :] = plane(2)
        fixed_ref[2, here, :] = plane(3)
    edge_ref[...] = edge_of(lambda i: rows_ref[i - SUB], range(SUB, rows + SUB), cols, lat)


def faces_between(here, there, opened=True):
    return jnp.where((here > 0.0) & (there > 0.0) & opened, 0.5 * (here + there), 0.0)


def closed_lane(cols):
    return jnp.where(lax.axis_index("lat") == 0, 2 * cols - 1, cols - 1)


def surface_faces(spread, closed):
    height, width = spread.shape
    below = faces_between(spread, pltpu.roll(spread, height - 1, 0))
    right = faces_between(
        spread, pltpu.roll(spread, width - 1, 1), iota(spread.shape, 1) != closed
    )
    return below, pltpu.roll(below, 1, 0), right, pltpu.roll(right, 1, 1)


def gathered(mine_ref, other_ref, field):
    return jnp.concatenate(
        [
            jnp.concatenate([mine_ref[i, field], other_ref[i, field]], axis=1)
            for i in range(mine_ref.shape[0])
        ],
        axis=0,
    )


def surface_outflow(value, to_below, to_above, to_right, to_left):
    height, width = value.shape
    result = to_right * (value - pltpu.roll(value, width - 1, 1))
    result = result + to_left * (value - pltpu.roll(value, 1, 1))
    result = result + to_below * (value - pltpu.roll(value, height - 1, 0))
    return result + to_above * (value - pltpu.roll(value, 1, 0))


def make_plan(mine_ref, other_ref, faces_ref, plan_ref):
    loops, _, rows, cols = mine_ref.shape
    closed = closed_lane(cols)
    for at, face in enumerate(surface_faces(gathered(mine_ref, other_ref, 3), closed)):
        faces_ref[at] = SURFACE_GAIN * face
    for field in (4, 5):
        faces_ref[field] = gathered(mine_ref, other_ref, field)
    count = plan_ref.shape[0] // 2
    gram = mine_ref[0, 2] + other_ref[0, 2]
    for i in range(1, loops):
        gram = gram + (mine_ref[i, 2] + other_ref[i, 2])
    wide = (count, cols)
    tables = [
        jnp.broadcast_to(gram[:, i : i + 1], wide)
        for i in range(FUNCTIONALS, FUNCTIONALS + 2 * count)
    ]
    step_change, change_change = tables[:count], tables[count:]
    last = count - 1
    gamma = step_change[last][last:] / change_change[last][last:]
    rho = [1.0 / step_change[i][i : i + 1] for i in range(count)]
    row = iota(wide, 0)
    lane = iota(wide, 1)
    step_grad = jnp.where(lane == row, 1.0, 0.0)
    change_grad = jnp.where(lane == row + count, 1.0, 0.0)
    factors = [None] * count
    for i in range(count - 1, -1, -1):
        factors[i] = rho[i] * step_grad[i : i + 1]
        step_grad = step_grad - factors[i] * step_change[i]
        change_grad = change_grad - factors[i] * change_change[i]
    change_grad = gamma * change_grad
    for i in range(count):
        weight = factors[i] - rho[i] * change_grad[i : i + 1]
        change_grad = change_grad + weight * step_change[i]
        plan_ref[pl.ds(i, 1), :] = -weight
        plan_ref[pl.ds(count + i, 1), :] = gamma * factors[i]
    at = lane[:1] == 2 * count
    plan_ref[pl.ds(0, 1), :] = jnp.where(at, -gamma, plan_ref[pl.ds(0, 1), :])


def received(first_ref, second_ref):
    even = lax.rem(lax.axis_index("loop"), 2) == 0

    def low(at, size):
        here = pl.ds(at, size)
        return jnp.where(even, second_ref[here, :], first_ref[here, :])

    def high(at, size):
        here = pl.ds(at, size)
        return jnp.where(even, first_ref[here, :], second_ref[here, :])

    return low, high


def border_kernel(
    levels, padded, edge_ref, first_ref, second_ref, rows_ref, hist_ref, out_ref, swap_ref
):
    rows, pairs, cols = hist_ref.shape
    close, distant = hist_rows(pairs)
    low, high = received(first_ref, second_ref)
    tall = 3 * rows
    fields = (rows + 2 * REACH) * pairs
    out_ref[pl.ds(fields, 8 * tall), :] = jnp.zeros((8 * tall, cols), F32)
    lane = iota((1, cols), 1)
    place = lane % WIDE_SLOT - REACH * lax.axis_index("lat")
    sent = (place >= 0) & (place < REACH)
    slots = cols // WIDE_SLOT
    groups = [None] * slot_groups(rows, cols)
    for at in range(-REACH, rows + REACH):
        get = low if at < 0 else high
        limit = None
        if 0 <= at < rows:
            own = rows_ref.at[at]
            limit = levels + 1
            get = lambda place, size: own[pl.ds(place, size), :]
            apart = hist_ref[at]
            places = {0: levels, 6: 0, 7: padded, 5: padded + levels}
            places.update({1 + field: levels + 2 + field for field in range(4)})
        elif -SUB <= at < rows + SUB:
            start = (at + SUB if at < 0 else at - rows) * close
            apart = get(start, pairs)
            start = start + pairs
            places = {0: start, 6: start + 1, 7: start + 2}
            places.update({1 + field: start + 3 + field for field in range(5)})
            limit = start + 8
        else:
            start = SUB * close + (at + REACH if at < 0 else at - rows - SUB) * distant
            apart = get(start, pairs)
            start = start + pairs
            places = {0: start, 6: start + 1, 7: start + 2}
        out_ref[pl.ds((at + REACH) * pairs, pairs), :] = apart
        group, slot = divmod(at + REACH, slots)
        moved = pltpu.roll(apart, WIDE_SLOT * slot + REACH, 1)
        moved = jnp.where(sent & (lane // WIDE_SLOT == slot), moved, 0.0)
        groups[group] = moved if groups[group] is None else groups[group] + moved
        for field, place in places.items():
            value = get(place, 1)
            if field == 0 and limit is not None:
                value = jnp.where(get(limit, 1) > 0.5, value, 0.0)
            out_ref[pl.ds(fields + field * tall + at + rows, 1), :] = value
    for at, group in enumerate(groups):
        swap_ref[pl.ds(at * pairs, pairs), :] = group
    total = None
    for field in range(8):
        moved = pltpu.roll(
            out_ref[pl.ds(fields + field * tall, tall), :], WIDE_SLOT * field + REACH, 1
        )
        moved = jnp.where(sent & (lane // WIDE_SLOT == field), moved, 0.0)
        total = moved if total is None else total + moved
    at = len(groups) * pairs
    swap_ref[pl.ds(at, tall), :] = total
    at = at + tall
    planes = edge_ref.shape[0]
    folds = first_ref.shape[0] - FOLD
    before = unfolded(low(folds, FOLD), planes, 0)
    after = unfolded(high(folds, FOLD), planes, SLOT * (rows + SUB))
    swap_ref[pl.ds(at, planes), :] = edge_ref[...] + (before + after)
    at = at + planes
    if at < swap_ref.shape[0]:
        swap_ref[pl.ds(at, swap_ref.shape[0] - at), :] = jnp.zeros(
            (swap_ref.shape[0] - at, cols), F32
        )


def slot_groups(rows, cols):
    slots = cols // WIDE_SLOT
    return (rows + 2 * REACH + slots - 1) // slots


def basis_kernel(
    rows, pairs, mine_ref, other_ref, step_ref, change_ref,
    out_ref, near_ref, base_ref, first_ref, *work
):
    cols = mine_ref.shape[1]
    width = 2 * cols
    tall = rows + 2 * REACH
    ahead = REACH - SUB
    high = 3 * rows
    fields = tall * pairs
    closed = closed_lane(cols)
    opened = iota((1, width), 1) != closed
    slots = cols // WIDE_SLOT
    other_fields = slot_groups(rows, cols) * pairs
    beside_ref = work[-2]
    lane = iota((1, cols), 1)
    start = jnp.where(lax.axis_index("lat") == 0, 0, cols - REACH)
    at_border = (lane >= start) & (lane < start + REACH)

    packed = other_ref[pl.ds(other_fields, high), :]
    for at in range(8):
        there = pltpu.roll(packed, (cols - WIDE_SLOT * at - REACH) % cols, 1)
        beside_ref[pl.ds(at * high, high), :] = jnp.where(at_border, there, 0.0)

    def wide(at, size):
        there = pl.ds(at - fields, size)
        return jnp.concatenate([mine_ref[pl.ds(at, size), :], beside_ref[there, :]], axis=1)

    def left(value):
        return pltpu.roll(value, width - 1, 1)

    def right(value):
        return pltpu.roll(value, 1, 1)

    def field(at):
        return wide(fields + at * high, high)

    def field_row(at, i):
        return wide(fields + at * high + i - REACH + rows, 1)

    faces = surface_faces(field(0), closed)
    for at in range(4):
        near_ref[at] = faces[at]
    sea = jnp.where(field(0) > 0.0, 1.0, 0.0)
    weight = field(3)
    near_ref[4] = weight * sea
    near_ref[5] = sea
    value = [field(6), field(7)]
    for sweep in range(SUB):
        value = [part - surface_outflow(part, *faces) for part in value]
    value = [weight * (value[0] - field(4)), weight * (value[1] - field(5))]
    for sweep in range(SUB):
        value = [part - surface_outflow(part, *faces) for part in value]
    base = [(part * sea)[rows : 2 * rows, :cols] for part in value]
    for tracer in range(2):
        base_ref[tracer] = base[tracer]
    for i in range(pairs // 2):
        total = jnp.zeros((1, cols), F32)
        for at, ref in ((0, step_ref), (cols // 2, change_ref)):
            part = ref[i, pl.ds(0, rows), :] * base[0] + ref[i, pl.ds(rows, rows), :] * base[1]
            part = jnp.sum(part, axis=(0, 1), keepdims=True)
            total = total + jnp.where(lane == at, part, 0.0)
        first_ref[pl.ds(i, 1), :] = total

    spread = [field_row(0, i) for i in range(tall)]
    to_right = [faces_between(value, left(value), opened) for value in spread]
    to_left = [right(value) for value in to_right]
    to_below = [faces_between(spread[i], spread[i + 1]) for i in range(tall - 1)]
    inner = range(ahead, tall - ahead)
    damping = {i: (field_row(1, i) - SHIFT) * (1.0 / SPAN) for i in inner}
    response_weight = {i: field_row(2, i) for i in inner}
    weight = {i: field_row(3, i) for i in inner}
    gain = SURFACE_GAIN / SPAN

    def outflow(get, i):
        value = get(i)
        total = to_right[i] * (value - left(value)) + to_left[i] * (value - right(value))
        total = total + to_below[i] * (value - get(i + 1))
        return value, total + to_below[i - 1] * (value - get(i - 1))

    def mixed(get, ref, reach):
        for i in range(REACH - reach, REACH + rows + reach):
            value, out = outflow(get, i)
            ref[i] = value - out
        return lambda i: ref[i]

    def applied(get, ref, reach):
        for i in range(REACH - reach, REACH + rows + reach):
            value, out = outflow(get, i)
            ref[i] = damping[i] * value + gain * out
        return lambda i: ref[i]

    def keep(slot, get):
        for i in range(rows):
            out_ref[slot, i] = get(i + REACH)[:, :cols]

    for i in range(tall):
        group, slot = divmod(i, slots)
        there = other_ref[pl.ds(group * pairs, pairs), :]
        there = pltpu.roll(there, (cols - WIDE_SLOT * slot - REACH) % cols, 1)
        work[-1][i, :, :cols] = mine_ref[pl.ds(i * pairs, pairs), :]
        work[-1][i, :, cols:] = jnp.where(at_border, there, 0.0)
    get = lambda i: work[-1][i]
    for sweep in range(SUB):
        get = mixed(get, work[sweep], REACH - 1 - sweep)
    reach = REACH - SUB
    powers = [get]
    for power in range(1, ITERS):
        powers.append(applied(powers[-1], work[SUB + power - 1], reach - power))
    for power in range(ITERS):
        keep(power, powers[power])
    reach = ITERS - 1
    slot = ITERS
    at = SUB + ITERS - 1
    chains = []
    for factor, power in [(weight, 0)] + [(response_weight, power) for power in range(ITERS)]:
        get = powers[power]
        chains.append(lambda i, factor=factor, get=get: factor[i] * get(i))
    for power in range(1, ITERS):
        for index in range(len(chains)):
            chains[index] = applied(chains[index], work[at], reach - power)
            at += 1
            keep(slot + index * (ITERS - 1) + power - 1, chains[index])


def mix_kernel(
    levels, padded, pairs, rows_ref, first_ref, second_ref, first_hist_ref, second_hist_ref,
    own_face_ref, inner_ref, _, out_ref, face_ref, outer_ref, halo_ref
):
    rows, _, cols = rows_ref.shape
    count = rows + 2 * SUB
    near, second = state_rows(levels)
    rest = jnp.zeros((padded - levels, cols), F32)
    close, _ = hist_rows(pairs)
    state_of = received(first_ref, second_ref)
    hist_of = received(first_hist_ref, second_hist_ref)
    for i in range(2 * SUB):
        at = i % SUB * near
        start = i % SUB * close + pairs
        state, hist = state_of[i // SUB], hist_of[i // SUB]
        halo_ref[i, pl.ds(levels, padded - levels), :] = rest
        halo_ref[i, pl.ds(padded + levels, padded - levels), :] = rest
        halo_ref[i, pl.ds(0, 1), :] = hist(start + 1, 1)
        halo_ref[i, pl.ds(1, levels - 1), :] = state(at, levels - 1)
        halo_ref[i, pl.ds(levels, 1), :] = hist(start, 1)
        halo_ref[i, pl.ds(levels + 1, 1), :] = hist(start + 8, 1)
        halo_ref[i, pl.ds(padded, 1), :] = hist(start + 2, 1)
        halo_ref[i, pl.ds(padded + 1, levels - 1), :] = state(at + second, levels - 1)
    level = iota((padded, cols), 0).astype(F32)

    def state_row(i):
        if i < SUB:
            return halo_ref.at[i]
        return rows_ref.at[i - SUB] if i < SUB + rows else halo_ref.at[i - rows]

    def face(kind, i):
        last = SUB + rows - (1 if kind == 0 else 0)
        return own_face_ref[kind, i - SUB] if SUB <= i < last else face_ref[kind, i]

    spreads = [state_row(i)[pl.ds(levels, 1), :] for i in range(count)]
    depths = [state_row(i)[pl.ds(levels + 1, 1), :] for i in range(count)]
    for i in range(count - 1):
        if not SUB <= i < SUB + rows - 1:
            face_ref[0, i] = level_face(level, depths[i], depths[i + 1], spreads[i], spreads[i + 1])
        if i > 0 and not SUB <= i < SUB + rows:
            face_ref[1, i], face_ref[2, i] = side_faces(level, depths[i], spreads[i])

    def after(sweep):
        def get(i):
            if sweep == 0:
                return state_row(i)
            if SUB + sweep <= i < SUB + rows - sweep:
                return inner_ref.at[sweep - 1, i - SUB]
            return outer_ref.at[sweep - 1, i]

        return get

    for sweep in range(1, SUB + 1):
        for i in range(sweep, count - sweep):
            done = SUB + sweep <= i < SUB + rows - sweep
            if done and sweep < SUB:
                continue
            into = out_ref.at[i - SUB] if sweep == SUB else outer_ref.at[sweep - 1, i]
            for tracer in range(2):
                at = pl.ds(tracer * padded, padded)
                if done:
                    into[at, :] = inner_ref[sweep - 1, i - SUB, at, :]
                else:
                    faces = face(0, i), face(0, i - 1), face(1, i), face(2, i)
                    into[at, :] = mixed_row(after(sweep - 1), faces, i, at)


def hold_kernel(weight_hbm, observed_hbm, weight_ref, observed_ref, sems):
    size = weight_hbm.shape[0]
    copies = [
        pltpu.make_async_copy(weight_hbm, weight_ref.at[pl.ds(0, size), :], sems.at[0]),
        pltpu.make_async_copy(observed_hbm, observed_ref.at[:, pl.ds(0, size), :], sems.at[1]),
    ]
    for copy in copies:
        copy.start()
    for copy in copies:
        copy.wait()


def strip_kernel(levels, padded, edge_at, mine_ref, other_ref, _, out_ref):
    cols = mine_ref.shape[1]
    planes = 2 * padded
    edge_ref = mine_ref.at[pl.ds(edge_at, planes)]
    other_ref = other_ref.at[pl.ds(edge_at, planes)]
    lat = lax.axis_index("lat")
    lane = iota((1, cols), 1)
    place = lane % SLOT
    level = iota((padded, cols), 0).astype(F32)

    def left(value, by=1):
        return pltpu.roll(value, (cols - by) % cols, 1)

    def right(value, by=1):
        return pltpu.roll(value, by, 1)

    spread = edge_ref[pl.ds(levels, 1), :] + other_ref[pl.ds(levels, 1), :]
    depth = edge_ref[pl.ds(levels + 1, 1), :] + other_ref[pl.ds(levels + 1, 1), :]
    within = place < 2 * SUB - 1
    col_depth = jnp.minimum(depth, jnp.where(within, left(depth), 0.0))
    col_spread = 0.5 * (spread + left(spread))
    row_depth = jnp.minimum(depth, left(depth, SLOT))
    row_spread = 0.5 * (spread + left(spread, SLOT))

    def strip_face(limit, value):
        return jnp.where(level < limit, value, 0.0)

    to_left = strip_face(right(col_depth), right(col_spread))
    to_right = strip_face(col_depth, col_spread)
    to_above = strip_face(right(row_depth, SLOT), right(row_spread, SLOT))
    to_below = strip_face(row_depth, row_spread)
    out_of_low = place == jnp.where(lat == 0, SUB - 1, SLOT)
    out_of_high = place == jnp.where(lat == 0, SLOT, SUB)
    over_low = jnp.where(out_of_low, to_right, 0.0)
    over_high = jnp.where(out_of_high, to_left, 0.0)
    own_right = jnp.where(place == SUB - 1, 0.0, to_right)
    own_left = jnp.where(place == SUB, 0.0, to_left)

    def spread_out(value, east, west):
        before, after = right(value), left(value)
        above, below = right(value, SLOT), left(value, SLOT)
        total = value + east * (after - value) + west * (before - value)
        return total + to_below * (below - value) + to_above * (above - value)

    parts = []
    extras = [None, None]
    for tracer in range(2):
        at = pl.ds(tracer * padded, padded)
        parts.append(edge_ref[at, :] + other_ref[at, :])

    for sweep in range(1, SUB + 1):
        for tracer in range(2):
            part = parts[tracer]
            across = over_low * (left(part) - part) + over_high * (right(part) - part)
            extra = extras[tracer]
            if extra is not None:
                across = across + spread_out(extra, own_right, own_left)
            extras[tracer] = across
            if sweep < SUB:
                parts[tracer] = spread_out(part, to_right, to_left)

    for tracer in range(2):
        out_ref[pl.ds(tracer * padded, padded), :] = extras[tracer]


def fields_kernel(
    levels, padded, scale,
    rows_ref, main_ref, extra_ref, weight_ref, observed_ref, basis_ref, first_ref, fixed_ref,
    mixed_ref, fields_ref, part_ref,
):
    rows, _, cols = rows_ref.shape
    pairs = basis_ref.shape[2]
    lat = lax.axis_index("lat")
    lane = iota((1, cols), 1)
    place = lane % SLOT
    level = iota((padded, cols), 0).astype(F32)

    def left(value, by=1):
        return pltpu.roll(value, (cols - by) % cols, 1)

    def right(value, by=1):
        return pltpu.roll(value, by, 1)

    start = jnp.where(lat == 0, cols - SUB, 0)
    at_border = (lane >= start) & (lane < start + SUB)

    for row in range(rows):
        i = row + SUB
        at = pl.ds(row, levels, stride=rows)
        mixed = []
        for tracer in range(2):
            border = jnp.where(at_border, left(extra_ref[pl.ds(tracer * padded, padded), :], SLOT * i + SUB), 0.0)
            mixed.append((main_ref[row, pl.ds(tracer * padded, padded), :] + border)[:levels])
        wet = level[:levels] < rows_ref[row, pl.ds(levels + 1, 1), :]
        weight = weight_ref[at, :]
        misfit = []
        for tracer in range(2):
            mixed_ref[tracer, at, :] = mixed[tracer]
            misfit.append(weight * (mixed[tracer] - observed_ref[tracer, at, :]))
        here = pl.ds(row, 1)
        part_ref[0, here, :] = scale * jnp.sum(
            jnp.where(wet, mixed[0] - mixed[1], 0.0), axis=0, keepdims=True
        )
        part_ref[1, here, :] = jnp.sum(
            jnp.where(wet, misfit[1] - misfit[0], 0.0), axis=0, keepdims=True
        )
    sums = [None] * FUNCTIONALS

    def add(at, slot, row, factor):
        value = basis_ref[slot, row] * factor
        sums[at] = value if sums[at] is None else sums[at] + value

    for row in range(rows):
        here = pl.ds(row, 1)
        surface, base = part_ref[0, here, :], part_ref[1, here, :]
        fixed = lambda plane: rows_ref[row, pl.ds(levels + plane, 1), :]
        add(1, 0, row, fixed(4) * surface)
        for power in range(1, ITERS):
            add(1 + power, ITERS + power - 1, row, surface)
        for j in range(ITERS):
            add(1 + ITERS + j, j, row, base)
            at = 1 + 2 * ITERS + j * ITERS
            add(at, j, row, fixed(3) * surface)
            for power in range(1, ITERS):
                add(at + power, ITERS + (1 + j) * (ITERS - 1) + power - 1, row, surface)
    half = pairs // 2
    total = first_ref[...] + fixed_ref[3]
    for at in range(1, FUNCTIONALS):
        value = jnp.sum(sums[at], axis=1, keepdims=True)
        total = total + jnp.where(lane == at, value[:half], 0.0)
        total = total + jnp.where(lane == cols // 2 + at, value[half:], 0.0)
    part_ref[2] = total
    for field in range(3):
        part_ref[3 + field] = fixed_ref[field]
    for copy in range(fields_ref.shape[0]):
        fields_ref[copy] = part_ref[...]


def solve_kernel(
    levels, scale,
    mine_ref, other_ref, near_ref, base_ref, mixed_ref, depth_ref, step_ref,
    change_ref, state_ref, gradient_ref, direction_ref, kept_ref, faces_ref, plan_ref,
):
    loops, _, rows, cols = mine_ref.shape
    loop = lax.axis_index("loop")
    make_plan(mine_ref, other_ref, faces_ref, plan_ref)

    def total(value):
        parts = [
            value[i * rows : (i + 1) * rows, j * cols : (j + 1) * cols]
            for i in range(loops)
            for j in range(2)
        ]
        while len(parts) > 1:
            half = (len(parts) + 1) // 2
            parts = [a + b for a, b in zip(parts, parts[half:])] + parts[len(parts) - half : half]
        return jnp.sum(jnp.sum(parts[0], axis=1, keepdims=True), axis=0, keepdims=True)

    count = step_ref.shape[0]
    inner = mine_ref[0, 2] + other_ref[0, 2]
    for i in range(1, loops):
        inner = inner + (mine_ref[i, 2] + other_ref[i, 2])
    plan = plan_ref[...]
    shifted = pltpu.roll(inner, cols // 2, 1)
    linear = None
    for i in range(2 * count):
        source = inner if i < count else shifted
        part = plan[:, i : i + 1] * source[i % count : i % count + 1]
        linear = part if linear is None else linear + part
    gamma = plan[:1, 2 * count : 2 * count + 1]

    gained = [faces_ref[i] for i in range(4)]
    damping = faces_ref[4]

    def conjugate(rhs):
        residual = rhs
        search = rhs
        solution = jnp.zeros_like(rhs)
        norm_now = total(rhs * rhs)
        one = jnp.ones((1, 1), F32)
        residual_of = [one]
        search_of = [one]
        solution_of = []
        for sweep in range(ITERS):
            image = damping * search + surface_outflow(search, *gained)
            alpha = norm_now / total(search * image)
            solution = solution + alpha * search
            solution_of = add_up(solution_of, alpha, search_of)
            if sweep < ITERS - 1:
                residual = residual - alpha * image
                norm_next = total(residual * residual)
                beta = norm_next / norm_now
                search = residual + beta * search
                norm_now = norm_next
                image_of = [SHIFT * value for value in search_of]
                image_of = add_up(image_of, SPAN, [None] + search_of)
                residual_of = add_up(residual_of, -alpha, image_of)
                search_of = add_up(residual_of, beta, search_of)
        return solution, solution_of

    def add_up(terms, factor, others):
        result = list(terms) + [None] * (len(others) - len(terms))
        for at, value in enumerate(others):
            if value is not None:
                value = factor * value
                result[at] = value if result[at] is None else result[at] + value
        return result

    def near(slot, value):
        for i in range(loops):
            kept_ref[slot, i] = value[i * rows : (i + 1) * rows]
        return jnp.concatenate(
            [kept_ref[slot, lax.rem(loop + shift, loops)] for shift in (loops - 1, 0, 1)], axis=0
        )

    elevation, elevation_of = conjugate(gathered(mine_ref, other_ref, 0))
    pressure = gathered(mine_ref, other_ref, 1) + faces_ref[5] * elevation
    elevation = near(0, elevation)
    depth = depth_ref[...]
    here = elevation[rows : 2 * rows, :cols]
    for level in range(levels):
        at = pl.ds(level * rows, rows)
        change = jnp.where(level < depth, here, 0.0)
        state_ref[0, at, :] = mixed_ref[0, at, :] - change
        state_ref[1, at, :] = mixed_ref[1, at, :] + change
    response, response_of = conjugate(pressure)
    response = near(1, response)

    lane = iota((1, cols), 1)
    factor = jnp.where(lane == 0, 1.0, 0.0)
    for j in range(ITERS):
        factor = jnp.where(lane == 1 + j, -elevation_of[j], factor)
        part = scale * response_of[j]
        factor = jnp.where(lane == 1 + ITERS + j, part, factor)
        for k in range(ITERS):
            at = 1 + 2 * ITERS + j * ITERS + k
            factor = jnp.where(lane == at, part * elevation_of[k], factor)
    weights = jnp.sum(linear * factor, axis=1, keepdims=True)
    weights = [
        jnp.broadcast_to(weights[i : i + 1], (rows, cols)) for i in range(2 * count)
    ]

    sea = near_ref[5]
    carried = near_ref[4] * elevation - (scale * sea) * response
    faces = [near_ref[i] for i in range(4)]
    for sweep in range(SUB):
        carried = carried - surface_outflow(carried, *faces)
    carried = (sea * carried)[rows : 2 * rows, :cols]
    for tracer in range(2):
        at = pl.ds(tracer * rows, rows)
        gradient = base_ref[tracer] - carried if tracer == 0 else base_ref[tracer] + carried
        gradient_ref[tracer] = gradient
        value = gamma * gradient
        for i in range(count):
            value = value + weights[i] * step_ref[i, at, :]
            value = value + weights[count + i] * change_ref[i, at, :]
        direction_ref[tracer] = value


def on_device(
    state, observed, weight, control, depth_index, diffusivity, damping, history_step, history_change
):
    _, levels, rows, cols = state.shape
    count = history_step.shape[0]
    padded = round_up(levels + 6, 8)
    planes = 2 * padded
    loops = lax.axis_size("loop")
    lats = lax.axis_size("lat")
    blocks = loops * lats
    scale = levels ** (-0.5)
    flat = (2, levels * rows, cols)
    state = state.reshape(flat)
    observed = observed.reshape(flat)
    weight = weight.reshape(flat[1:])

    pairs = 2 * count
    inputs = (
        state, control, depth_index, diffusivity,
        history_step.reshape(-1, cols), history_change.reshape(-1, cols), damping, weight, observed,
    )
    whole = round_up(levels, 8) * rows
    held = [(2, whole, cols)] + [x.shape for x in inputs[1:-1]] + [(2, rows, cols)]
    close, distant = hist_rows(pairs)
    sent_hist = (round_up(SUB * close + (REACH - SUB) * distant, 8) + FOLD, cols)
    sent = (round_up(SUB * state_rows(levels)[0], 8), cols)
    stored = (2 * count * rows, cols)
    shapes = ((rows, planes, cols), (rows, pairs, cols), sent_hist, sent_hist, stored, stored)
    packed, hist, first_hist, second_hist, step, change = pl.pallas_call(
        functools.partial(pack_kernel, levels, padded),
        out_shape=[jax.ShapeDtypeStruct(shape, F32) for shape in shapes],
        in_specs=[pl.BlockSpec(memory_space=pltpu.HBM)] * len(inputs),
        out_specs=[VMEM] * len(shapes),
        scratch_shapes=[
            pltpu.VMEM(shape, x.dtype) for at, (shape, x) in enumerate(zip(held, inputs)) if at not in (4, 5)
        ]
        + [pltpu.SemaphoreType.DMA((len(inputs),))],
        compiler_params=pltpu.CompilerParams(vmem_limit_bytes=VMEM_BYTES),
        name="pack",
    )(*(pltpu.with_memory_space_constraint(x, pltpu.HBM) for x in inputs))
    partner = [(i, i ^ 1) for i in range(loops)]
    following = [(i, (i - 1 + 2 * (i % 2)) % loops) for i in range(loops)]
    swap = [(0, 1), (1, 0)]
    first_hist = lax.ppermute(first_hist, "loop", partner)
    step = step.reshape(count, 2 * rows, cols)
    change = change.reshape(count, 2 * rows, cols)
    second_hist = lax.ppermute(second_hist, "loop", following)
    first, second, edge, depth, fixed, own_face, inner = call(
        functools.partial(pairs_kernel, levels, padded),
        [
            sent, sent, (planes, cols), (rows, cols), (4, rows, cols), (3, rows, padded, cols),
            (SUB, rows, planes, cols),
        ],
        name="pairs",
    )(packed, step, change)
    first = lax.ppermute(first, "loop", partner)
    second = lax.ppermute(second, "loop", following)
    height = loops * rows
    large = VMEM_BYTES if loops <= 16 else 2 * VMEM_BYTES
    fields = 8 * 3 * rows
    fields = 8 * 3 * rows
    edge_at = slot_groups(rows, cols) * pairs + 3 * rows
    border, border_mine = call(
        functools.partial(border_kernel, levels, padded),
        [((rows + 2 * REACH) * pairs + fields, cols), (max(SWAP_ROWS, edge_at + planes), cols)],
        name="border",
    )(edge, first_hist, second_hist, packed, hist)
    border_other = lax.ppermute(border_mine, "lat", swap)
    held_weight, held_observed = pl.pallas_call(
        hold_kernel,
        out_shape=[jax.ShapeDtypeStruct(shape, F32) for shape in ((whole, cols), (2, whole, cols))],
        in_specs=[pl.BlockSpec(memory_space=pltpu.HBM)] * 2,
        out_specs=[VMEM] * 2,
        scratch_shapes=[pltpu.SemaphoreType.DMA((2,))],
        compiler_params=pltpu.CompilerParams(vmem_limit_bytes=VMEM_BYTES),
        name="hold",
    )(*(pltpu.with_memory_space_constraint(x, pltpu.HBM) for x in (weight, observed)))
    (extra,) = pl.pallas_call(
        functools.partial(strip_kernel, levels, padded, edge_at),
        out_shape=[jax.ShapeDtypeStruct((planes, cols), F32)],
        in_specs=[VMEM] * 2 + [pl.BlockSpec(memory_space=pl.ANY)],
        out_specs=[VMEM],
        compiler_params=pltpu.CompilerParams(vmem_limit_bytes=VMEM_BYTES),
        name="strip",
    )(border_mine, border_other, held_weight)
    fields_height = fields
    chains = 1 + ITERS
    buffers = SUB + ITERS + chains * (ITERS - 1)
    shapes = (
        (ITERS + chains * (ITERS - 1), rows, pairs, cols),
        (6, 3 * rows, 2 * cols),
        (2, rows, cols),
        (count, cols),
    )
    basis, around, base, near_start = pl.pallas_call(
        functools.partial(basis_kernel, rows, pairs),
        out_shape=[jax.ShapeDtypeStruct(shape, F32) for shape in shapes],
        in_specs=[VMEM] * 4,
        out_specs=[VMEM] * len(shapes),
        scratch_shapes=[pltpu.VMEM((rows + 2 * REACH, pairs, 2 * cols), F32)] * (buffers - 1)
        + [
            pltpu.VMEM((fields_height, cols), F32),
            pltpu.VMEM((rows + 2 * REACH, pairs, 2 * cols), F32),
        ],
        compiler_params=pltpu.CompilerParams(vmem_limit_bytes=VMEM_BYTES),
        name="basis",
    )(border, border_other, step, change)
    tall = rows + 2 * SUB
    (mixed,) = call(
        functools.partial(mix_kernel, levels, padded, pairs),
        [(rows, planes, cols)],
        scratch=[
            pltpu.VMEM((3, tall, padded, cols), F32),
            pltpu.VMEM((SUB - 1, tall, planes, cols), F32),
            pltpu.VMEM((2 * SUB, planes, cols), F32),
        ],
        name="mix",
    )(packed, first, second, first_hist, second_hist, own_face, inner, near_start)
    mixed, fields = call(
        functools.partial(fields_kernel, levels, padded, scale),
        [(2, whole, cols), (loops, 6, rows, cols)],
        scratch=[pltpu.VMEM((6, rows, cols), F32)],
        name="fields",
    )(packed, mixed, extra, held_weight, held_observed, basis, near_start, fixed)
    mine = lax.all_to_all(fields, "loop", 0, 0)
    theirs = lax.ppermute(mine, "lat", swap)
    shapes = (flat, (2, rows, cols), (2, rows, cols))
    state_next, gradient, direction = call(
        functools.partial(solve_kernel, levels, scale),
        shapes,
        scratch=[
            pltpu.VMEM((2, loops, rows, 2 * cols), F32),
            pltpu.VMEM((6, height, 2 * cols), F32),
            pltpu.VMEM((pairs, cols), F32),
        ],
        vmem=large,
        name="solve",
    )(mine, theirs, around, base, mixed, depth, step, change)
    return (state_next.reshape(2, levels, rows, cols), gradient, direction)


def solution(mesh):
    return jax.shard_map(
        on_device,
        mesh=mesh,
        in_specs=(
            P("members", None, "loop", "lat"),
            P("members", None, "loop", "lat"),
            P(None, "loop", "lat"),
            P("members", "loop", "lat"),
            P("loop", "lat"),
            P("loop", "lat"),
            P("loop", "lat"),
            P("members", None, "loop", "lat"),
            P("members", None, "loop", "lat"),
        ),
        out_specs=(
            P("members", None, "loop", "lat"),
            P("members", "loop", "lat"),
            P("members", "loop", "lat"),
        ),
        check_vma=False,
    )
```
